32 devices in a mesh: expert: 4 (over y, x), cuts: 8 (over z, core).
Axes of the slice: x: 2, y: 2, z: 4, core: 2. Of those that a mesh axis runs over, the one named last changes fastest.
Arguments:
- tokens: bfloat16 [4, 2, 1024, 1024], P('expert', None, 'cuts'), may hold values from -6 to 6
- cotangent: bfloat16 [4, 2, 1024, 1024], P('expert', None, 'cuts'), may hold values from -6 to 6
- segments: int32 [4, 2, 1024], P('expert'), may hold values from 0 to 2, as said below
- expert_ids: int32 [4, 2, 1024], P('expert', None, 'cuts'), may hold values from 0 to 3
- slot_ids: int32 [4, 2, 1024], P('expert', None, 'cuts'), may hold values from 0 to 40, as said below
- kept_mask: int32 [4, 2, 1024], P('expert', None, 'cuts'), may hold values from 0 to 1, as said below
- norm1_gain: bfloat16 [1024], replicated, may hold values from 0.25 to 1.75
- w_query: bfloat16 [1024, 1024], replicated, may hold values from -0.1875 to 0.1875
- w_key: bfloat16 [1024, 1024], replicated, may hold values from -0.1875 to 0.1875
- w_value: bfloat16 [1024, 1024], replicated, may hold values from -0.1875 to 0.1875
- w_output: bfloat16 [1024, 1024], replicated, may hold values from -1.5 to 1.5
- norm2_gain: bfloat16 [1024], replicated, may hold values from 0.25 to 1.75
- dense_in: bfloat16 [1024, 4096], replicated, may hold values from -0.1875 to 0.1875
- dense_out: bfloat16 [4096, 1024], replicated, may hold values from -0.09375 to 0.09375
- router: bfloat16 [1024, 4], replicated, may hold values from -0.125 to 0.125
- mixer: bfloat16 [1024, 2], replicated, may hold values from -0.1875 to 0.1875
- expert_in: bfloat16 [4, 1024, 4096], P('expert', None, 'cuts'), may hold values from -0.1875 to 0.1875
- expert_out: bfloat16 [4, 4096, 1024], P('expert', 'cuts'), may hold values from -3 to 3
Outputs:
- output: bfloat16 [4, 2, 1024, 1024], P('expert', None, 'cuts')
- grad_tokens: float32 [4, 2, 1024, 1024], P('expert', None, 'cuts')
- grad_norm1: float32 [1024], P(('expert', 'cuts'))
- grad_query: float32 [1024, 1024], P(('expert', 'cuts'))
- grad_key: float32 [1024, 1024], P(('expert', 'cuts'))
- grad_value: float32 [1024, 1024], P(('expert', 'cuts'))
- grad_output: float32 [1024, 1024], P(('expert', 'cuts'))
- grad_norm2: float32 [1024], P(('expert', 'cuts'))
- grad_dense_in: float32 [1024, 4096], P(('expert', 'cuts'))
- grad_dense_out: float32 [4096, 1024], P(('expert', 'cuts'))
- grad_router: float32 [1024, 4], P(('expert', 'cuts'))
- grad_mixer: float32 [1024, 2], P(('expert', 'cuts'))
- grad_expert_in: float32 [4, 1024, 4096], P('expert', None, 'cuts')
- grad_expert_out: float32 [4, 4096, 1024], P('expert', 'cuts')
The draws below stay inside these ranges and needn't reach their ends.
Inputs may be any that keep to these rules, and one draw needn't show every extreme that they name: `segments`: document numbers never fall along a sequence; in every sequence the document numbered 1 begins within the first 128 positions and ends within the last 128. `slot_ids`: the rank of a token among the tokens of its block of 128 positions that go to the same expert, in order of position, or 40 where that rank is 40 or more. In every micro-batch one expert has more than 40 tokens in every block. `kept_mask`: 1 exactly where slot_ids is under 40.
All inputs are finite; a program needn't handle non-finite values.
Results may differ from the reference program's by a relative error of at most 0.02.
Values may be sent and summed in bfloat16 or wider, within the bound.
A program may use at most 256 MiB of HBM per device.

```python
import jax
import jax.numpy as jnp
from jax import lax

D = 1024
HEADS = 16
HD = 64
FF = 4096
EXPERTS = 4
TPM = 128
MICRO = 2
CAP = 40
SEQ = 1024
GROUPS = 4
N_CUTS = 8


def route_tables(key):
    first = jax.random.randint(jax.random.fold_in(key, 11), (GROUPS, MICRO, N_CUTS, TPM), 0, EXPERTS)
    second = jax.random.randint(jax.random.fold_in(key, 12), (GROUPS, MICRO, N_CUTS, TPM), 0, EXPERTS)
    order = jax.random.permutation(jax.random.fold_in(key, 13), EXPERTS)
    picks = order[jnp.minimum(first, second)]
    busiest = jax.random.randint(jax.random.fold_in(key, 14), (MICRO,), 0, EXPERTS)
    forced = jax.random.permutation(jax.random.fold_in(key, 15), TPM) < CAP + 2
    picks = jnp.where(forced[None, None, None, :], busiest[None, :, None, None], picks).astype(jnp.int32)
    onehot = (picks[..., None] == jnp.arange(EXPERTS, dtype=jnp.int32)).astype(jnp.int32)
    ranks = jnp.cumsum(onehot, axis=3) - 1
    slots = jnp.minimum(jnp.sum(onehot * ranks, axis=-1), CAP).astype(jnp.int32)
    return (picks, slots)


def draw_expert_ids(key, part):
    picks, slots = route_tables(key)
    return picks.reshape(GROUPS, MICRO, SEQ)


def draw_slot_ids(key, part):
    picks, slots = route_tables(key)
    return slots.reshape(GROUPS, MICRO, SEQ)


def draw_kept_mask(key, part):
    picks, slots = route_tables(key)
    return (slots < CAP).astype(jnp.int32).reshape(GROUPS, MICRO, SEQ)


def draw_segments(key, part):
    key = jax.random.fold_in(key, 5)
    leading = jax.random.randint(jax.random.fold_in(key, 1), (GROUPS, MICRO, 1), 0, TPM)
    trailing = jax.random.randint(jax.random.fold_in(key, 2), (GROUPS, MICRO, 1), SEQ - TPM + 1, SEQ + 1)
    spots = jnp.arange(SEQ, dtype=jnp.int32)[None, None, :]
    return ((spots >= leading).astype(jnp.int32) + (spots >= trailing).astype(jnp.int32)).astype(jnp.int32)


def spiked(drawn, own_key, source, target, blocks, factor):
    def block_of(dim):
        return (jnp.arange(drawn.shape[dim]) // (drawn.shape[dim] // blocks)).reshape((-1,) + (1,) * (drawn.ndim - 1 - dim))

    one_side = jax.random.permutation(own_key, blocks)[block_of(target)]
    second = (block_of(target) + blocks // 2) % blocks
    return jnp.where((block_of(source) == one_side) | (block_of(source) == second), factor * drawn, drawn)


def levels(stream_key, extent, shards, least, largest):
    def one(axis_at, shards_of):
        steps = jax.random.uniform(jax.random.fold_in(jax.random.fold_in(stream_key, 6), axis_at), (shards_of,), jnp.float32, least / len(shards), largest / len(shards))
        return jnp.repeat(jnp.exp(steps), extent[axis_at] // shards_of).reshape((-1,) + (1,) * (len(extent) - axis_at - 1))

    level = one(*shards[0])
    for cut in shards[1:]:
        level = level * one(*cut)
    return level


def normal_values(own_key, extent, scale, most, cuts=(), kind=jnp.bfloat16):
    level = levels(own_key, extent, cuts, -0.22, 0.18) if cuts else 1.0
    values = jax.random.normal(own_key, extent, jnp.float32) * scale * level
    return jnp.minimum(jnp.maximum(values, -most), most).astype(kind)


def noise_with(own_key, dims, width, reach, shards, heavy, kind=jnp.bfloat16):
    result = width * jax.random.normal(own_key, dims, jnp.float32)
    if shards:
        result = result * levels(own_key, dims, shards, -0.22, 0.18)
    return jnp.clip(spiked(result, jax.random.fold_in(own_key, 3), *heavy), -reach, reach).astype(kind)


def setup_inputs(seed: int = 0) -> dict:
    arg_keys = jax.random.split(jax.random.key(seed), 19)
    tokens = noise_with(arg_keys[0], (GROUPS, MICRO, SEQ, D), 1.0, 6.0, ((0, 4), (2, 8)), (0, 3, 4, 2.0))
    cotangent = normal_values(arg_keys[1], (GROUPS, MICRO, SEQ, D), 1.0, 6.0, ((0, 4), (2, 8)))
    segments = draw_segments(jax.random.fold_in(arg_keys[18], 71), 0)
    expert_ids = draw_expert_ids(jax.random.fold_in(arg_keys[18], 71), 0)
    slot_ids = draw_slot_ids(jax.random.fold_in(arg_keys[18], 71), 0)
    kept_mask = draw_kept_mask(jax.random.fold_in(arg_keys[18], 71), 0)
    norm1_gain = jnp.clip(1.0 + 0.15 * jax.random.normal(arg_keys[6], (D,), jnp.float32), 0.25, 1.75).astype(jnp.bfloat16)
    w_query = normal_values(arg_keys[7], (D, D), D ** -0.5, 0.1875)
    w_key = normal_values(arg_keys[8], (D, D), D ** -0.5, 0.1875)
    w_value = normal_values(arg_keys[9], (D, D), D ** -0.5, 0.1875)
    w_output = normal_values(arg_keys[10], (D, D), 16 ** -0.5, 1.5)
    norm2_gain = jnp.clip(1.0 + 0.15 * jax.random.normal(arg_keys[11], (D,), jnp.float32), 0.25, 1.75).astype(jnp.bfloat16)
    dense_in = normal_values(arg_keys[12], (D, FF), D ** -0.5, 0.1875)
    dense_out = normal_values(arg_keys[13], (FF, D), FF ** -0.5, 0.09375)
    router = normal_values(arg_keys[14], (D, EXPERTS), (2 * D) ** -0.5, 0.125)
    mixer = normal_values(arg_keys[15], (D, 2), D ** -0.5, 0.1875)
    expert_in = normal_values(arg_keys[16], (EXPERTS, D, FF), D ** -0.5, 0.1875, ((0, 4), (2, 8)))
    expert_out = normal_values(arg_keys[17], (EXPERTS, FF, D), (max(1, FF // 1024)) ** -0.5, 3.0, ((0, 4), (1, 8)))
    return {"tokens": tokens, "cotangent": cotangent, "segments": segments, "expert_ids": expert_ids, "slot_ids": slot_ids, "kept_mask": kept_mask, "norm1_gain": norm1_gain, "w_query": w_query, "w_key": w_key, "w_value": w_value, "w_output": w_output, "norm2_gain": norm2_gain, "dense_in": dense_in, "dense_out": dense_out, "router": router, "mixer": mixer, "expert_in": expert_in, "expert_out": expert_out}


score_scale = 0.125
masked_value = -1e+30
norm_eps = 1e-05

@jax.custom_vjp
def low(v):
    return lax.optimization_barrier(v.astype(jnp.bfloat16)).astype(jnp.float32)

@jax.custom_vjp
def low_back(v):
    return v

def low_keep(v):
    return (low(v), None)

def low_pass(kept, grad):
    return (grad,)

def back_keep(v):
    return (v, None)

def back_low(kept, grad):
    return (low(grad),)
low.defvjp(low_keep, low_pass)
low_back.defvjp(back_keep, back_low)

def matmul_high(left, right):
    return jnp.dot(left, right, precision=lax.Precision.HIGHEST, preferred_element_type=jnp.float32)

def layer_norm(values, gain):
    center = values - lax.optimization_barrier(jnp.mean(values, axis=-1, keepdims=True))
    spread = lax.optimization_barrier(jnp.mean(center * center, axis=-1, keepdims=True))
    return center * lax.rsqrt(spread + norm_eps) * gain

def gelu_exact(values):
    return jax.nn.gelu(values, approximate=False)

def softmax_rows(values):
    raised = jnp.exp(values - lax.optimization_barrier(jnp.max(values, axis=-1, keepdims=True)))
    return raised / lax.optimization_barrier(jnp.sum(raised, axis=-1, keepdims=True))

def mix_rows(norm_rows, router_w, mixer_w, dense_rows, expert_part, residual, hot_mask, kept_rows):
    logits = matmul_high(norm_rows, router_w)
    gate_value = lax.optimization_barrier(jnp.sum(jnp.where(hot_mask, softmax_rows(logits), 0.0), axis=-1)) * kept_rows
    mixing = softmax_rows(matmul_high(norm_rows, mixer_w))
    return residual + mixing[..., 0:1] * dense_rows + mixing[..., 1:2] * gate_value[..., None] * expert_part

def attend(query, keys, values, doc_row):
    spots = jnp.arange(SEQ, dtype=jnp.int32)
    key_heads = keys.reshape(SEQ, HEADS, HD)
    value_heads = values.reshape(SEQ, HEADS, HD)
    query_blocks = query.reshape(SEQ // TPM, TPM, HEADS, HD)
    starts = jnp.arange(SEQ // TPM, dtype=jnp.int32) * TPM

    def one_block(items):
        block, start = items
        places = start + jnp.arange(TPM, dtype=jnp.int32)
        query_docs = lax.dynamic_slice_in_dim(doc_row, start, TPM)
        raw = low_back(jnp.einsum('qhd,khd->hqk', block, key_heads, precision=lax.Precision.HIGHEST) * score_scale)
        allowed = (spots[None, :] <= places[:, None]) & (doc_row[None, :] == query_docs[:, None])
        masked = jnp.where(allowed[None], raw, masked_value)
        top = lax.optimization_barrier(jnp.max(masked, axis=-1, keepdims=True))
        logsum = top + jnp.log(lax.optimization_barrier(jnp.sum(jnp.exp(masked - top), axis=-1, keepdims=True)))
        probs = low(jnp.exp(masked - logsum))
        return jnp.einsum('hqk,khd->qhd', probs, value_heads, precision=lax.Precision.HIGHEST).reshape(TPM, D)
    return lax.map(jax.checkpoint(one_block), (query_blocks, starts)).reshape(SEQ, D)

def reference(tokens, cotangent, segments, expert_ids, slot_ids, kept_mask, norm1_gain, w_query, w_key, w_value, w_output, norm2_gain, dense_in, dense_out, router, mixer, expert_in, expert_out):
    blocks = GROUPS * MICRO * N_CUTS
    chosen = expert_ids.reshape(blocks, TPM).astype(jnp.int32)
    slot_rows = slot_ids.reshape(blocks, TPM).astype(jnp.int32)
    kept_int = kept_mask.reshape(blocks, TPM).astype(jnp.int32)
    columns = jnp.arange(EXPERTS * CAP, dtype=jnp.int32)
    table = jnp.where(((chosen * CAP + slot_rows)[..., None] == columns) & (kept_int[..., None] == 1), 1.0, 0.0).astype(jnp.float32)
    hot_mask = chosen[..., None] == jnp.arange(EXPERTS, dtype=jnp.int32)
    kept_rows = kept_int.astype(jnp.float32)
    doc_rows = segments.reshape(GROUPS * MICRO, SEQ).astype(jnp.int32)

    def forward(tokens_f, gain_one, wq, wk, wv, wo, gain_two, d_in, d_out, router_w, mixer_w, e_in, e_out):
        seqs = tokens_f.reshape(GROUPS * MICRO, SEQ, D)

        def token_part(items):
            x_rows, doc_row = items
            h_one = low(layer_norm(x_rows, gain_one))
            query = low(low_back(matmul_high(h_one, wq)))
            keys = low(low_back(matmul_high(h_one, wk)))
            values = low(low_back(matmul_high(h_one, wv)))
            attended = low(low_back(attend(query, keys, values, doc_row)))
            x_two = x_rows + low_back(matmul_high(attended, wo))
            h_two = low(layer_norm(x_two, gain_two))
            hidden = low(gelu_exact(low_back(matmul_high(h_two, d_in))))
            dense_rows = low_back(matmul_high(hidden, d_out))
            return (x_two, h_two, dense_rows)
        x_two, h_two, dense_rows = lax.map(jax.checkpoint(token_part), (seqs, doc_rows))
        x_two = x_two.reshape(blocks, TPM, D)
        h_two = h_two.reshape(blocks, TPM, D)
        dense_rows = dense_rows.reshape(blocks, TPM, D)
        sent = low_back(jnp.einsum('btc,btd->bcd', table, h_two, precision=lax.Precision.HIGHEST))
        grouped = sent.reshape(blocks, EXPERTS, CAP, D).transpose(1, 0, 2, 3).reshape(EXPERTS, blocks * CAP, D)

        def expert_part(items):
            rows_in, w_one, w_two = items
            inner = low(gelu_exact(low_back(matmul_high(rows_in, w_one))))
            return low(low_back(matmul_high(inner, w_two)))
        back = lax.map(jax.checkpoint(expert_part), (grouped, e_in, e_out))
        back = back.reshape(EXPERTS, blocks, CAP, D).transpose(1, 0, 2, 3).reshape(blocks, EXPERTS * CAP, D)
        from_experts = jnp.einsum('btc,bcd->btd', table, back, precision=lax.Precision.HIGHEST)
        mixed = mix_rows(h_two, router_w, mixer_w, dense_rows, from_experts, x_two, hot_mask, kept_rows)
        return mixed.reshape(GROUPS, MICRO, SEQ, D)
    output, pullback = jax.vjp(forward, tokens.astype(jnp.float32), norm1_gain.astype(jnp.float32), w_query.astype(jnp.float32), w_key.astype(jnp.float32), w_value.astype(jnp.float32), w_output.astype(jnp.float32), norm2_gain.astype(jnp.float32), dense_in.astype(jnp.float32), dense_out.astype(jnp.float32), router.astype(jnp.float32), mixer.astype(jnp.float32), expert_in.astype(jnp.float32), expert_out.astype(jnp.float32))
    grads = pullback(cotangent.astype(jnp.float32))
    return (output.astype(jnp.bfloat16), grads[0], grads[1], grads[2], grads[3], grads[4], grads[5], grads[6], grads[7], grads[8], grads[9], grads[10], grads[11], grads[12])
```

```python
from functools import partial

import jax
import jax.numpy as jnp
from jax import lax
from jax.experimental import pallas as pl
from jax.experimental.pallas import tpu as pltpu
from jax.sharding import PartitionSpec as P

MESH = pl.DeviceIdType.MESH
score_scale = 0.125
masked_value = -1e30
norm_eps = 1e-05


def softmax_rows(values):
    raised = jnp.exp(values - jnp.max(values, axis=-1, keepdims=True))
    return raised / jnp.sum(raised, axis=-1, keepdims=True)


def plain_dot(left, right):
    return jnp.dot(left, right, preferred_element_type=jnp.float32)


def lead_dot(left, right):
    return lax.dot_general(
        left, right, (((0,), (0,)), ((), ())), preferred_element_type=jnp.float32
    )


def tail_dot(left, right):
    return lax.dot_general(
        left, right, (((1,), (1,)), ((), ())), preferred_element_type=jnp.float32
    )


def greet_line(cut_count, every):
    cut = lax.axis_index("cuts")
    group = lax.axis_index("expert")
    barrier = pltpu.get_barrier_semaphore()
    hops = range(1, cut_count) if every else [1] + list(range(2, cut_count, 2))
    for hop in hops:
        pl.semaphore_signal(barrier, inc=1, device_id=(group, jnp.bitwise_xor(cut, hop)), device_id_type=MESH)
    pl.semaphore_wait(barrier, len(hops))


def gather_kernel(chain, x_ref, out_ref, send_sem, recv_sem, pair_send, pair_recv, own_sem):
    micro_count, cut_count = out_ref.shape[0], out_ref.shape[1]
    cut = lax.axis_index("cuts")
    group = lax.axis_index("expert")
    sibling = jnp.bitwise_xor(cut, 1)
    level, side = cut // 2, cut % 2
    levels = cut_count // 2
    greet_line(cut_count, False)

    def copy_to(m, src, source, target, ssem, rsem):
        return pltpu.make_async_remote_copy(
            src_ref=src, dst_ref=out_ref.at[m, source], send_sem=ssem, recv_sem=rsem,
            device_id=(group, target), device_id_type=MESH)

    own = []
    for m in range(micro_count):
        c = pltpu.make_async_copy(x_ref.at[m], out_ref.at[m, cut], own_sem.at[m])
        c.start()
        own.append(c)
    if chain:
        def hop(m, step, up, start):
            source = cut - 2 * step if up else cut + 2 * step
            target = cut + 2 if up else cut - 2
            ok = (level - step >= 0) & (level + 1 < levels) if up else (level + step < levels) & (level - 1 >= 0)
            src = x_ref.at[m] if step == 0 else out_ref.at[m, source]
            @pl.when(ok)
            def _():
                cp = copy_to(m, src, source, target, send_sem.at[m, step, 0 if up else 1], recv_sem.at[m, step, 0 if up else 1])
                if start:
                    cp.start()
                else:
                    cp.wait_send()
        def arrive(m, step, up):
            source = cut - 2 * (step + 1) if up else cut + 2 * (step + 1)
            ok = (level - step - 1 >= 0) if up else (level + step + 1 < levels)
            @pl.when(ok)
            def _():
                copy_to(m, x_ref.at[m], source, sibling, send_sem.at[m, step, 0 if up else 1], recv_sem.at[m, step, 0 if up else 1]).wait_recv()
            if step + 1 < levels - 1:
                hop(m, step + 1, up, True)
            @pl.when(ok)
            def _():
                copy_to(m, out_ref.at[m, source], source, sibling, pair_send.at[m, source], pair_recv.at[m, source]).start()
        for m in range(micro_count):
            hop(m, 0, True, True)
            hop(m, 0, False, True)
        for m in range(micro_count):
            copy_to(m, x_ref.at[m], cut, sibling, pair_send.at[m, cut], pair_recv.at[m, cut]).start()
        for step in range(levels - 1):
            for m in range(micro_count):
                arrive(m, step, True)
                arrive(m, step, False)
        for step in range(levels - 1):
            for m in range(micro_count):
                hop(m, step, True, False)
                hop(m, step, False, False)
    else:
        hops = list(range(2, cut_count, 2))
        def peer(m, k, hop_):
            return copy_to(m, x_ref.at[m], cut, jnp.bitwise_xor(cut, hop_), send_sem.at[m, k, 0], recv_sem.at[m, k, 0])
        for m in range(micro_count):
            for k, hop_ in enumerate(hops):
                peer(m, k, hop_).start()
            copy_to(m, x_ref.at[m], cut, sibling, pair_send.at[m, cut], pair_recv.at[m, cut]).start()
        for m in range(micro_count):
            for k, hop_ in enumerate(hops):
                source = jnp.bitwise_xor(cut, hop_)
                copy_to(m, x_ref.at[m], source, sibling, send_sem.at[m, k, 0], recv_sem.at[m, k, 0]).wait_recv()
                copy_to(m, out_ref.at[m, source], source, sibling, pair_send.at[m, source], pair_recv.at[m, source]).start()
        for m in range(micro_count):
            for k, hop_ in enumerate(hops):
                peer(m, k, hop_).wait_send()
    for m in range(micro_count):
        own[m].wait()
        for z in range(levels):
            mine = 2 * z + side
            theirs = 2 * z + 1 - side
            copy_to(m, out_ref.at[m, mine], mine, sibling, pair_send.at[m, mine], pair_recv.at[m, theirs]).wait_send()
            copy_to(m, out_ref.at[m, mine], theirs, sibling, pair_send.at[m, mine], pair_recv.at[m, theirs]).wait_recv()


def cut_gather(x, cut_count, call_id, chain=True, space=pltpu.VMEM):
    micro_count, rows, width = x.shape
    levels = cut_count // 2
    return pl.pallas_call(
        partial(gather_kernel, chain),
        out_shape=jax.ShapeDtypeStruct((micro_count, cut_count, rows, width), x.dtype),
        in_specs=[pl.BlockSpec(memory_space=pltpu.VMEM)],
        out_specs=pl.BlockSpec(memory_space=space),
        scratch_shapes=[
            pltpu.SemaphoreType.DMA((micro_count, levels - 1, 2)),
            pltpu.SemaphoreType.DMA((micro_count, levels - 1, 2)),
            pltpu.SemaphoreType.DMA((micro_count, cut_count)),
            pltpu.SemaphoreType.DMA((micro_count, cut_count)),
            pltpu.SemaphoreType.DMA((micro_count,)),
        ],
        compiler_params=pltpu.CompilerParams(collective_id=call_id, has_side_effects=True, vmem_limit_bytes=48 * 2**20),
    )(x)


def scatter_kernel(x_ref, out_ref, pair_buf, comb, far_buf, send_sem, recv_sem, pair_send, pair_recv):
    micro_count, cut_count, rows, width = x_ref.shape
    cut = lax.axis_index("cuts")
    group = lax.axis_index("expert")
    sibling = jnp.bitwise_xor(cut, 1)
    side = cut % 2
    levels = cut_count // 2
    greet_line(cut_count, False)
    hops = [levels - 1 - k for k in range(levels)]

    def pair_copy(m, k):
        dest = jnp.bitwise_xor(cut, 2 * k)
        return pltpu.make_async_remote_copy(
            src_ref=x_ref.at[m, jnp.bitwise_xor(dest, 1)], dst_ref=pair_buf.at[m, k],
            send_sem=pair_send.at[m, k], recv_sem=pair_recv.at[m, k],
            device_id=(group, sibling), device_id_type=MESH)

    def far_copy(m, k):
        return pltpu.make_async_remote_copy(
            src_ref=comb.at[m, k], dst_ref=far_buf.at[m, k],
            send_sem=send_sem.at[m, k], recv_sem=recv_sem.at[m, k],
            device_id=(group, jnp.bitwise_xor(cut, 2 * k)), device_id_type=MESH)

    for m in range(micro_count):
        for k in hops:
            pair_copy(m, k).start()
    for m in range(micro_count):
        for k in hops:
            pair_copy(m, k).wait_recv()
            total = x_ref[m, jnp.bitwise_xor(cut, 2 * k)].astype(jnp.float32) + pair_buf[m, k].astype(jnp.float32)
            if k:
                comb[m, k] = total.astype(comb.dtype)
                far_copy(m, k).start()
            else:
                out_ref[m] = total
    for m in range(micro_count):
        for k in hops:
            if k:
                far_copy(m, k).wait_recv()
                out_ref[m] = out_ref[m] + far_buf[m, k].astype(jnp.float32)
    for m in range(micro_count):
        for k in hops:
            pair_copy(m, k).wait_send()
            if k:
                far_copy(m, k).wait_send()


def cut_scatter(x, call_id):
    micro_count, cut_count, rows, width = x.shape
    levels = cut_count // 2
    return pl.pallas_call(
        scatter_kernel,
        out_shape=jax.ShapeDtypeStruct((micro_count, rows, width), jnp.float32),
        in_specs=[pl.BlockSpec(memory_space=pltpu.VMEM)],
        out_specs=pl.BlockSpec(memory_space=pltpu.VMEM),
        scratch_shapes=[
            pltpu.VMEM((micro_count, levels, rows, width), x.dtype),
            pltpu.VMEM((micro_count, levels, rows, width), x.dtype),
            pltpu.VMEM((micro_count, levels, rows, width), x.dtype),
            pltpu.SemaphoreType.DMA((micro_count, levels)),
            pltpu.SemaphoreType.DMA((micro_count, levels)),
            pltpu.SemaphoreType.DMA((micro_count, levels)),
            pltpu.SemaphoreType.DMA((micro_count, levels)),
        ],
        compiler_params=pltpu.CompilerParams(collective_id=call_id, has_side_effects=True, vmem_limit_bytes=48 * 2**20),
    )(x)


def swap_kernel(to_rows, x_ref, out_ref, send_sem, recv_sem, own_sem):
    micro_count = x_ref.shape[0]
    cut = lax.axis_index("cuts")
    group = lax.axis_index("expert")
    cut_count = max(x_ref.shape[1], out_ref.shape[1]) // min(x_ref.shape[1], out_ref.shape[1])
    rows = min(x_ref.shape[1], out_ref.shape[1])
    width = min(x_ref.shape[2], out_ref.shape[2])
    greet_line(cut_count, True)

    def by_rows(ref, m, who):
        return ref.at[m, pl.ds(pl.multiple_of(who * rows, rows), rows), :]

    def by_columns(ref, m, who):
        return ref.at[m, :, pl.ds(pl.multiple_of(who * width, width), width)]

    def copy(m, hop):
        target = jnp.bitwise_xor(cut, hop)
        src = by_rows(x_ref, m, target) if to_rows else by_columns(x_ref, m, target)
        dst = by_columns(out_ref, m, cut) if to_rows else by_rows(out_ref, m, cut)
        return pltpu.make_async_remote_copy(
            src_ref=src, dst_ref=dst, send_sem=send_sem.at[m, hop], recv_sem=recv_sem.at[m, hop],
            device_id=(group, target), device_id_type=MESH)

    for m in range(micro_count):
        for hop in range(cut_count - 1, 0, -1):
            copy(m, hop).start()
        src = by_rows(x_ref, m, cut) if to_rows else by_columns(x_ref, m, cut)
        dst = by_columns(out_ref, m, cut) if to_rows else by_rows(out_ref, m, cut)
        pltpu.make_async_copy(src, dst, own_sem.at[m]).start()
    for m in range(micro_count):
        for hop in range(cut_count - 1, 0, -1):
            copy(m, hop).wait()
        src = by_rows(x_ref, m, cut) if to_rows else by_columns(x_ref, m, cut)
        dst = by_columns(out_ref, m, cut) if to_rows else by_rows(out_ref, m, cut)
        pltpu.make_async_copy(src, dst, own_sem.at[m]).wait()


def cut_swap(x, cut_count, to_rows, call_id):
    micro_count, rows, width = x.shape
    shape = (micro_count, rows // cut_count, width * cut_count) if to_rows else (micro_count, rows * cut_count, width // cut_count)
    return pl.pallas_call(
        partial(swap_kernel, to_rows),
        out_shape=jax.ShapeDtypeStruct(shape, x.dtype),
        in_specs=[pl.BlockSpec(memory_space=pltpu.VMEM)],
        out_specs=pl.BlockSpec(memory_space=pltpu.VMEM),
        scratch_shapes=[
            pltpu.SemaphoreType.DMA((micro_count, cut_count)),
            pltpu.SemaphoreType.DMA((micro_count, cut_count)),
            pltpu.SemaphoreType.DMA((micro_count,)),
        ],
        compiler_params=pltpu.CompilerParams(collective_id=call_id, has_side_effects=True, vmem_limit_bytes=48 * 2**20),
    )(x)


def head_masks(width, heads):
    lane = lax.broadcasted_iota(jnp.int32, (1, width), 1)
    size = width // heads
    return [((lane >= h * size) & (lane < (h + 1) * size)) for h in range(heads)]


def allowed_mask(first_ref, start, rows, keys):
    query_spots = start + lax.broadcasted_iota(jnp.int32, (rows, keys), 0)
    key_spots = lax.broadcasted_iota(jnp.int32, (rows, keys), 1)
    return (key_spots <= query_spots) & (key_spots >= first_ref[0, pl.ds(start, rows), :])


def attend_kernel(heads, qkv_ref, first_ref, att_ref, lse_ref):
    length, width = att_ref.shape[1], att_ref.shape[2]
    rows = min(256, length)
    masks = head_masks(width, heads)
    for block in range(length // rows):
        start, keys = block * rows, (block + 1) * rows
        allowed = allowed_mask(first_ref, start, rows, keys)
        query = qkv_ref[0, pl.ds(start, rows), 0:width] * jnp.bfloat16(score_scale)
        key = qkv_ref[0, 0:keys, width : 2 * width]
        value = qkv_ref[0, 0:keys, 2 * width : 3 * width]
        att = jnp.zeros((rows, width), jnp.float32)
        logs = jnp.zeros((rows, width), jnp.float32)
        for mask in masks:
            scores = tail_dot(jnp.where(mask, query, jnp.bfloat16(0)), key)
            scores = jnp.where(allowed, scores, masked_value)
            top = jnp.max(scores, axis=-1, keepdims=True)
            raised = jnp.exp(scores - top)
            total = jnp.sum(raised, axis=-1, keepdims=True)
            probs = (raised * (1.0 / total)).astype(jnp.bfloat16)
            att = jnp.where(mask, plain_dot(probs, value), att)
            logs = jnp.where(mask, top + jnp.log(total), logs)
        att_ref[0, pl.ds(start, rows), :] = att.astype(jnp.bfloat16)
        lse_ref[0, pl.ds(start, rows), :] = logs


def attend(qkv, first, heads):
    micro_count, length, width = qkv.shape
    width = width // 3
    block = lambda w: pl.BlockSpec((1, length, w), lambda m: (m, 0, 0))
    return pl.pallas_call(
        partial(attend_kernel, heads),
        grid=(micro_count,),
        out_shape=(
            jax.ShapeDtypeStruct((micro_count, length, width), jnp.bfloat16),
            jax.ShapeDtypeStruct((micro_count, length, width), jnp.float32),
        ),
        in_specs=[block(3 * width), block(1)],
        out_specs=(block(width), block(width)),
        compiler_params=pltpu.CompilerParams(vmem_limit_bytes=48 * 2**20),
    )(qkv, first)


def attend_back_kernel(heads, qkv_ref, first_ref, lse_ref, back_ref, out_ref, key_acc, value_acc):
    length, width = back_ref.shape[1], back_ref.shape[2]
    rows = min(256, length)
    masks = head_masks(width, heads)
    key_acc[...] = jnp.zeros_like(key_acc)
    value_acc[...] = jnp.zeros_like(value_acc)
    zero = jnp.bfloat16(0)
    for block in range(length // rows):
        start, keys = block * rows, (block + 1) * rows
        allowed = allowed_mask(first_ref, start, rows, keys)
        query = qkv_ref[0, pl.ds(start, rows), 0:width] * jnp.bfloat16(score_scale)
        key = qkv_ref[0, 0:keys, width : 2 * width]
        value = qkv_ref[0, 0:keys, 2 * width : 3 * width]
        back = back_ref[0, pl.ds(start, rows), :]
        logs = lse_ref[0, pl.ds(start, rows), :]
        query_grad = jnp.zeros((rows, width), jnp.float32)
        for h, mask in enumerate(masks):
            one_query = jnp.where(mask, query, zero)
            one_back = jnp.where(mask, back, zero)
            scores = jnp.where(allowed, tail_dot(one_query, key), masked_value)
            spot = h * (width // heads)
            probs = jnp.exp(scores - logs[:, spot : spot + 1])
            dprobs = tail_dot(one_back, value)
            weighted = probs * dprobs
            delta = jnp.sum(weighted, axis=-1, keepdims=True)
            score_grad = (weighted - probs * delta).astype(jnp.bfloat16)
            query_grad = jnp.where(mask, plain_dot(score_grad, key), query_grad)
            key_acc[0:keys, :] += lead_dot(score_grad, one_query)
            value_acc[0:keys, :] += lead_dot(probs.astype(jnp.bfloat16), one_back)
        out_ref[0, pl.ds(start, rows), 0:width] = (query_grad * score_scale).astype(jnp.bfloat16)
    out_ref[0, :, width : 2 * width] = key_acc[...].astype(jnp.bfloat16)
    out_ref[0, :, 2 * width : 3 * width] = value_acc[...].astype(jnp.bfloat16)


def attend_back(qkv, first, lse, back, heads):
    micro_count, length, width = back.shape
    block = lambda w: pl.BlockSpec((1, length, w), lambda m: (m, 0, 0))
    return pl.pallas_call(
        partial(attend_back_kernel, heads),
        grid=(micro_count,),
        out_shape=jax.ShapeDtypeStruct((micro_count, length, 3 * width), jnp.bfloat16),
        in_specs=[block(3 * width), block(1), block(width), block(width)],
        out_specs=block(3 * width),
        scratch_shapes=[pltpu.VMEM((length, width), jnp.float32), pltpu.VMEM((length, width), jnp.float32)],
        compiler_params=pltpu.CompilerParams(vmem_limit_bytes=48 * 2**20),
    )(qkv, first, lse, back)


def norm_parts(values):
    center = values - jnp.mean(values, axis=-1, keepdims=True)
    spread = jnp.mean(center * center, axis=-1, keepdims=True)
    scale = lax.rsqrt(spread + norm_eps)
    return center * scale, scale


def norm_back(normed, scale, gain, grad):
    inner = grad * gain
    return scale * (
        inner
        - jnp.mean(inner, axis=-1, keepdims=True)
        - normed * jnp.mean(inner * normed, axis=-1, keepdims=True)
    )


def gelu_pair(values):
    phi = 0.5 * (1.0 + lax.erf(values * (0.5**0.5)))
    bell = jnp.exp(-0.5 * values * values) * ((2.0 * jnp.pi) ** -0.5)
    return values * phi, phi + values * bell


def softmax_back(probs, grad):
    return probs * (grad - jnp.sum(probs * grad, axis=-1, keepdims=True))


def local(
    tokens, cotangent, segments, expert_ids, slot_ids, kept_mask, norm1_gain, w_query, w_key, w_value, w_output,
    norm2_gain, dense_in, dense_out, router, mixer, expert_in, expert_out,
):
    micro_count, row_count, features = tokens.shape[1:]
    cut_count = lax.axis_size("cuts")
    group_count = lax.axis_size("expert")
    cut = lax.axis_index("cuts")
    length = cut_count * row_count
    head_width = features // cut_count
    heads = head_width // 64
    expert_count = router.shape[1]
    hidden_count = dense_in.shape[1]
    share = hidden_count // cut_count
    piece = share // group_count
    capacity = max(2, row_count * 5 // (4 * expert_count))
    slots = expert_count * capacity
    gain_one = norm1_gain.astype(jnp.float32)
    gain_two = norm2_gain.astype(jnp.float32)
    f32, low = jnp.float32, jnp.bfloat16

    code = jnp.where(kept_mask[0] == 1, expert_ids[0] * capacity + slot_ids[0], -1)
    codes = lax.all_gather(code, "cuts", axis=1, tiled=True)
    docs = segments[0]
    first = jnp.sum((docs[:, None, :] < docs[:, :, None]).astype(jnp.int32), axis=-1)[..., None]
    grad_all = lax.all_gather(cotangent[0], "cuts", axis=1, tiled=True)
    weights_in = lax.all_gather(expert_in[0], "expert", axis=0)
    weights_out = lax.all_gather(expert_out[0], "expert", axis=0)

    columns = lambda w: lax.dynamic_slice_in_dim(w, cut * head_width, head_width, 1)
    w_qkv = jnp.concatenate([columns(w_query), columns(w_key), columns(w_value)], axis=1)
    own_in = lax.dynamic_index_in_dim(
        dense_in.reshape(features, group_count, cut_count, piece), cut, 2, keepdims=False
    ).reshape(features, share)
    own_out = lax.dynamic_index_in_dim(
        dense_out.reshape(group_count, cut_count, piece, features), cut, 1, keepdims=False
    ).reshape(share, features)

    x_rows = tokens[0].astype(f32)
    norm_one, scale_one = norm_parts(x_rows)
    h_one = (norm_one * gain_one).astype(low)
    h_all = cut_gather(h_one, cut_count, 1).reshape(micro_count, length, features)
    qkv = jnp.einsum("mtf,fk->mtk", h_all, w_qkv, preferred_element_type=f32).astype(low)
    att_part, lse = attend(qkv, first, heads)
    attended = cut_swap(att_part, cut_count, True, 2).reshape(-1, features)
    x_two = x_rows.reshape(-1, features) + plain_dot(attended, w_output)
    norm_two, scale_two = norm_parts(x_two)
    h_two = (norm_two * gain_two).astype(low)
    h2_all = cut_gather(h_two.reshape(micro_count, row_count, features), cut_count, 3).reshape(-1, features)
    g_all = grad_all.reshape(-1, features)
    gy_all = g_all.astype(f32)
    tokens_all = micro_count * length

    code_all = codes.reshape(tokens_all)
    chosen = jnp.where(code_all >= 0, code_all // capacity, -1)
    hot = (chosen[:, None] == jnp.arange(expert_count, dtype=jnp.int32)[None, :]).astype(f32)
    routed = softmax_rows(plain_dot(h2_all, router))
    gate = jnp.sum(hot * routed, axis=-1, keepdims=True)
    mixing = softmax_rows(plain_dot(h2_all, mixer))
    mix_gate = mixing[:, 1:2] * gate

    pre = plain_dot(h2_all, own_in)
    act, slope = gelu_pair(pre)
    hidden = act.astype(low)
    dense_part = plain_dot(hidden, own_out)
    g_dense = (mixing[:, 0:1] * gy_all).astype(low)
    d_pre = (tail_dot(g_dense, own_out) * slope).astype(low)
    d_own_in = lead_dot(h2_all, d_pre)
    d_own_out = lead_dot(hidden, g_dense)

    blocks = tokens_all // row_count
    table = (code_all.reshape(blocks, row_count, 1) == jnp.arange(slots, dtype=jnp.int32)).astype(low)
    to_slots = lambda rows: (
        jnp.einsum("btc,btd->bcd", table, rows.reshape(blocks, row_count, features), preferred_element_type=f32)
        .astype(low)
        .reshape(blocks, expert_count, capacity, features)
        .transpose(1, 0, 2, 3)
        .reshape(expert_count, blocks * capacity, features)
    )
    to_rows = lambda rows: jnp.einsum(
        "btc,bcd->btd",
        table,
        rows.reshape(expert_count, blocks, capacity, features).transpose(1, 0, 2, 3).reshape(blocks, slots, features),
        preferred_element_type=f32,
    ).reshape(tokens_all, features)
    batched = lambda spec, a, b: jnp.einsum(spec, a, b, preferred_element_type=f32)
    sent = to_slots(h2_all)
    g_sent = to_slots((mix_gate * gy_all).astype(low))
    e_pre = batched("etf,efk->etk", sent, weights_in)
    e_act, e_slope = gelu_pair(e_pre)
    inner = e_act.astype(low)
    returned = batched("etk,ekf->etf", inner, weights_out).astype(low)
    d_e_pre = (batched("etf,ekf->etk", g_sent, weights_out) * e_slope).astype(low)
    d_sent = batched("etk,efk->etf", d_e_pre, weights_in).astype(low)
    d_weights_in = batched("etf,etk->efk", sent, d_e_pre).astype(low)
    d_weights_out = batched("etk,etf->ekf", inner, g_sent).astype(low)
    fe_part = to_rows(returned)

    dots = jnp.stack([jnp.sum(gy_all * dense_part, axis=-1), jnp.sum(gy_all * fe_part, axis=-1)], axis=-1)
    dots = lax.psum_scatter(
        dots.reshape(micro_count, length, 2), "cuts", scatter_dimension=1, tiled=True
    ).reshape(-1, 2)
    d_h2_part = (tail_dot(d_pre, own_in) + to_rows(d_sent)).astype(low)
    d_h2 = cut_scatter(d_h2_part.reshape(micro_count, cut_count, row_count, features), 4).reshape(-1, features)
    out_part = (mixing[:, 0:1] * dense_part + mix_gate * fe_part).astype(low)
    out_sum = lax.psum_scatter(
        out_part.reshape(micro_count, length, features), "cuts", scatter_dimension=1, tiled=True
    )
    output = (x_two.reshape(out_sum.shape) + out_sum.astype(f32)).astype(low)

    mine = lambda rows: lax.dynamic_slice_in_dim(
        rows.reshape(micro_count, length, -1), cut * row_count, row_count, 1
    ).reshape(micro_count * row_count, -1)
    gy = cotangent[0].reshape(-1, features).astype(f32)
    own_gate, own_mixing, own_hot, own_routed = mine(gate), mine(mixing), mine(hot), mine(routed)
    d_mixing = jnp.concatenate([dots[:, 0:1], own_gate * dots[:, 1:2]], axis=1)
    d_mixer_logits = softmax_back(own_mixing, d_mixing)
    d_router_logits = softmax_back(own_routed, own_hot * (own_mixing[:, 1:2] * dots[:, 1:2]))
    small = jnp.concatenate([router, mixer], axis=1).astype(f32)
    d_logits = jnp.concatenate([d_router_logits, d_mixer_logits], axis=1)
    d_h2 = d_h2 + lax.dot_general(d_logits, small, (((1,), (1,)), ((), ())), preferred_element_type=f32)
    d_small = lead_dot(h_two.astype(f32), d_logits)
    d_gain_two = jnp.sum(d_h2 * norm_two, axis=0)
    d_x_two = gy + norm_back(norm_two, scale_two, gain_two, d_h2)
    g_att = d_x_two.astype(low)
    d_output = lead_dot(attended, g_att)
    d_att = tail_dot(g_att, w_output).astype(low).reshape(micro_count, row_count, features)
    d_att_part = cut_swap(d_att, cut_count, False, 5)
    d_qkv = attend_back(qkv, first, lse, d_att_part, heads)
    d_w_qkv = lead_dot(h_all.reshape(tokens_all, features), d_qkv.reshape(tokens_all, -1))
    d_h1_part = tail_dot(d_qkv.reshape(tokens_all, -1), w_qkv).astype(low)
    d_h1 = cut_scatter(d_h1_part.reshape(micro_count, cut_count, row_count, features), 6)
    grad_tokens = d_x_two.reshape(d_h1.shape) + norm_back(norm_one, scale_one, gain_one, d_h1)

    rows = features // (group_count * cut_count)
    grad_expert_in = lax.psum_scatter(d_weights_in, "expert", scatter_dimension=0).astype(f32)
    grad_expert_out = lax.psum_scatter(d_weights_out, "expert", scatter_dimension=0).astype(f32)
    grad_dense_out = lax.psum_scatter(d_own_out.astype(low), "expert", scatter_dimension=0, tiled=True).astype(f32)

    def to_owner(part):
        summed = lax.psum_scatter(part.astype(low), "expert", scatter_dimension=0, tiled=True)
        return lax.all_to_all(summed.reshape(cut_count, rows, -1), "cuts", split_axis=0, concat_axis=0)

    grad_dense_in = (
        to_owner(d_own_in).astype(f32)
        .reshape(cut_count, rows, group_count, piece)
        .transpose(1, 2, 0, 3)
        .reshape(rows, hidden_count)
    )
    grad_qkv = to_owner(d_w_qkv).astype(f32).reshape(cut_count, rows, 3, head_width).transpose(2, 1, 0, 3)
    grad_qkv = grad_qkv.reshape(3, rows, features)
    wide = jnp.concatenate([d_output, d_small, d_gain_two[:, None]], axis=1).astype(low)
    wide = wide.reshape(group_count, cut_count, rows, -1).transpose(1, 0, 2, 3)
    wide = lax.psum_scatter(wide, "cuts", scatter_dimension=0)
    wide = lax.psum_scatter(wide, "expert", scatter_dimension=0).astype(f32)
    grad_output = wide[:, :features]
    grad_router = wide[:, features : features + expert_count]
    grad_mixer = wide[:, features + expert_count : -1]
    grad_norm2 = wide[:, -1]

    place = (lax.axis_index("expert") * cut_count + cut) * rows
    own_rows = lambda w: lax.dynamic_slice_in_dim(w, place, rows, 0).astype(f32)
    grad_norm1 = sum(
        jnp.sum(own_rows(w) * grad_qkv[k], axis=-1) for k, w in enumerate((w_query, w_key, w_value))
    ) / own_rows(gain_one)
    return (
        output[None], grad_tokens[None], grad_norm1, grad_qkv[0], grad_qkv[1], grad_qkv[2], grad_output, grad_norm2,
        grad_dense_in, grad_dense_out, grad_router, grad_mixer, grad_expert_in[None], grad_expert_out[None],
    )


def solution(mesh):
    in_specs = (
        P("expert", None, "cuts", None),
        P("expert", None, "cuts", None),
        P("expert", None, None),
        P("expert", None, "cuts"),
        P("expert", None, "cuts"),
        P("expert", None, "cuts"),
        P(),
        P(),
        P(),
        P(),
        P(),
        P(),
        P(),
        P(),
        P(),
        P(),
        P("expert", None, "cuts"),
        P("expert", "cuts", None),
    )
    out_specs = (
        P("expert", None, "cuts", None),
        P("expert", None, "cuts", None),
        P(("expert", "cuts")),
        P(("expert", "cuts"), None),
        P(("expert", "cuts"), None),
        P(("expert", "cuts"), None),
        P(("expert", "cuts"), None),
        P(("expert", "cuts")),
        P(("expert", "cuts"), None),
        P(("expert", "cuts"), None),
        P(("expert", "cuts"), None),
        P(("expert", "cuts"), None),
        P("expert", None, "cuts"),
        P("expert", "cuts", None),
    )
    return jax.shard_map(local, mesh=mesh, in_specs=in_specs, out_specs=out_specs, check_vma=False)
```

```python
from functools import partial

import jax
import jax.numpy as jnp
from jax import lax
from jax.experimental import pallas as pl
from jax.experimental.pallas import tpu as pltpu
from jax.sharding import PartitionSpec as P

MESH = pl.DeviceIdType.MESH
score_scale = 0.125
masked_value = -1e30
norm_eps = 1e-05


def softmax_rows(values):
    raised = jnp.exp(values - jnp.max(values, axis=-1, keepdims=True))
    return raised / jnp.sum(raised, axis=-1, keepdims=True)


def plain_dot(left, right):
    return jnp.dot(left, right, preferred_element_type=jnp.float32)


def lead_dot(left, right):
    return lax.dot_general(
        left, right, (((0,), (0,)), ((), ())), preferred_element_type=jnp.float32
    )


def tail_dot(left, right):
    return lax.dot_general(
        left, right, (((1,), (1,)), ((), ())), preferred_element_type=jnp.float32
    )


def greet_line(cut_count, every):
    cut = lax.axis_index("cuts")
    group = lax.axis_index("expert")
    barrier = pltpu.get_barrier_semaphore()
    hops = range(1, cut_count) if every else [1] + list(range(2, cut_count, 2))
    for hop in hops:
        pl.semaphore_signal(barrier, inc=1, device_id=(group, jnp.bitwise_xor(cut, hop)), device_id_type=MESH)
    pl.semaphore_wait(barrier, len(hops))


def gather_kernel(chain, x_ref, out_ref, send_sem, recv_sem, pair_send, pair_recv, own_sem):
    micro_count, cut_count = out_ref.shape[0], out_ref.shape[1]
    cut = lax.axis_index("cuts")
    group = lax.axis_index("expert")
    sibling = jnp.bitwise_xor(cut, 1)
    level, side = cut // 2, cut % 2
    levels = cut_count // 2
    greet_line(cut_count, False)

    def copy_to(m, src, source, target, ssem, rsem):
        return pltpu.make_async_remote_copy(
            src_ref=src, dst_ref=out_ref.at[m, source], send_sem=ssem, recv_sem=rsem,
            device_id=(group, target), device_id_type=MESH)

    own = []
    for m in range(micro_count):
        c = pltpu.make_async_copy(x_ref.at[m], out_ref.at[m, cut], own_sem.at[m])
        c.start()
        own.append(c)
    if chain:
        def hop(m, step, up, start):
            source = cut - 2 * step if up else cut + 2 * step
            target = cut + 2 if up else cut - 2
            ok = (level - step >= 0) & (level + 1 < levels) if up else (level + step < levels) & (level - 1 >= 0)
            src = x_ref.at[m] if step == 0 else out_ref.at[m, source]
            @pl.when(ok)
            def _():
                cp = copy_to(m, src, source, target, send_sem.at[m, step, 0 if up else 1], recv_sem.at[m, step, 0 if up else 1])
                if start:
                    cp.start()
                else:
                    cp.wait_send()
        def arrive(m, step, up):
            source = cut - 2 * (step + 1) if up else cut + 2 * (step + 1)
            ok = (level - step - 1 >= 0) if up else (level + step + 1 < levels)
            @pl.when(ok)
            def _():
                copy_to(m, x_ref.at[m], source, sibling, send_sem.at[m, step, 0 if up else 1], recv_sem.at[m, step, 0 if up else 1]).wait_recv()
            if step + 1 < levels - 1:
                hop(m, step + 1, up, True)
            @pl.when(ok)
            def _():
                copy_to(m, out_ref.at[m, source], source, sibling, pair_send.at[m, source], pair_recv.at[m, source]).start()
        for m in range(micro_count):
            hop(m, 0, True, True)
            hop(m, 0, False, True)
        for m in range(micro_count):
            copy_to(m, x_ref.at[m], cut, sibling, pair_send.at[m, cut], pair_recv.at[m, cut]).start()
        for step in range(levels - 1):
            for m in range(micro_count):
                arrive(m, step, True)
                arrive(m, step, False)
        for step in range(levels - 1):
            for m in range(micro_count):
                hop(m, step, True, False)
                hop(m, step, False, False)
    else:
        hops = list(range(2, cut_count, 2))
        def peer(m, k, hop_):
            return copy_to(m, x_ref.at[m], cut, jnp.bitwise_xor(cut, hop_), send_sem.at[m, k, 0], recv_sem.at[m, k, 0])
        for m in range(micro_count):
            for k, hop_ in enumerate(hops):
                peer(m, k, hop_).start()
            copy_to(m, x_ref.at[m], cut, sibling, pair_send.at[m, cut], pair_recv.at[m, cut]).start()
        for m in range(micro_count):
            for k, hop_ in enumerate(hops):
                source = jnp.bitwise_xor(cut, hop_)
                copy_to(m, x_ref.at[m], source, sibling, send_sem.at[m, k, 0], recv_sem.at[m, k, 0]).wait_recv()
                copy_to(m, out_ref.at[m, source], source, sibling, pair_send.at[m, source], pair_recv.at[m, source]).start()
        for m in range(micro_count):
            for k, hop_ in enumerate(hops):
                peer(m, k, hop_).wait_send()
    for m in range(micro_count):
        own[m].wait()
        for z in range(levels):
            mine = 2 * z + side
            theirs = 2 * z + 1 - side
            copy_to(m, out_ref.at[m, mine], mine, sibling, pair_send.at[m, mine], pair_recv.at[m, theirs]).wait_send()
            copy_to(m, out_ref.at[m, mine], theirs, sibling, pair_send.at[m, mine], pair_recv.at[m, theirs]).wait_recv()


def cut_gather(x, cut_count, call_id, chain=True, space=pltpu.VMEM):
    micro_count, rows, width = x.shape
    levels = cut_count // 2
    return pl.pallas_call(
        partial(gather_kernel, chain),
        out_shape=jax.ShapeDtypeStruct((micro_count, cut_count, rows, width), x.dtype),
        in_specs=[pl.BlockSpec(memory_space=pltpu.VMEM)],
        out_specs=pl.BlockSpec(memory_space=space),
        scratch_shapes=[
            pltpu.SemaphoreType.DMA((micro_count, levels - 1, 2)),
            pltpu.SemaphoreType.DMA((micro_count, levels - 1, 2)),
            pltpu.SemaphoreType.DMA((micro_count, cut_count)),
            pltpu.SemaphoreType.DMA((micro_count, cut_count)),
            pltpu.SemaphoreType.DMA((micro_count,)),
        ],
        compiler_params=pltpu.CompilerParams(collective_id=call_id, has_side_effects=True, vmem_limit_bytes=48 * 2**20),
    )(x)


def scatter_kernel(
    x_ref, dots_ref, out_ref, sums_ref, pair_buf, comb, far_buf, dots_in, pair_send, pair_recv, send, recv, dot_send, dot_recv
):
    micro_count, cut_count = x_ref.shape[:2]
    cut = lax.axis_index("cuts")
    greet_line(cut_count, True)
    line = LineSum(x_ref, pair_buf, comb, far_buf, pair_send, pair_recv, send, recv)

    def dot_copy(hop):
        target = jnp.bitwise_xor(cut, hop)
        return line_copy(
            dots_ref.at[target], dots_in.at[hop - 1], dot_send.at[hop - 1], dot_recv.at[hop - 1], line.group, target
        )

    for m in range(micro_count):
        line.start(m)
    for hop in range(1, cut_count):
        dot_copy(hop).start()
    for m in range(micro_count):
        line.forward(m)
    sums = dots_ref[cut]
    for hop in range(1, cut_count):
        dot_copy(hop).wait()
        sums = sums + dots_in[hop - 1]
    sums_ref[...] = sums
    for m in range(micro_count):
        out_ref[m] = line.finish(m)


def cut_scatter(x, dots, call_id):
    micro_count, cut_count, rows, width = x.shape
    levels = cut_count // 2
    dma = pltpu.SemaphoreType.DMA
    return pl.pallas_call(
        scatter_kernel,
        out_shape=(
            jax.ShapeDtypeStruct((micro_count, rows, width), jnp.float32),
            jax.ShapeDtypeStruct(dots.shape[1:], jnp.float32),
        ),
        in_specs=[pl.BlockSpec(memory_space=pltpu.VMEM)] * 2,
        out_specs=[pl.BlockSpec(memory_space=pltpu.VMEM)] * 2,
        scratch_shapes=[
            pltpu.VMEM((micro_count, levels, rows, width), x.dtype),
            pltpu.VMEM((micro_count, levels, rows, width), x.dtype),
            pltpu.VMEM((micro_count, levels, rows, width), x.dtype),
            pltpu.VMEM((cut_count - 1, *dots.shape[1:]), jnp.float32),
            dma((micro_count, levels)), dma((micro_count, levels)), dma((micro_count, levels)), dma((micro_count, levels)),
            dma((cut_count - 1,)), dma((cut_count - 1,)),
        ],
        compiler_params=pltpu.CompilerParams(collective_id=call_id, has_side_effects=True, vmem_limit_bytes=48 * 2**20),
    )(x, dots)


def swap_kernel(to_rows, x_ref, out_ref, send_sem, recv_sem, own_sem):
    micro_count = x_ref.shape[0]
    cut = lax.axis_index("cuts")
    group = lax.axis_index("expert")
    cut_count = max(x_ref.shape[1], out_ref.shape[1]) // min(x_ref.shape[1], out_ref.shape[1])
    rows = min(x_ref.shape[1], out_ref.shape[1])
    width = min(x_ref.shape[2], out_ref.shape[2])
    greet_line(cut_count, True)

    def by_rows(ref, m, who):
        return ref.at[m, pl.ds(pl.multiple_of(who * rows, rows), rows), :]

    def by_columns(ref, m, who):
        return ref.at[m, :, pl.ds(pl.multiple_of(who * width, width), width)]

    def copy(m, hop):
        target = jnp.bitwise_xor(cut, hop)
        src = by_rows(x_ref, m, target) if to_rows else by_columns(x_ref, m, target)
        dst = by_columns(out_ref, m, cut) if to_rows else by_rows(out_ref, m, cut)
        return pltpu.make_async_remote_copy(
            src_ref=src, dst_ref=dst, send_sem=send_sem.at[m, hop], recv_sem=recv_sem.at[m, hop],
            device_id=(group, target), device_id_type=MESH)

    for m in range(micro_count):
        for hop in range(cut_count - 1, 0, -1):
            copy(m, hop).start()
        src = by_rows(x_ref, m, cut) if to_rows else by_columns(x_ref, m, cut)
        dst = by_columns(out_ref, m, cut) if to_rows else by_rows(out_ref, m, cut)
        pltpu.make_async_copy(src, dst, own_sem.at[m]).start()
    for m in range(micro_count):
        for hop in range(cut_count - 1, 0, -1):
            copy(m, hop).wait()
        src = by_rows(x_ref, m, cut) if to_rows else by_columns(x_ref, m, cut)
        dst = by_columns(out_ref, m, cut) if to_rows else by_rows(out_ref, m, cut)
        pltpu.make_async_copy(src, dst, own_sem.at[m]).wait()


def cut_swap(x, cut_count, to_rows, call_id):
    micro_count, rows, width = x.shape
    shape = (micro_count, rows // cut_count, width * cut_count) if to_rows else (micro_count, rows * cut_count, width // cut_count)
    return pl.pallas_call(
        partial(swap_kernel, to_rows),
        out_shape=jax.ShapeDtypeStruct(shape, x.dtype),
        in_specs=[pl.BlockSpec(memory_space=pltpu.VMEM)],
        out_specs=pl.BlockSpec(memory_space=pltpu.VMEM),
        scratch_shapes=[
            pltpu.SemaphoreType.DMA((micro_count, cut_count)),
            pltpu.SemaphoreType.DMA((micro_count, cut_count)),
            pltpu.SemaphoreType.DMA((micro_count,)),
        ],
        compiler_params=pltpu.CompilerParams(collective_id=call_id, has_side_effects=True, vmem_limit_bytes=48 * 2**20),
    )(x)


def head_masks(width, heads):
    lane = lax.broadcasted_iota(jnp.int32, (1, width), 1)
    size = width // heads
    return [((lane >= h * size) & (lane < (h + 1) * size)) for h in range(heads)]


def allowed_mask(first_ref, m, start, rows, keys):
    query_spots = start + lax.broadcasted_iota(jnp.int32, (rows, keys), 0)
    key_spots = lax.broadcasted_iota(jnp.int32, (rows, keys), 1)
    return (key_spots <= query_spots) & (key_spots >= first_ref[m, pl.ds(start, rows), :])


def attend_kernel(heads, qkv_ref, first_ref, att_ref, lse_ref):
    length, width = att_ref.shape[1], att_ref.shape[2]
    rows = min(256, length)
    masks = head_masks(width, heads)
    for block in range(length // rows):
        start, keys = block * rows, (block + 1) * rows
        allowed = allowed_mask(first_ref, 0, start, rows, keys)
        query = qkv_ref[0, pl.ds(start, rows), 0:width] * jnp.bfloat16(score_scale)
        key = qkv_ref[0, 0:keys, width : 2 * width]
        value = qkv_ref[0, 0:keys, 2 * width : 3 * width]
        att = jnp.zeros((rows, width), jnp.float32)
        logs = jnp.zeros((rows, width), jnp.float32)
        for mask in masks:
            scores = tail_dot(jnp.where(mask, query, jnp.bfloat16(0)), key)
            scores = jnp.where(allowed, scores, masked_value)
            top = jnp.max(scores, axis=-1, keepdims=True)
            raised = jnp.exp(scores - top)
            total = jnp.sum(raised, axis=-1, keepdims=True)
            probs = (raised * (1.0 / total)).astype(jnp.bfloat16)
            att = jnp.where(mask, plain_dot(probs, value), att)
            logs = jnp.where(mask, top + jnp.log(total), logs)
        att_ref[0, pl.ds(start, rows), :] = att.astype(jnp.bfloat16)
        lse_ref[0, pl.ds(start, rows), :] = logs


def attend(qkv, first, heads):
    micro_count, length, width = qkv.shape
    width = width // 3
    block = lambda w: pl.BlockSpec((1, length, w), lambda m: (m, 0, 0))
    return pl.pallas_call(
        partial(attend_kernel, heads),
        grid=(micro_count,),
        out_shape=(
            jax.ShapeDtypeStruct((micro_count, length, width), jnp.bfloat16),
            jax.ShapeDtypeStruct((micro_count, length, width), jnp.float32),
        ),
        in_specs=[block(3 * width), block(1)],
        out_specs=(block(width), block(width)),
        compiler_params=pltpu.CompilerParams(vmem_limit_bytes=48 * 2**20),
    )(qkv, first)


def norm_parts(values):
    center = values - jnp.mean(values, axis=-1, keepdims=True)
    spread = jnp.mean(center * center, axis=-1, keepdims=True)
    scale = lax.rsqrt(spread + norm_eps)
    return center * scale, scale


def norm_back(normed, scale, gain, grad):
    inner = grad * gain
    return scale * (
        inner
        - jnp.mean(inner, axis=-1, keepdims=True)
        - normed * jnp.mean(inner * normed, axis=-1, keepdims=True)
    )


def gelu_pair(values):
    phi = 0.5 * (1.0 + lax.erf(values * (0.5**0.5)))
    bell = jnp.exp(-0.5 * values * values) * ((2.0 * jnp.pi) ** -0.5)
    return values * phi, phi + values * bell


def tile_slots(capacity, row_count, tile):
    return -(-capacity * (tile // row_count) // 16) * 16


def token_table(spot, width):
    return (spot == lax.broadcasted_iota(jnp.int32, (spot.shape[0], width), 1)).astype(jnp.bfloat16)


def lane_softmax(logits, lanes, first, count):
    inside = (lanes >= first) & (lanes < first + count)
    raised = jnp.exp(logits - jnp.max(jnp.where(inside, logits, masked_value), axis=-1, keepdims=True))
    raised = jnp.where(inside, raised, 0.0)
    return raised / jnp.sum(raised, axis=-1, keepdims=True)


def route(logits, chosen, expert_count):
    lanes = lax.broadcasted_iota(jnp.int32, logits.shape, 1)
    routed = lane_softmax(logits, lanes, 0, expert_count)
    mixing = lane_softmax(logits, lanes, expert_count, 2)
    pick = lambda values, lane: jnp.sum(jnp.where(lanes == lane, values, 0.0), axis=-1, keepdims=True)
    return pick(routed, chosen), pick(mixing, expert_count), pick(mixing, expert_count + 1), routed, mixing


def feed_kernel(
    tile, slots, h_ref, g_ref, chosen_ref, spot_ref, small_ref, own_in_ref, own_out_ref, in_ref, out_w_ref,
    out_ref, back_ref, dots_ref, d_own_in_ref, d_own_out_ref, d_in_ref, d_out_ref,
    sent, g_sent, hidden_buf, pre_buf, gate_buf, dots_buf,
):
    step = pl.program_id(0)
    expert_count = sent.shape[0]
    total, features = h_ref.shape
    tiles = total // tile
    low = jnp.bfloat16
    lanes = lax.broadcasted_iota(jnp.int32, (tile, 128), 1)

    @pl.when(step == 0)
    def _():
        def one(t, carry):
            rows = pl.ds(pl.multiple_of(t * tile, tile), tile)
            spots = pl.ds(pl.multiple_of(t * slots, slots), slots)
            h_two = h_ref[rows, :]
            gate, mix_dense, mix_expert, _, _ = route(plain_dot(h_two, small_ref[...]), chosen_ref[rows, :], expert_count)
            mix_gate = mix_expert * gate
            gate_buf[rows, :] = jnp.broadcast_to(mix_gate, (tile, 128))
            table = token_table(spot_ref[rows, :], expert_count * slots)
            grad_y = g_ref[rows, :].astype(jnp.float32)
            rows_sent = lead_dot(table, h_two).astype(low)
            rows_back = lead_dot(table, (mix_gate * grad_y).astype(low)).astype(low)
            for e in range(expert_count):
                sent[e, spots, :] = rows_sent[e * slots : (e + 1) * slots]
                g_sent[e, spots, :] = rows_back[e * slots : (e + 1) * slots]
            act, slope = gelu_pair(plain_dot(h_two, own_in_ref[...]))
            dense = plain_dot(act.astype(low), own_out_ref[...])
            dots_buf[rows, :] = jnp.where(lanes == 0, jnp.sum(grad_y * dense, axis=-1, keepdims=True), 0.0)
            d_pre = (tail_dot((mix_dense * grad_y).astype(low), own_out_ref[...]) * slope).astype(low)
            hidden_buf[rows, :] = (mix_dense * act).astype(low)
            pre_buf[rows, :] = d_pre
            out_ref[rows, :] = (mix_dense * dense).astype(low)
            back_ref[rows, :] = tail_dot(d_pre, own_in_ref[...]).astype(low)
            return carry

        lax.fori_loop(0, tiles, one, 0)

    @pl.when((step >= 1) & (step <= expert_count))
    def _():
        e = step - 1
        rows_in, rows_back = sent[e], g_sent[e]
        act, slope = gelu_pair(plain_dot(rows_in, in_ref[0]))
        inner = act.astype(low)
        d_pre = (tail_dot(rows_back, out_w_ref[0]) * slope).astype(low)
        d_in_ref[0] = lead_dot(rows_in, d_pre).astype(low)
        d_out_ref[0] = lead_dot(inner, rows_back).astype(low)
        sent[e] = tail_dot(d_pre, in_ref[0]).astype(low)
        g_sent[e] = plain_dot(inner, out_w_ref[0]).astype(low)

    @pl.when(step == expert_count + 1)
    def _():
        def one(t, carry):
            rows = pl.ds(pl.multiple_of(t * tile, tile), tile)
            spots = pl.ds(pl.multiple_of(t * slots, slots), slots)
            table = token_table(spot_ref[rows, :], expert_count * slots)
            grad_y = g_ref[rows, :].astype(jnp.float32)
            gather = lambda ref: jnp.concatenate([ref[e, spots, :] for e in range(expert_count)], axis=0)
            part = plain_dot(table, gather(g_sent))
            dots = jnp.where(lanes == 1, jnp.sum(grad_y * part, axis=-1, keepdims=True), dots_buf[rows, :])
            for k in range(tile // 128):
                dots_ref[t * (tile // 128) + k] = jnp.transpose(dots[k * 128 : (k + 1) * 128])[0:8]
            out_ref[rows, :] = (out_ref[rows, :].astype(jnp.float32) + gate_buf[rows, 0:1] * part).astype(low)
            back = plain_dot(table, gather(sent))
            back_ref[rows, :] = (back_ref[rows, :].astype(jnp.float32) + back).astype(low)
            return carry

        lax.fori_loop(0, tiles, one, 0)
        width = 256
        for k in range(features // width):
            part = slice(k * width, (k + 1) * width)
            d_own_in_ref[part, :] = lead_dot(h_ref[:, part], pre_buf[...]).astype(low)
            d_own_out_ref[:, part] = lead_dot(hidden_buf[...], g_ref[:, part]).astype(low)


def feed(h_all, g_all, chosen, spot, small, own_in, own_out, weights_in, weights_out, tile, slots):
    total, features = h_all.shape
    expert_count, _, share = weights_in.shape
    low, f32 = jnp.bfloat16, jnp.float32
    whole = lambda x: pl.BlockSpec(x.shape, lambda i: (0,) * len(x.shape), pipeline_mode=pl.Buffered(1))
    expert = lambda r, c: pl.BlockSpec((1, r, c), lambda i: (jnp.clip(i - 1, 0, expert_count - 1), 0, 0))
    outs = (
        jax.ShapeDtypeStruct((total, features), low),
        jax.ShapeDtypeStruct((total, features), low),
        jax.ShapeDtypeStruct((total // 128, 8, 128), f32),
        jax.ShapeDtypeStruct((features, share), low),
        jax.ShapeDtypeStruct((share, features), low),
        jax.ShapeDtypeStruct((expert_count, features, share), low),
        jax.ShapeDtypeStruct((expert_count, share, features), low),
    )
    rows = total // tile * slots
    return pl.pallas_call(
        partial(feed_kernel, tile, slots),
        grid=(expert_count + 2,),
        out_shape=outs,
        in_specs=[whole(x) for x in (h_all, g_all, chosen, spot, small, own_in, own_out)]
        + [expert(features, share), expert(share, features)],
        out_specs=[whole(x) for x in outs[:5]] + [expert(features, share), expert(share, features)],
        scratch_shapes=[
            pltpu.VMEM((expert_count, rows, features), low),
            pltpu.VMEM((expert_count, rows, features), low),
            pltpu.VMEM((total, share), low),
            pltpu.VMEM((total, share), low),
            pltpu.VMEM((total, 128), f32),
            pltpu.VMEM((total, 128), f32),
        ],
        compiler_params=pltpu.CompilerParams(vmem_limit_bytes=60 * 2**20),
    )(h_all, g_all, chosen, spot, small, own_in, own_out, weights_in, weights_out)


def softmax_back(probs, grad):
    return probs * (grad - jnp.sum(probs * grad, axis=-1, keepdims=True))


def line_copy(src, dst, send, recv, group, target):
    return pltpu.make_async_remote_copy(
        src_ref=src, dst_ref=dst, send_sem=send, recv_sem=recv, device_id=(group, target), device_id_type=MESH
    )


def greet_all(cut_count, group_count):
    cut = lax.axis_index("cuts")
    group = lax.axis_index("expert")
    barrier = pltpu.get_barrier_semaphore()
    for hop in range(1, cut_count):
        pl.semaphore_signal(barrier, inc=1, device_id=(group, jnp.bitwise_xor(cut, hop)), device_id_type=MESH)
    for hop in range(1, group_count):
        pl.semaphore_signal(barrier, inc=1, device_id=(lax.rem(group + hop, group_count), cut), device_id_type=MESH)
    pl.semaphore_wait(barrier, cut_count + group_count - 2)


class LineSum:
    def __init__(self, part, pair_buf, comb, far_buf, pair_send, pair_recv, send, recv):
        self.refs = (part, pair_buf, comb, far_buf, pair_send, pair_recv, send, recv)
        self.cut = lax.axis_index("cuts")
        self.group = lax.axis_index("expert")
        self.levels = part.shape[1] // 2
        self.order = list(range(self.levels - 1, -1, -1))

    def pair_copy(self, m, k):
        part, pair_buf, _, _, pair_send, pair_recv, _, _ = self.refs
        return line_copy(
            part.at[m, jnp.bitwise_xor(self.cut, 2 * k + 1)], pair_buf.at[m, k], pair_send.at[m, k], pair_recv.at[m, k],
            self.group, jnp.bitwise_xor(self.cut, 1),
        )

    def far_copy(self, m, k):
        _, _, comb, far_buf, _, _, send, recv = self.refs
        return line_copy(
            comb.at[m, k], far_buf.at[m, k], send.at[m, k], recv.at[m, k], self.group, jnp.bitwise_xor(self.cut, 2 * k)
        )

    def start(self, m):
        for k in self.order:
            self.pair_copy(m, k).start()

    def forward(self, m):
        part, pair_buf, comb = self.refs[:3]
        for k in self.order:
            self.pair_copy(m, k).wait_recv()
            total = part[m, jnp.bitwise_xor(self.cut, 2 * k)].astype(jnp.float32) + pair_buf[m, k].astype(jnp.float32)
            comb[m, k] = total.astype(comb.dtype)
            if k:
                self.far_copy(m, k).start()

    def finish(self, m):
        comb, far_buf = self.refs[2:4]
        total = comb[m, 0].astype(jnp.float32)
        for k in self.order:
            if k:
                self.far_copy(m, k).wait_recv()
                total = total + far_buf[m, k].astype(jnp.float32)
        for k in self.order:
            self.pair_copy(m, k).wait_send()
            if k:
                self.far_copy(m, k).wait_send()
        return total


def attend_back_one(heads, m, qkv_ref, first_ref, lse_ref, back_ref, out_ref, key_acc, value_acc):
    length, width = back_ref.shape[1], back_ref.shape[2]
    rows = min(256, length)
    masks = head_masks(width, heads)
    key_acc[...] = jnp.zeros_like(key_acc)
    value_acc[...] = jnp.zeros_like(value_acc)
    zero = jnp.bfloat16(0)
    for block in range(length // rows):
        start, keys = block * rows, (block + 1) * rows
        allowed = allowed_mask(first_ref, m, start, rows, keys)
        query = qkv_ref[m, pl.ds(start, rows), 0:width] * jnp.bfloat16(score_scale)
        key = qkv_ref[m, 0:keys, width : 2 * width]
        value = qkv_ref[m, 0:keys, 2 * width : 3 * width]
        back = back_ref[m, pl.ds(start, rows), :]
        logs = lse_ref[m, pl.ds(start, rows), :]
        query_grad = jnp.zeros((rows, width), jnp.float32)
        for h, mask in enumerate(masks):
            one_query = jnp.where(mask, query, zero)
            one_back = jnp.where(mask, back, zero)
            scores = jnp.where(allowed, tail_dot(one_query, key), masked_value)
            spot = h * (width // heads)
            probs = jnp.exp(scores - logs[:, spot : spot + 1])
            weighted = probs * tail_dot(one_back, value)
            delta = jnp.sum(weighted, axis=-1, keepdims=True)
            score_grad = (weighted - probs * delta).astype(jnp.bfloat16)
            query_grad = jnp.where(mask, plain_dot(score_grad, key), query_grad)
            key_acc[0:keys, :] += lead_dot(score_grad, one_query)
            value_acc[0:keys, :] += lead_dot(probs.astype(jnp.bfloat16), one_back)
        out_ref[m, pl.ds(start, rows), 0:width] = (query_grad * score_scale).astype(jnp.bfloat16)
    out_ref[m, :, width : 2 * width] = key_acc[...].astype(jnp.bfloat16)
    out_ref[m, :, 2 * width : 3 * width] = value_acc[...].astype(jnp.bfloat16)


def back_kernel(
    heads, expert_count, sums_here,
    dh_ref, dots_ref, chosen_ref, h_ref, x_two_ref, gy_ref, att_ref, w_out_ref, qkv_ref, first_ref, lse_ref, w_qkv_ref,
    h_all_ref, x_ref, gain_one_ref, gain_two_ref, small_ref, own_in_ref, own_out_ref, w_rows_ref,
    tokens_ref, wo_ref, small_out_ref, qkv_out_ref, in_out_ref, out_out_ref, norm_ref,
    d_x_two, g_att, d_att, back_all, d_qkv, key_acc, value_acc, d_small, part, pair_buf, comb, far_buf,
    wo_part, qkv_part, wo_in, qkv_in, own_in_in, own_out_in, wo_mid, qkv_mid, in_mid, wo_end, qkv_end, in_end,
    pair_send, pair_recv, far_send, far_recv, swap_send, swap_recv, swap_own, one_send, one_recv, two_send, two_recv, two_own,
):
    micro_count, cut_count, rows, features = part.shape
    group_count, split, piece_rows, _ = wo_part.shape
    group_rows = split * piece_rows
    width = features // cut_count
    cut = lax.axis_index("cuts")
    group = lax.axis_index("expert")
    low, f32 = jnp.bfloat16, jnp.float32
    greet_all(cut_count, group_count if sums_here else 1)

    ones = ((own_in_ref, own_in_in), (own_out_ref, own_out_in), (wo_part, wo_in), (qkv_part, qkv_in))

    def one_copy(kind, hop):
        src, dst = ones[kind]
        target = lax.rem(group + hop, group_count)
        return line_copy(
            src.at[target], dst.at[hop - 1], one_send.at[kind, hop - 1], one_recv.at[kind, hop - 1], target, cut
        )

    def one_start(kind):
        for hop in range(1, group_count):
            one_copy(kind, hop).start()

    def one_finish(kind):
        src, dst = ones[kind]
        total = src[group].astype(f32)
        for hop in range(1, group_count):
            one_copy(kind, hop).wait_recv()
            total = total + dst[hop - 1].astype(f32)
        for hop in range(1, group_count):
            one_copy(kind, hop).wait_send()
        return total

    twos = ((in_mid, in_end), None, (wo_mid, wo_end), (qkv_mid, qkv_end))

    def two_copy(kind, hop):
        src, dst = twos[kind]
        target = jnp.bitwise_xor(cut, hop)
        return line_copy(src.at[target], dst.at[cut], two_send.at[kind, hop], two_recv.at[kind, hop], group, target)

    def two_keep(kind):
        src, dst = twos[kind]
        return pltpu.make_async_copy(src.at[cut], dst.at[cut], two_own.at[kind])

    def two_start(kind):
        for hop in range(cut_count - 1, 0, -1):
            two_copy(kind, hop).start()
        two_keep(kind).start()

    def two_finish(kind):
        for hop in range(cut_count - 1, 0, -1):
            two_copy(kind, hop).wait()
        two_keep(kind).wait()

    if sums_here:
        one_start(0)
        one_start(1)

    def swap_copy(m, hop):
        target = jnp.bitwise_xor(cut, hop)
        return line_copy(
            d_att.at[m, :, pl.ds(pl.multiple_of(target * width, width), width)],
            back_all.at[m, pl.ds(pl.multiple_of(cut * rows, rows), rows), :],
            swap_send.at[m, hop], swap_recv.at[m, hop], group, target,
        )

    def swap_keep(m):
        return pltpu.make_async_copy(
            d_att.at[m, :, pl.ds(pl.multiple_of(cut * width, width), width)],
            back_all.at[m, pl.ds(pl.multiple_of(cut * rows, rows), rows), :],
            swap_own.at[m],
        )

    small = small_ref[...]
    gain_two = gain_two_ref[...]
    d_small[...] = jnp.zeros_like(d_small)
    lanes = lax.broadcasted_iota(jnp.int32, (rows, 128), 1)

    def norm_two_step(m, carry):
        dots = jnp.transpose(dots_ref[m])
        chosen = chosen_ref[m]
        h_two = h_ref[m]
        gate, _, mix_expert, routed, mixing = route(plain_dot(h_two, small), chosen, expert_count)
        d_mixing = jnp.where(lanes == expert_count, dots[:, 0:1], gate * dots[:, 1:2])
        d_gate = jnp.where(lanes == chosen, mix_expert * dots[:, 1:2], 0.0)
        d_logits = (softmax_back(mixing, d_mixing) + softmax_back(routed, d_gate)).astype(low)
        d_h = dh_ref[m] + tail_dot(d_logits, small)
        normed, scale = norm_parts(x_two_ref[m])
        one_lane = (lanes == expert_count + 2).astype(low)
        d_small[...] += lead_dot(h_two, d_logits) + lead_dot((d_h * normed).astype(low), one_lane)
        d_x = gy_ref[m].astype(f32) + norm_back(normed, scale, gain_two, d_h)
        d_x_two[m] = d_x
        grad = d_x.astype(low)
        g_att[pl.ds(pl.multiple_of(m * rows, rows), rows), :] = grad
        d_att[m] = tail_dot(grad, w_out_ref[...]).astype(low)
        for hop in range(cut_count - 1, 0, -1):
            swap_copy(m, hop).start()
        swap_keep(m).start()
        return carry

    lax.fori_loop(0, micro_count, norm_two_step, 0)

    def wo_step(g, carry):
        columns = pl.ds(pl.multiple_of(g * group_rows, group_rows), group_rows)
        grads = lead_dot(att_ref[:, columns], g_att[...]).astype(low)
        wo_part[g, :, :, 0:features] = grads.reshape(split, piece_rows, features)
        smalls = d_small[columns, :].astype(low)
        wo_part[g, :, :, features : features + 128] = smalls.reshape(split, piece_rows, 128)
        return carry

    lax.fori_loop(0, group_count, wo_step, 0)
    if sums_here:
        one_start(2)
    line = LineSum(part, pair_buf, comb, far_buf, pair_send, pair_recv, far_send, far_recv)

    def attend_step(m, carry):
        for hop in range(cut_count - 1, 0, -1):
            swap_copy(m, hop).wait()
        swap_keep(m).wait()
        attend_back_one(heads, m, qkv_ref, first_ref, lse_ref, back_all, d_qkv, key_acc, value_acc)
        for c in range(cut_count):
            part[m, c] = tail_dot(d_qkv[m, c * rows : (c + 1) * rows, :], w_qkv_ref[...]).astype(low)
        line.start(m)
        line.forward(m)
        return carry

    lax.fori_loop(0, micro_count, attend_step, 0)

    def qkv_step(g, carry):
        columns = pl.ds(pl.multiple_of(g * group_rows, group_rows), group_rows)
        grads = jnp.zeros((group_rows, 3 * width), f32)
        for m in range(micro_count):
            grads = grads + lead_dot(h_all_ref[m, :, columns], d_qkv[m])
        qkv_part[g] = grads.astype(low).reshape(split, piece_rows, 3 * width)
        return carry

    lax.fori_loop(0, group_count, qkv_step, 0)
    if sums_here:
        one_start(3)
        in_mid[...] = one_finish(0).astype(low)
        two_start(0)
        wo_mid[...] = one_finish(2).astype(low)
        two_start(2)
        out_out_ref[...] = one_finish(1)

    def norm_one_step(m, carry):
        total = line.finish(m)
        normed, scale = norm_parts(x_ref[m].astype(f32))
        tokens_ref[m] = d_x_two[m] + norm_back(normed, scale, gain_one_ref[...], total)
        return carry

    if not sums_here:
        lax.fori_loop(0, micro_count, norm_one_step, 0)
        wo_ref[...] = wo_part[...]
        qkv_out_ref[...] = qkv_part[...]
        return
    norm_one_step(0, 0)
    qkv_mid[...] = one_finish(3).astype(low)
    two_start(3)
    two_finish(0)
    share_piece = in_end.shape[2] // group_count
    for c in range(cut_count):
        for g in range(group_count):
            spot = (g * cut_count + c) * share_piece
            in_out_ref[:, spot : spot + share_piece] = in_end[c, :, g * share_piece : (g + 1) * share_piece].astype(f32)
    two_finish(2)
    total = wo_end[0].astype(f32)
    for c in range(1, cut_count):
        total = total + wo_end[c].astype(f32)
    wo_ref[...] = total[:, :features]
    small_out_ref[...] = total[:, features:]
    for m in range(1, micro_count):
        norm_one_step(m, 0)
    two_finish(3)
    norm = jnp.zeros((piece_rows, 1), f32)
    for c in range(cut_count):
        for k in range(3):
            grad = qkv_end[c, :, k * width : (k + 1) * width].astype(f32)
            qkv_out_ref[k, :, c * width : (c + 1) * width] = grad
            weights = w_rows_ref[k, :, c * width : (c + 1) * width].astype(f32)
            norm = norm + jnp.sum(grad * weights, axis=-1, keepdims=True)
    norm_ref[...] = jnp.broadcast_to(norm, norm_ref.shape)


def back(
    dh, dots, chosen, h_two, x_two, gy, attended, w_output, qkv, first, lse, w_qkv, h_all, x, gain_one, gain_two, small,
    own_in, own_out, w_rows, heads, expert_count, sums_here, call_id,
):
    micro_count, rows, features = x.shape
    length = qkv.shape[1]
    cut_count = length // rows
    width = features // cut_count
    group_count = own_out.shape[0]
    piece_rows = features // (group_count * cut_count)
    share, piece = own_in.shape[3], own_out.shape[1]
    low, f32 = jnp.bfloat16, jnp.float32
    levels = cut_count // 2
    wide = features + 128
    shape = jax.ShapeDtypeStruct
    parts = (group_count, cut_count, piece_rows) if sums_here else (features // 256, 1, 256)
    if sums_here:
        outs = (
            shape((micro_count, rows, features), f32), shape((piece_rows, features), f32), shape((piece_rows, 128), f32),
            shape((3, piece_rows, features), f32), shape((piece_rows, share * cut_count), f32), shape((piece, features), f32),
            shape((piece_rows, 128), f32),
        )
    else:
        outs = (
            shape((micro_count, rows, features), f32), shape((*parts, wide), low),
            shape((8, 128), f32), shape((*parts, 3 * width), low), shape((8, 128), f32),
            shape((8, 128), f32), shape((8, 128), f32),
        )
    peers = max(group_count - 1, 1) if sums_here else 1
    block = lambda *dims: pltpu.VMEM(dims, low)
    mids = lambda w: block(cut_count, piece_rows, w) if sums_here else block(16, 128)
    ins = lambda w: block(peers, cut_count, piece_rows, w) if sums_here else block(16, 128)
    dma = pltpu.SemaphoreType.DMA
    vmem = pl.BlockSpec(memory_space=pltpu.VMEM)
    operands = (
        dh, dots, chosen, h_two, x_two, gy, attended, w_output, qkv, first, lse, w_qkv, h_all, x, gain_one, gain_two, small,
        own_in, own_out, w_rows,
    )
    return pl.pallas_call(
        partial(back_kernel, heads, expert_count, sums_here),
        out_shape=outs,
        in_specs=[vmem] * len(operands),
        out_specs=[vmem] * len(outs),
        scratch_shapes=[
            pltpu.VMEM((micro_count, rows, features), f32),
            block(micro_count * rows, features),
            block(micro_count, rows, features),
            block(micro_count, length, width),
            block(micro_count, length, 3 * width),
            pltpu.VMEM((length, width), f32),
            pltpu.VMEM((length, width), f32),
            pltpu.VMEM((features, 128), f32),
            block(micro_count, cut_count, rows, features),
            block(micro_count, levels, rows, features),
            block(micro_count, levels, rows, features),
            block(micro_count, levels, rows, features),
            block(*parts, wide),
            block(*parts, 3 * width),
            ins(wide), ins(3 * width), ins(share),
            block(peers, piece, features) if sums_here else block(16, 128),
            mids(wide), mids(3 * width), mids(share), mids(wide), mids(3 * width), mids(share),
            dma((micro_count, levels)), dma((micro_count, levels)), dma((micro_count, levels)), dma((micro_count, levels)),
            dma((micro_count, cut_count)), dma((micro_count, cut_count)), dma((micro_count,)),
            dma((4, peers)), dma((4, peers)), dma((4, cut_count)), dma((4, cut_count)), dma((4,)),
        ],
        compiler_params=pltpu.CompilerParams(
            collective_id=call_id, has_side_effects=True, vmem_limit_bytes=60 * 2**20
        ),
    )(*operands)


def local(
    tokens, cotangent, segments, expert_ids, slot_ids, kept_mask, norm1_gain, w_query, w_key, w_value, w_output,
    norm2_gain, dense_in, dense_out, router, mixer, expert_in, expert_out,
):
    micro_count, row_count, features = tokens.shape[1:]
    cut_count = lax.axis_size("cuts")
    group_count = lax.axis_size("expert")
    cut = lax.axis_index("cuts")
    length = cut_count * row_count
    head_width = features // cut_count
    heads = head_width // 64
    expert_count = router.shape[1]
    hidden_count = dense_in.shape[1]
    share = hidden_count // cut_count
    piece = share // group_count
    capacity = max(2, row_count * 5 // (4 * expert_count))
    gain_one = norm1_gain.astype(jnp.float32)
    gain_two = norm2_gain.astype(jnp.float32)
    f32, low = jnp.float32, jnp.bfloat16

    code = jnp.where(kept_mask[0] == 1, expert_ids[0] * capacity + slot_ids[0], -1)
    codes = lax.all_gather(code, "cuts", axis=1, tiled=True)
    docs = segments[0]
    first = jnp.sum((docs[:, None, :] < docs[:, :, None]).astype(jnp.int32), axis=-1)[..., None]
    grad_all = lax.all_gather(cotangent[0], "cuts", axis=1, tiled=True)
    weights_in = lax.all_gather(expert_in[0], "expert", axis=0)
    weights_out = lax.all_gather(expert_out[0], "expert", axis=0)

    columns = lambda w: lax.dynamic_slice_in_dim(w, cut * head_width, head_width, 1)
    w_qkv = jnp.concatenate([columns(w_query), columns(w_key), columns(w_value)], axis=1)
    own_in = lax.dynamic_index_in_dim(
        dense_in.reshape(features, group_count, cut_count, piece), cut, 2, keepdims=False
    ).reshape(features, share)
    own_out = lax.dynamic_index_in_dim(
        dense_out.reshape(group_count, cut_count, piece, features), cut, 1, keepdims=False
    ).reshape(share, features)

    x_rows = tokens[0].astype(f32)
    norm_one, _ = norm_parts(x_rows)
    h_one = (norm_one * gain_one).astype(low)
    h_all = cut_gather(h_one, cut_count, 1).reshape(micro_count, length, features)
    qkv = jnp.einsum("mtf,fk->mtk", h_all, w_qkv, preferred_element_type=f32).astype(low)
    att_part, lse = attend(qkv, first, heads)
    attended = cut_swap(att_part, cut_count, True, 2).reshape(-1, features)
    x_two = x_rows.reshape(-1, features) + plain_dot(attended, w_output)
    norm_two, _ = norm_parts(x_two)
    h_two = (norm_two * gain_two).astype(low)
    h2_all = cut_gather(h_two.reshape(micro_count, row_count, features), cut_count, 3).reshape(-1, features)
    g_all = grad_all.reshape(-1, features)
    tokens_all = micro_count * length

    tile = 2 * row_count
    slots = tile_slots(capacity, row_count, tile)
    kept = codes >= 0
    chosen = jnp.where(kept, codes // capacity, -1)
    parity = (jnp.arange(length, dtype=jnp.int32) // row_count) % 2
    spot = jnp.where(kept, chosen * slots + parity * capacity + codes % capacity, -1).reshape(tokens_all, 1)
    small = jnp.concatenate([router, mixer, jnp.zeros((features, 126 - expert_count), low)], axis=1)
    out_part, d_h2_part, dots, d_own_in, d_own_out, d_weights_in, d_weights_out = feed(
        h2_all, g_all, chosen.reshape(tokens_all, 1), spot, small, own_in, own_out, weights_in, weights_out, tile, slots
    )
    dots = dots.reshape(micro_count, cut_count, 8, row_count).transpose(1, 0, 2, 3)
    d_h2, dots = cut_scatter(d_h2_part.reshape(micro_count, cut_count, row_count, features), dots, 4)
    out_sum = lax.psum_scatter(
        out_part.reshape(micro_count, length, features), "cuts", scatter_dimension=1, tiled=True
    )
    output = (x_two.reshape(out_sum.shape) + out_sum.astype(f32)).astype(low)

    rows = features // (group_count * cut_count)
    sums_here = rows % 16 == 0
    own_chosen = jnp.where(code >= 0, code // capacity, -1)[..., None]
    by_micro = lambda a: a.reshape(micro_count, row_count, features)
    place = (lax.axis_index("expert") * cut_count + cut) * rows
    own_rows = lambda w: lax.dynamic_slice_in_dim(w, place, rows, 0)
    w_rows = jnp.stack([own_rows(w) for w in (w_query, w_key, w_value)])
    grad_tokens, grad_output, grad_small, grad_qkv, grad_dense_in, grad_dense_out, norm_sum = back(
        d_h2, dots, own_chosen, by_micro(h_two), by_micro(x_two), cotangent[0], attended, w_output, qkv, first, lse, w_qkv,
        h_all, tokens[0], gain_one[None], gain_two[None], small,
        d_own_in.reshape(group_count, cut_count, rows, share), d_own_out.reshape(group_count, piece, features), w_rows,
        heads, expert_count, sums_here, 5,
    )
    sum_groups = lambda part: lax.psum_scatter(
        part.reshape(-1, part.shape[-1]), "expert", scatter_dimension=0, tiled=True
    )
    grad_expert_in = sum_groups(d_weights_in).astype(f32)
    grad_expert_out = sum_groups(d_weights_out).astype(f32)
    if not sums_here:
        swap = lambda part: lax.all_to_all(
            part.reshape(cut_count, rows, -1), "cuts", split_axis=0, concat_axis=0
        ).astype(f32)
        wide = jnp.sum(swap(sum_groups(grad_output)), axis=0)
        grad_output, grad_small = wide[:, :features], wide[:, features:]
        grad_qkv = swap(sum_groups(grad_qkv)).reshape(cut_count, rows, 3, head_width).transpose(2, 1, 0, 3)
        grad_qkv = grad_qkv.reshape(3, rows, features)
        grad_dense_in = swap(sum_groups(d_own_in)).reshape(cut_count, rows, group_count, piece).transpose(1, 2, 0, 3)
        grad_dense_in = grad_dense_in.reshape(rows, hidden_count)
        grad_dense_out = sum_groups(d_own_out).astype(f32)
        norm_sum = jnp.sum(grad_qkv * w_rows.astype(f32), axis=(0, 2))[:, None]

    grad_norm1 = norm_sum[:, 0] / own_rows(gain_one)
    return (
        output[None], grad_tokens[None], grad_norm1, grad_qkv[0], grad_qkv[1], grad_qkv[2], grad_output,
        grad_small[:, expert_count + 2], grad_dense_in, grad_dense_out, grad_small[:, :expert_count],
        grad_small[:, expert_count : expert_count + 2], grad_expert_in[None], grad_expert_out[None],
    )


def solution(mesh):
    in_specs = (
        P("expert", None, "cuts", None),
        P("expert", None, "cuts", None),
        P("expert", None, None),
        P("expert", None, "cuts"),
        P("expert", None, "cuts"),
        P("expert", None, "cuts"),
        P(),
        P(),
        P(),
        P(),
        P(),
        P(),
        P(),
        P(),
        P(),
        P(),
        P("expert", None, "cuts"),
        P("expert", "cuts", None),
    )
    out_specs = (
        P("expert", None, "cuts", None),
        P("expert", None, "cuts", None),
        P(("expert", "cuts")),
        P(("expert", "cuts"), None),
        P(("expert", "cuts"), None),
        P(("expert", "cuts"), None),
        P(("expert", "cuts"), None),
        P(("expert", "cuts")),
        P(("expert", "cuts"), None),
        P(("expert", "cuts"), None),
        P(("expert", "cuts"), None),
        P(("expert", "cuts"), None),
        P("expert", None, "cuts"),
        P("expert", "cuts", None),
    )
    return jax.shard_map(local, mesh=mesh, in_specs=in_specs, out_specs=out_specs, check_vma=False)
```

```python
from functools import partial

import jax
import jax.numpy as jnp
from jax import lax
from jax.experimental import pallas as pl
from jax.experimental.pallas import tpu as pltpu
from jax.sharding import PartitionSpec as P

MESH = pl.DeviceIdType.MESH
score_scale = 0.125
masked_value = -1e30
norm_eps = 1e-05


def plain_dot(left, right):
    return jnp.dot(left, right, preferred_element_type=jnp.float32)


def lead_dot(left, right):
    return lax.dot_general(
        left, right, (((0,), (0,)), ((), ())), preferred_element_type=jnp.float32
    )


def tail_dot(left, right):
    return lax.dot_general(
        left, right, (((1,), (1,)), ((), ())), preferred_element_type=jnp.float32
    )


def head_masks(width, heads):
    lane = lax.broadcasted_iota(jnp.int32, (1, width), 1)
    size = width // heads
    return [((lane >= h * size) & (lane < (h + 1) * size)) for h in range(heads)]


def allowed_mask(docs_ref, docs_col_ref, m, start, rows, keys):
    query_spots = start + lax.broadcasted_iota(jnp.int32, (rows, keys), 0)
    key_spots = lax.broadcasted_iota(jnp.int32, (rows, keys), 1)
    return (key_spots <= query_spots) & (docs_ref[m, :, 0:keys] == docs_col_ref[m, pl.ds(start, rows), :])


def attend_one(heads, m, qkv_ref, docs_ref, docs_col_ref, att_ref, lse_ref):
    length, width = att_ref.shape[1], att_ref.shape[2]
    rows = min(256, length)
    masks = head_masks(width, heads)
    for block in range(length // rows):
        start, keys = block * rows, (block + 1) * rows
        allowed = allowed_mask(docs_ref, docs_col_ref, m, start, rows, keys)
        query = qkv_ref[m, pl.ds(start, rows), 0:width] * jnp.bfloat16(score_scale)
        key = qkv_ref[m, 0:keys, width : 2 * width]
        value = qkv_ref[m, 0:keys, 2 * width : 3 * width]
        att = jnp.zeros((rows, width), jnp.float32)
        logs = jnp.zeros((rows, width), jnp.float32)
        for mask in masks:
            scores = tail_dot(jnp.where(mask, query, jnp.bfloat16(0)), key)
            scores = jnp.where(allowed, scores, masked_value)
            top = jnp.max(scores, axis=-1, keepdims=True)
            raised = jnp.exp(scores - top)
            total = jnp.sum(raised, axis=-1, keepdims=True)
            probs = (raised * (1.0 / total)).astype(jnp.bfloat16)
            att = jnp.where(mask, plain_dot(probs, value), att)
            logs = jnp.where(mask, top + jnp.log(total), logs)
        att_ref[m, pl.ds(start, rows), :] = att.astype(jnp.bfloat16)
        lse_ref[m, pl.ds(start, rows), :] = logs


def norm_parts(values):
    center = values - jnp.mean(values, axis=-1, keepdims=True)
    spread = jnp.mean(center * center, axis=-1, keepdims=True)
    scale = lax.rsqrt(spread + norm_eps)
    return center * scale, scale


def norm_back(normed, scale, gain, grad):
    inner = grad * gain
    return scale * (
        inner
        - jnp.mean(inner, axis=-1, keepdims=True)
        - normed * jnp.mean(inner * normed, axis=-1, keepdims=True)
    )


def gelu_pair(values):
    phi = 0.5 * (1.0 + lax.erf(values * (0.5**0.5)))
    bell = jnp.exp(-0.5 * values * values) * ((2.0 * jnp.pi) ** -0.5)
    return values * phi, phi + values * bell


def tile_slots(capacity, row_count, tile):
    return -(-capacity * (tile // row_count) // 16) * 16


def token_table(spot, width):
    return (spot == lax.broadcasted_iota(jnp.int32, (spot.shape[0], width), 1)).astype(jnp.bfloat16)


def lane_softmax(logits, lanes, first, count):
    inside = (lanes >= first) & (lanes < first + count)
    raised = jnp.exp(logits - jnp.max(jnp.where(inside, logits, masked_value), axis=-1, keepdims=True))
    raised = jnp.where(inside, raised, 0.0)
    return raised / jnp.sum(raised, axis=-1, keepdims=True)


def route(logits, chosen, expert_count):
    lanes = lax.broadcasted_iota(jnp.int32, logits.shape, 1)
    routed = lane_softmax(logits, lanes, 0, expert_count)
    mixing = lane_softmax(logits, lanes, expert_count, 2)
    pick = lambda values, lane: jnp.sum(jnp.where(lanes == lane, values, 0.0), axis=-1, keepdims=True)
    return pick(routed, chosen), pick(mixing, expert_count), pick(mixing, expert_count + 1), routed, mixing


def softmax_back(probs, grad):
    return probs * (grad - jnp.sum(probs * grad, axis=-1, keepdims=True))


def line_copy(src, dst, send, recv, group, target):
    return pltpu.make_async_remote_copy(
        src_ref=src, dst_ref=dst, send_sem=send, recv_sem=recv, device_id=(group, target), device_id_type=MESH
    )


def greet_all(cut_count, group_count):
    cut = lax.axis_index("cuts")
    group = lax.axis_index("expert")
    barrier = pltpu.get_barrier_semaphore()
    for hop in range(1, cut_count):
        pl.semaphore_signal(barrier, inc=1, device_id=(group, jnp.bitwise_xor(cut, hop)), device_id_type=MESH)
    for hop in range(1, group_count):
        pl.semaphore_signal(barrier, inc=1, device_id=(jnp.bitwise_xor(group, hop), cut), device_id_type=MESH)
    pl.semaphore_wait(barrier, cut_count + group_count - 2)


class LineGather:
    def __init__(self, buf, far_send, far_recv, pair_send, pair_recv):
        self.buf = buf
        self.sems = (far_send, far_recv, pair_send, pair_recv)
        self.cut = lax.axis_index("cuts")
        self.group = lax.axis_index("expert")
        self.level, self.side = self.cut // 2, self.cut % 2
        self.levels = buf.shape[1] // 2

    def place(self, n):
        low, high = self.level, self.levels - 1 - self.level
        near = jnp.minimum(low, high)
        paired = n <= 2 * near
        distance = jnp.where(paired, (n + 1) // 2, n - near)
        below = jnp.where(paired, n % 2 == 1, low > high)
        return jnp.where(below, self.level - distance, self.level + distance), below

    def far_copy(self, m, level, target, send):
        block = self.buf.at[m, 2 * level + self.side]
        return line_copy(block, block, self.sems[0].at[m, send], self.sems[1].at[m, level], self.group, target)

    def pair_copy(self, m, level, side):
        block = self.buf.at[m, 2 * level + side]
        return line_copy(
            block, block, self.sems[2].at[m, level], self.sems[3].at[m, level], self.group, jnp.bitwise_xor(self.cut, 1)
        )

    def start(self, m):
        @pl.when(self.level + 1 < self.levels)
        def _():
            self.far_copy(m, self.level, self.cut + 2, self.level).start()

        @pl.when(self.level > 0)
        def _():
            self.far_copy(m, self.level, self.cut - 2, self.levels).start()

        self.pair_copy(m, self.level, self.side).start()

    def take(self, m, n):
        level, below = self.place(n)

        @pl.when(n > 0)
        def _():
            target = jnp.where(below, self.cut + 2, self.cut - 2)
            self.far_copy(m, level, target, level).wait_recv()

            @pl.when(jnp.where(below, self.level + 1 < self.levels, self.level > 0))
            def _():
                self.far_copy(m, level, target, level).start()

            self.pair_copy(m, level, self.side).start()

        self.pair_copy(m, level, 1 - self.side).wait_recv()
        return level

    def finish(self, m):
        @pl.when(self.level + 1 < self.levels)
        def _():
            self.far_copy(m, self.level, self.cut + 2, self.level).wait_send()

        @pl.when(self.level > 0)
        def _():
            self.far_copy(m, self.level, self.cut - 2, self.levels).wait_send()

        for n in range(self.levels):
            level, below = self.place(n)
            if n:
                @pl.when(jnp.where(below, self.level + 1 < self.levels, self.level > 0))
                def _():
                    self.far_copy(m, level, self.cut, level).wait_send()

            self.pair_copy(m, level, self.side).wait_send()


class LineSum:
    def __init__(self, part, pair_buf, far_buf, pair_send, pair_recv, send, recv):
        self.part, self.pair_buf, self.far_buf = part, pair_buf, far_buf
        self.sems = (pair_send, pair_recv, send, recv)
        self.cut = lax.axis_index("cuts")
        self.group = lax.axis_index("expert")
        self.level, self.side = self.cut // 2, self.cut % 2
        self.levels = part.shape[1] // 2

    def pair_copy(self, m, level):
        return line_copy(
            self.part.at[m, 2 * level + 1 - self.side], self.pair_buf.at[m, level], self.sems[0].at[m, level],
            self.sems[1].at[m, level], self.group, jnp.bitwise_xor(self.cut, 1),
        )

    def far_copy(self, m, level, up):
        target = self.cut + 2 if up else self.cut - 2
        slot = level if up else jnp.where(level == self.level - 1, self.levels, level)
        return line_copy(
            self.pair_buf.at[m, level], self.far_buf.at[m, slot], self.sems[2].at[m, level], self.sems[3].at[m, slot],
            self.group, target,
        )

    def arrived(self, m, slot):
        line_copy(
            self.far_buf.at[m, slot], self.far_buf.at[m, slot], self.sems[2].at[m, 0], self.sems[3].at[m, slot],
            self.group, self.cut,
        ).wait_recv()
        return self.far_buf[m, slot].astype(jnp.float32)

    def start(self, m):
        def one(k, carry):
            self.pair_copy(m, jnp.where(k % 2 == 0, self.levels - 1 - k // 2, k // 2)).start()
            return carry

        lax.fori_loop(0, self.levels, one, 0)

    def pairs(self, m):
        def one(k, carry):
            level = jnp.where(k % 2 == 0, self.levels - 1 - k // 2, k // 2)
            self.pair_copy(m, level).wait_recv()
            total = self.part[m, 2 * level + self.side].astype(jnp.float32) + self.pair_buf[m, level].astype(jnp.float32)
            self.pair_buf[m, level] = total.astype(self.pair_buf.dtype)
            @pl.when((self.level == 0) & (level > 0))
            def _():
                self.far_copy(m, level, True).start()

            @pl.when((self.level == self.levels - 1) & (level < self.levels - 1))
            def _():
                self.far_copy(m, level, False).start()

            return carry

        lax.fori_loop(0, self.levels, one, 0)

    def pass_on(self, m, level, up):
        @pl.when((level > self.level) if up else (level < self.level))
        def _():
            total = self.pair_buf[m, level].astype(jnp.float32) + self.arrived(m, level)
            self.pair_buf[m, level] = total.astype(self.pair_buf.dtype)
            self.far_copy(m, level, up).start()

    def hop(self, m, j):
        inner = (self.level > 0) & (self.level < self.levels - 1)
        lower = 2 * self.level < self.levels

        @pl.when(inner & lower)
        def _():
            self.pass_on(m, self.levels - 1 - j, True)
            self.pass_on(m, j, False)

        @pl.when(inner & jnp.logical_not(lower))
        def _():
            self.pass_on(m, j, False)
            self.pass_on(m, self.levels - 1 - j, True)

    def finish(self, m, out_ref):
        out_ref[m] = self.pair_buf[m, self.level].astype(jnp.float32)

        @pl.when(self.level > 0)
        def _():
            out_ref[m] = out_ref[m] + self.arrived(m, self.level)

        @pl.when(self.level < self.levels - 1)
        def _():
            out_ref[m] = out_ref[m] + self.arrived(m, self.levels)

        def one(level, carry):
            self.pair_copy(m, level).wait_send()

            @pl.when(level > self.level)
            def _():
                self.far_copy(m, level, True).wait_send()

            @pl.when(level < self.level)
            def _():
                self.far_copy(m, level, False).wait_send()

            return carry

        lax.fori_loop(0, self.levels, one, 0)


def row_to_column(values):
    return jnp.transpose(values.astype(jnp.float32))


def front_kernel(
    heads, capacity, slots,
    x_ref, gain_ref, w_query_ref, w_key_ref, w_value_ref, docs_ref, docs_col_ref, ids_ref, slot_ref, kept_ref, expert_in_ref,
    h_all_ref, qkv_ref, lse_ref, att_ref, w_qkv_ref, codes_ref, weights_ref,
    att_part, own_code, far_send, far_recv, pair_send, pair_recv, load_sem, swap_send, swap_recv, swap_own, code_send,
    code_recv, weight_send, weight_recv, weight_own,
):
    micro_count, cut_count, rows, features = h_all_ref.shape
    group_count = weights_ref.shape[0]
    width = features // cut_count
    cut = lax.axis_index("cuts")
    group = lax.axis_index("expert")
    low = jnp.bfloat16
    loads = []
    for k, ref in enumerate((w_query_ref, w_key_ref, w_value_ref)):
        loads.append(pltpu.make_async_copy(
            ref.at[:, pl.ds(pl.multiple_of(cut * width, width), width)], w_qkv_ref.at[:, k * width : (k + 1) * width],
            load_sem.at[k],
        ))
        loads[-1].start()
    greet_all(cut_count, group_count)

    line = LineGather(h_all_ref, far_send, far_recv, pair_send, pair_recv)

    def norm_step(m, carry):
        normed, _ = norm_parts(x_ref[m].astype(jnp.float32))
        h_all_ref[m, cut] = (normed * gain_ref[...]).astype(low)
        line.start(m)
        return carry

    lax.fori_loop(0, micro_count, norm_step, 0)

    def weight_copy(hop):
        return line_copy(
            expert_in_ref, weights_ref.at[group], weight_send.at[hop - 1], weight_recv.at[hop - 1],
            jnp.bitwise_xor(group, hop), cut,
        )

    own_weight = pltpu.make_async_copy(expert_in_ref, weights_ref.at[group], weight_own)
    for hop in range(group_count - 1, 0, -1):
        weight_copy(hop).start()
    own_weight.start()

    chosen = jnp.where(kept_ref[...] == 1, ids_ref[...], -1)
    spot = jnp.where(kept_ref[...] == 1, ids_ref[...] * slots + cut % 2 * capacity + slot_ref[...], -1)
    own_code[...] = jnp.zeros_like(own_code)
    for m in range(micro_count):
        own_code[m, 0:1] = chosen[m : m + 1]
        own_code[m, 1:2] = spot[m : m + 1]
    codes_ref[cut] = own_code[...]

    def code_copy(hop):
        return line_copy(
            own_code, codes_ref.at[cut], code_send.at[hop], code_recv.at[hop], group, jnp.bitwise_xor(cut, hop)
        )

    for hop in range(1, cut_count):
        code_copy(hop).start()
    for load in loads:
        load.wait()

    def tile_step(n, m):
        level = line.take(m, n)
        h_tile = h_all_ref[m, pl.ds(2 * level, 2)].reshape(2 * rows, features)
        spots = pl.ds(pl.multiple_of(level * 2 * rows, 2 * rows), 2 * rows)
        qkv_ref[m, spots, :] = plain_dot(h_tile, w_qkv_ref[...]).astype(low)

    def early(i, carry):
        tile_step(i // micro_count, i % micro_count)
        return carry

    levels = cut_count // 2
    lax.fori_loop(0, (levels - 1) * micro_count, early, 0)

    def swap_copy(m, hop):
        target = jnp.bitwise_xor(cut, hop)
        return line_copy(
            att_part.at[m, pl.ds(pl.multiple_of(target * rows, rows), rows), :],
            att_ref.at[m, :, pl.ds(pl.multiple_of(cut * width, width), width)],
            swap_send.at[m, hop], swap_recv.at[m, hop], group, target,
        )

    def swap_keep(m):
        return pltpu.make_async_copy(
            att_part.at[m, pl.ds(pl.multiple_of(cut * rows, rows), rows), :],
            att_ref.at[m, :, pl.ds(pl.multiple_of(cut * width, width), width)],
            swap_own.at[m],
        )

    def late(m, carry):
        tile_step(levels - 1, m)
        attend_one(heads, m, qkv_ref, docs_ref, docs_col_ref, att_part, lse_ref)
        for hop in range(cut_count - 1, 0, -1):
            swap_copy(m, hop).start()
        swap_keep(m).start()
        return carry

    lax.fori_loop(0, micro_count, late, 0)
    for hop in range(1, cut_count):
        code_copy(hop).wait()
    for m in range(micro_count):
        line.finish(m)
    for m in range(micro_count):
        for hop in range(cut_count - 1, 0, -1):
            swap_copy(m, hop).wait()
        swap_keep(m).wait()
    for hop in range(1, group_count):
        weight_copy(hop).wait()
    own_weight.wait()


def front(
    x, gain, w_query, w_key, w_value, docs, docs_col, ids, slot_ids, kept, expert_in, group_count, cut_count, heads, capacity,
    slots, call_id,
):
    micro_count, rows, features = x.shape
    length, levels, width = cut_count * rows, cut_count // 2, features // cut_count
    low, f32 = jnp.bfloat16, jnp.float32
    shape = jax.ShapeDtypeStruct
    dma = pltpu.SemaphoreType.DMA
    vmem, far = pl.BlockSpec(memory_space=pltpu.VMEM), pl.BlockSpec(memory_space=pl.ANY)
    return pl.pallas_call(
        partial(front_kernel, heads, capacity, slots),
        out_shape=(
            shape((micro_count, cut_count, rows, features), low),
            shape((micro_count, length, 3 * width), low),
            shape((micro_count, length, width), f32),
            shape((micro_count, rows, features), low),
            shape((features, 3 * width), low),
            shape((cut_count, micro_count, 8, rows), jnp.int32),
            shape((group_count, *expert_in.shape), low),
        ),
        in_specs=[vmem, vmem, far, far, far, vmem, vmem, vmem, vmem, vmem, far],
        out_specs=[vmem] * 6 + [far],
        scratch_shapes=[
            pltpu.VMEM((micro_count, length, width), low),
            pltpu.VMEM((micro_count, 8, rows), jnp.int32),
            dma((micro_count, levels + 1)), dma((micro_count, levels)), dma((micro_count, levels)), dma((micro_count, levels)),
            dma((3,)), dma((micro_count, cut_count)), dma((micro_count, cut_count)), dma((micro_count,)),
            dma((cut_count,)), dma((cut_count,)), dma((group_count - 1,)), dma((group_count - 1,)), dma(()),
        ],
        compiler_params=pltpu.CompilerParams(collective_id=call_id, has_side_effects=True, vmem_limit_bytes=56 * 2**20),
    )(x, gain, w_query, w_key, w_value, docs, docs_col, ids, slot_ids, kept, expert_in)


def feed_kernel(
    slots, strided, early,
    x_ref, att_ref, w_out_ref, gain_ref, small_ref, codes_ref, g_ref, dense_in_ref, dense_out_ref, weights_in_ref,
    expert_out_ref,
    x_two_ref, h_own_ref, out_ref, dh_ref, sums_ref, d_own_in_ref, d_own_out_ref, d_in_ref, d_out_ref, weights_out_ref,
    got_in_ref, got_out_ref,
    h_all, g_buf, sent, g_sent, hidden_buf, pre_buf, back_buf, side_buf, own_in, own_out, in_buf, out_buf, in_stage, out_stage,
    dots, dots_in, pair_buf, far_buf,
    far_send, far_recv, pair_send, pair_recv, line_send, line_recv, two_send, two_recv, load_sem, in_sem, out_sem,
    stage_sem, dot_send, dot_recv, weight_send, weight_recv, weight_own,
    early_send, early_recv,
):
    micro_count, cut_count, rows, features = h_all.shape
    group_count = weights_out_ref.shape[0]
    share = own_in.shape[1]
    levels, tile = cut_count // 2, 2 * rows
    expert_count = group_count
    cut = lax.axis_index("cuts")
    group = lax.axis_index("expert")
    low, f32 = jnp.bfloat16, jnp.float32
    half = share
    loads = [pltpu.make_async_copy(g_ref, g_buf, load_sem.at[0])]
    for k in range(features // half):
        loads.append(pltpu.make_async_copy(w_out_ref.at[:, k * half : (k + 1) * half], in_buf.at[k], load_sem.at[1 + k]))
    first_load = len(loads)
    if strided:
        piece = share // group_count
        for g in range(group_count):
            spot = pl.ds(pl.multiple_of((g * cut_count + cut) * piece, piece), piece)
            here = pl.ds(g * piece, piece)
            loads.append(pltpu.make_async_copy(dense_in_ref.at[:, spot], own_in.at[:, here], load_sem.at[len(loads)]))
            loads.append(pltpu.make_async_copy(dense_out_ref.at[spot, :], own_out.at[here, :], load_sem.at[len(loads)]))
    else:
        loads.append(pltpu.make_async_copy(dense_in_ref, own_in, load_sem.at[len(loads)]))
        loads.append(pltpu.make_async_copy(dense_out_ref, own_out, load_sem.at[len(loads)]))
    for load in loads[1:]:
        load.start()
    loads[0].start()
    greet_all(cut_count, group_count)
    for load in loads[1:first_load]:
        load.wait()

    line = LineGather(h_all, far_send, far_recv, pair_send, pair_recv)

    def norm_step(m, carry):
        att = att_ref[m]
        projected = jnp.concatenate([plain_dot(att, in_buf[k]) for k in range(features // half)], axis=1)
        x_two = x_ref[m].astype(f32) + projected
        x_two_ref[m] = x_two
        normed, _ = norm_parts(x_two)
        h_two = (normed * gain_ref[...]).astype(low)
        h_all[m, cut] = h_two
        h_own_ref[m] = h_two
        line.start(m)
        return carry

    lax.fori_loop(0, micro_count, norm_step, 0)

    def weight_copy(hop):
        return line_copy(
            expert_out_ref, weights_out_ref.at[group], weight_send.at[hop - 1], weight_recv.at[hop - 1],
            jnp.bitwise_xor(group, hop), cut,
        )

    own_weight = pltpu.make_async_copy(expert_out_ref, weights_out_ref.at[group], weight_own)
    for hop in range(group_count - 1, 0, -1):
        weight_copy(hop).start()
    own_weight.start()
    for load in loads[first_load:]:
        load.wait()
    loads[0].wait()
    lanes = lax.broadcasted_iota(jnp.int32, (tile, 128), 1)

    def columns(m, level):
        both = [row_to_column(codes_ref[2 * level + k, m]) for k in range(2)]
        both = jnp.concatenate(both, axis=0).astype(jnp.int32)
        return both[:, 0:1], both[:, 1:2]

    def dense_step(i, carry):
        n, m = i // micro_count, i % micro_count
        level = line.take(m, n)
        t = m * levels + level
        blocks = pl.ds(2 * level, 2)
        here = pl.ds(pl.multiple_of(t * tile, tile), tile)
        spots = pl.ds(pl.multiple_of(t * slots, slots), slots)
        h_two = h_all[m, blocks].reshape(tile, features)
        chosen, spot = columns(m, level)
        gate, mix_dense, mix_expert, _, _ = route(plain_dot(h_two, small_ref[...]), chosen, expert_count)
        mix_gate = mix_expert * gate
        table = token_table(spot, expert_count * slots)
        grad_y = g_buf[m, blocks].reshape(tile, features).astype(f32)
        rows_sent = lead_dot(table, h_two).astype(low)
        rows_back = lead_dot(table, (mix_gate * grad_y).astype(low)).astype(low)
        for e in range(expert_count):
            sent[e, spots, :] = rows_sent[e * slots : (e + 1) * slots]
            g_sent[e, spots, :] = rows_back[e * slots : (e + 1) * slots]
        act, slope = gelu_pair(plain_dot(h_two, own_in[...]))
        dense = plain_dot(act.astype(low), own_out[...])
        side_buf[here, :] = jnp.where(lanes == 0, jnp.sum(grad_y * dense, axis=-1, keepdims=True), mix_gate)
        d_pre = (tail_dot((mix_dense * grad_y).astype(low), own_out[...]) * slope).astype(low)
        hidden_buf[here, :] = (mix_dense * act).astype(low)
        pre_buf[here, :] = d_pre
        out_ref[m, blocks] = (mix_dense * dense).astype(low).reshape(2, rows, features)
        back_buf[m, blocks] = tail_dot(d_pre, own_in[...]).astype(low).reshape(2, rows, features)
        return carry

    lax.fori_loop(0, levels * micro_count, dense_step, 0)

    for hop in range(1, group_count):
        weight_copy(hop).wait()
    own_weight.wait()

    def expert_at(i):
        return jnp.bitwise_xor(group, group_count - 1 - i)

    def load_in(i):
        return pltpu.make_async_copy(weights_in_ref.at[expert_at(i)], in_buf.at[i % 2], in_sem.at[i % 2])

    def load_out(i):
        return pltpu.make_async_copy(weights_out_ref.at[expert_at(i)], out_buf.at[i % 2], out_sem.at[i % 2])

    def keep_in(i):
        return pltpu.make_async_copy(in_stage, d_in_ref.at[expert_at(i)], stage_sem.at[0])

    def keep_out(i):
        return pltpu.make_async_copy(out_stage, d_out_ref.at[expert_at(i)], stage_sem.at[1])

    def early_copy(k):
        mask, kind, side, at = ((3, 0, 1, 1), (3, 1, 2, 1), (2, 1, 2, 0), (1, 0, 1, 0))[k]
        src, dst = ((d_in_ref, got_in_ref), (d_out_ref, got_out_ref))[kind]
        return line_copy(
            src.at[jnp.bitwise_xor(group, mask)], dst.at[at], early_send.at[k], early_recv.at[k],
            jnp.bitwise_xor(group, side), cut,
        )

    load_in(0).start()
    load_out(0).start()

    def expert_step(i, carry):
        @pl.when(i + 1 < expert_count)
        def _():
            load_in(i + 1).start()
            load_out(i + 1).start()

        load_in(i).wait()
        load_out(i).wait()
        e, at = expert_at(i), i % 2
        rows_in, rows_back = sent[e], g_sent[e]
        act, slope = gelu_pair(plain_dot(rows_in, in_buf[at]))
        inner = act.astype(low)
        d_pre = (tail_dot(rows_back, out_buf[at]) * slope).astype(low)

        @pl.when(i > 0)
        def _():
            keep_in(i).wait()
            keep_out(i).wait()

        if early:
            @pl.when(i == 1)
            def _():
                early_copy(0).start()
                early_copy(1).start()

            @pl.when(i == 2)
            def _():
                early_copy(2).start()

            @pl.when(i == 3)
            def _():
                early_copy(3).start()

        in_stage[...] = lead_dot(rows_in, d_pre).astype(low)
        keep_in(i).start()
        out_stage[...] = lead_dot(inner, rows_back).astype(low)
        keep_out(i).start()
        sent[e] = tail_dot(d_pre, in_buf[at]).astype(low)
        g_sent[e] = plain_dot(inner, out_buf[at]).astype(low)
        return carry

    lax.fori_loop(0, expert_count, expert_step, 0)
    total = LineSum(back_buf, pair_buf, far_buf, line_send, line_recv, two_send, two_recv)

    def combine_step(m, level, carry):
        t = m * levels + level
        blocks = pl.ds(2 * level, 2)
        here = pl.ds(pl.multiple_of(t * tile, tile), tile)
        spots = pl.ds(pl.multiple_of(t * slots, slots), slots)
        _, spot = columns(m, level)
        table = token_table(spot, expert_count * slots)
        gather = lambda ref: jnp.concatenate([ref[e, spots, :] for e in range(expert_count)], axis=0)
        back_rows = plain_dot(table, gather(sent)).reshape(2, rows, features)
        back_buf[m, blocks] = (back_buf[m, blocks].astype(f32) + back_rows).astype(low)
        grad_y = g_buf[m, blocks].reshape(tile, features).astype(f32)
        part = plain_dot(table, gather(g_sent))
        side = side_buf[here, :]
        scaled = (side[:, 1:2] * part).reshape(2, rows, features)
        out_ref[m, blocks] = (out_ref[m, blocks].astype(f32) + scaled).astype(low)
        side = jnp.where(lanes == 1, jnp.sum(grad_y * part, axis=-1, keepdims=True), side)
        for k in range(2):
            dots[2 * level + k, m] = jnp.transpose(side[k * rows : (k + 1) * rows])[0:8]
        return carry

    for m in range(micro_count):
        lax.fori_loop(0, levels, partial(combine_step, m), 0)
        total.start(m)
        total.pairs(m)

    def dot_copy(hop):
        target = jnp.bitwise_xor(cut, hop)
        return line_copy(dots.at[target], dots_in.at[hop - 1], dot_send.at[hop - 1], dot_recv.at[hop - 1], group, target)

    for hop in range(1, cut_count):
        dot_copy(hop).start()
    token_rows = micro_count * cut_count * rows
    h_flat, g_flat = h_all.reshape(token_rows, features), g_buf.reshape(token_rows, features)

    def dense_weights(k):
        part = pl.ds(k * 256, 256)
        d_own_in_ref[part, :] = lead_dot(h_flat[:, part], pre_buf[...]).astype(low)
        d_own_out_ref[:, part] = lead_dot(hidden_buf[...], g_flat[:, part]).astype(low)

    slices = features // 256
    for k in range(slices // 2):
        dense_weights(k)
    for j in range(levels - 1):
        total.hop(0, j)
    for k in range(slices // 2, slices):
        dense_weights(k)
    for m in range(1, micro_count):
        for j in range(levels - 1):
            total.hop(m, j)
    sums = dots[cut]
    for hop in range(1, cut_count):
        dot_copy(hop).wait()
        sums = sums + dots_in[hop - 1]
    sums_ref[...] = sums
    keep_in(0).wait()
    keep_out(0).wait()
    for k in range(4 if early else 0):
        early_copy(k).wait()
    for m in range(micro_count):
        line.finish(m)
    for m in range(micro_count):
        total.finish(m, dh_ref)


def feed(
    x, att, w_output, gain, small, codes, g_all, dense_in, dense_out, weights_in, expert_out, share, slots, strided, early,
    call_id,
):
    micro_count, rows, features = x.shape
    cut_count = codes.shape[0]
    group_count = weights_in.shape[0]
    levels, total = cut_count // 2, micro_count * cut_count * rows
    low, f32 = jnp.bfloat16, jnp.float32
    shape = jax.ShapeDtypeStruct
    dma = pltpu.SemaphoreType.DMA
    block = lambda *dims: pltpu.VMEM(dims, low)
    vmem, far = pl.BlockSpec(memory_space=pltpu.VMEM), pl.BlockSpec(memory_space=pl.ANY)
    whole = (micro_count, cut_count, rows, features)
    slot_rows = micro_count * levels * slots
    line = (micro_count, levels)
    return pl.pallas_call(
        partial(feed_kernel, slots, strided, early),
        out_shape=(
            shape((micro_count, rows, features), f32),
            shape((micro_count, rows, features), low),
            shape(whole, low),
            shape((micro_count, rows, features), f32),
            shape((micro_count, 8, rows), f32),
            shape((features, share), low),
            shape((share, features), low),
            shape((group_count, features, share), low),
            shape((group_count, share, features), low),
            shape((group_count, share, features), low),
            *(
                (shape((2, features, share), low), shape((2, share, features), low))
                if early else (shape((8, 128), low), shape((8, 128), low))
            ),
        ),
        in_specs=[vmem, vmem, far, vmem, vmem, vmem, far, far, far, far, far],
        out_specs=[vmem] * 7 + [far] * 5,
        scratch_shapes=[
            block(*whole), block(*whole),
            block(group_count, slot_rows, features), block(group_count, slot_rows, features),
            block(total, share), block(total, share), block(*whole), pltpu.VMEM((total, 128), f32),
            block(features, share), block(share, features), block(2, features, share), block(2, share, features),
            block(features, share), block(share, features),
            pltpu.VMEM((cut_count, micro_count, 8, rows), f32), pltpu.VMEM((cut_count - 1, micro_count, 8, rows), f32),
            block(*line, rows, features), block(micro_count, levels + 1, rows, features),
            dma((micro_count, levels + 1)), dma(line), dma(line), dma(line),
            dma(line), dma(line), dma(line), dma((micro_count, levels + 1)),
            dma((3 + 2 * group_count,)), dma((2,)), dma((2,)), dma((2,)),
            dma((cut_count - 1,)), dma((cut_count - 1,)), dma((group_count - 1,)), dma((group_count - 1,)), dma(()),
            dma((4,)), dma((4,)),
        ],
        compiler_params=pltpu.CompilerParams(collective_id=call_id, has_side_effects=True, vmem_limit_bytes=62 * 2**20),
    )(x, att, w_output, gain, small, codes, g_all, dense_in, dense_out, weights_in, expert_out)


def attend_back_one(heads, m, qkv_ref, docs_ref, docs_col_ref, lse_ref, back_ref, out_ref, key_acc, value_acc):
    length, width = back_ref.shape[1], back_ref.shape[2]
    rows = min(256, length)
    masks = head_masks(width, heads)
    key_acc[...] = jnp.zeros_like(key_acc)
    value_acc[...] = jnp.zeros_like(value_acc)
    zero = jnp.bfloat16(0)
    for block in range(length // rows):
        start, keys = block * rows, (block + 1) * rows
        allowed = allowed_mask(docs_ref, docs_col_ref, m, start, rows, keys)
        query = qkv_ref[m, pl.ds(start, rows), 0:width] * jnp.bfloat16(score_scale)
        key = qkv_ref[m, 0:keys, width : 2 * width]
        value = qkv_ref[m, 0:keys, 2 * width : 3 * width]
        back = back_ref[m, pl.ds(start, rows), :]
        logs = lse_ref[m, pl.ds(start, rows), :]
        query_grad = jnp.zeros((rows, width), jnp.float32)
        for h, mask in enumerate(masks):
            one_query = jnp.where(mask, query, zero)
            one_back = jnp.where(mask, back, zero)
            scores = jnp.where(allowed, tail_dot(one_query, key), masked_value)
            spot = h * (width // heads)
            probs = jnp.exp(scores - logs[:, spot : spot + 1])
            weighted = probs * tail_dot(one_back, value)
            delta = jnp.sum(weighted, axis=-1, keepdims=True)
            score_grad = (weighted - probs * delta).astype(jnp.bfloat16)
            query_grad = jnp.where(mask, plain_dot(score_grad, key), query_grad)
            key_acc[0:keys, :] += lead_dot(score_grad, one_query)
            value_acc[0:keys, :] += lead_dot(probs.astype(jnp.bfloat16), one_back)
        out_ref[m, pl.ds(start, rows), 0:width] = (query_grad * score_scale).astype(jnp.bfloat16)
    out_ref[m, :, width : 2 * width] = key_acc[...].astype(jnp.bfloat16)
    out_ref[m, :, 2 * width : 3 * width] = value_acc[...].astype(jnp.bfloat16)


def back_kernel(
    heads, expert_count, sums_here,
    dh_ref, dots_ref, codes_ref, h_ref, x_two_ref, gy_ref, att_ref, w_out_ref, qkv_ref, docs_ref, docs_col_ref, lse_ref,
    w_qkv_ref, h_all_ref, x_ref, gain_one_ref, gain_two_ref, small_ref, own_in_ref, own_out_ref, w_rows_ref, d_in_ref, d_out_ref,
    got_in_ref, got_out_ref,
    tokens_ref, wo_ref, small_out_ref, qkv_out_ref, in_out_ref, out_out_ref, norm_ref, late_in_ref, late_out_ref,
    d_x_two, g_att, d_att, back_all, d_qkv, key_acc, value_acc, d_small, part, pair_buf, far_buf, d_h_one, in_sum, out_sum,
    wo_part, qkv_part, wo_in, qkv_in, own_in_in, own_out_in, wo_mid, qkv_mid, in_mid, wo_end, qkv_end, in_end,
    pair_send, pair_recv, far_send, far_recv, swap_send, swap_recv, swap_own, one_send, one_recv, two_send, two_recv, two_own,
    late_send, late_recv, late_load_sem,
):
    micro_count, cut_count, rows, features = part.shape
    group_count, split, piece_rows, _ = wo_part.shape
    group_rows = split * piece_rows
    width = features // cut_count
    cut = lax.axis_index("cuts")
    group = lax.axis_index("expert")
    low, f32 = jnp.bfloat16, jnp.float32
    greet_all(cut_count, group_count if sums_here else 1)

    ones = ((own_in_ref, own_in_in), (own_out_ref, own_out_in), (wo_part, wo_in), (qkv_part, qkv_in))

    def one_copy(kind, hop):
        src, dst = ones[kind]
        target = jnp.bitwise_xor(group, hop)
        return line_copy(
            src.at[target], dst.at[hop - 1], one_send.at[kind, hop - 1], one_recv.at[kind, hop - 1], target, cut
        )

    def one_start(kind):
        for hop in range(1, group_count):
            one_copy(kind, hop).start()

    def one_finish(kind):
        src, dst = ones[kind]
        total = src[group].astype(f32)
        for hop in range(1, group_count):
            one_copy(kind, hop).wait_recv()
            total = total + dst[hop - 1].astype(f32)
        for hop in range(1, group_count):
            one_copy(kind, hop).wait_send()
        return total

    twos = ((in_mid, in_end), None, (wo_mid, wo_end), (qkv_mid, qkv_end))

    def two_copy(kind, hop):
        src, dst = twos[kind]
        target = jnp.bitwise_xor(cut, hop)
        return line_copy(src.at[target], dst.at[cut], two_send.at[kind, hop], two_recv.at[kind, hop], group, target)

    def two_keep(kind):
        src, dst = twos[kind]
        return pltpu.make_async_copy(src.at[cut], dst.at[cut], two_own.at[kind])

    def two_start(kind):
        for hop in range(cut_count - 1, 0, -1):
            two_copy(kind, hop).start()
        two_keep(kind).start()

    def two_finish(kind):
        for hop in range(cut_count - 1, 0, -1):
            two_copy(kind, hop).wait()
        two_keep(kind).wait()

    ends = ((d_in_ref, got_in_ref, in_sum, late_in_ref, 2), (d_out_ref, got_out_ref, out_sum, late_out_ref, 1))

    def late_load(kind, k):
        own, got, total, _, side = ends[kind]
        src = got.at[1] if k else own.at[jnp.bitwise_xor(group, side)]
        return pltpu.make_async_copy(src, total.at[k], late_load_sem.at[kind, k])

    def late_copy(kind):
        _, _, total, late, side = ends[kind]
        return line_copy(
            total.at[0], late, late_send.at[kind], late_recv.at[kind], jnp.bitwise_xor(group, side), cut
        )

    if sums_here:
        for kind in range(2):
            late_load(kind, 0).start()
            late_load(kind, 1).start()
        one_start(0)
        one_start(1)

    def swap_copy(m, hop):
        target = jnp.bitwise_xor(cut, hop)
        return line_copy(
            d_att.at[m, :, pl.ds(pl.multiple_of(target * width, width), width)],
            back_all.at[m, pl.ds(pl.multiple_of(cut * rows, rows), rows), :],
            swap_send.at[m, hop], swap_recv.at[m, hop], group, target,
        )

    def swap_keep(m):
        return pltpu.make_async_copy(
            d_att.at[m, :, pl.ds(pl.multiple_of(cut * width, width), width)],
            back_all.at[m, pl.ds(pl.multiple_of(cut * rows, rows), rows), :],
            swap_own.at[m],
        )

    small = small_ref[...]
    gain_two = gain_two_ref[...]
    d_small[...] = jnp.zeros_like(d_small)
    lanes = lax.broadcasted_iota(jnp.int32, (rows, 128), 1)

    def norm_two_step(m, carry):
        dots = jnp.transpose(dots_ref[m])
        chosen = row_to_column(codes_ref[cut, m])[:, 0:1].astype(jnp.int32)
        h_two = h_ref[m]
        gate, _, mix_expert, routed, mixing = route(plain_dot(h_two, small), chosen, expert_count)
        d_mixing = jnp.where(lanes == expert_count, dots[:, 0:1], gate * dots[:, 1:2])
        d_gate = jnp.where(lanes == chosen, mix_expert * dots[:, 1:2], 0.0)
        d_logits = (softmax_back(mixing, d_mixing) + softmax_back(routed, d_gate)).astype(low)
        d_h = dh_ref[m] + tail_dot(d_logits, small)
        normed, scale = norm_parts(x_two_ref[m])
        one_lane = (lanes == expert_count + 2).astype(low)
        d_small[...] += lead_dot(h_two, d_logits) + lead_dot((d_h * normed).astype(low), one_lane)
        d_x = gy_ref[m].astype(f32) + norm_back(normed, scale, gain_two, d_h)
        d_x_two[m] = d_x
        grad = d_x.astype(low)
        g_att[pl.ds(pl.multiple_of(m * rows, rows), rows), :] = grad
        d_att[m] = tail_dot(grad, w_out_ref[...]).astype(low)
        for hop in range(cut_count - 1, 0, -1):
            swap_copy(m, hop).start()
        swap_keep(m).start()
        return carry

    lax.fori_loop(0, micro_count, norm_two_step, 0)
    if sums_here:
        for kind in range(2):
            total = ends[kind][2]
            late_load(kind, 0).wait()
            late_load(kind, 1).wait()
            total[0] = (total[0].astype(f32) + total[1].astype(f32)).astype(low)
            late_copy(kind).start()

    def wo_step(g, carry):
        columns = pl.ds(pl.multiple_of(g * group_rows, group_rows), group_rows)
        grads = lead_dot(att_ref[:, columns], g_att[...]).astype(low)
        wo_part[g, :, :, 0:features] = grads.reshape(split, piece_rows, features)
        smalls = d_small[columns, :].astype(low)
        wo_part[g, :, :, features : features + 128] = smalls.reshape(split, piece_rows, 128)
        return carry

    lax.fori_loop(0, group_count, wo_step, 0)
    if sums_here:
        one_start(2)
    line = LineSum(part, pair_buf, far_buf, pair_send, pair_recv, far_send, far_recv)

    def attend_step(m, carry):
        for hop in range(cut_count - 1, 0, -1):
            swap_copy(m, hop).wait()
        swap_keep(m).wait()
        attend_back_one(heads, m, qkv_ref, docs_ref, docs_col_ref, lse_ref, back_all, d_qkv, key_acc, value_acc)
        for c in range(cut_count):
            part[m, c] = tail_dot(d_qkv[m, c * rows : (c + 1) * rows, :], w_qkv_ref[...]).astype(low)
        line.start(m)
        line.pairs(m)
        return carry

    lax.fori_loop(0, micro_count, attend_step, 0)

    def qkv_step(g, carry):
        columns = pl.ds(pl.multiple_of(g * group_rows, group_rows), group_rows)
        grads = jnp.zeros((group_rows, 3 * width), f32)
        for m in range(micro_count):
            grads = grads + lead_dot(h_all_ref[m, :, columns], d_qkv[m])
        qkv_part[g] = grads.astype(low).reshape(split, piece_rows, 3 * width)
        return carry

    for j in range(part.shape[1] // 2 - 1):
        line.hop(0, j)
    lax.fori_loop(0, group_count, qkv_step, 0)
    if sums_here:
        one_start(3)
        in_mid[...] = one_finish(0).astype(low)
        two_start(0)
        wo_mid[...] = one_finish(2).astype(low)
        two_start(2)
        out_out_ref[...] = one_finish(1)

    for m in range(1, micro_count):
        for j in range(part.shape[1] // 2 - 1):
            line.hop(m, j)

    def norm_one_step(m, carry):
        line.finish(m, d_h_one)
        total = d_h_one[m]
        normed, scale = norm_parts(x_ref[m].astype(f32))
        tokens_ref[m] = d_x_two[m] + norm_back(normed, scale, gain_one_ref[...], total)
        return carry

    if not sums_here:
        lax.fori_loop(0, micro_count, norm_one_step, 0)
        wo_ref[...] = wo_part[...]
        qkv_out_ref[...] = qkv_part[...]
        return
    norm_one_step(0, 0)
    qkv_mid[...] = one_finish(3).astype(low)
    two_start(3)
    two_finish(0)
    share_piece = in_end.shape[2] // group_count
    for c in range(cut_count):
        for g in range(group_count):
            spot = (g * cut_count + c) * share_piece
            in_out_ref[:, spot : spot + share_piece] = in_end[c, :, g * share_piece : (g + 1) * share_piece].astype(f32)
    two_finish(2)
    total = wo_end[0].astype(f32)
    for c in range(1, cut_count):
        total = total + wo_end[c].astype(f32)
    wo_ref[...] = total[:, :features]
    small_out_ref[...] = total[:, features:]
    for m in range(1, micro_count):
        norm_one_step(m, 0)
    two_finish(3)
    norm = jnp.zeros((piece_rows, 1), f32)
    for c in range(cut_count):
        for k in range(3):
            grad = qkv_end[c, :, k * width : (k + 1) * width].astype(f32)
            qkv_out_ref[k, :, c * width : (c + 1) * width] = grad
            weights = w_rows_ref[k, :, c * width : (c + 1) * width].astype(f32)
            norm = norm + jnp.sum(grad * weights, axis=-1, keepdims=True)
    norm_ref[...] = jnp.broadcast_to(norm, norm_ref.shape)
    for kind in range(2):
        late_copy(kind).wait()


def back(
    dh, dots, codes, h_two, x_two, gy, attended, w_output, qkv, docs, docs_col, lse, w_qkv, h_all, x, gain_one, gain_two,
    small, own_in, own_out, w_rows, d_in, d_out, got_in, got_out, heads, expert_count, sums_here,
    call_id,
):
    micro_count, rows, features = x.shape
    length = qkv.shape[1]
    cut_count = length // rows
    width = features // cut_count
    group_count = own_out.shape[0]
    piece_rows = features // (group_count * cut_count)
    share, piece = own_in.shape[3], own_out.shape[1]
    low, f32 = jnp.bfloat16, jnp.float32
    levels = cut_count // 2
    wide = features + 128
    shape = jax.ShapeDtypeStruct
    parts = (group_count, cut_count, piece_rows) if sums_here else (features // 256, 1, 256)
    if sums_here:
        outs = (
            shape((micro_count, rows, features), f32), shape((piece_rows, features), f32), shape((piece_rows, 128), f32),
            shape((3, piece_rows, features), f32), shape((piece_rows, share * cut_count), f32), shape((piece, features), f32),
            shape((piece_rows, 128), f32), shape((features, share), low), shape((share, features), low),
        )
    else:
        outs = (
            shape((micro_count, rows, features), f32), shape((*parts, wide), low),
            shape((8, 128), f32), shape((*parts, 3 * width), low), shape((8, 128), f32),
            shape((8, 128), f32), shape((8, 128), f32), shape((8, 128), low), shape((8, 128), low),
        )
    peers = max(group_count - 1, 1) if sums_here else 1
    block = lambda *dims: pltpu.VMEM(dims, low)
    mids = lambda w: block(cut_count, piece_rows, w) if sums_here else block(16, 128)
    ins = lambda w: block(peers, cut_count, piece_rows, w) if sums_here else block(16, 128)
    dma = pltpu.SemaphoreType.DMA
    vmem, far = pl.BlockSpec(memory_space=pltpu.VMEM), pl.BlockSpec(memory_space=pl.ANY)
    operands = (
        dh, dots, codes, h_two, x_two, gy, attended, w_output, qkv, docs, docs_col, lse, w_qkv, h_all, x, gain_one, gain_two,
        small, own_in, own_out, w_rows, d_in, d_out, got_in, got_out,
    )
    return pl.pallas_call(
        partial(back_kernel, heads, expert_count, sums_here),
        out_shape=outs,
        in_specs=[vmem] * (len(operands) - 4) + [far] * 4,
        out_specs=[vmem] * (len(outs) - 2) + [far] * 2,
        scratch_shapes=[
            pltpu.VMEM((micro_count, rows, features), f32),
            block(micro_count * rows, features),
            block(micro_count, rows, features),
            block(micro_count, length, width),
            block(micro_count, length, 3 * width),
            pltpu.VMEM((length, width), f32),
            pltpu.VMEM((length, width), f32),
            pltpu.VMEM((features, 128), f32),
            block(micro_count, cut_count, rows, features),
            block(micro_count, levels, rows, features),
            block(micro_count, levels + 1, rows, features),
            pltpu.VMEM((micro_count, rows, features), f32),
            *((block(2, features, share), block(2, share, features)) if sums_here else (block(16, 128), block(16, 128))),
            block(*parts, wide),
            block(*parts, 3 * width),
            ins(wide), ins(3 * width), ins(share),
            block(peers, piece, features) if sums_here else block(16, 128),
            mids(wide), mids(3 * width), mids(share), mids(wide), mids(3 * width), mids(share),
            dma((micro_count, levels)), dma((micro_count, levels)), dma((micro_count, levels)),
            dma((micro_count, levels + 1)), dma((micro_count, cut_count)), dma((micro_count, cut_count)), dma((micro_count,)),
            dma((4, peers)), dma((4, peers)), dma((4, cut_count)), dma((4, cut_count)), dma((4,)),
            dma((2,)), dma((2,)), dma((2, 2)),
        ],
        compiler_params=pltpu.CompilerParams(
            collective_id=call_id, has_side_effects=True, vmem_limit_bytes=60 * 2**20
        ),
    )(*operands)


def local(
    tokens, cotangent, segments, expert_ids, slot_ids, kept_mask, norm1_gain, w_query, w_key, w_value, w_output,
    norm2_gain, dense_in, dense_out, router, mixer, expert_in, expert_out,
):
    micro_count, row_count, features = tokens.shape[1:]
    cut_count = lax.axis_size("cuts")
    group_count = lax.axis_size("expert")
    cut = lax.axis_index("cuts")
    group = lax.axis_index("expert")
    length = cut_count * row_count
    head_width = features // cut_count
    heads = head_width // 64
    expert_count = router.shape[1]
    hidden_count = dense_in.shape[1]
    share = hidden_count // cut_count
    piece = share // group_count
    capacity = max(2, row_count * 5 // (4 * expert_count))
    slots = tile_slots(capacity, row_count, 2 * row_count)
    rows = features // (group_count * cut_count)
    sums_here = rows % 16 == 0 and group_count == 4
    gain_one = norm1_gain.astype(jnp.float32)
    gain_two = norm2_gain.astype(jnp.float32)
    f32, low = jnp.float32, jnp.bfloat16

    strided = piece % 128 == 0
    if strided:
        own_in, own_out = dense_in, dense_out
    else:
        own_in = lax.dynamic_index_in_dim(
            dense_in.reshape(features, group_count, cut_count, piece), cut, 2, keepdims=False
        ).reshape(features, share)
        own_out = lax.dynamic_index_in_dim(
            dense_out.reshape(group_count, cut_count, piece, features), cut, 1, keepdims=False
        ).reshape(share, features)
    g_all = lax.all_gather(cotangent[0], "cuts", axis=1, tiled=True)
    docs, docs_col = segments[0][:, None, :], segments[0][:, :, None]
    small = jnp.concatenate([router, mixer, jnp.zeros((features, 126 - expert_count), low)], axis=1)

    h_all, qkv, lse, attended, w_qkv, codes, weights_in = front(
        tokens[0], gain_one[None], w_query, w_key, w_value, docs, docs_col, expert_ids[0], slot_ids[0], kept_mask[0],
        expert_in[0], group_count, cut_count, heads, capacity, slots, 1,
    )
    x_two, h_two, out_part, d_h2, dots, d_own_in, d_own_out, d_in, d_out, _, got_in, got_out = feed(
        tokens[0], attended, w_output, gain_two[None], small, codes,
        g_all.reshape(micro_count, cut_count, row_count, features), own_in, own_out, weights_in, expert_out[0], share, slots,
        strided, sums_here, 2,
    )
    out_sum = lax.psum_scatter(
        out_part.reshape(micro_count, length, features), "cuts", scatter_dimension=1, tiled=True
    )
    output = (x_two + out_sum.astype(f32)).astype(low)

    place = (group * cut_count + cut) * rows
    own_rows = lambda w: lax.dynamic_slice_in_dim(w, place, rows, 0)
    w_rows = jnp.stack([own_rows(w) for w in (w_query, w_key, w_value)])
    (
        grad_tokens, grad_output, grad_small, grad_qkv, grad_dense_in, grad_dense_out, norm_sum, late_in, late_out
    ) = back(
        d_h2, dots, codes, h_two, x_two, cotangent[0], attended.reshape(-1, features), w_output, qkv, docs, docs_col, lse,
        w_qkv, h_all.reshape(micro_count, length, features), tokens[0], gain_one[None], gain_two[None], small,
        d_own_in.reshape(group_count, cut_count, rows, share), d_own_out.reshape(group_count, piece, features), w_rows,
        d_in, d_out, got_in, got_out, heads, expert_count, sums_here, 3,
    )
    sum_groups = lambda part: lax.psum_scatter(
        part.reshape(-1, part.shape[-1]), "expert", scatter_dimension=0, tiled=True
    )
    if sums_here:
        expert_sum = lambda own, got, late: (
            lax.dynamic_index_in_dim(own, group, 0, keepdims=False).astype(f32) + got[0].astype(f32) + late.astype(f32)
        )
        grad_expert_in = expert_sum(d_in, got_in, late_in)
        grad_expert_out = expert_sum(d_out, got_out, late_out)
    else:
        swap = lambda part: lax.all_to_all(
            part.reshape(cut_count, rows, -1), "cuts", split_axis=0, concat_axis=0
        ).astype(f32)
        wide = jnp.sum(swap(sum_groups(grad_output)), axis=0)
        grad_output, grad_small = wide[:, :features], wide[:, features:]
        grad_qkv = swap(sum_groups(grad_qkv)).reshape(cut_count, rows, 3, head_width).transpose(2, 1, 0, 3)
        grad_qkv = grad_qkv.reshape(3, rows, features)
        grad_dense_in = swap(sum_groups(d_own_in)).reshape(cut_count, rows, group_count, piece).transpose(1, 2, 0, 3)
        grad_dense_in = grad_dense_in.reshape(rows, hidden_count)
        grad_dense_out = sum_groups(d_own_out).astype(f32)
        norm_sum = jnp.sum(grad_qkv * w_rows.astype(f32), axis=(0, 2))[:, None]
        grad_expert_in = sum_groups(d_in).astype(f32)
        grad_expert_out = sum_groups(d_out).astype(f32)

    grad_norm1 = norm_sum[:, 0] / own_rows(gain_one)
    return (
        output[None], grad_tokens[None], grad_norm1, grad_qkv[0], grad_qkv[1], grad_qkv[2], grad_output,
        grad_small[:, expert_count + 2], grad_dense_in, grad_dense_out, grad_small[:, :expert_count],
        grad_small[:, expert_count : expert_count + 2], grad_expert_in[None], grad_expert_out[None],
    )


def solution(mesh):
    in_specs = (
        P("expert", None, "cuts", None),
        P("expert", None, "cuts", None),
        P("expert", None, None),
        P("expert", None, "cuts"),
        P("expert", None, "cuts"),
        P("expert", None, "cuts"),
        P(),
        P(),
        P(),
        P(),
        P(),
        P(),
        P(),
        P(),
        P(),
        P(),
        P("expert", None, "cuts"),
        P("expert", "cuts", None),
    )
    out_specs = (
        P("expert", None, "cuts", None),
        P("expert", None, "cuts", None),
        P(("expert", "cuts")),
        P(("expert", "cuts"), None),
        P(("expert", "cuts"), None),
        P(("expert", "cuts"), None),
        P(("expert", "cuts"), None),
        P(("expert", "cuts")),
        P(("expert", "cuts"), None),
        P(("expert", "cuts"), None),
        P(("expert", "cuts"), None),
        P(("expert", "cuts"), None),
        P("expert", None, "cuts"),
        P("expert", "cuts", None),
    )
    return jax.shard_map(local, mesh=mesh, in_specs=in_specs, out_specs=out_specs, check_vma=False)
```

```python
from functools import partial

import jax
import jax.numpy as jnp
from jax import lax
from jax.experimental import pallas as pl
from jax.experimental.pallas import tpu as pltpu
from jax.sharding import PartitionSpec as P

MESH = pl.DeviceIdType.MESH
score_scale = 0.125
masked_value = -1e30
norm_eps = 1e-05


def plain_dot(left, right):
    return jnp.dot(left, right, preferred_element_type=jnp.float32)


def lead_dot(left, right):
    return lax.dot_general(
        left, right, (((0,), (0,)), ((), ())), preferred_element_type=jnp.float32
    )


def tail_dot(left, right):
    return lax.dot_general(
        left, right, (((1,), (1,)), ((), ())), preferred_element_type=jnp.float32
    )


def head_masks(width, heads):
    lane = lax.broadcasted_iota(jnp.int32, (1, width), 1)
    size = width // heads
    return [((lane >= h * size) & (lane < (h + 1) * size)) for h in range(heads)]


def allowed_mask(docs_ref, docs_col_ref, m, start, rows, keys):
    query_spots = start + lax.broadcasted_iota(jnp.int32, (rows, keys), 0)
    key_spots = lax.broadcasted_iota(jnp.int32, (rows, keys), 1)
    return (key_spots <= query_spots) & (docs_ref[pl.ds(m, 1), 0:keys] == docs_col_ref[m, pl.ds(start, rows), :])


def attend_one(heads, m, qkv_ref, docs_ref, docs_col_ref, att_ref, lse_ref):
    length, width = att_ref.shape[1], att_ref.shape[2]
    rows = min(256, length)
    masks = head_masks(width, heads)
    for block in range(length // rows):
        start, keys = block * rows, (block + 1) * rows
        allowed = allowed_mask(docs_ref, docs_col_ref, m, start, rows, keys)
        query = qkv_ref[m, pl.ds(start, rows), 0:width] * jnp.bfloat16(score_scale)
        key = qkv_ref[m, 0:keys, width : 2 * width]
        value = qkv_ref[m, 0:keys, 2 * width : 3 * width]
        att = jnp.zeros((rows, width), jnp.float32)
        logs = jnp.zeros((rows, width), jnp.float32)
        for mask in masks:
            scores = tail_dot(jnp.where(mask, query, jnp.bfloat16(0)), key)
            scores = jnp.where(allowed, scores, masked_value)
            top = jnp.max(scores, axis=-1, keepdims=True)
            raised = jnp.exp(scores - top)
            total = jnp.sum(raised, axis=-1, keepdims=True)
            probs = (raised * (1.0 / total)).astype(jnp.bfloat16)
            att = jnp.where(mask, plain_dot(probs, value), att)
            logs = jnp.where(mask, top + jnp.log(total), logs)
        att_ref[m, pl.ds(start, rows), :] = att.astype(jnp.bfloat16)
        lse_ref[m, pl.ds(start, rows), :] = logs


def norm_parts(values):
    center = values - jnp.mean(values, axis=-1, keepdims=True)
    spread = jnp.mean(center * center, axis=-1, keepdims=True)
    scale = lax.rsqrt(spread + norm_eps)
    return center * scale, scale


def norm_back(normed, scale, gain, grad):
    inner = grad * gain
    return scale * (
        inner
        - jnp.mean(inner, axis=-1, keepdims=True)
        - normed * jnp.mean(inner * normed, axis=-1, keepdims=True)
    )


def gelu_pair(values):
    phi = 0.5 * (1.0 + lax.erf(values * (0.5**0.5)))
    bell = jnp.exp(-0.5 * values * values) * ((2.0 * jnp.pi) ** -0.5)
    return values * phi, phi + values * bell


def tile_slots(capacity, row_count, tile):
    return -(-capacity * (tile // row_count) // 16) * 16


def token_table(spot, width):
    return (spot == lax.broadcasted_iota(jnp.int32, (spot.shape[0], width), 1)).astype(jnp.bfloat16)


def lane_softmax(logits, lanes, first, count):
    inside = (lanes >= first) & (lanes < first + count)
    raised = jnp.exp(logits - jnp.max(jnp.where(inside, logits, masked_value), axis=-1, keepdims=True))
    raised = jnp.where(inside, raised, 0.0)
    return raised / jnp.sum(raised, axis=-1, keepdims=True)


def route(logits, chosen, expert_count):
    lanes = lax.broadcasted_iota(jnp.int32, logits.shape, 1)
    routed = lane_softmax(logits, lanes, 0, expert_count)
    mixing = lane_softmax(logits, lanes, expert_count, 2)
    pick = lambda values, lane: jnp.sum(jnp.where(lanes == lane, values, 0.0), axis=-1, keepdims=True)
    return pick(routed, chosen), pick(mixing, expert_count), pick(mixing, expert_count + 1), routed, mixing


def softmax_back(probs, grad):
    return probs * (grad - jnp.sum(probs * grad, axis=-1, keepdims=True))


def line_copy(src, dst, send, recv, group, target):
    return pltpu.make_async_remote_copy(
        src_ref=src, dst_ref=dst, send_sem=send, recv_sem=recv, device_id=(group, target), device_id_type=MESH
    )


def greet_all(cut_count, group_count):
    cut = lax.axis_index("cuts")
    group = lax.axis_index("expert")
    barrier = pltpu.get_barrier_semaphore()
    for hop in range(1, cut_count):
        pl.semaphore_signal(barrier, inc=1, device_id=(group, jnp.bitwise_xor(cut, hop)), device_id_type=MESH)
    for hop in range(1, group_count):
        pl.semaphore_signal(barrier, inc=1, device_id=(jnp.bitwise_xor(group, hop), cut), device_id_type=MESH)
    pl.semaphore_wait(barrier, cut_count + group_count - 2)


class LineGather:
    def __init__(self, buf, far_send, far_recv, pair_send, pair_recv):
        self.buf = buf
        self.sems = (far_send, far_recv, pair_send, pair_recv)
        self.cut = lax.axis_index("cuts")
        self.group = lax.axis_index("expert")
        self.level, self.side = self.cut // 2, self.cut % 2
        self.levels = buf.shape[1] // 2

    def place(self, n):
        low, high = self.level, self.levels - 1 - self.level
        near = jnp.minimum(low, high)
        paired = n <= 2 * near
        distance = jnp.where(paired, (n + 1) // 2, n - near)
        below = jnp.where(paired, n % 2 == 1, low > high)
        return jnp.where(below, self.level - distance, self.level + distance), below

    def far_copy(self, m, level, target, send):
        block = self.buf.at[m, 2 * level + self.side]
        return line_copy(block, block, self.sems[0].at[m, send], self.sems[1].at[m, level], self.group, target)

    def pair_copy(self, m, level, side):
        block = self.buf.at[m, 2 * level + side]
        return line_copy(
            block, block, self.sems[2].at[m, level], self.sems[3].at[m, level], self.group, jnp.bitwise_xor(self.cut, 1)
        )

    def start(self, m):
        @pl.when(self.level + 1 < self.levels)
        def _():
            self.far_copy(m, self.level, self.cut + 2, self.level).start()

        @pl.when(self.level > 0)
        def _():
            self.far_copy(m, self.level, self.cut - 2, self.levels).start()

        self.pair_copy(m, self.level, self.side).start()

    def take(self, m, n):
        level, below = self.place(n)

        @pl.when(n > 0)
        def _():
            target = jnp.where(below, self.cut + 2, self.cut - 2)
            self.far_copy(m, level, target, level).wait_recv()

            @pl.when(jnp.where(below, self.level + 1 < self.levels, self.level > 0))
            def _():
                self.far_copy(m, level, target, level).start()

            self.pair_copy(m, level, self.side).start()

        self.pair_copy(m, level, 1 - self.side).wait_recv()
        return level

    def finish(self, m):
        @pl.when(self.level + 1 < self.levels)
        def _():
            self.far_copy(m, self.level, self.cut + 2, self.level).wait_send()

        @pl.when(self.level > 0)
        def _():
            self.far_copy(m, self.level, self.cut - 2, self.levels).wait_send()

        for n in range(self.levels):
            level, below = self.place(n)
            if n:
                @pl.when(jnp.where(below, self.level + 1 < self.levels, self.level > 0))
                def _():
                    self.far_copy(m, level, self.cut, level).wait_send()

            self.pair_copy(m, level, self.side).wait_send()


class LineSum:
    def __init__(self, part, pair_buf, far_buf, pair_send, pair_recv, send, recv, own=None):
        self.own = own
        self.part, self.pair_buf, self.far_buf = part, pair_buf, far_buf
        self.sems = (pair_send, pair_recv, send, recv)
        self.cut = lax.axis_index("cuts")
        self.group = lax.axis_index("expert")
        self.level, self.side = self.cut // 2, self.cut % 2
        self.levels = part.shape[1] // 2

    def pair_copy(self, m, level):
        return line_copy(
            self.part.at[m, 2 * level + 1 - self.side], self.pair_buf.at[m, level], self.sems[0].at[m, level],
            self.sems[1].at[m, level], self.group, jnp.bitwise_xor(self.cut, 1),
        )

    def far_copy(self, m, level, up):
        target = self.cut + 2 if up else self.cut - 2
        slot = level if up else jnp.where(level == self.level - 1, self.levels, level)
        return line_copy(
            self.pair_buf.at[m, level], self.far_buf.at[m, slot], self.sems[2].at[m, level], self.sems[3].at[m, slot],
            self.group, target,
        )

    def arrived(self, m, slot):
        line_copy(
            self.far_buf.at[m, slot], self.far_buf.at[m, slot], self.sems[2].at[m, 0], self.sems[3].at[m, slot],
            self.group, self.cut,
        ).wait_recv()
        return self.far_buf[m, slot].astype(jnp.float32)

    def start(self, m):
        def one(k, carry):
            self.pair_copy(m, jnp.where(k % 2 == 0, self.levels - 1 - k // 2, k // 2)).start()
            return carry

        lax.fori_loop(0, self.levels, one, 0)

    def pairs(self, m):
        def one(k, carry):
            level = jnp.where(k % 2 == 0, self.levels - 1 - k // 2, k // 2)
            self.pair_copy(m, level).wait_recv()
            mine = self.part[m, 2 * level + self.side] if self.own is None else self.own[m, level]
            total = mine.astype(jnp.float32) + self.pair_buf[m, level].astype(jnp.float32)
            self.pair_buf[m, level] = total.astype(self.pair_buf.dtype)
            @pl.when((self.level == 0) & (level > 0))
            def _():
                self.far_copy(m, level, True).start()

            @pl.when((self.level == self.levels - 1) & (level < self.levels - 1))
            def _():
                self.far_copy(m, level, False).start()

            return carry

        lax.fori_loop(0, self.levels, one, 0)

    def pass_on(self, m, level, up):
        @pl.when((level > self.level) if up else (level < self.level))
        def _():
            total = self.pair_buf[m, level].astype(jnp.float32) + self.arrived(m, level)
            self.pair_buf[m, level] = total.astype(self.pair_buf.dtype)
            self.far_copy(m, level, up).start()

    def hop(self, m, j):
        inner = (self.level > 0) & (self.level < self.levels - 1)
        lower = 2 * self.level < self.levels

        @pl.when(inner & lower)
        def _():
            self.pass_on(m, self.levels - 1 - j, True)
            self.pass_on(m, j, False)

        @pl.when(inner & jnp.logical_not(lower))
        def _():
            self.pass_on(m, j, False)
            self.pass_on(m, self.levels - 1 - j, True)

    def finish(self, m, out_ref):
        out_ref[m] = self.pair_buf[m, self.level].astype(jnp.float32)

        @pl.when(self.level > 0)
        def _():
            out_ref[m] = out_ref[m] + self.arrived(m, self.level)

        @pl.when(self.level < self.levels - 1)
        def _():
            out_ref[m] = out_ref[m] + self.arrived(m, self.levels)

        def one(level, carry):
            self.pair_copy(m, level).wait_send()

            @pl.when(level > self.level)
            def _():
                self.far_copy(m, level, True).wait_send()

            @pl.when(level < self.level)
            def _():
                self.far_copy(m, level, False).wait_send()

            return carry

        lax.fori_loop(0, self.levels, one, 0)


def row_to_column(values):
    return jnp.transpose(values.astype(jnp.float32))


def one_row(ref):
    values = ref[...].astype(jnp.float32)
    return jnp.concatenate([values[k : k + 1] for k in range(values.shape[0])], axis=1)


def stack_small(router_ref, mixer_ref, stage, small):
    count = router_ref.shape[0]
    stage[...] = jnp.zeros_like(stage)
    stage[0:count] = router_ref[...].astype(jnp.float32)
    stage[count : count + 2] = mixer_ref[...].astype(jnp.float32)
    small[...] = stage[...].astype(small.dtype)


def fill_docs(docs_ref, stage, docs_col):
    stage[...] = jnp.zeros_like(stage)
    micro_count = docs_ref.shape[0]
    stage[0:micro_count] = docs_ref[...].astype(jnp.float32)
    for k in range(stage.shape[1] // 128):
        turned = jnp.transpose(stage[:, k * 128 : (k + 1) * 128]).astype(jnp.int32)
        for m in range(micro_count):
            docs_col[m, k * 128 : (k + 1) * 128, :] = turned[:, m : m + 1]


def front_kernel(
    heads, capacity, slots,
    x_ref, gy_ref, gain_ref, w_query_ref, w_key_ref, w_value_ref, docs_ref, ids_ref, slot_ref, kept_ref, expert_in_ref,
    h_out_ref, qkv_out_ref, lse_out_ref, att_ref, w_qkv_ref, codes_ref, weights_ref, g_all_ref,
    h_all_ref, qkv_ref, lse_ref, docs_stage, docs_col_ref, att_part, own_code, far_send, far_recv, pair_send, pair_recv, load_sem, swap_send, swap_recv, swap_own, code_send,
    code_recv, weight_send, weight_recv, g_far_send, g_far_recv, g_pair_send, g_pair_recv, g_own, keep_sem,
):
    micro_count, cut_count, rows, features = h_all_ref.shape
    group_count = weights_ref.shape[0]
    width = features // cut_count
    cut = lax.axis_index("cuts")
    group = lax.axis_index("expert")
    low = jnp.bfloat16
    loads = []
    for k, ref in enumerate((w_query_ref, w_key_ref, w_value_ref)):
        loads.append(pltpu.make_async_copy(
            ref.at[:, pl.ds(pl.multiple_of(cut * width, width), width)], w_qkv_ref.at[:, k * width : (k + 1) * width],
            load_sem.at[k],
        ))
        loads[-1].start()
    g_keep = [pltpu.make_async_copy(gy_ref.at[m], g_all_ref.at[m, cut], g_own.at[m]) for m in range(micro_count)]
    for keep in g_keep:
        keep.start()
    gain = one_row(gain_ref)
    greet_all(cut_count, group_count)

    line = LineGather(h_all_ref, far_send, far_recv, pair_send, pair_recv)
    g_line = LineGather(g_all_ref, g_far_send, g_far_recv, g_pair_send, g_pair_recv)

    def norm_step(m, carry):
        normed, _ = norm_parts(x_ref[m].astype(jnp.float32))
        h_all_ref[m, cut] = (normed * gain).astype(low)
        line.start(m)
        return carry

    lax.fori_loop(0, micro_count, norm_step, 0)

    def weight_copy(hop):
        return line_copy(
            expert_in_ref, weights_ref.at[group], weight_send.at[hop - 1], weight_recv.at[hop - 1],
            jnp.bitwise_xor(group, hop), cut,
        )

    for hop in range(group_count - 1, 0, -1):
        weight_copy(hop).start()

    chosen = jnp.where(kept_ref[...] == 1, ids_ref[...], -1)
    spot = jnp.where(kept_ref[...] == 1, ids_ref[...] * slots + cut % 2 * capacity + slot_ref[...], -1)
    own_code[...] = jnp.zeros_like(own_code)
    for m in range(micro_count):
        own_code[m, 0:1] = chosen[m : m + 1]
        own_code[m, 1:2] = spot[m : m + 1]
    codes_ref[cut] = own_code[...]

    def code_copy(hop):
        return line_copy(
            own_code, codes_ref.at[cut], code_send.at[hop], code_recv.at[hop], group, jnp.bitwise_xor(cut, hop)
        )

    for hop in range(1, cut_count):
        code_copy(hop).start()
    fill_docs(docs_ref, docs_stage, docs_col_ref)
    for load in loads:
        load.wait()

    def tile_step(n, m):
        level = line.take(m, n)
        h_tile = h_all_ref[m, pl.ds(2 * level, 2)].reshape(2 * rows, features)
        spots = pl.ds(pl.multiple_of(level * 2 * rows, 2 * rows), 2 * rows)
        qkv_ref[m, spots, :] = plain_dot(h_tile, w_qkv_ref[...]).astype(low)

    def early(i, carry):
        tile_step(i // micro_count, i % micro_count)
        return carry

    levels = cut_count // 2
    lax.fori_loop(0, (levels - 1) * micro_count, early, 0)
    for m in range(micro_count):
        g_keep[m].wait()
        g_line.start(m)

    def swap_copy(m, hop):
        target = jnp.bitwise_xor(cut, hop)
        return line_copy(
            att_part.at[m, pl.ds(pl.multiple_of(target * rows, rows), rows), :],
            att_ref.at[m, :, pl.ds(pl.multiple_of(cut * width, width), width)],
            swap_send.at[m, hop], swap_recv.at[m, hop], group, target,
        )

    def swap_keep(m):
        return pltpu.make_async_copy(
            att_part.at[m, pl.ds(pl.multiple_of(cut * rows, rows), rows), :],
            att_ref.at[m, :, pl.ds(pl.multiple_of(cut * width, width), width)],
            swap_own.at[m],
        )

    def late(m, carry):
        tile_step(levels - 1, m)
        attend_one(heads, m, qkv_ref, docs_ref, docs_col_ref, att_part, lse_ref)
        for hop in range(cut_count - 1, 0, -1):
            swap_copy(m, hop).start()
        swap_keep(m).start()
        g_line.take(m, 0)
        if levels > 1:
            g_line.take(m, 1)
        return carry

    lax.fori_loop(0, micro_count, late, 0)
    keeps = [
        pltpu.make_async_copy(src, dst, keep_sem.at[k])
        for k, (src, dst) in enumerate(((h_all_ref, h_out_ref), (qkv_ref, qkv_out_ref), (lse_ref, lse_out_ref)))
    ]
    for keep in keeps:
        keep.start()

    def pass_on(i, carry):
        g_line.take(i % micro_count, 2 + i // micro_count)
        return carry

    lax.fori_loop(0, (levels - 2) * micro_count, pass_on, 0)
    for hop in range(1, cut_count):
        code_copy(hop).wait()
    for m in range(micro_count):
        line.finish(m)
    for m in range(micro_count):
        for hop in range(cut_count - 1, 0, -1):
            swap_copy(m, hop).wait()
        swap_keep(m).wait()
    for m in range(micro_count):
        g_line.finish(m)
    for keep in keeps:
        keep.wait()
    for hop in range(1, group_count):
        weight_copy(hop).wait()


def front(
    x, gy, gain, w_query, w_key, w_value, docs, ids, slot_ids, kept, expert_in, group_count, cut_count, heads, capacity,
    slots, call_id,
):
    micro_count, rows, features = x.shape
    length, levels, width = cut_count * rows, cut_count // 2, features // cut_count
    low, f32 = jnp.bfloat16, jnp.float32
    shape = jax.ShapeDtypeStruct
    dma = pltpu.SemaphoreType.DMA
    vmem, far = pl.BlockSpec(memory_space=pltpu.VMEM), pl.BlockSpec(memory_space=pl.ANY)
    return pl.pallas_call(
        partial(front_kernel, heads, capacity, slots),
        out_shape=(
            shape((micro_count, cut_count, rows, features), low),
            shape((micro_count, length, 3 * width), low),
            shape((micro_count, length, width), f32),
            shape((micro_count, rows, features), low),
            shape((features, 3 * width), low),
            shape((cut_count, micro_count, 8, rows), jnp.int32),
            shape((group_count, *expert_in.shape), low),
            shape((micro_count, cut_count, rows, features), low),
        ),
        in_specs=[vmem, vmem, vmem, far, far, far, vmem, vmem, vmem, vmem, far],
        out_specs=[far] * 3 + [vmem] * 3 + [far] * 2,
        scratch_shapes=[
            pltpu.VMEM((micro_count, cut_count, rows, features), low),
            pltpu.VMEM((micro_count, length, 3 * width), low),
            pltpu.VMEM((micro_count, length, width), f32),
            pltpu.VMEM((8, length), f32),
            pltpu.VMEM((micro_count, length, 1), jnp.int32),
            pltpu.VMEM((micro_count, length, width), low),
            pltpu.VMEM((micro_count, 8, rows), jnp.int32),
            dma((micro_count, levels + 1)), dma((micro_count, levels)), dma((micro_count, levels)), dma((micro_count, levels)),
            dma((3,)), dma((micro_count, cut_count)), dma((micro_count, cut_count)), dma((micro_count,)),
            dma((cut_count,)), dma((cut_count,)), dma((group_count - 1,)), dma((group_count - 1,)),
            dma((micro_count, levels + 1)), dma((micro_count, levels)), dma((micro_count, levels)), dma((micro_count, levels)),
            dma((micro_count,)), dma((3,)),
        ],
        compiler_params=pltpu.CompilerParams(collective_id=call_id, has_side_effects=True, vmem_limit_bytes=62 * 2**20),
    )(x, gy, gain, w_query, w_key, w_value, docs, ids, slot_ids, kept, expert_in)


def feed_kernel(
    slots, strided, early,
    x_ref, att_ref, w_out_ref, gain_ref, router_ref, mixer_ref, codes_ref, g_ref, dense_in_ref, dense_out_ref, weights_in_ref,
    expert_in_ref, expert_out_ref,
    x_two_ref, h_own_ref, out_all_ref, dh_ref, sums_ref, d_own_in_ref, d_own_out_ref, d_in_ref, d_out_ref, weights_out_ref,
    got_in_ref, got_out_ref,
    h_all, g_buf, sent, g_sent, hidden_buf, pre_buf, back_buf, side_buf, own_in, own_out, in_buf, out_buf, in_stage, out_stage,
    dots, dots_in, pair_buf, far_buf, out_ref, small_stage, small_ref,
    far_send, far_recv, pair_send, pair_recv, line_send, line_recv, two_send, two_recv, load_sem, in_sem, out_sem,
    stage_sem, dot_send, dot_recv, weight_send, weight_recv,
    early_send, early_recv, keep_sem,
):
    micro_count, cut_count, rows, features = h_all.shape
    group_count = weights_out_ref.shape[0]
    share = own_in.shape[1]
    levels, tile = cut_count // 2, 2 * rows
    expert_count = group_count
    cut = lax.axis_index("cuts")
    group = lax.axis_index("expert")
    low, f32 = jnp.bfloat16, jnp.float32
    half = share
    loads = [pltpu.make_async_copy(g_ref, g_buf, load_sem.at[0])]
    for k in range(features // half):
        loads.append(pltpu.make_async_copy(w_out_ref.at[:, k * half : (k + 1) * half], in_buf.at[k], load_sem.at[1 + k]))
    first_load = len(loads)
    if strided:
        piece = share // group_count
        for g in range(group_count):
            spot = pl.ds(pl.multiple_of((g * cut_count + cut) * piece, piece), piece)
            here = pl.ds(g * piece, piece)
            loads.append(pltpu.make_async_copy(dense_in_ref.at[:, spot], own_in.at[:, here], load_sem.at[len(loads)]))
            loads.append(pltpu.make_async_copy(dense_out_ref.at[spot, :], own_out.at[here, :], load_sem.at[len(loads)]))
    else:
        loads.append(pltpu.make_async_copy(dense_in_ref, own_in, load_sem.at[len(loads)]))
        loads.append(pltpu.make_async_copy(dense_out_ref, own_out, load_sem.at[len(loads)]))
    for load in loads[1:]:
        load.start()
    loads[0].start()
    stack_small(router_ref, mixer_ref, small_stage, small_ref)
    gain = one_row(gain_ref)
    greet_all(cut_count, group_count)
    for load in loads[1:first_load]:
        load.wait()

    line = LineGather(h_all, far_send, far_recv, pair_send, pair_recv)

    def norm_step(m, carry):
        att = att_ref[m]
        projected = jnp.concatenate([plain_dot(att, in_buf[k]) for k in range(features // half)], axis=1)
        x_two = x_ref[m].astype(f32) + projected
        x_two_ref[m] = x_two
        normed, _ = norm_parts(x_two)
        h_two = (normed * gain).astype(low)
        h_all[m, cut] = h_two
        h_own_ref[m] = h_two
        line.start(m)
        return carry

    lax.fori_loop(0, micro_count, norm_step, 0)

    def weight_copy(hop):
        return line_copy(
            expert_out_ref, weights_out_ref.at[group], weight_send.at[hop - 1], weight_recv.at[hop - 1],
            jnp.bitwise_xor(group, hop), cut,
        )

    for hop in range(group_count - 1, 0, -1):
        weight_copy(hop).start()
    for load in loads[first_load:]:
        load.wait()
    loads[0].wait()
    lanes = lax.broadcasted_iota(jnp.int32, (tile, 128), 1)

    def columns(m, level):
        both = [row_to_column(codes_ref[2 * level + k, m]) for k in range(2)]
        both = jnp.concatenate(both, axis=0).astype(jnp.int32)
        return both[:, 0:1], both[:, 1:2]

    def dense_step(i, carry):
        n, m = i // micro_count, i % micro_count
        level = line.take(m, n)
        t = m * levels + level
        blocks = pl.ds(2 * level, 2)
        here = pl.ds(pl.multiple_of(t * tile, tile), tile)
        spots = pl.ds(pl.multiple_of(t * slots, slots), slots)
        h_two = h_all[m, blocks].reshape(tile, features)
        chosen, spot = columns(m, level)
        gate, mix_dense, mix_expert, _, _ = route(tail_dot(h_two, small_ref[...]), chosen, expert_count)
        mix_gate = mix_expert * gate
        table = token_table(spot, expert_count * slots)
        grad_y = g_buf[m, blocks].reshape(tile, features).astype(f32)
        rows_sent = lead_dot(table, h_two).astype(low)
        rows_back = lead_dot(table, (mix_gate * grad_y).astype(low)).astype(low)
        for e in range(expert_count):
            sent[e, spots, :] = rows_sent[e * slots : (e + 1) * slots]
            g_sent[e, spots, :] = rows_back[e * slots : (e + 1) * slots]
        act, slope = gelu_pair(plain_dot(h_two, own_in[...]))
        dense = plain_dot(act.astype(low), own_out[...])
        side_buf[here, :] = jnp.where(lanes == 0, jnp.sum(grad_y * dense, axis=-1, keepdims=True), mix_gate)
        d_pre = (tail_dot((mix_dense * grad_y).astype(low), own_out[...]) * slope).astype(low)
        hidden_buf[here, :] = (mix_dense * act).astype(low)
        pre_buf[here, :] = d_pre
        out_ref[m, blocks] = (mix_dense * dense).astype(low).reshape(2, rows, features)
        back_buf[m, blocks] = tail_dot(d_pre, own_in[...]).astype(low).reshape(2, rows, features)
        return carry

    lax.fori_loop(0, levels * micro_count, dense_step, 0)

    for hop in range(1, group_count):
        weight_copy(hop).wait()

    def expert_at(i):
        return jnp.bitwise_xor(group, group_count - 1 - i)

    def load_in(i, own=False):
        src = expert_in_ref if own else weights_in_ref.at[expert_at(i)]
        return pltpu.make_async_copy(src, in_buf.at[i % 2], in_sem.at[i % 2])

    def load_out(i, own=False):
        src = expert_out_ref if own else weights_out_ref.at[expert_at(i)]
        return pltpu.make_async_copy(src, out_buf.at[i % 2], out_sem.at[i % 2])

    def keep_in(i):
        return pltpu.make_async_copy(in_stage, d_in_ref.at[expert_at(i)], stage_sem.at[0])

    def keep_out(i):
        return pltpu.make_async_copy(out_stage, d_out_ref.at[expert_at(i)], stage_sem.at[1])

    def early_copy(k):
        mask, kind, side, at = ((3, 0, 1, 1), (3, 1, 2, 1), (2, 1, 2, 0), (1, 0, 1, 0))[k]
        src, dst = ((d_in_ref, got_in_ref), (d_out_ref, got_out_ref))[kind]
        return line_copy(
            src.at[jnp.bitwise_xor(group, mask)], dst.at[at], early_send.at[k], early_recv.at[k],
            jnp.bitwise_xor(group, side), cut,
        )

    load_in(0).start()
    load_out(0).start()

    def expert_step(i, carry):
        @pl.when(i + 2 < expert_count)
        def _():
            load_in(i + 1).start()
            load_out(i + 1).start()

        @pl.when(i + 2 == expert_count)
        def _():
            load_in(i + 1, True).start()
            load_out(i + 1, True).start()

        load_in(i).wait()
        load_out(i).wait()
        e, at = expert_at(i), i % 2
        rows_in, rows_back = sent[e], g_sent[e]
        act, slope = gelu_pair(plain_dot(rows_in, in_buf[at]))
        inner = act.astype(low)
        d_pre = (tail_dot(rows_back, out_buf[at]) * slope).astype(low)

        @pl.when(i > 0)
        def _():
            keep_in(i).wait()
            keep_out(i).wait()

        if early:
            @pl.when(i == 1)
            def _():
                early_copy(0).start()
                early_copy(1).start()

            @pl.when(i == 2)
            def _():
                early_copy(2).start()

            @pl.when(i == 3)
            def _():
                early_copy(3).start()

        in_stage[...] = lead_dot(rows_in, d_pre).astype(low)
        keep_in(i).start()
        out_stage[...] = lead_dot(inner, rows_back).astype(low)
        keep_out(i).start()
        sent[e] = tail_dot(d_pre, in_buf[at]).astype(low)
        g_sent[e] = plain_dot(inner, out_buf[at]).astype(low)
        return carry

    lax.fori_loop(0, expert_count, expert_step, 0)
    total = LineSum(back_buf, pair_buf, far_buf, line_send, line_recv, two_send, two_recv)

    def combine_step(m, level, carry):
        t = m * levels + level
        blocks = pl.ds(2 * level, 2)
        here = pl.ds(pl.multiple_of(t * tile, tile), tile)
        spots = pl.ds(pl.multiple_of(t * slots, slots), slots)
        _, spot = columns(m, level)
        table = token_table(spot, expert_count * slots)
        gather = lambda ref: jnp.concatenate([ref[e, spots, :] for e in range(expert_count)], axis=0)
        back_rows = plain_dot(table, gather(sent)).reshape(2, rows, features)
        back_buf[m, blocks] = (back_buf[m, blocks].astype(f32) + back_rows).astype(low)
        grad_y = g_buf[m, blocks].reshape(tile, features).astype(f32)
        part = plain_dot(table, gather(g_sent))
        side = side_buf[here, :]
        scaled = (side[:, 1:2] * part).reshape(2, rows, features)
        out_ref[m, blocks] = (out_ref[m, blocks].astype(f32) + scaled).astype(low)
        side = jnp.where(lanes == 1, jnp.sum(grad_y * part, axis=-1, keepdims=True), side)
        for k in range(2):
            dots[2 * level + k, m] = jnp.transpose(side[k * rows : (k + 1) * rows])[0:8]
        return carry

    out_keep = [pltpu.make_async_copy(out_ref.at[m], out_all_ref.at[m], keep_sem.at[m]) for m in range(micro_count)]
    for m in range(micro_count):
        lax.fori_loop(0, levels, partial(combine_step, m), 0)
        total.start(m)
        out_keep[m].start()
        total.pairs(m)

    def dot_copy(hop):
        target = jnp.bitwise_xor(cut, hop)
        return line_copy(dots.at[target], dots_in.at[hop - 1], dot_send.at[hop - 1], dot_recv.at[hop - 1], group, target)

    for hop in range(1, cut_count):
        dot_copy(hop).start()
    token_rows = micro_count * cut_count * rows
    h_flat, g_flat = h_all.reshape(token_rows, features), g_buf.reshape(token_rows, features)

    def dense_weights(k):
        part = pl.ds(k * 256, 256)
        d_own_in_ref[part, :] = lead_dot(h_flat[:, part], pre_buf[...]).astype(low)
        d_own_out_ref[:, part] = lead_dot(hidden_buf[...], g_flat[:, part]).astype(low)

    slices = features // 256
    for k in range(slices // 2):
        dense_weights(k)
    for j in range(levels - 1):
        total.hop(0, j)
    for k in range(slices // 2, slices):
        dense_weights(k)
    for m in range(1, micro_count):
        for j in range(levels - 1):
            total.hop(m, j)
    sums = dots[cut]
    for hop in range(1, cut_count):
        dot_copy(hop).wait()
        sums = sums + dots_in[hop - 1]
    sums_ref[...] = sums
    keep_in(0).wait()
    keep_out(0).wait()
    for k in range(4 if early else 0):
        early_copy(k).wait()
    for m in range(micro_count):
        line.finish(m)
        out_keep[m].wait()
    for m in range(micro_count):
        total.finish(m, dh_ref)


def feed(
    x, att, w_output, gain, router, mixer, codes, g_all, dense_in, dense_out, weights_in, expert_in, expert_out, share, slots,
    strided, early, call_id,
):
    micro_count, rows, features = x.shape
    cut_count = codes.shape[0]
    group_count = weights_in.shape[0]
    levels, total = cut_count // 2, micro_count * cut_count * rows
    low, f32 = jnp.bfloat16, jnp.float32
    shape = jax.ShapeDtypeStruct
    dma = pltpu.SemaphoreType.DMA
    block = lambda *dims: pltpu.VMEM(dims, low)
    vmem, far = pl.BlockSpec(memory_space=pltpu.VMEM), pl.BlockSpec(memory_space=pl.ANY)
    whole = (micro_count, cut_count, rows, features)
    slot_rows = micro_count * levels * slots
    line = (micro_count, levels)
    return pl.pallas_call(
        partial(feed_kernel, slots, strided, early),
        out_shape=(
            shape((micro_count, rows, features), f32),
            shape((micro_count, rows, features), low),
            shape(whole, low),
            shape((micro_count, rows, features), f32),
            shape((micro_count, 8, rows), f32),
            shape((features, share), low),
            shape((share, features), low),
            shape((group_count, features, share), low),
            shape((group_count, share, features), low),
            shape((group_count, share, features), low),
            *(
                (shape((2, features, share), low), shape((2, share, features), low))
                if early else (shape((8, 128), low), shape((8, 128), low))
            ),
        ),
        in_specs=[vmem, vmem, far, vmem, vmem, vmem, vmem, far, far, far, far, far, far],
        out_specs=[vmem, vmem, far] + [vmem] * 4 + [far] * 5,
        scratch_shapes=[
            block(*whole), block(*whole),
            block(group_count, slot_rows, features), block(group_count, slot_rows, features),
            block(total, share), block(total, share), block(*whole), pltpu.VMEM((total, 128), f32),
            block(features, share), block(share, features), block(2, features, share), block(2, share, features),
            block(features, share), block(share, features),
            pltpu.VMEM((cut_count, micro_count, 8, rows), f32), pltpu.VMEM((cut_count - 1, micro_count, 8, rows), f32),
            block(*line, rows, features), block(micro_count, levels + 1, rows, features), block(*whole),
            pltpu.VMEM((128, features), f32), block(128, features),
            dma((micro_count, levels + 1)), dma(line), dma(line), dma(line),
            dma(line), dma(line), dma(line), dma((micro_count, levels + 1)),
            dma((3 + 2 * group_count,)), dma((2,)), dma((2,)), dma((2,)),
            dma((cut_count - 1,)), dma((cut_count - 1,)), dma((group_count - 1,)), dma((group_count - 1,)),
            dma((4,)), dma((4,)), dma((micro_count,)),
        ],
        compiler_params=pltpu.CompilerParams(collective_id=call_id, has_side_effects=True, vmem_limit_bytes=62 * 2**20),
    )(x, att, w_output, gain, router, mixer, codes, g_all, dense_in, dense_out, weights_in, expert_in, expert_out)


def attend_back_one(heads, m, qkv_ref, docs_ref, docs_col_ref, lse_ref, back_ref, out_ref, key_acc, value_acc):
    length, width = back_ref.shape[1], back_ref.shape[2]
    rows = min(256, length)
    masks = head_masks(width, heads)
    key_acc[...] = jnp.zeros_like(key_acc)
    value_acc[...] = jnp.zeros_like(value_acc)
    zero = jnp.bfloat16(0)
    for block in range(length // rows):
        start, keys = block * rows, (block + 1) * rows
        allowed = allowed_mask(docs_ref, docs_col_ref, m, start, rows, keys)
        query = qkv_ref[m, pl.ds(start, rows), 0:width] * jnp.bfloat16(score_scale)
        key = qkv_ref[m, 0:keys, width : 2 * width]
        value = qkv_ref[m, 0:keys, 2 * width : 3 * width]
        back = back_ref[m, pl.ds(start, rows), :]
        logs = lse_ref[m, pl.ds(start, rows), :]
        query_grad = jnp.zeros((rows, width), jnp.float32)
        for h, mask in enumerate(masks):
            one_query = jnp.where(mask, query, zero)
            one_back = jnp.where(mask, back, zero)
            scores = jnp.where(allowed, tail_dot(one_query, key), masked_value)
            spot = h * (width // heads)
            probs = jnp.exp(scores - logs[:, spot : spot + 1])
            weighted = probs * tail_dot(one_back, value)
            delta = jnp.sum(weighted, axis=-1, keepdims=True)
            score_grad = (weighted - probs * delta).astype(jnp.bfloat16)
            query_grad = jnp.where(mask, plain_dot(score_grad, key), query_grad)
            key_acc[0:keys, :] += lead_dot(score_grad, one_query)
            value_acc[0:keys, :] += lead_dot(probs.astype(jnp.bfloat16), one_back)
        out_ref[m, pl.ds(start, rows), 0:width] = (query_grad * score_scale).astype(jnp.bfloat16)
    out_ref[m, :, width : 2 * width] = key_acc[...].astype(jnp.bfloat16)
    out_ref[m, :, 2 * width : 3 * width] = value_acc[...].astype(jnp.bfloat16)


def back_kernel(
    heads, expert_count, sums_here,
    dh_ref, dots_ref, codes_ref, h_ref, x_two_ref, gy_ref, att_ref, w_out_ref, docs_ref,
    x_ref, gain_one_ref, gain_two_ref, router_ref, mixer_ref, own_in_ref, own_out_ref,
    qkv_far, lse_far, w_qkv_far, h_all_far, out_part, w_query_ref, w_key_ref, w_value_ref, d_in_ref, d_out_ref,
    got_in_ref, got_out_ref,
    output_ref, tokens_ref, wo_ref, tiny_ref, query_out_ref, key_out_ref, value_out_ref, in_out_ref, out_out_ref, late_in_ref,
    late_out_ref,
    qkv_ref, lse_ref, w_qkv_ref, h_all_ref, w_rows, docs_stage, docs_col_ref, small_stage, small_ref, out_own, out_pair,
    out_far, g_att, d_att, back_all, d_qkv, key_acc, value_acc, d_small, part, pair_buf, far_buf, d_h_one, in_sum, out_sum,
    wo_part, qkv_part, wo_in, qkv_in, own_in_in, own_out_in, wo_mid, qkv_mid, in_mid, wo_end, qkv_end, in_end,
    pair_send, pair_recv, far_send, far_recv, swap_send, swap_recv, swap_own, one_send, one_recv, two_send, two_recv, two_own,
    late_send, late_recv, late_load_sem, load_sem, own_sem, o_pair_send, o_pair_recv, o_far_send, o_far_recv,
):
    micro_count, cut_count, rows, features = part.shape
    group_count, split, piece_rows, _ = wo_part.shape
    group_rows = split * piece_rows
    width = features // cut_count
    cut = lax.axis_index("cuts")
    group = lax.axis_index("expert")
    low, f32 = jnp.bfloat16, jnp.float32
    levels = cut_count // 2
    place = (group * cut_count + cut) * piece_rows
    loads = [
        pltpu.make_async_copy(src, dst, load_sem.at[k])
        for k, (src, dst) in enumerate(
            ((qkv_far, qkv_ref), (lse_far, lse_ref), (w_qkv_far, w_qkv_ref), (h_all_far, h_all_ref))
        )
    ]
    if sums_here:
        own_rows = pl.ds(pl.multiple_of(place, piece_rows), piece_rows)
        for k, ref in enumerate((w_query_ref, w_key_ref, w_value_ref)):
            loads.append(pltpu.make_async_copy(ref.at[own_rows, :], w_rows.at[k], load_sem.at[4 + k]))
    for load in loads:
        load.start()

    def own_load(m, level):
        return pltpu.make_async_copy(out_part.at[m, 2 * level + cut % 2], out_own.at[m, level], own_sem.at[m, level])

    for m in range(micro_count):
        for level in range(levels):
            own_load(m, level).start()
    stack_small(router_ref, mixer_ref, small_stage, small_ref)
    fill_docs(docs_ref, docs_stage, docs_col_ref)
    greet_all(cut_count, group_count if sums_here else 1)
    out_line = LineSum(out_part, out_pair, out_far, o_pair_send, o_pair_recv, o_far_send, o_far_recv, out_own)

    ones = ((own_in_ref, own_in_in), (own_out_ref, own_out_in), (wo_part, wo_in), (qkv_part, qkv_in))

    def one_copy(kind, hop):
        src, dst = ones[kind]
        target = jnp.bitwise_xor(group, hop)
        return line_copy(
            src.at[target], dst.at[hop - 1], one_send.at[kind, hop - 1], one_recv.at[kind, hop - 1], target, cut
        )

    def one_start(kind):
        for hop in range(1, group_count):
            one_copy(kind, hop).start()

    def one_finish(kind):
        src, dst = ones[kind]
        total = src[group].astype(f32)
        for hop in range(1, group_count):
            one_copy(kind, hop).wait_recv()
            total = total + dst[hop - 1].astype(f32)
        for hop in range(1, group_count):
            one_copy(kind, hop).wait_send()
        return total

    twos = ((in_mid, in_end), None, (wo_mid, wo_end), (qkv_mid, qkv_end))

    def two_copy(kind, hop):
        src, dst = twos[kind]
        target = jnp.bitwise_xor(cut, hop)
        return line_copy(src.at[target], dst.at[cut], two_send.at[kind, hop], two_recv.at[kind, hop], group, target)

    def two_keep(kind):
        src, dst = twos[kind]
        return pltpu.make_async_copy(src.at[cut], dst.at[cut], two_own.at[kind])

    def two_start(kind):
        for hop in range(cut_count - 1, 0, -1):
            two_copy(kind, hop).start()
        two_keep(kind).start()

    def two_finish(kind):
        for hop in range(cut_count - 1, 0, -1):
            two_copy(kind, hop).wait()
        two_keep(kind).wait()

    ends = ((d_in_ref, got_in_ref, in_sum, late_in_ref, 2), (d_out_ref, got_out_ref, out_sum, late_out_ref, 1))

    def late_load(kind, k):
        own, got, total, _, side = ends[kind]
        src = got.at[1] if k else own.at[jnp.bitwise_xor(group, side)]
        return pltpu.make_async_copy(src, total.at[k], late_load_sem.at[kind, k])

    def late_copy(kind):
        _, _, total, late, side = ends[kind]
        return line_copy(
            total.at[0], late, late_send.at[kind], late_recv.at[kind], jnp.bitwise_xor(group, side), cut
        )

    if sums_here:
        for kind in range(2):
            late_load(kind, 0).start()
            late_load(kind, 1).start()
        one_start(0)
        one_start(1)

    def swap_copy(m, hop):
        target = jnp.bitwise_xor(cut, hop)
        return line_copy(
            d_att.at[m, :, pl.ds(pl.multiple_of(target * width, width), width)],
            back_all.at[m, pl.ds(pl.multiple_of(cut * rows, rows), rows), :],
            swap_send.at[m, hop], swap_recv.at[m, hop], group, target,
        )

    def swap_keep(m):
        return pltpu.make_async_copy(
            d_att.at[m, :, pl.ds(pl.multiple_of(cut * width, width), width)],
            back_all.at[m, pl.ds(pl.multiple_of(cut * rows, rows), rows), :],
            swap_own.at[m],
        )

    small = small_ref[...]
    gain_one, gain_two = one_row(gain_one_ref), one_row(gain_two_ref)
    d_small[...] = jnp.zeros_like(d_small)
    lanes = lax.broadcasted_iota(jnp.int32, (rows, 128), 1)

    def norm_two_step(m, carry):
        dots = jnp.transpose(dots_ref[m])
        chosen = row_to_column(codes_ref[cut, m])[:, 0:1].astype(jnp.int32)
        h_two = h_ref[m]
        gate, _, mix_expert, routed, mixing = route(tail_dot(h_two, small), chosen, expert_count)
        d_mixing = jnp.where(lanes == expert_count, dots[:, 0:1], gate * dots[:, 1:2])
        d_gate = jnp.where(lanes == chosen, mix_expert * dots[:, 1:2], 0.0)
        d_logits = (softmax_back(mixing, d_mixing) + softmax_back(routed, d_gate)).astype(low)
        d_h = dh_ref[m] + plain_dot(d_logits, small)
        normed, scale = norm_parts(x_two_ref[m])
        one_lane = (lanes == expert_count + 2).astype(low)
        d_small[...] += lead_dot(h_two, d_logits) + lead_dot((d_h * normed).astype(low), one_lane)
        d_x = gy_ref[m].astype(f32) + norm_back(normed, scale, gain_two, d_h)
        tokens_ref[m] = d_x
        grad = d_x.astype(low)
        g_att[pl.ds(pl.multiple_of(m * rows, rows), rows), :] = grad
        d_att[m] = tail_dot(grad, w_out_ref[...]).astype(low)
        for hop in range(cut_count - 1, 0, -1):
            swap_copy(m, hop).start()
        swap_keep(m).start()
        return carry

    lax.fori_loop(0, micro_count, norm_two_step, 0)
    for m in range(micro_count):
        out_line.start(m)
    if sums_here:
        for kind in range(2):
            total = ends[kind][2]
            late_load(kind, 0).wait()
            late_load(kind, 1).wait()
            total[0] = (total[0].astype(f32) + total[1].astype(f32)).astype(low)
            late_copy(kind).start()

    def wo_step(g, carry):
        columns = pl.ds(pl.multiple_of(g * group_rows, group_rows), group_rows)
        grads = lead_dot(att_ref[:, columns], g_att[...]).astype(low)
        wo_part[g, :, :, 0:features] = grads.reshape(split, piece_rows, features)
        smalls = d_small[columns, :].astype(low)
        wo_part[g, :, :, features : features + 128] = smalls.reshape(split, piece_rows, 128)
        return carry

    lax.fori_loop(0, group_count, wo_step, 0)
    if sums_here:
        one_start(2)
    for m in range(micro_count):
        for level in range(levels):
            own_load(m, level).wait()
        out_line.pairs(m)
    for load in loads[:3]:
        load.wait()
    line = LineSum(part, pair_buf, far_buf, pair_send, pair_recv, far_send, far_recv)

    def attend_step(m, carry):
        for hop in range(cut_count - 1, 0, -1):
            swap_copy(m, hop).wait()
        swap_keep(m).wait()
        attend_back_one(heads, m, qkv_ref, docs_ref, docs_col_ref, lse_ref, back_all, d_qkv, key_acc, value_acc)
        for c in range(cut_count):
            part[m, c] = tail_dot(d_qkv[m, c * rows : (c + 1) * rows, :], w_qkv_ref[...]).astype(low)
        line.start(m)
        line.pairs(m)
        for j in range(levels - 1):
            out_line.hop(m, j)
        return carry

    lax.fori_loop(0, micro_count, attend_step, 0)

    def qkv_step(g, carry):
        columns = pl.ds(pl.multiple_of(g * group_rows, group_rows), group_rows)
        grads = jnp.zeros((group_rows, 3 * width), f32)
        for m in range(micro_count):
            grads = grads + lead_dot(h_all_ref[m, :, columns], d_qkv[m])
        qkv_part[g] = grads.astype(low).reshape(split, piece_rows, 3 * width)
        return carry

    for j in range(levels - 1):
        line.hop(0, j)
    for load in loads[3:]:
        load.wait()
    lax.fori_loop(0, group_count, qkv_step, 0)
    if sums_here:
        one_start(3)
        in_mid[...] = one_finish(0).astype(low)
        two_start(0)
        wo_mid[...] = one_finish(2).astype(low)
        two_start(2)
        out_out_ref[...] = one_finish(1)

    for m in range(1, micro_count):
        for j in range(levels - 1):
            line.hop(m, j)
    for m in range(micro_count):
        out_line.finish(m, d_h_one)
        output_ref[m] = (x_two_ref[m] + d_h_one[m]).astype(low)

    def norm_one_step(m, carry):
        line.finish(m, d_h_one)
        total = d_h_one[m]
        normed, scale = norm_parts(x_ref[m].astype(f32))
        tokens_ref[m] = tokens_ref[m] + norm_back(normed, scale, gain_one, total)
        return carry

    if not sums_here:
        lax.fori_loop(0, micro_count, norm_one_step, 0)
        wo_ref[...] = wo_part[...]
        query_out_ref[...] = qkv_part[...]
        return
    norm_one_step(0, 0)
    qkv_mid[...] = one_finish(3).astype(low)
    two_start(3)
    two_finish(0)
    share_piece = in_end.shape[2] // group_count
    for c in range(cut_count):
        for g in range(group_count):
            spot = (g * cut_count + c) * share_piece
            in_out_ref[:, spot : spot + share_piece] = in_end[c, :, g * share_piece : (g + 1) * share_piece].astype(f32)
    two_finish(2)
    total = wo_end[0].astype(f32)
    for c in range(1, cut_count):
        total = total + wo_end[c].astype(f32)
    wo_ref[...] = total[:, :features]
    small_sums = total[:, features:]
    for m in range(1, micro_count):
        norm_one_step(m, 0)
    two_finish(3)
    norm = jnp.zeros((piece_rows, 1), f32)
    outs = (query_out_ref, key_out_ref, value_out_ref)
    for c in range(cut_count):
        for k in range(3):
            grad = qkv_end[c, :, k * width : (k + 1) * width].astype(f32)
            outs[k][:, c * width : (c + 1) * width] = grad
            weights = w_rows[k, :, c * width : (c + 1) * width].astype(f32)
            norm = norm + jnp.sum(grad * weights, axis=-1, keepdims=True)
    spots = lax.broadcasted_iota(jnp.int32, (piece_rows, features), 1)
    mine = spots == place + lax.broadcasted_iota(jnp.int32, (piece_rows, features), 0)
    norm = norm / jnp.sum(jnp.where(mine, gain_one, 0.0), axis=-1, keepdims=True)
    tiny_lanes = lax.broadcasted_iota(jnp.int32, (piece_rows, 128), 1)
    tiny_ref[...] = jnp.where(tiny_lanes == expert_count + 3, norm, small_sums)
    for kind in range(2):
        late_copy(kind).wait()


def back(
    dh, dots, codes, h_two, x_two, gy, attended, w_output, docs, x, gain_one, gain_two, router, mixer, own_in, own_out,
    qkv, lse, w_qkv, h_all, out_part, w_query, w_key, w_value, d_in, d_out, got_in, got_out, heads, expert_count, sums_here,
    call_id,
):
    micro_count, rows, features = x.shape
    length = qkv.shape[1]
    cut_count = length // rows
    width = features // cut_count
    group_count = own_out.shape[0]
    piece_rows = features // (group_count * cut_count)
    share, piece = own_in.shape[3], own_out.shape[1]
    low, f32 = jnp.bfloat16, jnp.float32
    levels = cut_count // 2
    wide = features + 128
    shape = jax.ShapeDtypeStruct
    parts = (group_count, cut_count, piece_rows) if sums_here else (features // 256, 1, 256)
    tokens = (micro_count, rows, features)
    none = shape((16, 128), low)
    if sums_here:
        outs = (
            shape(tokens, low), shape(tokens, f32), shape((piece_rows, features), f32), shape((piece_rows, 128), f32),
            *[shape((piece_rows, features), f32)] * 3, shape((piece_rows, share * cut_count), f32),
            shape((piece, features), f32), shape((features, share), low), shape((share, features), low),
        )
    else:
        outs = (
            shape(tokens, low), shape(tokens, f32), shape((*parts, wide), low), none, shape((*parts, 3 * width), low),
            *[none] * 6,
        )
    peers = max(group_count - 1, 1) if sums_here else 1
    block = lambda *dims: pltpu.VMEM(dims, low)
    mids = lambda w: block(cut_count, piece_rows, w) if sums_here else block(16, 128)
    ins = lambda w: block(peers, cut_count, piece_rows, w) if sums_here else block(16, 128)
    dma = pltpu.SemaphoreType.DMA
    line = (micro_count, levels)
    vmem, far = pl.BlockSpec(memory_space=pltpu.VMEM), pl.BlockSpec(memory_space=pl.ANY)
    operands = (
        dh, dots, codes, h_two, x_two, gy, attended, w_output, docs, x, gain_one, gain_two, router, mixer, own_in, own_out,
        qkv, lse, w_qkv, h_all, out_part, w_query, w_key, w_value, d_in, d_out, got_in, got_out,
    )
    return pl.pallas_call(
        partial(back_kernel, heads, expert_count, sums_here),
        out_shape=outs,
        in_specs=[vmem] * 16 + [far] * 12,
        out_specs=[vmem] * 9 + [far] * 2,
        scratch_shapes=[
            block(micro_count, length, 3 * width), pltpu.VMEM((micro_count, length, width), f32), block(features, 3 * width),
            block(micro_count, length, features), block(3, piece_rows, features), pltpu.VMEM((8, length), f32),
            pltpu.VMEM((micro_count, length, 1), jnp.int32), pltpu.VMEM((128, features), f32), block(128, features),
            block(*line, rows, features), block(*line, rows, features), block(micro_count, levels + 1, rows, features),
            block(micro_count * rows, features),
            block(micro_count, rows, features),
            block(micro_count, length, width),
            block(micro_count, length, 3 * width),
            pltpu.VMEM((length, width), f32),
            pltpu.VMEM((length, width), f32),
            pltpu.VMEM((features, 128), f32),
            block(micro_count, cut_count, rows, features),
            block(*line, rows, features),
            block(micro_count, levels + 1, rows, features),
            pltpu.VMEM(tokens, f32),
            *((block(2, features, share), block(2, share, features)) if sums_here else (block(16, 128), block(16, 128))),
            block(*parts, wide),
            block(*parts, 3 * width),
            ins(wide), ins(3 * width), ins(share),
            block(peers, piece, features) if sums_here else block(16, 128),
            mids(wide), mids(3 * width), mids(share), mids(wide), mids(3 * width), mids(share),
            dma(line), dma(line), dma(line), dma((micro_count, levels + 1)),
            dma((micro_count, cut_count)), dma((micro_count, cut_count)), dma((micro_count,)),
            dma((4, peers)), dma((4, peers)), dma((4, cut_count)), dma((4, cut_count)), dma((4,)),
            dma((2,)), dma((2,)), dma((2, 2)), dma((7,)), dma(line),
            dma(line), dma(line), dma(line), dma((micro_count, levels + 1)),
        ],
        compiler_params=pltpu.CompilerParams(
            collective_id=call_id, has_side_effects=True, vmem_limit_bytes=62 * 2**20
        ),
    )(*operands)


def last_kernel(
    expert_count, d_in_ref, got_in_ref, late_in_ref, d_out_ref, got_out_ref, late_out_ref, tiny_ref, *refs,
):
    passed = (len(refs) - 6 - 10) // 3
    given, refs = refs[:passed], refs[passed:]
    taken, refs = refs[:passed], refs[passed:]
    held, refs = refs[-passed:], refs[:-passed]
    router_ref, mixer_ref, norm_one_ref, norm_two_ref, sum_in_ref, sum_out_ref = refs[:6]
    in_buf, out_buf, in_sum, out_sum, in_sem, out_sem, in_done, out_done, pass_sem, keep_sem = refs[6:]
    group = lax.axis_index("expert")
    passes = [pltpu.make_async_copy(src, dst, pass_sem.at[k]) for k, (src, dst) in enumerate(zip(given, held))]
    keeps = [pltpu.make_async_copy(src, dst, keep_sem.at[k]) for k, (src, dst) in enumerate(zip(held, taken))]
    chunks = in_sem.shape[0]
    work = []
    for ends in (
        ((d_in_ref.at[group], got_in_ref.at[0], late_in_ref), in_buf, in_sum, sum_in_ref, in_sem, in_done),
        ((d_out_ref.at[group], got_out_ref.at[0], late_out_ref), out_buf, out_sum, sum_out_ref, out_sem, out_done),
    ):
        sources, buf, total, target, sem, done = ends
        step = buf.shape[1] // chunks
        for k in range(chunks):
            part = pl.ds(k * step, step)
            loads = [
                pltpu.make_async_copy(src.at[part, :], buf.at[at, part, :], sem.at[k, at]) for at, src in enumerate(sources)
            ]
            work.append((loads, buf, total, part, pltpu.make_async_copy(total.at[part, :], target.at[part, :], done.at[k])))
    for copy in passes:
        copy.start()
    for loads, *_ in work:
        for load in loads:
            load.start()
    turned = jnp.transpose(tiny_ref[...])
    router_ref[...] = turned[0:expert_count]
    mixer_ref[...] = turned[expert_count : expert_count + 2]
    norm_two_ref[...] = turned[expert_count + 2 : expert_count + 3]
    norm_one_ref[...] = turned[expert_count + 3 : expert_count + 4]
    for copy, keep in zip(passes, keeps):
        copy.wait()
        keep.start()
    for loads, buf, total, part, keep in work:
        for load in loads:
            load.wait()
        total[part, :] = sum(buf[at, part, :].astype(jnp.float32) for at in range(3))
        keep.start()
    for *_, keep in work:
        keep.wait()
    for keep in keeps:
        keep.wait()


def last(d_in, got_in, late_in, d_out, got_out, late_out, tiny, others, expert_count):
    f32, dma = jnp.float32, pltpu.SemaphoreType.DMA
    shape = jax.ShapeDtypeStruct
    piece_rows = tiny.shape[0]
    vmem, far = pl.BlockSpec(memory_space=pltpu.VMEM), pl.BlockSpec(memory_space=pl.ANY)
    chunks = 4
    return pl.pallas_call(
        partial(last_kernel, expert_count),
        out_shape=(
            *[shape(x.shape, x.dtype) for x in others], shape((expert_count, piece_rows), f32), shape((2, piece_rows), f32),
            shape((1, piece_rows), f32), shape((1, piece_rows), f32), shape(late_in.shape, f32), shape(late_out.shape, f32),
        ),
        in_specs=[far] * 6 + [vmem] + [far] * len(others),
        out_specs=[far] * len(others) + [vmem] * 4 + [far] * 2,
        scratch_shapes=[
            pltpu.VMEM((3, *late_in.shape), late_in.dtype), pltpu.VMEM((3, *late_out.shape), late_out.dtype),
            pltpu.VMEM(late_in.shape, f32), pltpu.VMEM(late_out.shape, f32),
            dma((chunks, 3)), dma((chunks, 3)), dma((chunks,)), dma((chunks,)), dma((len(others),)), dma((len(others),)),
            *[pltpu.VMEM(x.shape, x.dtype) for x in others],
        ],
        compiler_params=pltpu.CompilerParams(vmem_limit_bytes=62 * 2**20),
    )(d_in, got_in, late_in, d_out, got_out, late_out, tiny, *others)


def local(
    tokens, cotangent, segments, expert_ids, slot_ids, kept_mask, norm1_gain, w_query, w_key, w_value, w_output,
    norm2_gain, dense_in, dense_out, router, mixer, expert_in, expert_out,
):
    micro_count, row_count, features = tokens.shape[1:]
    cut_count = lax.axis_size("cuts")
    group_count = lax.axis_size("expert")
    cut = lax.axis_index("cuts")
    group = lax.axis_index("expert")
    length = cut_count * row_count
    head_width = features // cut_count
    heads = head_width // 64
    expert_count = router.shape[1]
    hidden_count = dense_in.shape[1]
    share = hidden_count // cut_count
    piece = share // group_count
    capacity = max(2, row_count * 5 // (4 * expert_count))
    slots = tile_slots(capacity, row_count, 2 * row_count)
    rows = features // (group_count * cut_count)
    sums_here = rows % 16 == 0 and group_count == 4
    by_rows = lambda v: v.reshape(-1, 128)
    router_t, mixer_t = router.T, mixer.T
    f32, low = jnp.float32, jnp.bfloat16

    strided = piece % 128 == 0
    if strided:
        own_in, own_out = dense_in, dense_out
    else:
        own_in = lax.dynamic_index_in_dim(
            dense_in.reshape(features, group_count, cut_count, piece), cut, 2, keepdims=False
        ).reshape(features, share)
        own_out = lax.dynamic_index_in_dim(
            dense_out.reshape(group_count, cut_count, piece, features), cut, 1, keepdims=False
        ).reshape(share, features)
    h_all, qkv, lse, attended, w_qkv, codes, weights_in, g_all = front(
        tokens[0], cotangent[0], by_rows(norm1_gain), w_query, w_key, w_value, segments[0], expert_ids[0], slot_ids[0],
        kept_mask[0], expert_in[0], group_count, cut_count, heads, capacity, slots, 1,
    )
    x_two, h_two, out_part, d_h2, dots, d_own_in, d_own_out, d_in, d_out, _, got_in, got_out = feed(
        tokens[0], attended, w_output, by_rows(norm2_gain), router_t, mixer_t, codes, g_all, own_in, own_out, weights_in,
        expert_in[0], expert_out[0], share, slots, strided, sums_here, 2,
    )
    output, grad_tokens, grad_output, tiny, grad_query, grad_key, grad_value, grad_dense_in, grad_dense_out, late_in, late_out = back(
        d_h2, dots, codes, h_two, x_two, cotangent[0], attended.reshape(-1, features), w_output, segments[0], tokens[0],
        by_rows(norm1_gain), by_rows(norm2_gain), router_t, mixer_t, d_own_in.reshape(group_count, cut_count, rows, share),
        d_own_out.reshape(group_count, piece, features), qkv, lse, w_qkv, h_all.reshape(micro_count, length, features),
        out_part, w_query, w_key, w_value, d_in, d_out, got_in, got_out, heads, expert_count, sums_here, 3,
    )
    sum_groups = lambda part: lax.psum_scatter(
        part.reshape(-1, part.shape[-1]), "expert", scatter_dimension=0, tiled=True
    )
    if sums_here:
        others = (
            output, grad_tokens, grad_query, grad_key, grad_value, grad_output, grad_dense_in, grad_dense_out
        )
        *others, grad_router, grad_mixer, grad_norm1, grad_norm2, grad_expert_in, grad_expert_out = last(
            d_in, got_in, late_in, d_out, got_out, late_out, tiny, others, expert_count
        )
        output, grad_tokens, grad_query, grad_key, grad_value, grad_output, grad_dense_in, grad_dense_out = others
        grad_router, grad_mixer, grad_norm1, grad_norm2 = grad_router.T, grad_mixer.T, grad_norm1[0], grad_norm2[0]
    else:
        swap = lambda part: lax.all_to_all(
            part.reshape(cut_count, rows, -1), "cuts", split_axis=0, concat_axis=0
        ).astype(f32)
        wide = jnp.sum(swap(sum_groups(grad_output)), axis=0)
        grad_output, grad_small = wide[:, :features], wide[:, features:]
        grad_router, grad_mixer = grad_small[:, :expert_count], grad_small[:, expert_count : expert_count + 2]
        grad_norm2 = grad_small[:, expert_count + 2]
        grad_qkv = swap(sum_groups(grad_query)).reshape(cut_count, rows, 3, head_width).transpose(2, 1, 0, 3)
        grad_qkv = grad_qkv.reshape(3, rows, features)
        grad_query, grad_key, grad_value = grad_qkv
        grad_dense_in = swap(sum_groups(d_own_in)).reshape(cut_count, rows, group_count, piece).transpose(1, 2, 0, 3)
        grad_dense_in = grad_dense_in.reshape(rows, hidden_count)
        grad_dense_out = sum_groups(d_own_out).astype(f32)
        grad_expert_in = sum_groups(d_in).astype(f32)
        grad_expert_out = sum_groups(d_out).astype(f32)
        place = (group * cut_count + cut) * rows
        own_rows = lambda w: lax.dynamic_slice_in_dim(w, place, rows, 0).astype(f32)
        grad_norm1 = sum(
            jnp.sum(own_rows(w) * grad_qkv[k], axis=-1) for k, w in enumerate((w_query, w_key, w_value))
        ) / own_rows(norm1_gain)
    return (
        output[None], grad_tokens[None], grad_norm1, grad_query, grad_key, grad_value, grad_output, grad_norm2, grad_dense_in,
        grad_dense_out, grad_router, grad_mixer, grad_expert_in[None], grad_expert_out[None],
    )


def solution(mesh):
    in_specs = (
        P("expert", None, "cuts", None),
        P("expert", None, "cuts", None),
        P("expert", None, None),
        P("expert", None, "cuts"),
        P("expert", None, "cuts"),
        P("expert", None, "cuts"),
        P(),
        P(),
        P(),
        P(),
        P(),
        P(),
        P(),
        P(),
        P(),
        P(),
        P("expert", None, "cuts"),
        P("expert", "cuts", None),
    )
    out_specs = (
        P("expert", None, "cuts", None),
        P("expert", None, "cuts", None),
        P(("expert", "cuts")),
        P(("expert", "cuts"), None),
        P(("expert", "cuts"), None),
        P(("expert", "cuts"), None),
        P(("expert", "cuts"), None),
        P(("expert", "cuts")),
        P(("expert", "cuts"), None),
        P(("expert", "cuts"), None),
        P(("expert", "cuts"), None),
        P(("expert", "cuts"), None),
        P("expert", None, "cuts"),
        P("expert", "cuts", None),
    )
    return jax.shard_map(local, mesh=mesh, in_specs=in_specs, out_specs=out_specs, check_vma=False)
```

```python
from functools import partial

import jax
import jax.numpy as jnp
from jax import lax
from jax.experimental import pallas as pl
from jax.experimental.pallas import tpu as pltpu
from jax.sharding import PartitionSpec as P

MESH = pl.DeviceIdType.MESH
score_scale = 0.125
masked_value = -1e30
norm_eps = 1e-05


def plain_dot(left, right):
    return jnp.dot(left, right, preferred_element_type=jnp.float32)


def lead_dot(left, right):
    return lax.dot_general(
        left, right, (((0,), (0,)), ((), ())), preferred_element_type=jnp.float32
    )


def tail_dot(left, right):
    return lax.dot_general(
        left, right, (((1,), (1,)), ((), ())), preferred_element_type=jnp.float32
    )


def head_masks(width, heads):
    lane = lax.broadcasted_iota(jnp.int32, (1, width), 1)
    size = width // heads
    return [((lane >= h * size) & (lane < (h + 1) * size)) for h in range(heads)]


def allowed_mask(docs_ref, docs_col_ref, m, start, rows, keys):
    query_spots = start + lax.broadcasted_iota(jnp.int32, (rows, keys), 0)
    key_spots = lax.broadcasted_iota(jnp.int32, (rows, keys), 1)
    return (key_spots <= query_spots) & (docs_ref[pl.ds(m, 1), 0:keys] == docs_col_ref[m, pl.ds(start, rows), :])


def attend_one(heads, m, qkv_ref, docs_ref, docs_col_ref, att_ref, lse_ref):
    length, width = att_ref.shape[1], att_ref.shape[2]
    rows = min(256, length)
    masks = head_masks(width, heads)
    for block in range(length // rows):
        start, keys = block * rows, (block + 1) * rows
        allowed = allowed_mask(docs_ref, docs_col_ref, m, start, rows, keys)
        query = qkv_ref[m, pl.ds(start, rows), 0:width] * jnp.bfloat16(score_scale)
        key = qkv_ref[m, 0:keys, width : 2 * width]
        value = qkv_ref[m, 0:keys, 2 * width : 3 * width]
        att = jnp.zeros((rows, width), jnp.float32)
        logs = jnp.zeros((rows, width), jnp.float32)
        for mask in masks:
            scores = tail_dot(jnp.where(mask, query, jnp.bfloat16(0)), key)
            scores = jnp.where(allowed, scores, masked_value)
            top = jnp.max(scores, axis=-1, keepdims=True)
            raised = jnp.exp(scores - top)
            total = jnp.sum(raised, axis=-1, keepdims=True)
            probs = (raised * (1.0 / total)).astype(jnp.bfloat16)
            att = jnp.where(mask, plain_dot(probs, value), att)
            logs = jnp.where(mask, top + jnp.log(total), logs)
        att_ref[m, pl.ds(start, rows), :] = att.astype(jnp.bfloat16)
        lse_ref[m, pl.ds(start, rows), :] = logs


def norm_parts(values):
    center = values - jnp.mean(values, axis=-1, keepdims=True)
    spread = jnp.mean(center * center, axis=-1, keepdims=True)
    scale = lax.rsqrt(spread + norm_eps)
    return center * scale, scale


def norm_back(normed, scale, gain, grad):
    inner = grad * gain
    return scale * (
        inner
        - jnp.mean(inner, axis=-1, keepdims=True)
        - normed * jnp.mean(inner * normed, axis=-1, keepdims=True)
    )


def gelu_pair(values):
    phi = 0.5 * (1.0 + lax.erf(values * (0.5**0.5)))
    bell = jnp.exp(-0.5 * values * values) * ((2.0 * jnp.pi) ** -0.5)
    return values * phi, phi + values * bell


def tile_slots(capacity, row_count, tile):
    return -(-capacity * (tile // row_count) // 16) * 16


def token_table(spot, width):
    return (spot == lax.broadcasted_iota(jnp.int32, (spot.shape[0], width), 1)).astype(jnp.bfloat16)


def lane_softmax(logits, lanes, first, count):
    inside = (lanes >= first) & (lanes < first + count)
    raised = jnp.exp(logits - jnp.max(jnp.where(inside, logits, masked_value), axis=-1, keepdims=True))
    raised = jnp.where(inside, raised, 0.0)
    return raised / jnp.sum(raised, axis=-1, keepdims=True)


def route(logits, chosen, expert_count):
    lanes = lax.broadcasted_iota(jnp.int32, logits.shape, 1)
    routed = lane_softmax(logits, lanes, 0, expert_count)
    mixing = lane_softmax(logits, lanes, expert_count, 2)
    pick = lambda values, lane: jnp.sum(jnp.where(lanes == lane, values, 0.0), axis=-1, keepdims=True)
    return pick(routed, chosen), pick(mixing, expert_count), pick(mixing, expert_count + 1), routed, mixing


def softmax_back(probs, grad):
    return probs * (grad - jnp.sum(probs * grad, axis=-1, keepdims=True))


def line_copy(src, dst, send, recv, group, target):
    return pltpu.make_async_remote_copy(
        src_ref=src, dst_ref=dst, send_sem=send, recv_sem=recv, device_id=(group, target), device_id_type=MESH
    )


def greet_all(cut_count, group_count):
    cut = lax.axis_index("cuts")
    group = lax.axis_index("expert")
    barrier = pltpu.get_barrier_semaphore()
    for hop in range(1, cut_count):
        pl.semaphore_signal(barrier, inc=1, device_id=(group, jnp.bitwise_xor(cut, hop)), device_id_type=MESH)
    for hop in range(1, group_count):
        pl.semaphore_signal(barrier, inc=1, device_id=(jnp.bitwise_xor(group, hop), cut), device_id_type=MESH)
    pl.semaphore_wait(barrier, cut_count + group_count - 2)


class LineGather:
    def __init__(self, buf, far_send, far_recv, pair_send, pair_recv):
        self.buf = buf
        self.sems = (far_send, far_recv, pair_send, pair_recv)
        self.cut = lax.axis_index("cuts")
        self.group = lax.axis_index("expert")
        self.level, self.side = self.cut // 2, self.cut % 2
        self.levels = buf.shape[1] // 2

    def place(self, n):
        low, high = self.level, self.levels - 1 - self.level
        near = jnp.minimum(low, high)
        paired = n <= 2 * near
        distance = jnp.where(paired, (n + 1) // 2, n - near)
        below = jnp.where(paired, n % 2 == 1, low > high)
        return jnp.where(below, self.level - distance, self.level + distance), below

    def far_copy(self, m, level, target, send):
        block = self.buf.at[m, 2 * level + self.side]
        return line_copy(block, block, self.sems[0].at[m, send], self.sems[1].at[m, level], self.group, target)

    def pair_copy(self, m, level, side):
        block = self.buf.at[m, 2 * level + side]
        return line_copy(
            block, block, self.sems[2].at[m, level], self.sems[3].at[m, level], self.group, jnp.bitwise_xor(self.cut, 1)
        )

    def start(self, m):
        @pl.when(self.level + 1 < self.levels)
        def _():
            self.far_copy(m, self.level, self.cut + 2, self.level).start()

        @pl.when(self.level > 0)
        def _():
            self.far_copy(m, self.level, self.cut - 2, self.levels).start()

        self.pair_copy(m, self.level, self.side).start()

    def take(self, m, n):
        level, below = self.place(n)

        @pl.when(n > 0)
        def _():
            target = jnp.where(below, self.cut + 2, self.cut - 2)
            self.far_copy(m, level, target, level).wait_recv()

            @pl.when(jnp.where(below, self.level + 1 < self.levels, self.level > 0))
            def _():
                self.far_copy(m, level, target, level).start()

            self.pair_copy(m, level, self.side).start()

        self.pair_copy(m, level, 1 - self.side).wait_recv()
        return level

    def finish(self, m):
        @pl.when(self.level + 1 < self.levels)
        def _():
            self.far_copy(m, self.level, self.cut + 2, self.level).wait_send()

        @pl.when(self.level > 0)
        def _():
            self.far_copy(m, self.level, self.cut - 2, self.levels).wait_send()

        for n in range(self.levels):
            level, below = self.place(n)
            if n:
                @pl.when(jnp.where(below, self.level + 1 < self.levels, self.level > 0))
                def _():
                    self.far_copy(m, level, self.cut, level).wait_send()

            self.pair_copy(m, level, self.side).wait_send()


class LineSum:
    def __init__(self, part, pair_buf, far_buf, pair_send, pair_recv, send, recv, own=None):
        self.part, self.pair_buf, self.far_buf, self.own = part, pair_buf, far_buf, own
        self.sems = (pair_send, pair_recv, send, recv)
        self.cut = lax.axis_index("cuts")
        self.group = lax.axis_index("expert")
        self.level, self.side = self.cut // 2, self.cut % 2
        self.levels = part.shape[1] // 2

    def pair_copy(self, m, level):
        return line_copy(
            self.part.at[m, 2 * level + 1 - self.side], self.pair_buf.at[m, level], self.sems[0].at[m, level],
            self.sems[1].at[m, level], self.group, jnp.bitwise_xor(self.cut, 1),
        )

    def far_copy(self, m, level, up):
        target = self.cut + 2 if up else self.cut - 2
        slot = level if up else jnp.where(level == self.level - 1, self.levels, level)
        return line_copy(
            self.pair_buf.at[m, level], self.far_buf.at[m, slot], self.sems[2].at[m, level], self.sems[3].at[m, slot],
            self.group, target,
        )

    def arrived(self, m, slot):
        line_copy(
            self.far_buf.at[m, slot], self.far_buf.at[m, slot], self.sems[2].at[m, 0], self.sems[3].at[m, slot],
            self.group, self.cut,
        ).wait_recv()
        return self.far_buf[m, slot].astype(jnp.float32)

    def start(self, m):
        def one(k, carry):
            self.pair_copy(m, jnp.where(k % 2 == 0, self.levels - 1 - k // 2, k // 2)).start()
            return carry

        lax.fori_loop(0, self.levels, one, 0)

    def pairs(self, m):
        def one(k, carry):
            level = jnp.where(k % 2 == 0, self.levels - 1 - k // 2, k // 2)
            self.pair_copy(m, level).wait_recv()
            mine = self.part[m, 2 * level + self.side] if self.own is None else self.own[m, level]
            total = mine.astype(jnp.float32) + self.pair_buf[m, level].astype(jnp.float32)
            self.pair_buf[m, level] = total.astype(self.pair_buf.dtype)
            @pl.when((self.level == 0) & (level > 0))
            def _():
                self.far_copy(m, level, True).start()

            @pl.when((self.level == self.levels - 1) & (level < self.levels - 1))
            def _():
                self.far_copy(m, level, False).start()

            return carry

        lax.fori_loop(0, self.levels, one, 0)

    def pass_on(self, m, level, up):
        @pl.when((level > self.level) if up else (level < self.level))
        def _():
            total = self.pair_buf[m, level].astype(jnp.float32) + self.arrived(m, level)
            self.pair_buf[m, level] = total.astype(self.pair_buf.dtype)
            self.far_copy(m, level, up).start()

    def hop(self, m, j):
        inner = (self.level > 0) & (self.level < self.levels - 1)
        lower = 2 * self.level < self.levels

        @pl.when(inner & lower)
        def _():
            self.pass_on(m, self.levels - 1 - j, True)
            self.pass_on(m, j, False)

        @pl.when(inner & jnp.logical_not(lower))
        def _():
            self.pass_on(m, j, False)
            self.pass_on(m, self.levels - 1 - j, True)

    def finish(self, m, out_ref):
        out_ref[m] = self.pair_buf[m, self.level].astype(jnp.float32)

        @pl.when(self.level > 0)
        def _():
            out_ref[m] = out_ref[m] + self.arrived(m, self.level)

        @pl.when(self.level < self.levels - 1)
        def _():
            out_ref[m] = out_ref[m] + self.arrived(m, self.levels)

        def one(level, carry):
            self.pair_copy(m, level).wait_send()

            @pl.when(level > self.level)
            def _():
                self.far_copy(m, level, True).wait_send()

            @pl.when(level < self.level)
            def _():
                self.far_copy(m, level, False).wait_send()

            return carry

        lax.fori_loop(0, self.levels, one, 0)


def row_to_column(values):
    return jnp.transpose(values.astype(jnp.float32))


def one_row(ref):
    values = ref[...].astype(jnp.float32)
    return jnp.concatenate([values[k : k + 1] for k in range(values.shape[0])], axis=1)


def stack_small(router_ref, mixer_ref, stage, small):
    count = router_ref.shape[0]
    stage[...] = jnp.zeros_like(stage)
    stage[0:count] = router_ref[...].astype(jnp.float32)
    stage[count : count + 2] = mixer_ref[...].astype(jnp.float32)
    small[...] = stage[...].astype(small.dtype)


def fill_docs(docs_ref, stage, docs_col):
    stage[...] = jnp.zeros_like(stage)
    micro_count = docs_ref.shape[0]
    stage[0:micro_count] = docs_ref[...].astype(jnp.float32)
    for k in range(stage.shape[1] // 128):
        turned = jnp.transpose(stage[:, k * 128 : (k + 1) * 128]).astype(jnp.int32)
        for m in range(micro_count):
            docs_col[m, k * 128 : (k + 1) * 128, :] = turned[:, m : m + 1]


def front_kernel(
    heads, capacity, slots,
    x_ref, gy_ref, gain_ref, w_query_ref, w_key_ref, w_value_ref, docs_ref, ids_ref, slot_ref, kept_ref, expert_in_ref,
    expert_out_ref,
    h_out_ref, qkv_out_ref, lse_out_ref, att_ref, w_qkv_ref, codes_ref, weights_ref, weights_out_ref, g_all_ref,
    h_all_ref, qkv_ref, lse_ref, docs_stage, docs_col_ref, att_part, own_code, far_send, far_recv, pair_send, pair_recv, load_sem, swap_send, swap_recv, swap_own, code_send,
    code_recv, weight_send, weight_recv, pass_send, pass_recv, keep_sem,
    g_far_send, g_far_recv, g_pair_send, g_pair_recv, g_own,
):
    micro_count, cut_count, rows, features = h_all_ref.shape
    group_count = weights_ref.shape[0]
    width = features // cut_count
    cut = lax.axis_index("cuts")
    group = lax.axis_index("expert")
    low = jnp.bfloat16
    loads = []
    for k, ref in enumerate((w_query_ref, w_key_ref, w_value_ref)):
        loads.append(pltpu.make_async_copy(
            ref.at[:, pl.ds(pl.multiple_of(cut * width, width), width)], w_qkv_ref.at[:, k * width : (k + 1) * width],
            load_sem.at[k],
        ))
        loads[-1].start()
    g_keep = pltpu.make_async_copy(gy_ref, g_all_ref.at[0, cut], g_own)
    g_keep.start()
    gain = one_row(gain_ref)
    greet_all(cut_count, group_count)
    g_line = LineGather(g_all_ref, g_far_send, g_far_recv, g_pair_send, g_pair_recv)

    line = LineGather(h_all_ref, far_send, far_recv, pair_send, pair_recv)

    def norm_step(m, carry):
        normed, _ = norm_parts(x_ref[m].astype(jnp.float32))
        h_all_ref[m, cut] = (normed * gain).astype(low)
        line.start(m)
        return carry

    lax.fori_loop(0, micro_count, norm_step, 0)

    square = group_count == 4

    def weight_copy(kind, hop):
        src, dst = ((expert_in_ref, weights_ref), (expert_out_ref, weights_out_ref))[kind]
        return line_copy(
            src, dst.at[group], weight_send.at[kind, hop - 1], weight_recv.at[kind, hop - 1],
            jnp.bitwise_xor(group, hop), cut,
        )

    def pass_copy(k):
        half = pl.ds(k * (features // 2), features // 2)
        block = weights_ref.at[jnp.bitwise_xor(group, 2 - k), half, :]
        return line_copy(block, block, pass_send.at[k], pass_recv.at[k], jnp.bitwise_xor(group, 1 + k), cut)

    weight_hops = [(0, 1), (0, 2)] if square else [(kind, hop) for kind in range(2) for hop in range(1, group_count)]
    for kind, hop in weight_hops:
        weight_copy(kind, hop).start()

    chosen = jnp.where(kept_ref[...] == 1, ids_ref[...], -1)
    spot = jnp.where(kept_ref[...] == 1, ids_ref[...] * slots + cut % 2 * capacity + slot_ref[...], -1)
    own_code[...] = jnp.zeros_like(own_code)
    for m in range(micro_count):
        own_code[m, 0:1] = chosen[m : m + 1]
        own_code[m, 1:2] = spot[m : m + 1]
    codes_ref[cut] = own_code[...]

    def code_copy(hop):
        return line_copy(
            own_code, codes_ref.at[cut], code_send.at[hop], code_recv.at[hop], group, jnp.bitwise_xor(cut, hop)
        )

    for hop in range(1, cut_count):
        code_copy(hop).start()
    fill_docs(docs_ref, docs_stage, docs_col_ref)
    for load in loads:
        load.wait()

    def tile_step(n, m):
        level = line.take(m, n)
        h_tile = h_all_ref[m, pl.ds(2 * level, 2)].reshape(2 * rows, features)
        spots = pl.ds(pl.multiple_of(level * 2 * rows, 2 * rows), 2 * rows)
        qkv_ref[m, spots, :] = plain_dot(h_tile, w_qkv_ref[...]).astype(low)

    def early(i, carry):
        tile_step(i // micro_count, i % micro_count)
        return carry

    levels = cut_count // 2
    lax.fori_loop(0, (levels - 1) * micro_count, early, 0)
    g_keep.wait()
    g_line.start(0)
    if square:
        for hop in (1, 2):
            weight_copy(0, hop).wait()
        for k in range(2):
            pass_copy(k).start()
        for hop in (1, 2):
            weight_copy(1, hop).start()

    def swap_copy(m, hop):
        target = jnp.bitwise_xor(cut, hop)
        return line_copy(
            att_part.at[m, pl.ds(pl.multiple_of(target * rows, rows), rows), :],
            att_ref.at[m, :, pl.ds(pl.multiple_of(cut * width, width), width)],
            swap_send.at[m, hop], swap_recv.at[m, hop], group, target,
        )

    def swap_keep(m):
        return pltpu.make_async_copy(
            att_part.at[m, pl.ds(pl.multiple_of(cut * rows, rows), rows), :],
            att_ref.at[m, :, pl.ds(pl.multiple_of(cut * width, width), width)],
            swap_own.at[m],
        )

    def late(m, carry):
        tile_step(levels - 1, m)
        attend_one(heads, m, qkv_ref, docs_ref, docs_col_ref, att_part, lse_ref)
        for hop in range(cut_count - 1, 0, -1):
            swap_copy(m, hop).start()
        swap_keep(m).start()

        @pl.when(m == 0)
        def _():
            g_line.take(0, 0)
            g_line.take(0, 1)

        return carry

    lax.fori_loop(0, micro_count, late, 0)
    for n in range(2, levels):
        g_line.take(0, n)
    keeps = [
        pltpu.make_async_copy(src, dst, keep_sem.at[k])
        for k, (src, dst) in enumerate(((h_all_ref, h_out_ref), (qkv_ref, qkv_out_ref), (lse_ref, lse_out_ref)))
    ]
    for keep in keeps:
        keep.start()

    for hop in range(1, cut_count):
        code_copy(hop).wait()
    for m in range(micro_count):
        line.finish(m)
    for m in range(micro_count):
        for hop in range(cut_count - 1, 0, -1):
            swap_copy(m, hop).wait()
        swap_keep(m).wait()
    g_line.finish(0)
    for keep in keeps:
        keep.wait()
    if square:
        for k in range(2):
            pass_copy(k).wait()
        for hop in (1, 2):
            weight_copy(1, hop).wait()
    else:
        for kind, hop in weight_hops:
            weight_copy(kind, hop).wait()


def front(
    x, gy, gain, w_query, w_key, w_value, docs, ids, slot_ids, kept, expert_in, expert_out, group_count, cut_count, heads, capacity,
    slots, call_id,
):
    micro_count, rows, features = x.shape
    length, levels, width = cut_count * rows, cut_count // 2, features // cut_count
    low, f32 = jnp.bfloat16, jnp.float32
    shape = jax.ShapeDtypeStruct
    dma = pltpu.SemaphoreType.DMA
    vmem, far = pl.BlockSpec(memory_space=pltpu.VMEM), pl.BlockSpec(memory_space=pl.ANY)
    return pl.pallas_call(
        partial(front_kernel, heads, capacity, slots),
        out_shape=(
            shape((micro_count, cut_count, rows, features), low),
            shape((micro_count, length, 3 * width), low),
            shape((micro_count, length, width), f32),
            shape((micro_count, rows, features), low),
            shape((features, 3 * width), low),
            shape((cut_count, micro_count, 8, rows), jnp.int32),
            shape((group_count, *expert_in.shape), low),
            shape((group_count, *expert_out.shape), low),
            shape((1, cut_count, rows, features), low),
        ),
        in_specs=[vmem, vmem, vmem, far, far, far, vmem, vmem, vmem, vmem, far, far],
        out_specs=[far] * 3 + [vmem] * 3 + [far] * 3,
        scratch_shapes=[
            pltpu.VMEM((micro_count, cut_count, rows, features), low),
            pltpu.VMEM((micro_count, length, 3 * width), low),
            pltpu.VMEM((micro_count, length, width), f32),
            pltpu.VMEM((8, length), f32),
            pltpu.VMEM((micro_count, length, 1), jnp.int32),
            pltpu.VMEM((micro_count, length, width), low),
            pltpu.VMEM((micro_count, 8, rows), jnp.int32),
            dma((micro_count, levels + 1)), dma((micro_count, levels)), dma((micro_count, levels)), dma((micro_count, levels)),
            dma((3,)), dma((micro_count, cut_count)), dma((micro_count, cut_count)), dma((micro_count,)),
            dma((cut_count,)), dma((cut_count,)), dma((2, group_count - 1)), dma((2, group_count - 1)), dma((2,)), dma((2,)),
            dma((3,)), dma((1, levels + 1)), dma((1, levels)), dma((1, levels)), dma((1, levels)), dma(()),
        ],
        compiler_params=pltpu.CompilerParams(collective_id=call_id, has_side_effects=True, vmem_limit_bytes=62 * 2**20),
    )(x, gy, gain, w_query, w_key, w_value, docs, ids, slot_ids, kept, expert_in, expert_out)


def feed_kernel(
    slots, strided, early, stored,
    x_ref, att_ref, gy_ref, g_first_ref, w_out_ref, gain_ref, router_ref, mixer_ref, codes_ref, dense_in_ref, dense_out_ref,
    weights_in_ref, weights_out_ref, expert_in_ref, expert_out_ref,
    x_two_ref, h_own_ref, output_ref, dh_ref, sums_ref, d_own_in_ref, d_own_out_ref, d_in_ref, d_out_ref, across_ref,
    got_in_ref, got_out_ref, out_rest_ref,
    h_all, g_buf, sent, g_sent, hidden_buf, pre_buf, back_buf, side_buf, own_in, own_out, in_buf, out_buf, inner_buf,
    slope_buf, dots, dots_in, pair_buf, far_buf, o_pair_buf, o_far_buf, out_ref, small_stage, small_ref,
    far_send, far_recv, pair_send, pair_recv, g_far_send, g_far_recv, g_pair_send, g_pair_recv,
    line_send, line_recv, two_send, two_recv, o_line_send, o_line_recv, o_two_send, o_two_recv,
    load_sem, in_sem, out_sem, stage_sem, dot_send, dot_recv, weight_send, weight_recv, early_send, early_recv,
):
    micro_count, cut_count, rows, features = h_all.shape
    group_count = weights_out_ref.shape[0]
    share = own_in.shape[1]
    levels, tile = cut_count // 2, 2 * rows
    expert_count = group_count
    cut = lax.axis_index("cuts")
    group = lax.axis_index("expert")
    low, f32 = jnp.bfloat16, jnp.float32
    half = share
    loads = []
    for k in range(features // half):
        loads.append(pltpu.make_async_copy(w_out_ref.at[:, k * half : (k + 1) * half], in_buf.at[k], load_sem.at[k]))
    g_load = pltpu.make_async_copy(g_first_ref.at[0], g_buf.at[0], load_sem.at[2 + 2 * group_count])
    first_load = len(loads)
    if strided:
        piece = share // group_count
        for g in range(group_count):
            spot = pl.ds(pl.multiple_of((g * cut_count + cut) * piece, piece), piece)
            here = pl.ds(g * piece, piece)
            loads.append(pltpu.make_async_copy(dense_in_ref.at[:, spot], own_in.at[:, here], load_sem.at[len(loads)]))
            loads.append(pltpu.make_async_copy(dense_out_ref.at[spot, :], own_out.at[here, :], load_sem.at[len(loads)]))
    else:
        loads.append(pltpu.make_async_copy(dense_in_ref, own_in, load_sem.at[len(loads)]))
        loads.append(pltpu.make_async_copy(dense_out_ref, own_out, load_sem.at[len(loads)]))
    for load in loads:
        load.start()
    stack_small(router_ref, mixer_ref, small_stage, small_ref)
    gain = one_row(gain_ref)
    g_load.start()
    for m in range(1, micro_count):
        g_buf[m, cut] = gy_ref[m]
    greet_all(cut_count, group_count)
    line = LineGather(h_all, far_send, far_recv, pair_send, pair_recv)
    g_line = LineGather(g_buf, g_far_send, g_far_recv, g_pair_send, g_pair_recv)
    for m in range(1, micro_count):
        g_line.start(m)
    for load in loads[:first_load]:
        load.wait()

    def norm_step(m, carry):
        att = att_ref[m]
        projected = jnp.concatenate([plain_dot(att, in_buf[k]) for k in range(features // half)], axis=1)
        x_two = x_ref[m].astype(f32) + projected
        x_two_ref[m] = x_two
        normed, _ = norm_parts(x_two)
        h_two = (normed * gain).astype(low)
        h_all[m, cut] = h_two
        h_own_ref[m] = h_two
        line.start(m)
        return carry

    lax.fori_loop(0, micro_count, norm_step, 0)

    square = group_count == 4

    def pass_copy(k):
        half = pl.ds(k * (share // 2), share // 2)
        return line_copy(
            weights_out_ref.at[jnp.bitwise_xor(group, 2 - k), half, :], across_ref.at[half, :], weight_send.at[k],
            weight_recv.at[k], jnp.bitwise_xor(group, 1 + k), cut,
        )

    for k in range(2 if square else 0):
        pass_copy(k).start()
    for load in loads[first_load:]:
        load.wait()
    lanes = lax.broadcasted_iota(jnp.int32, (tile, 128), 1)

    def columns(m, level):
        both = [row_to_column(codes_ref[2 * level + k, m]) for k in range(2)]
        both = jnp.concatenate(both, axis=0).astype(jnp.int32)
        return both[:, 0:1], both[:, 1:2]

    def places(m, level):
        t = m * levels + level
        return (
            pl.ds(2 * level, 2), pl.ds(pl.multiple_of(t * tile, tile), tile), pl.ds(pl.multiple_of(t * slots, slots), slots)
        )

    def dense_step(i, carry):
        n, m = i // micro_count, i % micro_count
        level = line.take(m, n)
        blocks, here, spots = places(m, level)
        h_two = h_all[m, blocks].reshape(tile, features)
        chosen, spot = columns(m, level)
        gate, mix_dense, mix_expert, _, _ = route(tail_dot(h_two, small_ref[...]), chosen, expert_count)
        side_buf[here, :] = jnp.where(lanes == 0, mix_dense, mix_expert * gate)
        rows_sent = lead_dot(token_table(spot, expert_count * slots), h_two).astype(low)
        for e in range(expert_count):
            sent[e, spots, :] = rows_sent[e * slots : (e + 1) * slots]
        act, slope = gelu_pair(plain_dot(h_two, own_in[...]))
        pre_buf[here, :] = slope.astype(low)
        hidden_buf[here, :] = (mix_dense * act).astype(low)
        out_ref[m, blocks] = plain_dot(act.astype(low), own_out[...]).astype(low).reshape(2, rows, features)
        return carry

    lax.fori_loop(0, levels * micro_count, dense_step, 0)

    def load_at(i, mask, own=False, across=False):
        e = jnp.bitwise_xor(group, mask)
        src_in = expert_in_ref if own else weights_in_ref.at[e]
        src_out = expert_out_ref if own else across_ref if across else weights_out_ref.at[e]
        return (
            pltpu.make_async_copy(src_in, in_buf.at[i % 2], in_sem.at[i % 2]),
            pltpu.make_async_copy(src_out, out_buf.at[i % 2], out_sem.at[i % 2]),
        )

    def load_start(i, mask, own=False, across=False):
        for load in load_at(i, mask, own, across):
            load.start()

    def load_wait(i):
        for load in load_at(i, 0, True):
            load.wait()

    load_start(0, 0, True)

    def forward_step(i, carry):
        @pl.when(i + 1 < expert_count - square)
        def _():
            load_start(i + 1, i + 1)

        if square:
            @pl.when(i == 2)
            def _():
                for k in range(2):
                    pass_copy(k).wait()
                load_start(3, 3, across=True)

        load_wait(i)
        e, at = jnp.bitwise_xor(group, i), i % 2
        act, slope = gelu_pair(plain_dot(sent[e], in_buf[at]))
        inner = act.astype(low)
        if stored:
            inner_buf[e] = inner
            slope_buf[e] = slope.astype(low)
        g_sent[e] = plain_dot(inner, out_buf[at]).astype(low)
        for n in range(1, levels if micro_count > 1 else 0):
            @pl.when(i == n - 1)
            def _():
                g_line.take(1, n)

        return carry

    lax.fori_loop(0, expert_count, forward_step, 0)

    def mask_at(i):
        return group_count - 1 - i

    load_start(0, mask_at(0), across=square)
    out_total = LineSum(out_ref, o_pair_buf, o_far_buf, o_line_send, o_line_recv, o_two_send, o_two_recv)

    def mix_step(m, n, carry):
        if m:
            @pl.when((n == 0) | (m > 1))
            def _():
                g_line.take(m, n)

        level, _ = line.place(n)
        blocks, here, spots = places(m, level)
        _, spot = columns(m, level)
        table = token_table(spot, expert_count * slots)
        side = side_buf[here, :]
        mix_dense, mix_gate = side[:, 0:1], side[:, 1:2]
        grad_y = g_buf[m, blocks].reshape(tile, features).astype(f32)
        dense = out_ref[m, blocks].reshape(tile, features).astype(f32)
        part = plain_dot(table, jnp.concatenate([g_sent[e, spots, :] for e in range(expert_count)], axis=0))
        out_ref[m, blocks] = (mix_dense * dense + mix_gate * part).astype(low).reshape(2, rows, features)
        d_dense = jnp.sum(grad_y * dense, axis=-1, keepdims=True)
        d_part = jnp.sum(grad_y * part, axis=-1, keepdims=True)
        d_mix = jnp.where(lanes == 0, d_dense, d_part)
        for k in range(2):
            dots[2 * level + k, m] = jnp.transpose(d_mix[k * rows : (k + 1) * rows])[0:8]
        d_pre = tail_dot((mix_dense * grad_y).astype(low), own_out[...]) * pre_buf[here, :].astype(f32)
        d_pre = d_pre.astype(low)
        pre_buf[here, :] = d_pre
        back_buf[m, blocks] = tail_dot(d_pre, own_in[...]).astype(low).reshape(2, rows, features)
        rows_back = lead_dot(table, (mix_gate * grad_y).astype(low)).astype(low)
        for e in range(expert_count):
            g_sent[e, spots, :] = rows_back[e * slots : (e + 1) * slots]
        return carry

    g_load.wait()
    out_keep = pltpu.make_async_copy(out_ref.at[pl.ds(1, micro_count - 1)], out_rest_ref, out_sem.at[2])
    for m in range(micro_count):
        lax.fori_loop(0, levels, partial(mix_step, m), 0)
        if m == 0:
            out_total.start(0)
            out_total.pairs(0)
    out_keep.start()

    def dot_copy(hop):
        target = jnp.bitwise_xor(cut, hop)
        return line_copy(dots.at[target], dots_in.at[hop - 1], dot_send.at[hop - 1], dot_recv.at[hop - 1], group, target)

    for hop in range(1, cut_count):
        dot_copy(hop).start()

    in_stage, out_stage = own_in, own_out

    def keep_in(i):
        return pltpu.make_async_copy(in_stage, d_in_ref.at[jnp.bitwise_xor(group, mask_at(i))], stage_sem.at[0])

    def keep_out(i):
        return pltpu.make_async_copy(out_stage, d_out_ref.at[jnp.bitwise_xor(group, mask_at(i))], stage_sem.at[1])

    def early_copy(k):
        mask, kind, side, at = ((3, 0, 1, 1), (3, 1, 2, 1), (2, 1, 2, 0), (1, 0, 1, 0))[k]
        src, dst = ((d_in_ref, got_in_ref), (d_out_ref, got_out_ref))[kind]
        return line_copy(
            src.at[jnp.bitwise_xor(group, mask)], dst.at[at], early_send.at[k], early_recv.at[k],
            jnp.bitwise_xor(group, side), cut,
        )

    def backward_step(i, carry):
        @pl.when(i + 2 < expert_count)
        def _():
            load_start(i + 1, mask_at(i + 1))

        @pl.when(i + 2 == expert_count)
        def _():
            load_start(i + 1, 0, True)

        load_wait(i)
        e, at = jnp.bitwise_xor(group, mask_at(i)), i % 2
        rows_in, rows_back = sent[e], g_sent[e]
        if stored:
            inner, slope = inner_buf[e], slope_buf[e].astype(f32)
        else:
            act, slope = gelu_pair(plain_dot(rows_in, in_buf[at]))
            inner = act.astype(low)
        d_pre = (tail_dot(rows_back, out_buf[at]) * slope).astype(low)

        @pl.when(i > 0)
        def _():
            keep_in(i).wait()
            keep_out(i).wait()

        if early:
            @pl.when(i == 1)
            def _():
                early_copy(0).start()
                early_copy(1).start()

            @pl.when(i == 2)
            def _():
                early_copy(2).start()

            @pl.when(i == 3)
            def _():
                early_copy(3).start()

        in_stage[...] = lead_dot(rows_in, d_pre).astype(low)
        keep_in(i).start()
        out_stage[...] = lead_dot(inner, rows_back).astype(low)
        keep_out(i).start()
        sent[e] = tail_dot(d_pre, in_buf[at]).astype(low)

        @pl.when(i == 0)
        def _():
            for j in range(levels - 1):
                out_total.hop(0, j)

        return carry

    lax.fori_loop(0, expert_count, backward_step, 0)
    total = LineSum(back_buf, pair_buf, far_buf, line_send, line_recv, two_send, two_recv)

    def combine_step(m, level, carry):
        blocks, here, spots = places(m, level)
        _, spot = columns(m, level)
        table = token_table(spot, expert_count * slots)
        rows_back = jnp.concatenate([sent[e, spots, :] for e in range(expert_count)], axis=0)
        back_rows = plain_dot(table, rows_back).reshape(2, rows, features)
        back_buf[m, blocks] = (back_buf[m, blocks].astype(f32) + back_rows).astype(low)
        return carry

    for m in range(micro_count):
        lax.fori_loop(0, levels, partial(combine_step, m), 0)
        total.start(m)
        total.pairs(m)

    token_rows = micro_count * cut_count * rows
    h_flat, g_flat = h_all.reshape(token_rows, features), g_buf.reshape(token_rows, features)

    def dense_weights(k):
        part = pl.ds(k * 256, 256)
        in_buf[0, part, :] = lead_dot(h_flat[:, part], pre_buf[...]).astype(low)
        out_buf[0, :, part] = lead_dot(hidden_buf[...], g_flat[:, part]).astype(low)

    slices = features // 256
    for k in range(slices // 2):
        dense_weights(k)
    for j in range(levels - 1):
        total.hop(0, j)
    for k in range(slices // 2, slices):
        dense_weights(k)
    own_keep = (
        pltpu.make_async_copy(in_buf.at[0], d_own_in_ref, in_sem.at[0]),
        pltpu.make_async_copy(out_buf.at[0], d_own_out_ref, out_sem.at[0]),
    )
    for keep in own_keep:
        keep.start()
    for m in range(1, micro_count):
        for j in range(levels - 1):
            total.hop(m, j)
    sums = dots[cut]
    for hop in range(1, cut_count):
        dot_copy(hop).wait()
        sums = sums + dots_in[hop - 1]
    sums_ref[...] = sums
    keep_in(0).wait()
    keep_out(0).wait()
    for k in range(4 if early else 0):
        early_copy(k).wait()
    for keep in own_keep:
        keep.wait()
    out_keep.wait()
    for m in range(micro_count):
        line.finish(m)
        if m:
            g_line.finish(m)
    out_total.finish(0, dh_ref)
    output_ref[...] = (x_two_ref[0] + dh_ref[0]).astype(low)
    for m in range(micro_count):
        total.finish(m, dh_ref)


def feed(
    x, att, gy, g_first, w_output, gain, router, mixer, codes, dense_in, dense_out, weights_in, weights_out, expert_in,
    expert_out, share, slots, strided, early, call_id,
):
    micro_count, rows, features = x.shape
    cut_count = codes.shape[0]
    group_count = weights_in.shape[0]
    levels, total = cut_count // 2, micro_count * cut_count * rows
    low, f32 = jnp.bfloat16, jnp.float32
    shape = jax.ShapeDtypeStruct
    dma = pltpu.SemaphoreType.DMA
    block = lambda *dims: pltpu.VMEM(dims, low)
    vmem, far = pl.BlockSpec(memory_space=pltpu.VMEM), pl.BlockSpec(memory_space=pl.ANY)
    whole = (micro_count, cut_count, rows, features)
    stored = group_count <= 4
    slot_rows = micro_count * levels * slots
    line = (micro_count, levels)
    return pl.pallas_call(
        partial(feed_kernel, slots, strided, early, stored),
        out_shape=(
            shape((micro_count, rows, features), f32),
            shape((micro_count, rows, features), low),
            shape((rows, features), low),
            shape((micro_count, rows, features), f32),
            shape((micro_count, 8, rows), f32),
            shape((features, share), low),
            shape((share, features), low),
            shape((group_count, features, share), low),
            shape((group_count, share, features), low),
            shape((share, features) if group_count == 4 else (16, 128), low),
            *(
                (shape((2, features, share), low), shape((2, share, features), low))
                if early else (shape((8, 128), low), shape((8, 128), low))
            ),
            shape((micro_count - 1, cut_count, rows, features), low),
        ),
        in_specs=[vmem, vmem, vmem, far, far, vmem, vmem, vmem, vmem, far, far, far, far, far, far],
        out_specs=[vmem] * 5 + [far] * 8,
        scratch_shapes=[
            block(*whole), block(*whole),
            block(group_count, slot_rows, features), block(group_count, slot_rows, features),
            block(total, share), block(total, share), block(*whole), pltpu.VMEM((total, 128), f32),
            block(features, share), block(share, features), block(2, features, share), block(2, share, features),
            *([block(group_count, slot_rows, share)] * 2 if stored else [block(16, 128)] * 2),
            pltpu.VMEM((cut_count, micro_count, 8, rows), f32), pltpu.VMEM((cut_count - 1, micro_count, 8, rows), f32),
            block(*line, rows, features), block(micro_count, levels + 1, rows, features),
            block(1, levels, rows, features), block(1, levels + 1, rows, features), block(*whole),
            pltpu.VMEM((128, features), f32), block(128, features),
            *[dma((micro_count, levels + 1)), dma(line), dma(line), dma(line)] * 2,
            *[dma(line), dma(line), dma(line), dma((micro_count, levels + 1))] * 2,
            dma((3 + 2 * group_count,)), dma((2,)), dma((3,)), dma((2,)),
            dma((cut_count - 1,)), dma((cut_count - 1,)), dma((2,)), dma((2,)), dma((4,)), dma((4,)),
        ],
        compiler_params=pltpu.CompilerParams(collective_id=call_id, has_side_effects=True, vmem_limit_bytes=62 * 2**20),
    )(x, att, gy, g_first, w_output, gain, router, mixer, codes, dense_in, dense_out, weights_in, weights_out, expert_in, expert_out)


def attend_back_one(heads, m, qkv_ref, docs_ref, docs_col_ref, lse_ref, back_ref, out_ref, key_acc, value_acc):
    length, width = back_ref.shape[1], back_ref.shape[2]
    rows = min(256, length)
    masks = head_masks(width, heads)
    key_acc[...] = jnp.zeros_like(key_acc)
    value_acc[...] = jnp.zeros_like(value_acc)
    zero = jnp.bfloat16(0)
    for block in range(length // rows):
        start, keys = block * rows, (block + 1) * rows
        allowed = allowed_mask(docs_ref, docs_col_ref, m, start, rows, keys)
        query = qkv_ref[m, pl.ds(start, rows), 0:width] * jnp.bfloat16(score_scale)
        key = qkv_ref[m, 0:keys, width : 2 * width]
        value = qkv_ref[m, 0:keys, 2 * width : 3 * width]
        back = back_ref[m, pl.ds(start, rows), :]
        logs = lse_ref[m, pl.ds(start, rows), :]
        query_grad = jnp.zeros((rows, width), jnp.float32)
        for h, mask in enumerate(masks):
            one_query = jnp.where(mask, query, zero)
            one_back = jnp.where(mask, back, zero)
            scores = jnp.where(allowed, tail_dot(one_query, key), masked_value)
            spot = h * (width // heads)
            probs = jnp.exp(scores - logs[:, spot : spot + 1])
            weighted = probs * tail_dot(one_back, value)
            delta = jnp.sum(weighted, axis=-1, keepdims=True)
            score_grad = (weighted - probs * delta).astype(jnp.bfloat16)
            query_grad = jnp.where(mask, plain_dot(score_grad, key), query_grad)
            key_acc[0:keys, :] += lead_dot(score_grad, one_query)
            value_acc[0:keys, :] += lead_dot(probs.astype(jnp.bfloat16), one_back)
        out_ref[m, pl.ds(start, rows), 0:width] = (query_grad * score_scale).astype(jnp.bfloat16)
    out_ref[m, :, width : 2 * width] = key_acc[...].astype(jnp.bfloat16)
    out_ref[m, :, 2 * width : 3 * width] = value_acc[...].astype(jnp.bfloat16)


def back_kernel(
    heads, expert_count, sums_here,
    dh_ref, dots_ref, codes_ref, h_ref, x_two_ref, gy_ref, att_ref, w_out_ref, docs_ref,
    x_ref, gain_one_ref, gain_two_ref, router_ref, mixer_ref, own_in_ref, own_out_ref,
    qkv_far, lse_far, w_qkv_far, h_all_far, out_part, w_query_ref, w_key_ref, w_value_ref, d_in_ref, d_out_ref,
    got_in_ref, got_out_ref,
    output_ref, tokens_ref, wo_ref, tiny_ref, query_out_ref, key_out_ref, value_out_ref, in_out_ref, out_out_ref, late_in_ref,
    late_out_ref,
    qkv_ref, lse_ref, w_qkv_ref, h_all_ref, w_rows, docs_stage, docs_col_ref, small_stage, small_ref, out_own, out_pair,
    out_far, g_att, d_att, back_all, d_qkv, key_acc, value_acc, d_small, part, pair_buf, far_buf, d_h_one, in_sum, out_sum,
    wo_part, qkv_part, wo_in, qkv_in, own_in_in, own_out_in, wo_mid, wo_pair, wo_far, wo_sum, qkv_mid, in_mid, qkv_end, in_end,
    pair_send, pair_recv, far_send, far_recv, swap_send, swap_recv, swap_own, one_send, one_recv, two_send, two_recv, two_own,
    late_send, late_recv, late_load_sem, load_sem,
    wo_pair_send, wo_pair_recv, wo_far_send, wo_far_recv, own_sem, o_pair_send, o_pair_recv, o_far_send, o_far_recv,
):
    micro_count, cut_count, rows, features = part.shape
    group_count, split, piece_rows, _ = wo_part.shape
    group_rows = split * piece_rows
    width = features // cut_count
    cut = lax.axis_index("cuts")
    group = lax.axis_index("expert")
    low, f32 = jnp.bfloat16, jnp.float32
    levels = cut_count // 2
    place = (group * cut_count + cut) * piece_rows
    loads = [
        pltpu.make_async_copy(src, dst, load_sem.at[k])
        for k, (src, dst) in enumerate(
            ((qkv_far, qkv_ref), (lse_far, lse_ref), (w_qkv_far, w_qkv_ref), (h_all_far, h_all_ref))
        )
    ]
    if sums_here:
        own_rows = pl.ds(pl.multiple_of(place, piece_rows), piece_rows)
        for k, ref in enumerate((w_query_ref, w_key_ref, w_value_ref)):
            loads.append(pltpu.make_async_copy(ref.at[own_rows, :], w_rows.at[k], load_sem.at[4 + k]))
    for load in loads:
        load.start()

    rest = micro_count - 1

    def own_load(m, level):
        return pltpu.make_async_copy(out_part.at[m, 2 * level + cut % 2], out_own.at[m, level], own_sem.at[m, level])

    for m in range(rest):
        for level in range(levels):
            own_load(m, level).start()
    stack_small(router_ref, mixer_ref, small_stage, small_ref)
    fill_docs(docs_ref, docs_stage, docs_col_ref)
    greet_all(cut_count, group_count if sums_here else 1)
    out_line = LineSum(out_part, out_pair, out_far, o_pair_send, o_pair_recv, o_far_send, o_far_recv, out_own)

    ones = ((own_in_ref, own_in_in), (own_out_ref, own_out_in), (wo_part, wo_in), (qkv_part, qkv_in))

    def one_copy(kind, hop):
        src, dst = ones[kind]
        target = jnp.bitwise_xor(group, hop)
        return line_copy(
            src.at[target], dst.at[hop - 1], one_send.at[kind, hop - 1], one_recv.at[kind, hop - 1], target, cut
        )

    def one_start(kind):
        for hop in range(1, group_count):
            one_copy(kind, hop).start()

    def one_finish(kind):
        src, dst = ones[kind]
        total = src[group].astype(f32)
        for hop in range(1, group_count):
            one_copy(kind, hop).wait_recv()
            total = total + dst[hop - 1].astype(f32)
        for hop in range(1, group_count):
            one_copy(kind, hop).wait_send()
        return total

    twos = ((in_mid, in_end), None, None, (qkv_mid, qkv_end))

    def two_copy(kind, hop):
        src, dst = twos[kind]
        target = jnp.bitwise_xor(cut, hop)
        return line_copy(src.at[target], dst.at[cut], two_send.at[kind, hop], two_recv.at[kind, hop], group, target)

    def two_keep(kind):
        src, dst = twos[kind]
        return pltpu.make_async_copy(src.at[cut], dst.at[cut], two_own.at[kind])

    def two_start(kind):
        for hop in range(cut_count - 1, 0, -1):
            two_copy(kind, hop).start()
        two_keep(kind).start()

    def two_finish(kind):
        for hop in range(cut_count - 1, 0, -1):
            two_copy(kind, hop).wait()
        two_keep(kind).wait()

    ends = ((d_in_ref, got_in_ref, in_sum, late_in_ref, 2), (d_out_ref, got_out_ref, out_sum, late_out_ref, 1))

    def late_load(kind, k):
        own, got, total, _, side = ends[kind]
        src = got.at[1] if k else own.at[jnp.bitwise_xor(group, side)]
        return pltpu.make_async_copy(src, total.at[k], late_load_sem.at[kind, k])

    def late_copy(kind):
        _, _, total, late, side = ends[kind]
        return line_copy(
            total.at[0], late, late_send.at[kind], late_recv.at[kind], jnp.bitwise_xor(group, side), cut
        )

    if sums_here:
        for kind in range(2):
            late_load(kind, 0).start()
            late_load(kind, 1).start()
        one_start(0)
        one_start(1)

    def swap_copy(m, hop):
        target = jnp.bitwise_xor(cut, hop)
        return line_copy(
            d_att.at[m, :, pl.ds(pl.multiple_of(target * width, width), width)],
            back_all.at[m, pl.ds(pl.multiple_of(cut * rows, rows), rows), :],
            swap_send.at[m, hop], swap_recv.at[m, hop], group, target,
        )

    def swap_keep(m):
        return pltpu.make_async_copy(
            d_att.at[m, :, pl.ds(pl.multiple_of(cut * width, width), width)],
            back_all.at[m, pl.ds(pl.multiple_of(cut * rows, rows), rows), :],
            swap_own.at[m],
        )

    small = small_ref[...]
    gain_one, gain_two = one_row(gain_one_ref), one_row(gain_two_ref)
    d_small[...] = jnp.zeros_like(d_small)
    lanes = lax.broadcasted_iota(jnp.int32, (rows, 128), 1)

    def norm_two_step(m, carry):
        dots = jnp.transpose(dots_ref[m])
        chosen = row_to_column(codes_ref[cut, m])[:, 0:1].astype(jnp.int32)
        h_two = h_ref[m]
        gate, _, mix_expert, routed, mixing = route(tail_dot(h_two, small), chosen, expert_count)
        d_mixing = jnp.where(lanes == expert_count, dots[:, 0:1], gate * dots[:, 1:2])
        d_gate = jnp.where(lanes == chosen, mix_expert * dots[:, 1:2], 0.0)
        d_logits = (softmax_back(mixing, d_mixing) + softmax_back(routed, d_gate)).astype(low)
        d_h = dh_ref[m] + plain_dot(d_logits, small)
        normed, scale = norm_parts(x_two_ref[m])
        one_lane = (lanes == expert_count + 2).astype(low)
        d_small[...] += lead_dot(h_two, d_logits) + lead_dot((d_h * normed).astype(low), one_lane)
        d_x = gy_ref[m].astype(f32) + norm_back(normed, scale, gain_two, d_h)
        tokens_ref[m] = d_x
        grad = d_x.astype(low)
        g_att[pl.ds(pl.multiple_of(m * rows, rows), rows), :] = grad
        d_att[m] = tail_dot(grad, w_out_ref[...]).astype(low)
        for hop in range(cut_count - 1, 0, -1):
            swap_copy(m, hop).start()
        swap_keep(m).start()
        return carry

    lax.fori_loop(0, micro_count, norm_two_step, 0)
    for m in range(rest):
        out_line.start(m)

    def wo_step(g, carry):
        columns = pl.ds(pl.multiple_of(g * group_rows, group_rows), group_rows)
        grads = lead_dot(att_ref[:, columns], g_att[...]).astype(low)
        wo_part[g, :, :, 0:features] = grads.reshape(split, piece_rows, features)
        smalls = d_small[columns, :].astype(low)
        wo_part[g, :, :, features : features + 128] = smalls.reshape(split, piece_rows, 128)
        return carry

    lax.fori_loop(0, group_count, wo_step, 0)
    if sums_here:
        one_start(2)
    for load in loads[:3]:
        load.wait()
    line = LineSum(part, pair_buf, far_buf, pair_send, pair_recv, far_send, far_recv)

    def attend_step(m, carry):
        for hop in range(cut_count - 1, 0, -1):
            swap_copy(m, hop).wait()
        swap_keep(m).wait()

        @pl.when(m == 0)
        def _():
            for k in range(rest):
                for level in range(levels):
                    own_load(k, level).wait()
                out_line.pairs(k)

        attend_back_one(heads, m, qkv_ref, docs_ref, docs_col_ref, lse_ref, back_all, d_qkv, key_acc, value_acc)
        for c in range(cut_count):
            part[m, c] = tail_dot(d_qkv[m, c * rows : (c + 1) * rows, :], w_qkv_ref[...]).astype(low)
        line.start(m)
        line.pairs(m)
        return carry

    lax.fori_loop(0, micro_count, attend_step, 0)

    def qkv_step(g, carry):
        columns = pl.ds(pl.multiple_of(g * group_rows, group_rows), group_rows)
        grads = jnp.zeros((group_rows, 3 * width), f32)
        for m in range(micro_count):
            grads = grads + lead_dot(h_all_ref[m, :, columns], d_qkv[m])
        qkv_part[g] = grads.astype(low).reshape(split, piece_rows, 3 * width)
        return carry

    for m in range(rest):
        for j in range(levels - 1):
            out_line.hop(m, j)
    for j in range(levels - 1):
        line.hop(0, j)
    for load in loads[3:]:
        load.wait()
    lax.fori_loop(0, group_count, qkv_step, 0)
    if sums_here:
        one_start(3)
        for kind in range(2):
            total = ends[kind][2]
            late_load(kind, 0).wait()
            late_load(kind, 1).wait()
            total[0] = (total[0].astype(f32) + total[1].astype(f32)).astype(low)
            late_copy(kind).start()
    for m in range(1, micro_count):
        for j in range(levels - 1):
            line.hop(m, j)

    def norm_one_step(m, carry):
        line.finish(m, d_h_one)
        total = d_h_one[m]
        normed, scale = norm_parts(x_ref[m].astype(f32))
        tokens_ref[m] = tokens_ref[m] + norm_back(normed, scale, gain_one, total)
        return carry

    for m in range(rest):
        out_line.finish(m, d_h_one)
        output_ref[m] = (x_two_ref[1 + m] + d_h_one[m]).astype(low)
    if not sums_here:
        lax.fori_loop(0, micro_count, norm_one_step, 0)
        wo_ref[...] = wo_part[...]
        query_out_ref[...] = qkv_part[...]
        return
    in_mid[...] = one_finish(0).astype(low)
    two_start(0)
    wo_line = LineSum(wo_mid, wo_pair, wo_far, wo_pair_send, wo_pair_recv, wo_far_send, wo_far_recv)
    wo_mid[0] = one_finish(2).astype(low)
    wo_line.start(0)
    wo_line.pairs(0)
    norm_one_step(0, 0)
    qkv_mid[...] = one_finish(3).astype(low)
    two_start(3)
    out_out_ref[...] = one_finish(1)
    for j in range(levels - 1):
        wo_line.hop(0, j)
    for m in range(1, micro_count):
        norm_one_step(m, 0)
    two_finish(0)
    share_piece = in_end.shape[2] // group_count
    for c in range(cut_count):
        for g in range(group_count):
            spot = (g * cut_count + c) * share_piece
            in_out_ref[:, spot : spot + share_piece] = in_end[c, :, g * share_piece : (g + 1) * share_piece].astype(f32)
    wo_line.finish(0, wo_sum)
    wo_ref[...] = wo_sum[0, :, :features]
    small_sums = wo_sum[0, :, features:]
    two_finish(3)
    norm = jnp.zeros((piece_rows, 1), f32)
    outs = (query_out_ref, key_out_ref, value_out_ref)
    for c in range(cut_count):
        for k in range(3):
            grad = qkv_end[c, :, k * width : (k + 1) * width].astype(f32)
            outs[k][:, c * width : (c + 1) * width] = grad
            weights = w_rows[k, :, c * width : (c + 1) * width].astype(f32)
            norm = norm + jnp.sum(grad * weights, axis=-1, keepdims=True)
    spots = lax.broadcasted_iota(jnp.int32, (piece_rows, features), 1)
    mine = spots == place + lax.broadcasted_iota(jnp.int32, (piece_rows, features), 0)
    norm = norm / jnp.sum(jnp.where(mine, gain_one, 0.0), axis=-1, keepdims=True)
    tiny_lanes = lax.broadcasted_iota(jnp.int32, (piece_rows, 128), 1)
    tiny_ref[...] = jnp.where(tiny_lanes == expert_count + 3, norm, small_sums)
    for kind in range(2):
        late_copy(kind).wait()


def back(
    dh, dots, codes, h_two, x_two, gy, attended, w_output, docs, x, gain_one, gain_two, router, mixer, own_in, own_out,
    qkv, lse, w_qkv, h_all, out_rest, w_query, w_key, w_value, d_in, d_out, got_in, got_out, heads, expert_count, sums_here,
    call_id,
):
    micro_count, rows, features = x.shape
    length = qkv.shape[1]
    cut_count = length // rows
    width = features // cut_count
    group_count = own_out.shape[0]
    piece_rows = features // (group_count * cut_count)
    share, piece = own_in.shape[3], own_out.shape[1]
    low, f32 = jnp.bfloat16, jnp.float32
    levels = cut_count // 2
    wide = features + 128
    shape = jax.ShapeDtypeStruct
    parts = (group_count, cut_count, piece_rows) if sums_here else (features // 256, 1, 256)
    tokens = (micro_count, rows, features)
    none = shape((16, 128), low)
    if sums_here:
        outs = (
            shape((micro_count - 1, rows, features), low),
            shape(tokens, f32), shape((piece_rows, features), f32), shape((piece_rows, 128), f32),
            *[shape((piece_rows, features), f32)] * 3, shape((piece_rows, share * cut_count), f32),
            shape((piece, features), f32), shape((features, share), low), shape((share, features), low),
        )
    else:
        outs = (
            shape((micro_count - 1, rows, features), low),
            shape(tokens, f32), shape((*parts, wide), low), none, shape((*parts, 3 * width), low),
            *[none] * 6,
        )
    peers = max(group_count - 1, 1) if sums_here else 1
    block = lambda *dims: pltpu.VMEM(dims, low)
    mids = lambda w: block(cut_count, piece_rows, w) if sums_here else block(16, 128)
    ins = lambda w: block(peers, cut_count, piece_rows, w) if sums_here else block(16, 128)
    dma = pltpu.SemaphoreType.DMA
    line = (micro_count, levels)
    vmem, far = pl.BlockSpec(memory_space=pltpu.VMEM), pl.BlockSpec(memory_space=pl.ANY)
    operands = (
        dh, dots, codes, h_two, x_two, gy, attended, w_output, docs, x, gain_one, gain_two, router, mixer, own_in, own_out,
        qkv, lse, w_qkv, h_all, out_rest, w_query, w_key, w_value, d_in, d_out, got_in, got_out,
    )
    rest = (micro_count - 1, levels)
    return pl.pallas_call(
        partial(back_kernel, heads, expert_count, sums_here),
        out_shape=outs,
        in_specs=[vmem] * 16 + [far] * 12,
        out_specs=[vmem] * 9 + [far] * 2,
        scratch_shapes=[
            block(micro_count, length, 3 * width), pltpu.VMEM((micro_count, length, width), f32), block(features, 3 * width),
            block(micro_count, length, features), block(3, piece_rows, features), pltpu.VMEM((8, length), f32),
            pltpu.VMEM((micro_count, length, 1), jnp.int32), pltpu.VMEM((128, features), f32), block(128, features),
            block(*rest, rows, features), block(*rest, rows, features), block(micro_count - 1, levels + 1, rows, features),
            block(micro_count * rows, features),
            block(micro_count, rows, features),
            block(micro_count, length, width),
            block(micro_count, length, 3 * width),
            pltpu.VMEM((length, width), f32),
            pltpu.VMEM((length, width), f32),
            pltpu.VMEM((features, 128), f32),
            block(micro_count, cut_count, rows, features),
            block(*line, rows, features),
            block(micro_count, levels + 1, rows, features),
            pltpu.VMEM(tokens, f32),
            *((block(2, features, share), block(2, share, features)) if sums_here else (block(16, 128), block(16, 128))),
            block(*parts, wide),
            block(*parts, 3 * width),
            ins(wide), ins(3 * width), ins(share),
            block(peers, piece, features) if sums_here else block(16, 128),
            *(
                (
                    block(1, cut_count, piece_rows, wide), block(1, levels, piece_rows, wide),
                    block(1, levels + 1, piece_rows, wide), pltpu.VMEM((1, piece_rows, wide), f32),
                )
                if sums_here else [block(16, 128)] * 4
            ),
            mids(3 * width), mids(share), mids(3 * width), mids(share),
            dma(line), dma(line), dma(line), dma((micro_count, levels + 1)),
            dma((micro_count, cut_count)), dma((micro_count, cut_count)), dma((micro_count,)),
            dma((4, peers)), dma((4, peers)), dma((4, cut_count)), dma((4, cut_count)), dma((4,)),
            dma((2,)), dma((2,)), dma((2, 2)), dma((7,)),
            dma((1, levels)), dma((1, levels)), dma((1, levels)), dma((1, levels + 1)),
            dma(rest), dma(rest), dma(rest), dma(rest), dma((micro_count - 1, levels + 1)),
        ],
        compiler_params=pltpu.CompilerParams(
            collective_id=call_id, has_side_effects=True, vmem_limit_bytes=62 * 2**20
        ),
    )(*operands)


def last_kernel(
    expert_count, d_in_ref, got_in_ref, late_in_ref, d_out_ref, got_out_ref, late_out_ref, tiny_ref, *refs,
):
    passed = (len(refs) - 6 - 10 - 1) // 3
    given, refs = refs[: passed + 1], refs[passed + 1 :]
    taken, refs = refs[:passed], refs[passed:]
    held, refs = refs[-passed:], refs[:-passed]
    router_ref, mixer_ref, norm_one_ref, norm_two_ref, sum_in_ref, sum_out_ref = refs[:6]
    in_buf, out_buf, in_sum, out_sum, in_sem, out_sem, in_done, out_done, pass_sem, keep_sem = refs[6:]
    group = lax.axis_index("expert")
    held_parts = (held[0].at[0], held[0].at[pl.ds(1, held[0].shape[0] - 1)], *held[1:])
    passes = [pltpu.make_async_copy(src, dst, pass_sem.at[k]) for k, (src, dst) in enumerate(zip(given, held_parts))]
    keeps = [pltpu.make_async_copy(src, dst, keep_sem.at[k]) for k, (src, dst) in enumerate(zip(held, taken))]
    chunks = in_sem.shape[0]
    work = []
    for ends in (
        ((d_in_ref.at[group], got_in_ref.at[0], late_in_ref), in_buf, in_sum, sum_in_ref, in_sem, in_done),
        ((d_out_ref.at[group], got_out_ref.at[0], late_out_ref), out_buf, out_sum, sum_out_ref, out_sem, out_done),
    ):
        sources, buf, total, target, sem, done = ends
        step = buf.shape[1] // chunks
        for k in range(chunks):
            part = pl.ds(k * step, step)
            loads = [
                pltpu.make_async_copy(src.at[part, :], buf.at[at, part, :], sem.at[k, at]) for at, src in enumerate(sources)
            ]
            work.append((loads, buf, total, part, pltpu.make_async_copy(total.at[part, :], target.at[part, :], done.at[k])))
    for copy in passes:
        copy.start()
    for loads, *_ in work:
        for load in loads:
            load.start()
    turned = jnp.transpose(tiny_ref[...])
    router_ref[...] = turned[0:expert_count]
    mixer_ref[...] = turned[expert_count : expert_count + 2]
    norm_two_ref[...] = turned[expert_count + 2 : expert_count + 3]
    norm_one_ref[...] = turned[expert_count + 3 : expert_count + 4]
    passes[0].wait()
    for copy, keep in zip(passes[1:], keeps):
        copy.wait()
        keep.start()
    for loads, buf, total, part, keep in work:
        for load in loads:
            load.wait()
        total[part, :] = sum(buf[at, part, :].astype(jnp.float32) for at in range(3))
        keep.start()
    for *_, keep in work:
        keep.wait()
    for keep in keeps:
        keep.wait()


def last(d_in, got_in, late_in, d_out, got_out, late_out, tiny, others, expert_count):
    f32, dma = jnp.float32, pltpu.SemaphoreType.DMA
    shape = jax.ShapeDtypeStruct
    piece_rows = tiny.shape[0]
    micro_count = 1 + others[1].shape[0]
    whole = [shape((micro_count, *others[0].shape), others[0].dtype), *[shape(x.shape, x.dtype) for x in others[2:]]]
    vmem, far = pl.BlockSpec(memory_space=pltpu.VMEM), pl.BlockSpec(memory_space=pl.ANY)
    chunks = 4
    return pl.pallas_call(
        partial(last_kernel, expert_count),
        out_shape=(
            *whole, shape((expert_count, piece_rows), f32), shape((2, piece_rows), f32),
            shape((1, piece_rows), f32), shape((1, piece_rows), f32), shape(late_in.shape, f32), shape(late_out.shape, f32),
        ),
        in_specs=[far] * 6 + [vmem] + [far] * len(others),
        out_specs=[far] * len(whole) + [vmem] * 4 + [far] * 2,
        scratch_shapes=[
            pltpu.VMEM((3, *late_in.shape), late_in.dtype), pltpu.VMEM((3, *late_out.shape), late_out.dtype),
            pltpu.VMEM(late_in.shape, f32), pltpu.VMEM(late_out.shape, f32),
            dma((chunks, 3)), dma((chunks, 3)), dma((chunks,)), dma((chunks,)), dma((len(others),)), dma((len(others),)),
            *[pltpu.VMEM(x.shape, x.dtype) for x in whole],
        ],
        compiler_params=pltpu.CompilerParams(vmem_limit_bytes=62 * 2**20),
    )(d_in, got_in, late_in, d_out, got_out, late_out, tiny, *others)


def local(
    tokens, cotangent, segments, expert_ids, slot_ids, kept_mask, norm1_gain, w_query, w_key, w_value, w_output,
    norm2_gain, dense_in, dense_out, router, mixer, expert_in, expert_out,
):
    micro_count, row_count, features = tokens.shape[1:]
    cut_count = lax.axis_size("cuts")
    group_count = lax.axis_size("expert")
    cut = lax.axis_index("cuts")
    group = lax.axis_index("expert")
    length = cut_count * row_count
    head_width = features // cut_count
    heads = head_width // 64
    expert_count = router.shape[1]
    hidden_count = dense_in.shape[1]
    share = hidden_count // cut_count
    piece = share // group_count
    capacity = max(2, row_count * 5 // (4 * expert_count))
    slots = tile_slots(capacity, row_count, 2 * row_count)
    rows = features // (group_count * cut_count)
    sums_here = rows % 16 == 0 and group_count == 4
    by_rows = lambda v: v.reshape(-1, 128)
    router_t, mixer_t = router.T, mixer.T
    f32, low = jnp.float32, jnp.bfloat16

    strided = piece % 128 == 0
    if strided:
        own_in, own_out = dense_in, dense_out
    else:
        own_in = lax.dynamic_index_in_dim(
            dense_in.reshape(features, group_count, cut_count, piece), cut, 2, keepdims=False
        ).reshape(features, share)
        own_out = lax.dynamic_index_in_dim(
            dense_out.reshape(group_count, cut_count, piece, features), cut, 1, keepdims=False
        ).reshape(share, features)
    h_all, qkv, lse, attended, w_qkv, codes, weights_in, weights_out, g_first = front(
        tokens[0], cotangent[0, 0], by_rows(norm1_gain), w_query, w_key, w_value, segments[0], expert_ids[0], slot_ids[0],
        kept_mask[0], expert_in[0], expert_out[0], group_count, cut_count, heads, capacity, slots, 1,
    )
    x_two, h_two, first_output, d_h2, dots, d_own_in, d_own_out, d_in, d_out, _, got_in, got_out, out_rest = feed(
        tokens[0], attended, cotangent[0], g_first, w_output, by_rows(norm2_gain), router_t, mixer_t, codes, own_in, own_out, weights_in,
        weights_out, expert_in[0], expert_out[0], share, slots, strided, sums_here, 2,
    )
    rest_output, grad_tokens, grad_output, tiny, grad_query, grad_key, grad_value, grad_dense_in, grad_dense_out, late_in, late_out = back(
        d_h2, dots, codes, h_two, x_two, cotangent[0], attended.reshape(-1, features), w_output, segments[0], tokens[0],
        by_rows(norm1_gain), by_rows(norm2_gain), router_t, mixer_t, d_own_in.reshape(group_count, cut_count, rows, share),
        d_own_out.reshape(group_count, piece, features), qkv, lse, w_qkv, h_all.reshape(micro_count, length, features),
        out_rest, w_query, w_key, w_value, d_in, d_out, got_in, got_out, heads, expert_count, sums_here, 3,
    )
    sum_groups = lambda part: lax.psum_scatter(
        part.reshape(-1, part.shape[-1]), "expert", scatter_dimension=0, tiled=True
    )
    if sums_here:
        others = (
            first_output, rest_output, grad_tokens, grad_query, grad_key, grad_value, grad_output, grad_dense_in, grad_dense_out
        )
        *others, grad_router, grad_mixer, grad_norm1, grad_norm2, grad_expert_in, grad_expert_out = last(
            d_in, got_in, late_in, d_out, got_out, late_out, tiny, others, expert_count
        )
        output, grad_tokens, grad_query, grad_key, grad_value, grad_output, grad_dense_in, grad_dense_out = others
        grad_router, grad_mixer, grad_norm1, grad_norm2 = grad_router.T, grad_mixer.T, grad_norm1[0], grad_norm2[0]
    else:
        swap = lambda part: lax.all_to_all(
            part.reshape(cut_count, rows, -1), "cuts", split_axis=0, concat_axis=0
        ).astype(f32)
        output = jnp.concatenate([first_output[None], rest_output])
        wide = jnp.sum(swap(sum_groups(grad_output)), axis=0)
        grad_output, grad_small = wide[:, :features], wide[:, features:]
        grad_router, grad_mixer = grad_small[:, :expert_count], grad_small[:, expert_count : expert_count + 2]
        grad_norm2 = grad_small[:, expert_count + 2]
        grad_qkv = swap(sum_groups(grad_query)).reshape(cut_count, rows, 3, head_width).transpose(2, 1, 0, 3)
        grad_qkv = grad_qkv.reshape(3, rows, features)
        grad_query, grad_key, grad_value = grad_qkv
        grad_dense_in = swap(sum_groups(d_own_in)).reshape(cut_count, rows, group_count, piece).transpose(1, 2, 0, 3)
        grad_dense_in = grad_dense_in.reshape(rows, hidden_count)
        grad_dense_out = sum_groups(d_own_out).astype(f32)
        grad_expert_in = sum_groups(d_in).astype(f32)
        grad_expert_out = sum_groups(d_out).astype(f32)
        place = (group * cut_count + cut) * rows
        own_rows = lambda w: lax.dynamic_slice_in_dim(w, place, rows, 0).astype(f32)
        grad_norm1 = sum(
            jnp.sum(own_rows(w) * grad_qkv[k], axis=-1) for k, w in enumerate((w_query, w_key, w_value))
        ) / own_rows(norm1_gain)
    return (
        output[None], grad_tokens[None], grad_norm1, grad_query, grad_key, grad_value, grad_output, grad_norm2, grad_dense_in,
        grad_dense_out, grad_router, grad_mixer, grad_expert_in[None], grad_expert_out[None],
    )


def solution(mesh):
    in_specs = (
        P("expert", None, "cuts", None),
        P("expert", None, "cuts", None),
        P("expert", None, None),
        P("expert", None, "cuts"),
        P("expert", None, "cuts"),
        P("expert", None, "cuts"),
        P(),
        P(),
        P(),
        P(),
        P(),
        P(),
        P(),
        P(),
        P(),
        P(),
        P("expert", None, "cuts"),
        P("expert", "cuts", None),
    )
    out_specs = (
        P("expert", None, "cuts", None),
        P("expert", None, "cuts", None),
        P(("expert", "cuts")),
        P(("expert", "cuts"), None),
        P(("expert", "cuts"), None),
        P(("expert", "cuts"), None),
        P(("expert", "cuts"), None),
        P(("expert", "cuts")),
        P(("expert", "cuts"), None),
        P(("expert", "cuts"), None),
        P(("expert", "cuts"), None),
        P(("expert", "cuts"), None),
        P("expert", None, "cuts"),
        P("expert", "cuts", None),
    )
    return jax.shard_map(local, mesh=mesh, in_specs=in_specs, out_specs=out_specs, check_vma=False)
```

```python
from functools import partial

import jax
import jax.numpy as jnp
from jax import lax
from jax.experimental import pallas as pl
from jax.experimental.pallas import tpu as pltpu
from jax.sharding import PartitionSpec as P

MESH = pl.DeviceIdType.MESH
score_scale = 0.125
masked_value = -1e30
norm_eps = 1e-05


def plain_dot(left, right):
    return jnp.dot(left, right, preferred_element_type=jnp.float32)


def lead_dot(left, right):
    return lax.dot_general(
        left, right, (((0,), (0,)), ((), ())), preferred_element_type=jnp.float32
    )


def tail_dot(left, right):
    return lax.dot_general(
        left, right, (((1,), (1,)), ((), ())), preferred_element_type=jnp.float32
    )


def head_masks(width, heads):
    lane = lax.broadcasted_iota(jnp.int32, (1, width), 1)
    size = width // heads
    return [((lane >= h * size) & (lane < (h + 1) * size)) for h in range(heads)]


def allowed_mask(docs_ref, docs_col_ref, m, start, rows, keys):
    query_spots = start + lax.broadcasted_iota(jnp.int32, (rows, keys), 0)
    key_spots = lax.broadcasted_iota(jnp.int32, (rows, keys), 1)
    return (key_spots <= query_spots) & (docs_ref[pl.ds(m, 1), 0:keys] == docs_col_ref[m, pl.ds(start, rows), :])


def attend_one(heads, m, qkv_ref, docs_ref, docs_col_ref, att_ref, lse_ref):
    length, width = att_ref.shape[1], att_ref.shape[2]
    rows = min(256, length)
    masks = head_masks(width, heads)
    for block in range(length // rows):
        start, keys = block * rows, (block + 1) * rows
        allowed = allowed_mask(docs_ref, docs_col_ref, m, start, rows, keys)
        query = qkv_ref[m, pl.ds(start, rows), 0:width] * jnp.bfloat16(score_scale)
        key = qkv_ref[m, 0:keys, width : 2 * width]
        value = qkv_ref[m, 0:keys, 2 * width : 3 * width]
        att = jnp.zeros((rows, width), jnp.float32)
        logs = jnp.zeros((rows, width), jnp.float32)
        for mask in masks:
            scores = tail_dot(jnp.where(mask, query, jnp.bfloat16(0)), key)
            scores = jnp.where(allowed, scores, masked_value)
            top = jnp.max(scores, axis=-1, keepdims=True)
            raised = jnp.exp(scores - top)
            total = jnp.sum(raised, axis=-1, keepdims=True)
            probs = (raised * (1.0 / total)).astype(jnp.bfloat16)
            att = jnp.where(mask, plain_dot(probs, value), att)
            logs = jnp.where(mask, top + jnp.log(total), logs)
        att_ref[m, pl.ds(start, rows), :] = att.astype(jnp.bfloat16)
        lse_ref[m, pl.ds(start, rows), :] = logs


def norm_parts(values):
    center = values - jnp.mean(values, axis=-1, keepdims=True)
    spread = jnp.mean(center * center, axis=-1, keepdims=True)
    scale = lax.rsqrt(spread + norm_eps)
    return center * scale, scale


def norm_back(normed, scale, gain, grad):
    inner = grad * gain
    return scale * (
        inner
        - jnp.mean(inner, axis=-1, keepdims=True)
        - normed * jnp.mean(inner * normed, axis=-1, keepdims=True)
    )


def gelu_pair(values):
    phi = 0.5 * (1.0 + lax.erf(values * (0.5**0.5)))
    bell = jnp.exp(-0.5 * values * values) * ((2.0 * jnp.pi) ** -0.5)
    return values * phi, phi + values * bell


def tile_slots(capacity, row_count, tile):
    return -(-capacity * (tile // row_count) // 16) * 16


def token_table(spot, width):
    return (spot == lax.broadcasted_iota(jnp.int32, (spot.shape[0], width), 1)).astype(jnp.bfloat16)


def lane_softmax(logits, lanes, first, count):
    inside = (lanes >= first) & (lanes < first + count)
    raised = jnp.exp(logits - jnp.max(jnp.where(inside, logits, masked_value), axis=-1, keepdims=True))
    raised = jnp.where(inside, raised, 0.0)
    return raised / jnp.sum(raised, axis=-1, keepdims=True)


def route(logits, chosen, expert_count):
    lanes = lax.broadcasted_iota(jnp.int32, logits.shape, 1)
    routed = lane_softmax(logits, lanes, 0, expert_count)
    mixing = lane_softmax(logits, lanes, expert_count, 2)
    pick = lambda values, lane: jnp.sum(jnp.where(lanes == lane, values, 0.0), axis=-1, keepdims=True)
    return pick(routed, chosen), pick(mixing, expert_count), pick(mixing, expert_count + 1), routed, mixing


def softmax_back(probs, grad):
    return probs * (grad - jnp.sum(probs * grad, axis=-1, keepdims=True))


def line_copy(src, dst, send, recv, group, target):
    return pltpu.make_async_remote_copy(
        src_ref=src, dst_ref=dst, send_sem=send, recv_sem=recv, device_id=(group, target), device_id_type=MESH
    )


def greet_all(cut_count, group_count):
    cut = lax.axis_index("cuts")
    group = lax.axis_index("expert")
    barrier = pltpu.get_barrier_semaphore()
    for hop in range(1, cut_count):
        pl.semaphore_signal(barrier, inc=1, device_id=(group, jnp.bitwise_xor(cut, hop)), device_id_type=MESH)
    for hop in range(1, group_count):
        pl.semaphore_signal(barrier, inc=1, device_id=(jnp.bitwise_xor(group, hop), cut), device_id_type=MESH)
    pl.semaphore_wait(barrier, cut_count + group_count - 2)


class LineGather:
    def __init__(self, buf, far_send, far_recv, pair_send, pair_recv, direct=False):
        self.direct = direct
        self.buf = buf
        self.sems = (far_send, far_recv, pair_send, pair_recv)
        self.cut = lax.axis_index("cuts")
        self.group = lax.axis_index("expert")
        self.level, self.side = self.cut // 2, self.cut % 2
        self.levels = buf.shape[1] // 2

    def place(self, n):
        low, high = self.level, self.levels - 1 - self.level
        near = jnp.minimum(low, high)
        paired = n <= 2 * near
        distance = jnp.where(paired, (n + 1) // 2, n - near)
        below = jnp.where(paired, n % 2 == 1, low > high)
        return jnp.where(below, self.level - distance, self.level + distance), below

    def far_copy(self, m, level, target, send):
        block = self.buf.at[m, 2 * level + self.side]
        return line_copy(block, block, self.sems[0].at[m, send], self.sems[1].at[m, level], self.group, target)

    def pair_copy(self, m, level, side):
        block = self.buf.at[m, 2 * level + side]
        return line_copy(
            block, block, self.sems[2].at[m, level], self.sems[3].at[m, level], self.group, jnp.bitwise_xor(self.cut, 1)
        )

    def straight_copy(self, m, n):
        level, _ = self.place(n)
        return self.far_copy(m, self.level, 2 * level + self.side, level)

    def start(self, m):
        if self.direct:
            for n in range(1, self.levels):
                self.straight_copy(m, n).start()
        else:
            @pl.when(self.level + 1 < self.levels)
            def _():
                self.far_copy(m, self.level, self.cut + 2, self.level).start()

            @pl.when(self.level > 0)
            def _():
                self.far_copy(m, self.level, self.cut - 2, self.levels).start()

        self.pair_copy(m, self.level, self.side).start()

    def receive(self, m, n):
        level, _ = self.place(n)
        self.far_copy(m, level, self.cut, level).wait_recv()
        self.pair_copy(m, level, self.side).start()

    def take_pair(self, m, n):
        level, _ = self.place(n)
        self.pair_copy(m, level, 1 - self.side).wait_recv()

    def take(self, m, n):
        level, below = self.place(n)

        @pl.when(n > 0)
        def _():
            target = jnp.where(below, self.cut + 2, self.cut - 2)
            self.far_copy(m, level, target, level).wait_recv()

            @pl.when(jnp.where(below, self.level + 1 < self.levels, self.level > 0))
            def _():
                self.far_copy(m, level, target, level).start()

            self.pair_copy(m, level, self.side).start()

        self.pair_copy(m, level, 1 - self.side).wait_recv()
        return level

    def finish(self, m):
        if self.direct:
            self.pair_copy(m, self.level, self.side).wait_send()
            for n in range(1, self.levels):
                level, _ = self.place(n)
                self.straight_copy(m, n).wait_send()
                self.pair_copy(m, level, self.side).wait_send()
            return

        @pl.when(self.level + 1 < self.levels)
        def _():
            self.far_copy(m, self.level, self.cut + 2, self.level).wait_send()

        @pl.when(self.level > 0)
        def _():
            self.far_copy(m, self.level, self.cut - 2, self.levels).wait_send()

        for n in range(self.levels):
            level, below = self.place(n)
            if n:
                @pl.when(jnp.where(below, self.level + 1 < self.levels, self.level > 0))
                def _():
                    self.far_copy(m, level, self.cut, level).wait_send()

            self.pair_copy(m, level, self.side).wait_send()


class LineSum:
    def __init__(self, part, pair_buf, far_buf, pair_send, pair_recv, send, recv, own=None, direct=False):
        self.direct = direct
        self.part, self.pair_buf, self.far_buf, self.own = part, pair_buf, far_buf, own
        self.sems = (pair_send, pair_recv, send, recv)
        self.cut = lax.axis_index("cuts")
        self.group = lax.axis_index("expert")
        self.level, self.side = self.cut // 2, self.cut % 2
        self.levels = pair_buf.shape[1]

    def pair_copy(self, m, level):
        return line_copy(
            self.part.at[m, 2 * level + 1 - self.side], self.pair_buf.at[m, level], self.sems[0].at[m, level],
            self.sems[1].at[m, level], self.group, jnp.bitwise_xor(self.cut, 1),
        )

    def far_copy(self, m, level, up):
        target = self.cut + 2 if up else self.cut - 2
        slot = level if up else jnp.where(level == self.level - 1, self.levels, level)
        return line_copy(
            self.pair_buf.at[m, level], self.far_buf.at[m, slot], self.sems[2].at[m, level], self.sems[3].at[m, slot],
            self.group, target,
        )

    def arrived(self, m, slot):
        line_copy(
            self.far_buf.at[m, slot], self.far_buf.at[m, slot], self.sems[2].at[m, 0], self.sems[3].at[m, slot],
            self.group, self.cut,
        ).wait_recv()
        return self.far_buf[m, slot].astype(jnp.float32)

    def start(self, m):
        def one(k, carry):
            self.pair_copy(m, jnp.where(k % 2 == 0, self.levels - 1 - k // 2, k // 2)).start()
            return carry

        lax.fori_loop(0, self.levels, one, 0)

    def pairs(self, m):
        def one(k, carry):
            level = jnp.where(k % 2 == 0, self.levels - 1 - k // 2, k // 2)
            self.pair_copy(m, level).wait_recv()
            mine = self.part[m, 2 * level + self.side] if self.own is None else self.own[m, level]
            total = mine.astype(jnp.float32) + self.pair_buf[m, level].astype(jnp.float32)
            self.pair_buf[m, level] = total.astype(self.pair_buf.dtype)
            self.first(m, level)
            return carry

        lax.fori_loop(0, self.levels, one, 0)

    def straight_copy(self, m, level):
        return line_copy(
            self.pair_buf.at[m, level], self.far_buf.at[m, self.level], self.sems[2].at[m, level],
            self.sems[3].at[m, self.level], self.group, 2 * level + self.side,
        )

    def first(self, m, level):
        if self.direct:
            @pl.when(level != self.level)
            def _():
                self.straight_copy(m, level).start()

            return

        @pl.when((self.level == 0) & (level > 0))
        def _():
            self.far_copy(m, level, True).start()

        @pl.when((self.level == self.levels - 1) & (level < self.levels - 1))
        def _():
            self.far_copy(m, level, False).start()

    def pass_on(self, m, level, up):
        @pl.when((level > self.level) if up else (level < self.level))
        def _():
            total = self.pair_buf[m, level].astype(jnp.float32) + self.arrived(m, level)
            self.pair_buf[m, level] = total.astype(self.pair_buf.dtype)
            self.far_copy(m, level, up).start()

    def hop(self, m, j):
        inner = (self.level > 0) & (self.level < self.levels - 1)
        lower = 2 * self.level < self.levels

        @pl.when(inner & lower)
        def _():
            self.pass_on(m, self.levels - 1 - j, True)
            self.pass_on(m, j, False)

        @pl.when(inner & jnp.logical_not(lower))
        def _():
            self.pass_on(m, j, False)
            self.pass_on(m, self.levels - 1 - j, True)

    def finish(self, m, out_ref):
        if self.direct:
            total = self.pair_buf[m, self.level].astype(jnp.float32)
            for k in range(1, self.levels):
                total = total + self.arrived(m, jnp.bitwise_xor(self.level, k))
            out_ref[m] = total
            for k in range(1, self.levels):
                self.straight_copy(m, jnp.bitwise_xor(self.level, k)).wait_send()
            for level in range(self.levels):
                self.pair_copy(m, level).wait_send()
            return

        out_ref[m] = self.pair_buf[m, self.level].astype(jnp.float32)

        @pl.when(self.level > 0)
        def _():
            out_ref[m] = out_ref[m] + self.arrived(m, self.level)

        @pl.when(self.level < self.levels - 1)
        def _():
            out_ref[m] = out_ref[m] + self.arrived(m, self.levels)

        def one(level, carry):
            if self.part is not None:
                self.pair_copy(m, level).wait_send()

            @pl.when(level > self.level)
            def _():
                self.far_copy(m, level, True).wait_send()

            @pl.when(level < self.level)
            def _():
                self.far_copy(m, level, False).wait_send()

            return carry

        lax.fori_loop(0, self.levels, one, 0)


def row_to_column(values):
    return jnp.transpose(values.astype(jnp.float32))


def one_row(ref):
    values = ref[...].astype(jnp.float32)
    return jnp.concatenate([values[k : k + 1] for k in range(values.shape[0])], axis=1)


def stack_small(router_ref, mixer_ref, stage, small):
    count = router_ref.shape[0]
    stage[...] = jnp.zeros_like(stage)
    stage[0:count] = router_ref[...].astype(jnp.float32)
    stage[count : count + 2] = mixer_ref[...].astype(jnp.float32)
    small[...] = stage[...].astype(small.dtype)


def fill_docs(docs_ref, stage, docs_col):
    stage[...] = jnp.zeros_like(stage)
    micro_count = docs_ref.shape[0]
    stage[0:micro_count] = docs_ref[...].astype(jnp.float32)
    for k in range(stage.shape[1] // 128):
        turned = jnp.transpose(stage[:, k * 128 : (k + 1) * 128]).astype(jnp.int32)
        for m in range(micro_count):
            docs_col[m, k * 128 : (k + 1) * 128, :] = turned[:, m : m + 1]


def front_kernel(
    heads, capacity, slots,
    x_ref, gy_ref, gain_ref, w_query_ref, w_key_ref, w_value_ref, docs_ref, ids_ref, slot_ref, kept_ref, expert_in_ref,
    expert_out_ref,
    h_out_ref, qkv_out_ref, lse_out_ref, att_ref, w_qkv_ref, codes_ref, weights_ref, weights_out_ref, g_all_ref,
    h_all_ref, qkv_ref, lse_ref, docs_stage, docs_col_ref, att_part, own_code, far_send, far_recv, pair_send, pair_recv, load_sem, swap_send, swap_recv, swap_own, code_send,
    code_recv, weight_send, weight_recv, pass_send, pass_recv, keep_sem,
    g_far_send, g_far_recv, g_pair_send, g_pair_recv, g_own,
):
    micro_count, cut_count, rows, features = h_all_ref.shape
    group_count = weights_ref.shape[0]
    width = features // cut_count
    cut = lax.axis_index("cuts")
    group = lax.axis_index("expert")
    low = jnp.bfloat16
    loads = []
    for k, ref in enumerate((w_query_ref, w_key_ref, w_value_ref)):
        loads.append(pltpu.make_async_copy(
            ref.at[:, pl.ds(pl.multiple_of(cut * width, width), width)], w_qkv_ref.at[:, k * width : (k + 1) * width],
            load_sem.at[k],
        ))
        loads[-1].start()
    g_keep = pltpu.make_async_copy(gy_ref, g_all_ref.at[0, cut], g_own)
    g_keep.start()
    gain = one_row(gain_ref)
    greet_all(cut_count, group_count)
    g_line = LineGather(g_all_ref, g_far_send, g_far_recv, g_pair_send, g_pair_recv)

    line = LineGather(h_all_ref, far_send, far_recv, pair_send, pair_recv)

    def norm_step(m, carry):
        normed, _ = norm_parts(x_ref[m].astype(jnp.float32))
        h_all_ref[m, cut] = (normed * gain).astype(low)
        line.start(m)
        return carry

    lax.fori_loop(0, micro_count, norm_step, 0)

    square = group_count == 4

    def weight_copy(kind, hop):
        src, dst = ((expert_in_ref, weights_ref), (expert_out_ref, weights_out_ref))[kind]
        return line_copy(
            src, dst.at[group], weight_send.at[kind, hop - 1], weight_recv.at[kind, hop - 1],
            jnp.bitwise_xor(group, hop), cut,
        )

    def pass_copy(k):
        half = pl.ds(k * (features // 2), features // 2)
        block = weights_ref.at[jnp.bitwise_xor(group, 2 - k), half, :]
        return line_copy(block, block, pass_send.at[k], pass_recv.at[k], jnp.bitwise_xor(group, 1 + k), cut)

    weight_hops = [(0, 1), (0, 2)] if square else [(kind, hop) for kind in range(2) for hop in range(1, group_count)]
    for kind, hop in weight_hops:
        weight_copy(kind, hop).start()

    chosen = jnp.where(kept_ref[...] == 1, ids_ref[...], -1)
    spot = jnp.where(kept_ref[...] == 1, ids_ref[...] * slots + cut % 2 * capacity + slot_ref[...], -1)
    own_code[...] = jnp.zeros_like(own_code)
    for m in range(micro_count):
        own_code[m, 0:1] = chosen[m : m + 1]
        own_code[m, 1:2] = spot[m : m + 1]
    codes_ref[cut] = own_code[...]

    def code_copy(hop):
        return line_copy(
            own_code, codes_ref.at[cut], code_send.at[hop], code_recv.at[hop], group, jnp.bitwise_xor(cut, hop)
        )

    for hop in range(1, cut_count):
        code_copy(hop).start()
    fill_docs(docs_ref, docs_stage, docs_col_ref)
    for load in loads:
        load.wait()

    def tile_step(n, m):
        level = line.take(m, n)
        h_tile = h_all_ref[m, pl.ds(2 * level, 2)].reshape(2 * rows, features)
        spots = pl.ds(pl.multiple_of(level * 2 * rows, 2 * rows), 2 * rows)
        qkv_ref[m, spots, :] = plain_dot(h_tile, w_qkv_ref[...]).astype(low)

    def early(i, carry):
        tile_step(i // micro_count, i % micro_count)
        return carry

    levels = cut_count // 2
    lax.fori_loop(0, (levels - 1) * micro_count, early, 0)
    g_keep.wait()
    g_line.start(0)
    if square:
        for hop in (1, 2):
            weight_copy(0, hop).wait()
        for k in range(2):
            pass_copy(k).start()
        for hop in (1, 2):
            weight_copy(1, hop).start()

    def swap_copy(m, hop):
        target = jnp.bitwise_xor(cut, hop)
        return line_copy(
            att_part.at[m, pl.ds(pl.multiple_of(target * rows, rows), rows), :],
            att_ref.at[m, :, pl.ds(pl.multiple_of(cut * width, width), width)],
            swap_send.at[m, hop], swap_recv.at[m, hop], group, target,
        )

    def swap_keep(m):
        return pltpu.make_async_copy(
            att_part.at[m, pl.ds(pl.multiple_of(cut * rows, rows), rows), :],
            att_ref.at[m, :, pl.ds(pl.multiple_of(cut * width, width), width)],
            swap_own.at[m],
        )

    def late(m, carry):
        tile_step(levels - 1, m)
        attend_one(heads, m, qkv_ref, docs_ref, docs_col_ref, att_part, lse_ref)
        for hop in range(cut_count - 1, 0, -1):
            swap_copy(m, hop).start()
        swap_keep(m).start()

        @pl.when(m == 0)
        def _():
            g_line.take(0, 0)
            g_line.take(0, 1)

        return carry

    lax.fori_loop(0, micro_count, late, 0)
    for n in range(2, levels):
        g_line.take(0, n)
    keeps = [
        pltpu.make_async_copy(src, dst, keep_sem.at[k])
        for k, (src, dst) in enumerate(((h_all_ref, h_out_ref), (qkv_ref, qkv_out_ref), (lse_ref, lse_out_ref)))
    ]
    for keep in keeps:
        keep.start()

    for hop in range(1, cut_count):
        code_copy(hop).wait()
    for m in range(micro_count):
        line.finish(m)
    for m in range(micro_count):
        for hop in range(cut_count - 1, 0, -1):
            swap_copy(m, hop).wait()
        swap_keep(m).wait()
    g_line.finish(0)
    for keep in keeps:
        keep.wait()
    if square:
        for k in range(2):
            pass_copy(k).wait()
        for hop in (1, 2):
            weight_copy(1, hop).wait()
    else:
        for kind, hop in weight_hops:
            weight_copy(kind, hop).wait()


def front(
    x, gy, gain, w_query, w_key, w_value, docs, ids, slot_ids, kept, expert_in, expert_out, group_count, cut_count, heads, capacity,
    slots, call_id,
):
    micro_count, rows, features = x.shape
    length, levels, width = cut_count * rows, cut_count // 2, features // cut_count
    low, f32 = jnp.bfloat16, jnp.float32
    shape = jax.ShapeDtypeStruct
    dma = pltpu.SemaphoreType.DMA
    vmem, far = pl.BlockSpec(memory_space=pltpu.VMEM), pl.BlockSpec(memory_space=pl.ANY)
    return pl.pallas_call(
        partial(front_kernel, heads, capacity, slots),
        out_shape=(
            shape((micro_count, cut_count, rows, features), low),
            shape((micro_count, length, 3 * width), low),
            shape((micro_count, length, width), f32),
            shape((micro_count, rows, features), low),
            shape((features, 3 * width), low),
            shape((cut_count, micro_count, 8, rows), jnp.int32),
            shape((group_count, *expert_in.shape), low),
            shape((group_count, *expert_out.shape), low),
            shape((1, cut_count, rows, features), low),
        ),
        in_specs=[vmem, vmem, vmem, far, far, far, vmem, vmem, vmem, vmem, far, far],
        out_specs=[far] * 3 + [vmem] * 3 + [far] * 3,
        scratch_shapes=[
            pltpu.VMEM((micro_count, cut_count, rows, features), low),
            pltpu.VMEM((micro_count, length, 3 * width), low),
            pltpu.VMEM((micro_count, length, width), f32),
            pltpu.VMEM((8, length), f32),
            pltpu.VMEM((micro_count, length, 1), jnp.int32),
            pltpu.VMEM((micro_count, length, width), low),
            pltpu.VMEM((micro_count, 8, rows), jnp.int32),
            dma((micro_count, levels + 1)), dma((micro_count, levels)), dma((micro_count, levels)), dma((micro_count, levels)),
            dma((3,)), dma((micro_count, cut_count)), dma((micro_count, cut_count)), dma((micro_count,)),
            dma((cut_count,)), dma((cut_count,)), dma((2, group_count - 1)), dma((2, group_count - 1)), dma((2,)), dma((2,)),
            dma((3,)), dma((1, levels + 1)), dma((1, levels)), dma((1, levels)), dma((1, levels)), dma(()),
        ],
        compiler_params=pltpu.CompilerParams(collective_id=call_id, has_side_effects=True, vmem_limit_bytes=62 * 2**20),
    )(x, gy, gain, w_query, w_key, w_value, docs, ids, slot_ids, kept, expert_in, expert_out)


def feed_kernel(
    slots, strided, early, stored,
    x_ref, att_ref, gy_ref, g_first_ref, w_out_ref, gain_ref, router_ref, mixer_ref, codes_ref, dense_in_ref, dense_out_ref,
    weights_in_ref, weights_out_ref, expert_in_ref, expert_out_ref,
    x_two_ref, h_own_ref, output_ref, dh_ref, sums_ref, d_own_in_ref, d_own_out_ref, d_in_ref, d_out_ref, across_ref,
    got_in_ref, got_out_ref, out_rest_ref,
    h_all, g_buf, sent, g_sent, d_sent, hidden_buf, pre_buf, back_buf, side_buf, own_in, own_out, in_buf, out_buf, inner_buf,
    slope_buf, dots, dots_in, pair_buf, far_buf, o_pair_buf, o_far_buf, out_ref, small_stage, small_ref,
    far_send, far_recv, pair_send, pair_recv, g_far_send, g_far_recv, g_pair_send, g_pair_recv,
    line_send, line_recv, two_send, two_recv, o_line_send, o_line_recv, o_two_send, o_two_recv,
    load_sem, in_sem, out_sem, stage_sem, dot_send, dot_recv, weight_send, weight_recv, early_send, early_recv,
):
    micro_count, cut_count, rows, features = h_all.shape
    group_count = weights_out_ref.shape[0]
    share = own_in.shape[1]
    levels, tile = cut_count // 2, 2 * rows
    expert_count = group_count
    cut = lax.axis_index("cuts")
    group = lax.axis_index("expert")
    low, f32 = jnp.bfloat16, jnp.float32
    half = share
    loads = []
    for k in range(features // half):
        loads.append(pltpu.make_async_copy(w_out_ref.at[:, k * half : (k + 1) * half], in_buf.at[k], load_sem.at[k]))
    g_load = pltpu.make_async_copy(g_first_ref.at[0], g_buf.at[0], load_sem.at[2 + 2 * group_count])
    first_load = len(loads)
    if strided:
        piece = share // group_count
        for g in range(group_count):
            spot = pl.ds(pl.multiple_of((g * cut_count + cut) * piece, piece), piece)
            here = pl.ds(g * piece, piece)
            loads.append(pltpu.make_async_copy(dense_in_ref.at[:, spot], own_in.at[:, here], load_sem.at[len(loads)]))
            loads.append(pltpu.make_async_copy(dense_out_ref.at[spot, :], own_out.at[here, :], load_sem.at[len(loads)]))
    else:
        loads.append(pltpu.make_async_copy(dense_in_ref, own_in, load_sem.at[len(loads)]))
        loads.append(pltpu.make_async_copy(dense_out_ref, own_out, load_sem.at[len(loads)]))
    for load in loads:
        load.start()
    stack_small(router_ref, mixer_ref, small_stage, small_ref)
    gain = one_row(gain_ref)
    g_load.start()
    for m in range(1, micro_count):
        g_buf[m, cut] = gy_ref[m]
    greet_all(cut_count, group_count)
    line = LineGather(h_all, far_send, far_recv, pair_send, pair_recv)
    g_line = LineGather(g_buf, g_far_send, g_far_recv, g_pair_send, g_pair_recv, direct=True)
    for load in loads[:first_load]:
        load.wait()

    def norm_step(m, carry):
        att = att_ref[m]
        projected = jnp.concatenate([plain_dot(att, in_buf[k]) for k in range(features // half)], axis=1)
        x_two = x_ref[m].astype(f32) + projected
        x_two_ref[m] = x_two
        normed, _ = norm_parts(x_two)
        h_two = (normed * gain).astype(low)
        h_all[m, cut] = h_two
        h_own_ref[m] = h_two
        line.start(m)
        return carry

    lax.fori_loop(0, micro_count, norm_step, 0)

    square = group_count == 4

    def pass_copy(k):
        half = pl.ds(k * (share // 2), share // 2)
        return line_copy(
            weights_out_ref.at[jnp.bitwise_xor(group, 2 - k), half, :], across_ref.at[half, :], weight_send.at[k],
            weight_recv.at[k], jnp.bitwise_xor(group, 1 + k), cut,
        )

    for k in range(2 if square else 0):
        pass_copy(k).start()
    for load in loads[first_load:]:
        load.wait()
    if not stored:
        d_sent = sent
    lanes = lax.broadcasted_iota(jnp.int32, (tile, 128), 1)

    def columns(m, level):
        both = [row_to_column(codes_ref[2 * level + k, m]) for k in range(2)]
        both = jnp.concatenate(both, axis=0).astype(jnp.int32)
        return both[:, 0:1], both[:, 1:2]

    def places(m, level):
        t = m * levels + level
        return (
            pl.ds(2 * level, 2), pl.ds(pl.multiple_of(t * tile, tile), tile), pl.ds(pl.multiple_of(t * slots, slots), slots)
        )

    def dense_step(i, carry):
        n, m = i // micro_count, i % micro_count
        level = line.take(m, n)
        blocks, here, spots = places(m, level)
        h_two = h_all[m, blocks].reshape(tile, features)
        chosen, spot = columns(m, level)
        gate, mix_dense, mix_expert, _, _ = route(tail_dot(h_two, small_ref[...]), chosen, expert_count)
        side_buf[here, :] = jnp.where(lanes == 0, mix_dense, mix_expert * gate)
        rows_sent = lead_dot(token_table(spot, expert_count * slots), h_two).astype(low)
        for e in range(expert_count):
            sent[e, spots, :] = rows_sent[e * slots : (e + 1) * slots]
        act, slope = gelu_pair(plain_dot(h_two, own_in[...]))
        pre_buf[here, :] = slope.astype(low)
        hidden_buf[here, :] = (mix_dense * act).astype(low)
        out_ref[m, blocks] = plain_dot(act.astype(low), own_out[...]).astype(low).reshape(2, rows, features)
        return carry

    lax.fori_loop(0, levels * micro_count, dense_step, 0)

    def load_at(i, mask, own=False, across=False):
        e = jnp.bitwise_xor(group, mask)
        src_in = expert_in_ref if own else weights_in_ref.at[e]
        src_out = expert_out_ref if own else across_ref if across else weights_out_ref.at[e]
        return (
            pltpu.make_async_copy(src_in, in_buf.at[i % 2], in_sem.at[i % 2]),
            pltpu.make_async_copy(src_out, out_buf.at[i % 2], out_sem.at[i % 2]),
        )

    def load_start(i, mask, own=False, across=False):
        for load in load_at(i, mask, own, across):
            load.start()

    def load_wait(i):
        for load in load_at(i, 0, True):
            load.wait()

    load_start(0, 0, True)
    for m in range(1, micro_count):
        g_line.start(m)

    def forward_step(i, carry):
        @pl.when(i + 1 < expert_count - square)
        def _():
            load_start(i + 1, i + 1)

        if square:
            @pl.when(i == 2)
            def _():
                for k in range(2):
                    pass_copy(k).wait()
                load_start(3, 3, across=True)

        load_wait(i)
        e, at = jnp.bitwise_xor(group, i), i % 2
        act, slope = gelu_pair(plain_dot(sent[e], in_buf[at]))
        inner = act.astype(low)
        if stored:
            inner_buf[e] = inner
            slope_buf[e] = slope.astype(low)
        g_sent[e] = plain_dot(inner, out_buf[at]).astype(low)
        return carry

    lax.fori_loop(0, expert_count, forward_step, 0)

    def mask_at(i):
        return group_count - 1 - i

    load_start(0, mask_at(0), across=square)
    out_total = LineSum(out_ref, o_pair_buf, o_far_buf, o_line_send, o_line_recv, o_two_send, o_two_recv, direct=True)

    def mix_step(m, n, carry):
        if m:
            g_line.take_pair(m, n)

        level, _ = line.place(n)
        blocks, here, spots = places(m, level)
        _, spot = columns(m, level)
        table = token_table(spot, expert_count * slots)
        side = side_buf[here, :]
        mix_dense, mix_gate = side[:, 0:1], side[:, 1:2]
        grad_y = g_buf[m, blocks].reshape(tile, features).astype(f32)
        dense = out_ref[m, blocks].reshape(tile, features).astype(f32)
        part = plain_dot(table, jnp.concatenate([g_sent[e, spots, :] for e in range(expert_count)], axis=0))
        out_ref[m, blocks] = (mix_dense * dense + mix_gate * part).astype(low).reshape(2, rows, features)
        d_dense = jnp.sum(grad_y * dense, axis=-1, keepdims=True)
        d_part = jnp.sum(grad_y * part, axis=-1, keepdims=True)
        d_mix = jnp.where(lanes == 0, d_dense, d_part)
        for k in range(2):
            dots[2 * level + k, m] = jnp.transpose(d_mix[k * rows : (k + 1) * rows])[0:8]
        if m == 0:
            out_total.pair_copy(0, level).start()
        d_pre = tail_dot((mix_dense * grad_y).astype(low), own_out[...]) * pre_buf[here, :].astype(f32)
        d_pre = d_pre.astype(low)
        pre_buf[here, :] = d_pre
        back_buf[m, blocks] = tail_dot(d_pre, own_in[...]).astype(low).reshape(2, rows, features)
        rows_back = lead_dot(table, (mix_gate * grad_y).astype(low)).astype(low)
        for e in range(expert_count):
            g_sent[e, spots, :] = rows_back[e * slots : (e + 1) * slots]
        return carry

    def combine_step(m, k, carry):
        level = jnp.where(k % 2 == 0, levels - 1 - k // 2, k // 2)
        blocks, here, spots = places(m, level)
        if stored:
            spots = pl.ds(pl.multiple_of(level * slots, slots), slots)
        _, spot = columns(m, level)
        table = token_table(spot, expert_count * slots)
        rows_back = jnp.concatenate([d_sent[e, spots, :] for e in range(expert_count)], axis=0)
        back_rows = plain_dot(table, rows_back).reshape(2, rows, features)
        back_buf[m, blocks] = (back_buf[m, blocks].astype(f32) + back_rows).astype(low)
        total.pair_copy(m, level).start()
        return carry

    def input_step(m, i, carry):
        @pl.when(i + 2 < expert_count)
        def _():
            load_start(i + 1, mask_at(i + 1))

        @pl.when(i + 2 == expert_count)
        def _():
            load_start(i + 1, 0, True)

        load_wait(i)
        e, at = jnp.bitwise_xor(group, mask_at(i)), i % 2
        spots = pl.ds(m * levels * slots, levels * slots)
        d_pre = (tail_dot(g_sent[e, spots, :], out_buf[at]) * slope_buf[e, spots, :].astype(f32)).astype(low)
        slope_buf[e, spots, :] = d_pre
        d_sent[e] = tail_dot(d_pre, in_buf[at]).astype(low)
        return carry

    total = LineSum(back_buf, pair_buf, far_buf, line_send, line_recv, two_send, two_recv)
    g_load.wait()
    out_keep = pltpu.make_async_copy(out_ref.at[pl.ds(1, micro_count - 1)], out_rest_ref, out_sem.at[2])
    for m in range(micro_count):
        if m:
            for n in range(1, levels):
                g_line.receive(m, n)
        lax.fori_loop(0, levels, partial(mix_step, m), 0)
        if m == 0:
            out_total.pairs(0)
        if stored:
            lax.fori_loop(0, expert_count, partial(input_step, m), 0)
            if m + 1 < micro_count:
                load_start(0, mask_at(0), across=square)
            lax.fori_loop(0, levels, partial(combine_step, m), 0)
            total.pairs(m)
    out_keep.start()

    def dot_copy(hop):
        target = jnp.bitwise_xor(cut, hop)
        return line_copy(dots.at[target], dots_in.at[hop - 1], dot_send.at[hop - 1], dot_recv.at[hop - 1], group, target)

    for hop in range(1, cut_count):
        dot_copy(hop).start()

    in_stage, out_stage = own_in, own_out

    def keep_in(i):
        return pltpu.make_async_copy(in_stage, d_in_ref.at[jnp.bitwise_xor(group, mask_at(i))], stage_sem.at[0])

    def keep_out(i):
        return pltpu.make_async_copy(out_stage, d_out_ref.at[jnp.bitwise_xor(group, mask_at(i))], stage_sem.at[1])

    def early_copy(kind):
        src, dst = ((d_in_ref, got_in_ref), (d_out_ref, got_out_ref))[kind]
        return line_copy(
            src.at[jnp.bitwise_xor(group, 3)], dst, early_send.at[kind], early_recv.at[kind],
            jnp.bitwise_xor(group, 1 + kind), cut,
        )

    def keep_step(i):
        @pl.when(i > 0)
        def _():
            keep_in(i).wait()
            keep_out(i).wait()

        if early:
            @pl.when(i == 1)
            def _():
                early_copy(0).start()
                early_copy(1).start()

    def weight_step(i, carry):
        e = jnp.bitwise_xor(group, mask_at(i))
        keep_step(i)
        in_stage[...] = lead_dot(sent[e], slope_buf[e]).astype(low)
        keep_in(i).start()
        out_stage[...] = lead_dot(inner_buf[e], g_sent[e]).astype(low)
        keep_out(i).start()
        for j in range(levels - 1):
            @pl.when(i == j + 1)
            def _():
                total.hop(0, j)

        return carry

    def backward_step(i, carry):
        @pl.when(i + 2 < expert_count)
        def _():
            load_start(i + 1, mask_at(i + 1))

        @pl.when(i + 2 == expert_count)
        def _():
            load_start(i + 1, 0, True)

        load_wait(i)
        e, at = jnp.bitwise_xor(group, mask_at(i)), i % 2
        rows_in, rows_back = sent[e], g_sent[e]
        act, slope = gelu_pair(plain_dot(rows_in, in_buf[at]))
        d_pre = (tail_dot(rows_back, out_buf[at]) * slope).astype(low)
        keep_step(i)
        in_stage[...] = lead_dot(rows_in, d_pre).astype(low)
        keep_in(i).start()
        out_stage[...] = lead_dot(act.astype(low), rows_back).astype(low)
        keep_out(i).start()
        d_sent[e] = tail_dot(d_pre, in_buf[at]).astype(low)
        return carry

    if stored:
        lax.fori_loop(0, expert_count, weight_step, 0)
    else:
        lax.fori_loop(0, expert_count, backward_step, 0)
        for m in range(micro_count):
            lax.fori_loop(0, levels, partial(combine_step, m), 0)
            total.pairs(m)
    token_rows = micro_count * cut_count * rows
    h_flat, g_flat = h_all.reshape(token_rows, features), g_buf.reshape(token_rows, features)

    def dense_weights(k):
        part = pl.ds(k * 256, 256)
        in_buf[0, part, :] = lead_dot(h_flat[:, part], pre_buf[...]).astype(low)
        out_buf[0, :, part] = lead_dot(hidden_buf[...], g_flat[:, part]).astype(low)

    slices = features // 256
    for k in range(slices):
        dense_weights(k)
        if k == 0 and not stored:
            for j in range(levels - 1):
                total.hop(0, j)
        if k == slices // 2:
            for m in range(1, micro_count):
                total.hop(m, 0)
    own_keep = (
        pltpu.make_async_copy(in_buf.at[0], d_own_in_ref, in_sem.at[0]),
        pltpu.make_async_copy(out_buf.at[0], d_own_out_ref, out_sem.at[0]),
    )
    for keep in own_keep:
        keep.start()
    for m in range(1, micro_count):
        for j in range(1, levels - 1):
            total.hop(m, j)
    sums = dots[cut]
    for hop in range(1, cut_count):
        dot_copy(hop).wait()
        sums = sums + dots_in[hop - 1]
    sums_ref[...] = sums
    keep_in(0).wait()
    keep_out(0).wait()
    for kind in range(2 if early else 0):
        early_copy(kind).wait()
    for keep in own_keep:
        keep.wait()
    out_keep.wait()
    for m in range(micro_count):
        line.finish(m)
        if m:
            g_line.finish(m)
    out_total.finish(0, dh_ref)
    output_ref[...] = (x_two_ref[0] + dh_ref[0]).astype(low)
    for m in range(micro_count):
        total.finish(m, dh_ref)


def feed(
    x, att, gy, g_first, w_output, gain, router, mixer, codes, dense_in, dense_out, weights_in, weights_out, expert_in,
    expert_out, share, slots, strided, early, call_id,
):
    micro_count, rows, features = x.shape
    cut_count = codes.shape[0]
    group_count = weights_in.shape[0]
    levels, total = cut_count // 2, micro_count * cut_count * rows
    low, f32 = jnp.bfloat16, jnp.float32
    shape = jax.ShapeDtypeStruct
    dma = pltpu.SemaphoreType.DMA
    block = lambda *dims: pltpu.VMEM(dims, low)
    vmem, far = pl.BlockSpec(memory_space=pltpu.VMEM), pl.BlockSpec(memory_space=pl.ANY)
    whole = (micro_count, cut_count, rows, features)
    stored = group_count <= 4
    slot_rows = micro_count * levels * slots
    line = (micro_count, levels)
    return pl.pallas_call(
        partial(feed_kernel, slots, strided, early, stored),
        out_shape=(
            shape((micro_count, rows, features), f32),
            shape((micro_count, rows, features), low),
            shape((rows, features), low),
            shape((micro_count, rows, features), f32),
            shape((micro_count, 8, rows), f32),
            shape((features, share), low),
            shape((share, features), low),
            shape((group_count, features, share), low),
            shape((group_count, share, features), low),
            shape((share, features) if group_count == 4 else (16, 128), low),
            *(
                (shape((features, share), low), shape((share, features), low))
                if early else (shape((8, 128), low), shape((8, 128), low))
            ),
            shape((micro_count - 1, cut_count, rows, features), low),
        ),
        in_specs=[vmem, vmem, vmem, far, far, vmem, vmem, vmem, vmem, far, far, far, far, far, far],
        out_specs=[vmem] * 5 + [far] * 8,
        scratch_shapes=[
            block(*whole), block(*whole),
            block(group_count, slot_rows, features), block(group_count, slot_rows, features),
            block(group_count, slot_rows // micro_count, features) if stored else block(16, 128),
            block(total, share), block(total, share), block(*whole), pltpu.VMEM((total, 128), f32),
            block(features, share), block(share, features), block(2, features, share), block(2, share, features),
            *([block(group_count, slot_rows, share)] * 2 if stored else [block(16, 128)] * 2),
            pltpu.VMEM((cut_count, micro_count, 8, rows), f32), pltpu.VMEM((cut_count - 1, micro_count, 8, rows), f32),
            block(*line, rows, features), block(micro_count, levels + 1, rows, features),
            block(1, levels, rows, features), block(1, levels + 1, rows, features), block(*whole),
            pltpu.VMEM((128, features), f32), block(128, features),
            *[dma((micro_count, levels + 1)), dma(line), dma(line), dma(line)] * 2,
            *[dma(line), dma(line), dma(line), dma((micro_count, levels + 1))] * 2,
            dma((3 + 2 * group_count,)), dma((2,)), dma((3,)), dma((2,)),
            dma((cut_count - 1,)), dma((cut_count - 1,)), dma((2,)), dma((2,)), dma((4,)), dma((4,)),
        ],
        compiler_params=pltpu.CompilerParams(collective_id=call_id, has_side_effects=True, vmem_limit_bytes=62 * 2**20),
    )(x, att, gy, g_first, w_output, gain, router, mixer, codes, dense_in, dense_out, weights_in, weights_out, expert_in, expert_out)


def attend_back_one(heads, m, qkv_ref, docs_ref, docs_col_ref, lse_ref, back_ref, out_ref, key_acc, value_acc):
    length, width = back_ref.shape[1], back_ref.shape[2]
    rows = min(256, length)
    masks = head_masks(width, heads)
    key_acc[...] = jnp.zeros_like(key_acc)
    value_acc[...] = jnp.zeros_like(value_acc)
    zero = jnp.bfloat16(0)
    for block in range(length // rows):
        start, keys = block * rows, (block + 1) * rows
        allowed = allowed_mask(docs_ref, docs_col_ref, m, start, rows, keys)
        query = qkv_ref[m, pl.ds(start, rows), 0:width] * jnp.bfloat16(score_scale)
        key = qkv_ref[m, 0:keys, width : 2 * width]
        value = qkv_ref[m, 0:keys, 2 * width : 3 * width]
        back = back_ref[m, pl.ds(start, rows), :]
        logs = lse_ref[m, pl.ds(start, rows), :]
        query_grad = jnp.zeros((rows, width), jnp.float32)
        for h, mask in enumerate(masks):
            one_query = jnp.where(mask, query, zero)
            one_back = jnp.where(mask, back, zero)
            scores = jnp.where(allowed, tail_dot(one_query, key), masked_value)
            spot = h * (width // heads)
            probs = jnp.exp(scores - logs[:, spot : spot + 1])
            weighted = probs * tail_dot(one_back, value)
            delta = jnp.sum(weighted, axis=-1, keepdims=True)
            score_grad = (weighted - probs * delta).astype(jnp.bfloat16)
            query_grad = jnp.where(mask, plain_dot(score_grad, key), query_grad)
            key_acc[0:keys, :] += lead_dot(score_grad, one_query)
            value_acc[0:keys, :] += lead_dot(probs.astype(jnp.bfloat16), one_back)
        out_ref[m, pl.ds(start, rows), 0:width] = (query_grad * score_scale).astype(jnp.bfloat16)
    out_ref[m, :, width : 2 * width] = key_acc[...].astype(jnp.bfloat16)
    out_ref[m, :, 2 * width : 3 * width] = value_acc[...].astype(jnp.bfloat16)


def back_kernel(
    heads, expert_count, sums_here,
    dh_ref, dots_ref, codes_ref, h_ref, x_two_ref, gy_ref, att_ref, w_out_ref, docs_ref,
    x_ref, gain_one_ref, gain_two_ref, router_ref, mixer_ref, own_in_ref, own_out_ref,
    qkv_far, lse_far, w_qkv_far, h_all_far, out_part, w_query_ref, w_key_ref, w_value_ref, d_in_ref, d_out_ref,
    got_in_ref, got_out_ref,
    output_ref, tokens_ref, wo_ref, tiny_ref, query_out_ref, key_out_ref, value_out_ref, in_out_ref, out_out_ref, late_in_ref,
    late_out_ref, direct_in_ref, direct_out_ref,
    qkv_ref, lse_ref, w_qkv_ref, h_all_ref, w_rows, docs_stage, docs_col_ref, small_stage, small_ref, out_own, out_pair,
    out_far, g_att, d_att, back_all, d_qkv, key_acc, value_acc, d_small, part, pair_buf, far_buf, d_h_one, in_sum, out_sum,
    wo_part, qkv_part, wo_in, qkv_in, own_in_in, own_out_in, wo_mid, wo_pair, wo_far, wo_sum, qkv_mid, in_mid, qkv_end, in_end,
    pair_send, pair_recv, far_send, far_recv, swap_send, swap_recv, swap_own, one_send, one_recv, two_send, two_recv, two_own,
    late_send, late_recv, late_load_sem, load_sem,
    wo_pair_send, wo_pair_recv, wo_far_send, wo_far_recv, own_sem, o_pair_send, o_pair_recv, o_far_send, o_far_recv,
    direct_send, direct_recv,
):
    micro_count, cut_count, rows, features = part.shape
    group_count, split, _ = qkv_part.shape[:3]
    piece_rows = qkv_part.shape[2]
    group_rows = split * piece_rows
    sides, side_rows = wo_part.shape[1:3]
    width = features // cut_count
    cut = lax.axis_index("cuts")
    group = lax.axis_index("expert")
    low, f32 = jnp.bfloat16, jnp.float32
    levels = cut_count // 2
    place = (group * cut_count + cut) * piece_rows
    loads = [
        pltpu.make_async_copy(src, dst, load_sem.at[k])
        for k, (src, dst) in enumerate(
            ((qkv_far, qkv_ref), (lse_far, lse_ref), (w_qkv_far, w_qkv_ref), (h_all_far, h_all_ref))
        )
    ]
    if sums_here:
        own_rows = pl.ds(pl.multiple_of(place, piece_rows), piece_rows)
        for k, ref in enumerate((w_query_ref, w_key_ref, w_value_ref)):
            loads.append(pltpu.make_async_copy(ref.at[own_rows, :], w_rows.at[k], load_sem.at[4 + k]))
    for load in loads:
        load.start()

    rest = micro_count - 1

    def own_load(m, level):
        return pltpu.make_async_copy(out_part.at[m, 2 * level + cut % 2], out_own.at[m, level], own_sem.at[m, level])

    for m in range(rest):
        for level in range(levels):
            own_load(m, level).start()
    stack_small(router_ref, mixer_ref, small_stage, small_ref)
    fill_docs(docs_ref, docs_stage, docs_col_ref)
    greet_all(cut_count, group_count if sums_here else 1)
    out_line = LineSum(out_part, out_pair, out_far, o_pair_send, o_pair_recv, o_far_send, o_far_recv, out_own, direct=True)

    ones = ((own_in_ref, own_in_in), (own_out_ref, own_out_in), (wo_part, wo_in), (qkv_part, qkv_in))

    def one_copy(kind, hop):
        src, dst = ones[kind]
        target = jnp.bitwise_xor(group, hop)
        return line_copy(
            src.at[target, cut % 2] if kind == 2 else src.at[target], dst.at[hop - 1], one_send.at[kind, hop - 1], one_recv.at[kind, hop - 1], target, cut
        )

    def one_start(kind):
        for hop in range(1, group_count):
            one_copy(kind, hop).start()

    def one_finish(kind):
        src, dst = ones[kind]
        total = (src[group, cut % 2] if kind == 2 else src[group]).astype(f32)
        for hop in range(1, group_count):
            one_copy(kind, hop).wait_recv()
            total = total + dst[hop - 1].astype(f32)
        for hop in range(1, group_count):
            one_copy(kind, hop).wait_send()
        return total

    twos = ((in_mid, in_end), None, None, (qkv_mid, qkv_end))

    def two_copy(kind, hop):
        src, dst = twos[kind]
        target = jnp.bitwise_xor(cut, hop)
        return line_copy(src.at[target], dst.at[cut], two_send.at[kind, hop], two_recv.at[kind, hop], group, target)

    def two_keep(kind):
        src, dst = twos[kind]
        return pltpu.make_async_copy(src.at[cut], dst.at[cut], two_own.at[kind])

    def two_start(kind):
        for hop in range(cut_count - 1, 0, -1):
            two_copy(kind, hop).start()
        two_keep(kind).start()

    def two_finish(kind):
        for hop in range(cut_count - 1, 0, -1):
            two_copy(kind, hop).wait()
        two_keep(kind).wait()

    ends = ((d_in_ref, got_in_ref, in_sum, late_in_ref, 2), (d_out_ref, got_out_ref, out_sum, late_out_ref, 1))

    def late_load(kind, k):
        own, got, total, _, side = ends[kind]
        src = got if k else own.at[jnp.bitwise_xor(group, side)]
        return pltpu.make_async_copy(src, total.at[k], late_load_sem.at[kind, k])

    def late_copy(kind):
        _, _, total, late, side = ends[kind]
        return line_copy(
            total.at[0], late, late_send.at[kind], late_recv.at[kind], jnp.bitwise_xor(group, side), cut
        )

    if sums_here:
        for kind in range(2):
            late_load(kind, 0).start()
            late_load(kind, 1).start()
        one_start(0)
        one_start(1)

    def swap_copy(m, hop):
        target = jnp.bitwise_xor(cut, hop)
        return line_copy(
            d_att.at[m, :, pl.ds(pl.multiple_of(target * width, width), width)],
            back_all.at[m, pl.ds(pl.multiple_of(cut * rows, rows), rows), :],
            swap_send.at[m, hop], swap_recv.at[m, hop], group, target,
        )

    def swap_keep(m):
        return pltpu.make_async_copy(
            d_att.at[m, :, pl.ds(pl.multiple_of(cut * width, width), width)],
            back_all.at[m, pl.ds(pl.multiple_of(cut * rows, rows), rows), :],
            swap_own.at[m],
        )

    small = small_ref[...]
    gain_one, gain_two = one_row(gain_one_ref), one_row(gain_two_ref)
    d_small[...] = jnp.zeros_like(d_small)
    lanes = lax.broadcasted_iota(jnp.int32, (rows, 128), 1)

    def norm_two_step(m, carry):
        dots = jnp.transpose(dots_ref[m])
        chosen = row_to_column(codes_ref[cut, m])[:, 0:1].astype(jnp.int32)
        h_two = h_ref[m]
        gate, _, mix_expert, routed, mixing = route(tail_dot(h_two, small), chosen, expert_count)
        d_mixing = jnp.where(lanes == expert_count, dots[:, 0:1], gate * dots[:, 1:2])
        d_gate = jnp.where(lanes == chosen, mix_expert * dots[:, 1:2], 0.0)
        d_logits = (softmax_back(mixing, d_mixing) + softmax_back(routed, d_gate)).astype(low)
        d_h = dh_ref[m] + plain_dot(d_logits, small)
        normed, scale = norm_parts(x_two_ref[m])
        one_lane = (lanes == expert_count + 2).astype(low)
        d_small[...] += lead_dot(h_two, d_logits) + lead_dot((d_h * normed).astype(low), one_lane)
        d_x = gy_ref[m].astype(f32) + norm_back(normed, scale, gain_two, d_h)
        tokens_ref[m] = d_x
        grad = d_x.astype(low)
        g_att[pl.ds(pl.multiple_of(m * rows, rows), rows), :] = grad
        d_att[m] = tail_dot(grad, w_out_ref[...]).astype(low)
        for hop in range(cut_count - 1, 0, -1):
            swap_copy(m, hop).start()
        swap_keep(m).start()
        return carry

    lax.fori_loop(0, micro_count, norm_two_step, 0)
    for m in range(rest):
        out_line.start(m)

    def wo_step(g, carry):
        columns = pl.ds(pl.multiple_of(g * group_rows, group_rows), group_rows)
        grads = lead_dot(att_ref[:, columns], g_att[...]).astype(low)
        smalls = d_small[columns, :].astype(low)
        for side in range(sides):
            for k in range(side_rows):
                part_rows = slice((k * sides + side) * piece_rows, (k * sides + side + 1) * piece_rows)
                wo_part[g, side, k, :, 0:features] = grads[part_rows]
                wo_part[g, side, k, :, features : features + 128] = smalls[part_rows]
        return carry

    lax.fori_loop(0, group_count, wo_step, 0)
    def wo_pair_copy(g):
        return line_copy(
            wo_part.at[g, 1 - cut % 2], wo_pair.at[g], wo_pair_send.at[g], wo_pair_recv.at[g], group,
            jnp.bitwise_xor(cut, 1),
        )

    def wo_pair_step(g, carry):
        wo_pair_copy(g).wait()
        wo_part[g, cut % 2] = (wo_part[g, cut % 2].astype(f32) + wo_pair[g].astype(f32)).astype(low)
        return carry

    def direct_copy(kind):
        src, dst = ((d_in_ref, direct_in_ref), (d_out_ref, direct_out_ref))[kind]
        target = jnp.bitwise_xor(group, 1 + kind)
        return line_copy(src.at[target], dst, direct_send.at[kind], direct_recv.at[kind], target, cut)

    if sums_here:
        for g in range(group_count):
            wo_pair_copy(g).start()
        lax.fori_loop(0, group_count, wo_pair_step, 0)
        one_start(2)
        for kind in range(2):
            direct_copy(kind).start()
    for load in loads[:3]:
        load.wait()
    line = LineSum(part, pair_buf, far_buf, pair_send, pair_recv, far_send, far_recv)

    def attend_step(m, carry):
        for hop in range(cut_count - 1, 0, -1):
            swap_copy(m, hop).wait()
        swap_keep(m).wait()

        @pl.when(m == 0)
        def _():
            for k in range(rest):
                for level in range(levels):
                    own_load(k, level).wait()
                out_line.pairs(k)

        attend_back_one(heads, m, qkv_ref, docs_ref, docs_col_ref, lse_ref, back_all, d_qkv, key_acc, value_acc)
        for c in range(cut_count):
            part[m, c] = tail_dot(d_qkv[m, c * rows : (c + 1) * rows, :], w_qkv_ref[...]).astype(low)
        line.start(m)
        line.pairs(m)
        return carry

    lax.fori_loop(0, micro_count, attend_step, 0)

    def qkv_step(g, carry):
        columns = pl.ds(pl.multiple_of(g * group_rows, group_rows), group_rows)
        grads = jnp.zeros((group_rows, 3 * width), f32)
        for m in range(micro_count):
            grads = grads + lead_dot(h_all_ref[m, :, columns], d_qkv[m])
        qkv_part[g] = grads.astype(low).reshape(split, piece_rows, 3 * width)
        return carry

    for j in range(levels - 1):
        line.hop(0, j)
    for load in loads[3:]:
        load.wait()
    lax.fori_loop(0, group_count, qkv_step, 0)
    if sums_here:
        one_start(3)
        for kind in range(2):
            total = ends[kind][2]
            late_load(kind, 0).wait()
            late_load(kind, 1).wait()
            total[0] = (total[0].astype(f32) + total[1].astype(f32)).astype(low)
            late_copy(kind).start()
    for m in range(1, micro_count):
        for j in range(levels - 1):
            line.hop(m, j)

    def norm_one_step(m, carry):
        line.finish(m, d_h_one)
        total = d_h_one[m]
        normed, scale = norm_parts(x_ref[m].astype(f32))
        tokens_ref[m] = tokens_ref[m] + norm_back(normed, scale, gain_one, total)
        return carry

    for m in range(rest):
        out_line.finish(m, d_h_one)
        output_ref[m] = (x_two_ref[1 + m] + d_h_one[m]).astype(low)
    if not sums_here:
        lax.fori_loop(0, micro_count, norm_one_step, 0)
        wo_ref[...] = wo_part[...]
        query_out_ref[...] = qkv_part[...]
        return
    in_mid[...] = one_finish(0).astype(low)
    two_start(0)
    wo_line = LineSum(None, wo_mid, wo_far, None, None, wo_far_send, wo_far_recv)
    wo_mid[0] = one_finish(2).astype(low)
    for k in range(levels):
        wo_line.first(0, levels - 1 - k // 2 if k % 2 == 0 else k // 2)
    norm_one_step(0, 0)
    qkv_mid[...] = one_finish(3).astype(low)
    two_start(3)
    out_out_ref[...] = one_finish(1)
    for j in range(levels - 1):
        wo_line.hop(0, j)
    for m in range(1, micro_count):
        norm_one_step(m, 0)
    two_finish(0)
    share_piece = in_end.shape[2] // group_count
    for c in range(cut_count):
        for g in range(group_count):
            spot = (g * cut_count + c) * share_piece
            in_out_ref[:, spot : spot + share_piece] = in_end[c, :, g * share_piece : (g + 1) * share_piece].astype(f32)
    wo_line.finish(0, wo_sum)
    wo_ref[...] = wo_sum[0, :, :features]
    small_sums = wo_sum[0, :, features:]
    two_finish(3)
    norm = jnp.zeros((piece_rows, 1), f32)
    outs = (query_out_ref, key_out_ref, value_out_ref)
    for c in range(cut_count):
        for k in range(3):
            grad = qkv_end[c, :, k * width : (k + 1) * width].astype(f32)
            outs[k][:, c * width : (c + 1) * width] = grad
            weights = w_rows[k, :, c * width : (c + 1) * width].astype(f32)
            norm = norm + jnp.sum(grad * weights, axis=-1, keepdims=True)
    spots = lax.broadcasted_iota(jnp.int32, (piece_rows, features), 1)
    mine = spots == place + lax.broadcasted_iota(jnp.int32, (piece_rows, features), 0)
    norm = norm / jnp.sum(jnp.where(mine, gain_one, 0.0), axis=-1, keepdims=True)
    tiny_lanes = lax.broadcasted_iota(jnp.int32, (piece_rows, 128), 1)
    tiny_ref[...] = jnp.where(tiny_lanes == expert_count + 3, norm, small_sums)
    for kind in range(2):
        late_copy(kind).wait()
        direct_copy(kind).wait()


def back(
    dh, dots, codes, h_two, x_two, gy, attended, w_output, docs, x, gain_one, gain_two, router, mixer, own_in, own_out,
    qkv, lse, w_qkv, h_all, out_rest, w_query, w_key, w_value, d_in, d_out, got_in, got_out, heads, expert_count, sums_here,
    call_id,
):
    micro_count, rows, features = x.shape
    length = qkv.shape[1]
    cut_count = length // rows
    width = features // cut_count
    group_count = own_out.shape[0]
    piece_rows = features // (group_count * cut_count)
    share, piece = own_in.shape[3], own_out.shape[1]
    low, f32 = jnp.bfloat16, jnp.float32
    levels = cut_count // 2
    wide = features + 128
    shape = jax.ShapeDtypeStruct
    parts = (group_count, 2, levels, piece_rows) if sums_here else (features // 256, 1, 1, 256)
    flat = (group_count, cut_count, piece_rows) if sums_here else (features // 256, 1, 256)
    tokens = (micro_count, rows, features)
    none = shape((16, 128), low)
    if sums_here:
        outs = (
            shape((micro_count - 1, rows, features), low),
            shape(tokens, f32), shape((piece_rows, features), f32), shape((piece_rows, 128), f32),
            *[shape((piece_rows, features), f32)] * 3, shape((piece_rows, share * cut_count), f32),
            shape((piece, features), f32), *[shape((features, share), low), shape((share, features), low)] * 2,
        )
    else:
        outs = (
            shape((micro_count - 1, rows, features), low),
            shape(tokens, f32), shape((*parts, wide), low), none, shape((*flat, 3 * width), low),
            *[none] * 8,
        )
    peers = max(group_count - 1, 1) if sums_here else 1
    block = lambda *dims: pltpu.VMEM(dims, low)
    mids = lambda w: block(cut_count, piece_rows, w) if sums_here else block(16, 128)
    ins = lambda w: block(peers, cut_count, piece_rows, w) if sums_here else block(16, 128)
    dma = pltpu.SemaphoreType.DMA
    line = (micro_count, levels)
    vmem, far = pl.BlockSpec(memory_space=pltpu.VMEM), pl.BlockSpec(memory_space=pl.ANY)
    operands = (
        dh, dots, codes, h_two, x_two, gy, attended, w_output, docs, x, gain_one, gain_two, router, mixer, own_in, own_out,
        qkv, lse, w_qkv, h_all, out_rest, w_query, w_key, w_value, d_in, d_out, got_in, got_out,
    )
    rest = (micro_count - 1, levels)
    return pl.pallas_call(
        partial(back_kernel, heads, expert_count, sums_here),
        out_shape=outs,
        in_specs=[vmem] * 16 + [far] * 12,
        out_specs=[vmem] * 9 + [far] * 4,
        scratch_shapes=[
            block(micro_count, length, 3 * width), pltpu.VMEM((micro_count, length, width), f32), block(features, 3 * width),
            block(micro_count, length, features), block(3, piece_rows, features), pltpu.VMEM((8, length), f32),
            pltpu.VMEM((micro_count, length, 1), jnp.int32), pltpu.VMEM((128, features), f32), block(128, features),
            block(*rest, rows, features), block(*rest, rows, features), block(micro_count - 1, levels + 1, rows, features),
            block(micro_count * rows, features),
            block(micro_count, rows, features),
            block(micro_count, length, width),
            block(micro_count, length, 3 * width),
            pltpu.VMEM((length, width), f32),
            pltpu.VMEM((length, width), f32),
            pltpu.VMEM((features, 128), f32),
            block(micro_count, cut_count, rows, features),
            block(*line, rows, features),
            block(micro_count, levels + 1, rows, features),
            pltpu.VMEM(tokens, f32),
            *((block(2, features, share), block(2, share, features)) if sums_here else (block(16, 128), block(16, 128))),
            block(*parts, wide),
            block(*flat, 3 * width),
            block(peers, levels, piece_rows, wide) if sums_here else block(16, 128), ins(3 * width), ins(share),
            block(peers, piece, features) if sums_here else block(16, 128),
            *(
                (
                    block(1, levels, piece_rows, wide), block(group_count, levels, piece_rows, wide),
                    block(1, levels + 1, piece_rows, wide), pltpu.VMEM((1, piece_rows, wide), f32),
                )
                if sums_here else [block(16, 128)] * 4
            ),
            mids(3 * width), mids(share), mids(3 * width), mids(share),
            dma(line), dma(line), dma(line), dma((micro_count, levels + 1)),
            dma((micro_count, cut_count)), dma((micro_count, cut_count)), dma((micro_count,)),
            dma((4, peers)), dma((4, peers)), dma((4, cut_count)), dma((4, cut_count)), dma((4,)),
            dma((2,)), dma((2,)), dma((2, 2)), dma((7,)),
            dma((group_count,)), dma((group_count,)), dma((1, levels)), dma((1, levels + 1)),
            dma(rest), dma(rest), dma(rest), dma(rest), dma((micro_count - 1, levels + 1)),
            dma((2,)), dma((2,)),
        ],
        compiler_params=pltpu.CompilerParams(
            collective_id=call_id, has_side_effects=True, vmem_limit_bytes=62 * 2**20
        ),
    )(*operands)


def last_kernel(
    expert_count, d_in_ref, got_in_ref, late_in_ref, d_out_ref, got_out_ref, late_out_ref, tiny_ref, *refs,
):
    passed = (len(refs) - 6 - 10 - 1) // 3
    given, refs = refs[: passed + 1], refs[passed + 1 :]
    taken, refs = refs[:passed], refs[passed:]
    held, refs = refs[-passed:], refs[:-passed]
    router_ref, mixer_ref, norm_one_ref, norm_two_ref, sum_in_ref, sum_out_ref = refs[:6]
    in_buf, out_buf, in_sum, out_sum, in_sem, out_sem, in_done, out_done, pass_sem, keep_sem = refs[6:]
    group = lax.axis_index("expert")
    held_parts = (held[0].at[0], held[0].at[pl.ds(1, held[0].shape[0] - 1)], *held[1:])
    passes = [pltpu.make_async_copy(src, dst, pass_sem.at[k]) for k, (src, dst) in enumerate(zip(given, held_parts))]
    keeps = [pltpu.make_async_copy(src, dst, keep_sem.at[k]) for k, (src, dst) in enumerate(zip(held, taken))]
    chunks = in_sem.shape[0]
    work = []
    for ends in (
        ((d_in_ref.at[group], got_in_ref, late_in_ref), in_buf, in_sum, sum_in_ref, in_sem, in_done),
        ((d_out_ref.at[group], got_out_ref, late_out_ref), out_buf, out_sum, sum_out_ref, out_sem, out_done),
    ):
        sources, buf, total, target, sem, done = ends
        step = buf.shape[1] // chunks
        for k in range(chunks):
            part = pl.ds(k * step, step)
            loads = [
                pltpu.make_async_copy(src.at[part, :], buf.at[at, part, :], sem.at[k, at]) for at, src in enumerate(sources)
            ]
            work.append((loads, buf, total, part, pltpu.make_async_copy(total.at[part, :], target.at[part, :], done.at[k])))
    for copy in passes:
        copy.start()
    for loads, *_ in work:
        for load in loads:
            load.start()
    turned = jnp.transpose(tiny_ref[...])
    router_ref[...] = turned[0:expert_count]
    mixer_ref[...] = turned[expert_count : expert_count + 2]
    norm_two_ref[...] = turned[expert_count + 2 : expert_count + 3]
    norm_one_ref[...] = turned[expert_count + 3 : expert_count + 4]
    passes[0].wait()
    for copy, keep in zip(passes[1:], keeps):
        copy.wait()
        keep.start()
    for loads, buf, total, part, keep in work:
        for load in loads:
            load.wait()
        total[part, :] = sum(buf[at, part, :].astype(jnp.float32) for at in range(3))
        keep.start()
    for *_, keep in work:
        keep.wait()
    for keep in keeps:
        keep.wait()


def last(d_in, got_in, late_in, d_out, got_out, late_out, tiny, others, expert_count):
    f32, dma = jnp.float32, pltpu.SemaphoreType.DMA
    shape = jax.ShapeDtypeStruct
    piece_rows = tiny.shape[0]
    micro_count = 1 + others[1].shape[0]
    whole = [shape((micro_count, *others[0].shape), others[0].dtype), *[shape(x.shape, x.dtype) for x in others[2:]]]
    vmem, far = pl.BlockSpec(memory_space=pltpu.VMEM), pl.BlockSpec(memory_space=pl.ANY)
    chunks = 4
    return pl.pallas_call(
        partial(last_kernel, expert_count),
        out_shape=(
            *whole, shape((expert_count, piece_rows), f32), shape((2, piece_rows), f32),
            shape((1, piece_rows), f32), shape((1, piece_rows), f32), shape(late_in.shape, f32), shape(late_out.shape, f32),
        ),
        in_specs=[far] * 6 + [vmem] + [far] * len(others),
        out_specs=[far] * len(whole) + [vmem] * 4 + [far] * 2,
        scratch_shapes=[
            pltpu.VMEM((3, *late_in.shape), late_in.dtype), pltpu.VMEM((3, *late_out.shape), late_out.dtype),
            pltpu.VMEM(late_in.shape, f32), pltpu.VMEM(late_out.shape, f32),
            dma((chunks, 3)), dma((chunks, 3)), dma((chunks,)), dma((chunks,)), dma((len(others),)), dma((len(others),)),
            *[pltpu.VMEM(x.shape, x.dtype) for x in whole],
        ],
        compiler_params=pltpu.CompilerParams(vmem_limit_bytes=62 * 2**20),
    )(d_in, got_in, late_in, d_out, got_out, late_out, tiny, *others)


def local(
    tokens, cotangent, segments, expert_ids, slot_ids, kept_mask, norm1_gain, w_query, w_key, w_value, w_output,
    norm2_gain, dense_in, dense_out, router, mixer, expert_in, expert_out,
):
    micro_count, row_count, features = tokens.shape[1:]
    cut_count = lax.axis_size("cuts")
    group_count = lax.axis_size("expert")
    cut = lax.axis_index("cuts")
    group = lax.axis_index("expert")
    length = cut_count * row_count
    head_width = features // cut_count
    heads = head_width // 64
    expert_count = router.shape[1]
    hidden_count = dense_in.shape[1]
    share = hidden_count // cut_count
    piece = share // group_count
    capacity = max(2, row_count * 5 // (4 * expert_count))
    slots = tile_slots(capacity, row_count, 2 * row_count)
    rows = features // (group_count * cut_count)
    sums_here = rows % 16 == 0 and group_count == 4
    by_rows = lambda v: v.reshape(-1, 128)
    router_t, mixer_t = router.T, mixer.T
    f32, low = jnp.float32, jnp.bfloat16

    strided = piece % 128 == 0
    if strided:
        own_in, own_out = dense_in, dense_out
    else:
        own_in = lax.dynamic_index_in_dim(
            dense_in.reshape(features, group_count, cut_count, piece), cut, 2, keepdims=False
        ).reshape(features, share)
        own_out = lax.dynamic_index_in_dim(
            dense_out.reshape(group_count, cut_count, piece, features), cut, 1, keepdims=False
        ).reshape(share, features)
    h_all, qkv, lse, attended, w_qkv, codes, weights_in, weights_out, g_first = front(
        tokens[0], cotangent[0, 0], by_rows(norm1_gain), w_query, w_key, w_value, segments[0], expert_ids[0], slot_ids[0],
        kept_mask[0], expert_in[0], expert_out[0], group_count, cut_count, heads, capacity, slots, 1,
    )
    x_two, h_two, first_output, d_h2, dots, d_own_in, d_own_out, d_in, d_out, _, got_in, got_out, out_rest = feed(
        tokens[0], attended, cotangent[0], g_first, w_output, by_rows(norm2_gain), router_t, mixer_t, codes, own_in, own_out, weights_in,
        weights_out, expert_in[0], expert_out[0], share, slots, strided, sums_here, 2,
    )
    rest_output, grad_tokens, grad_output, tiny, grad_query, grad_key, grad_value, grad_dense_in, grad_dense_out, late_in, late_out, *direct = back(
        d_h2, dots, codes, h_two, x_two, cotangent[0], attended.reshape(-1, features), w_output, segments[0], tokens[0],
        by_rows(norm1_gain), by_rows(norm2_gain), router_t, mixer_t, d_own_in.reshape(group_count, cut_count, rows, share),
        d_own_out.reshape(group_count, piece, features), qkv, lse, w_qkv, h_all.reshape(micro_count, length, features),
        out_rest, w_query, w_key, w_value, d_in, d_out, got_in, got_out, heads, expert_count, sums_here, 3,
    )
    sum_groups = lambda part: lax.psum_scatter(
        part.reshape(-1, part.shape[-1]), "expert", scatter_dimension=0, tiled=True
    )
    if sums_here:
        others = (
            first_output, rest_output, grad_tokens, grad_query, grad_key, grad_value, grad_output, grad_dense_in, grad_dense_out
        )
        *others, grad_router, grad_mixer, grad_norm1, grad_norm2, grad_expert_in, grad_expert_out = last(
            d_in, direct[0], late_in, d_out, direct[1], late_out, tiny, others, expert_count
        )
        output, grad_tokens, grad_query, grad_key, grad_value, grad_output, grad_dense_in, grad_dense_out = others
        grad_router, grad_mixer, grad_norm1, grad_norm2 = grad_router.T, grad_mixer.T, grad_norm1[0], grad_norm2[0]
    else:
        swap = lambda part: lax.all_to_all(
            part.reshape(cut_count, rows, -1), "cuts", split_axis=0, concat_axis=0
        ).astype(f32)
        output = jnp.concatenate([first_output[None], rest_output])
        wide = jnp.sum(swap(sum_groups(grad_output)), axis=0)
        grad_output, grad_small = wide[:, :features], wide[:, features:]
        grad_router, grad_mixer = grad_small[:, :expert_count], grad_small[:, expert_count : expert_count + 2]
        grad_norm2 = grad_small[:, expert_count + 2]
        grad_qkv = swap(sum_groups(grad_query)).reshape(cut_count, rows, 3, head_width).transpose(2, 1, 0, 3)
        grad_qkv = grad_qkv.reshape(3, rows, features)
        grad_query, grad_key, grad_value = grad_qkv
        grad_dense_in = swap(sum_groups(d_own_in)).reshape(cut_count, rows, group_count, piece).transpose(1, 2, 0, 3)
        grad_dense_in = grad_dense_in.reshape(rows, hidden_count)
        grad_dense_out = sum_groups(d_own_out).astype(f32)
        grad_expert_in = sum_groups(d_in).astype(f32)
        grad_expert_out = sum_groups(d_out).astype(f32)
        place = (group * cut_count + cut) * rows
        own_rows = lambda w: lax.dynamic_slice_in_dim(w, place, rows, 0).astype(f32)
        grad_norm1 = sum(
            jnp.sum(own_rows(w) * grad_qkv[k], axis=-1) for k, w in enumerate((w_query, w_key, w_value))
        ) / own_rows(norm1_gain)
    return (
        output[None], grad_tokens[None], grad_norm1, grad_query, grad_key, grad_value, grad_output, grad_norm2, grad_dense_in,
        grad_dense_out, grad_router, grad_mixer, grad_expert_in[None], grad_expert_out[None],
    )


def solution(mesh):
    in_specs = (
        P("expert", None, "cuts", None),
        P("expert", None, "cuts", None),
        P("expert", None, None),
        P("expert", None, "cuts"),
        P("expert", None, "cuts"),
        P("expert", None, "cuts"),
        P(),
        P(),
        P(),
        P(),
        P(),
        P(),
        P(),
        P(),
        P(),
        P(),
        P("expert", None, "cuts"),
        P("expert", "cuts", None),
    )
    out_specs = (
        P("expert", None, "cuts", None),
        P("expert", None, "cuts", None),
        P(("expert", "cuts")),
        P(("expert", "cuts"), None),
        P(("expert", "cuts"), None),
        P(("expert", "cuts"), None),
        P(("expert", "cuts"), None),
        P(("expert", "cuts")),
        P(("expert", "cuts"), None),
        P(("expert", "cuts"), None),
        P(("expert", "cuts"), None),
        P(("expert", "cuts"), None),
        P("expert", None, "cuts"),
        P("expert", "cuts", None),
    )
    return jax.shard_map(local, mesh=mesh, in_specs=in_specs, out_specs=out_specs, check_vma=False)
```

```python
from functools import partial

import jax
import jax.numpy as jnp
from jax import lax
from jax.experimental import pallas as pl
from jax.experimental.pallas import tpu as pltpu
from jax.sharding import PartitionSpec as P

MESH = pl.DeviceIdType.MESH
score_scale = 0.125
masked_value = -1e30
norm_eps = 1e-05


def plain_dot(left, right):
    return jnp.dot(left, right, preferred_element_type=jnp.float32)


def lead_dot(left, right):
    return lax.dot_general(
        left, right, (((0,), (0,)), ((), ())), preferred_element_type=jnp.float32
    )


def tail_dot(left, right):
    return lax.dot_general(
        left, right, (((1,), (1,)), ((), ())), preferred_element_type=jnp.float32
    )


def head_masks(width, heads):
    lane = lax.broadcasted_iota(jnp.int32, (1, width), 1)
    size = width // heads
    return [((lane >= h * size) & (lane < (h + 1) * size)) for h in range(heads)]


def allowed_mask(docs_ref, docs_col_ref, m, start, rows, keys):
    query_spots = start + lax.broadcasted_iota(jnp.int32, (rows, keys), 0)
    key_spots = lax.broadcasted_iota(jnp.int32, (rows, keys), 1)
    return (key_spots <= query_spots) & (docs_ref[pl.ds(m, 1), 0:keys] == docs_col_ref[m, pl.ds(start, rows), :])


def attend_one(heads, m, qkv_ref, docs_ref, docs_col_ref, att_ref, lse_ref):
    length, width = att_ref.shape[1], att_ref.shape[2]
    rows = min(256, length)
    masks = head_masks(width, heads)
    for block in range(length // rows):
        start, keys = block * rows, (block + 1) * rows
        allowed = allowed_mask(docs_ref, docs_col_ref, m, start, rows, keys)
        query = qkv_ref[m, pl.ds(start, rows), 0:width] * jnp.bfloat16(score_scale)
        key = qkv_ref[m, 0:keys, width : 2 * width]
        value = qkv_ref[m, 0:keys, 2 * width : 3 * width]
        att = jnp.zeros((rows, width), jnp.float32)
        logs = jnp.zeros((rows, width), jnp.float32)
        for mask in masks:
            scores = tail_dot(jnp.where(mask, query, jnp.bfloat16(0)), key)
            scores = jnp.where(allowed, scores, masked_value)
            top = jnp.max(scores, axis=-1, keepdims=True)
            raised = jnp.exp(scores - top)
            total = jnp.sum(raised, axis=-1, keepdims=True)
            probs = (raised * (1.0 / total)).astype(jnp.bfloat16)
            att = jnp.where(mask, plain_dot(probs, value), att)
            logs = jnp.where(mask, top + jnp.log(total), logs)
        att_ref[m, pl.ds(start, rows), :] = att.astype(jnp.bfloat16)
        lse_ref[m, pl.ds(start, rows), :] = logs


def norm_parts(values):
    center = values - jnp.mean(values, axis=-1, keepdims=True)
    spread = jnp.mean(center * center, axis=-1, keepdims=True)
    scale = lax.rsqrt(spread + norm_eps)
    return center * scale, scale


def norm_back(normed, scale, gain, grad):
    inner = grad * gain
    return scale * (
        inner
        - jnp.mean(inner, axis=-1, keepdims=True)
        - normed * jnp.mean(inner * normed, axis=-1, keepdims=True)
    )


def gelu_pair(values):
    phi = 0.5 * (1.0 + lax.erf(values * (0.5**0.5)))
    bell = jnp.exp(-0.5 * values * values) * ((2.0 * jnp.pi) ** -0.5)
    return values * phi, phi + values * bell


def tile_slots(capacity, row_count, tile):
    return -(-capacity * (tile // row_count) // 16) * 16


def token_table(spot, width):
    return (spot == lax.broadcasted_iota(jnp.int32, (spot.shape[0], width), 1)).astype(jnp.bfloat16)


def lane_softmax(logits, lanes, first, count):
    inside = (lanes >= first) & (lanes < first + count)
    raised = jnp.exp(logits - jnp.max(jnp.where(inside, logits, masked_value), axis=-1, keepdims=True))
    raised = jnp.where(inside, raised, 0.0)
    return raised / jnp.sum(raised, axis=-1, keepdims=True)


def route(logits, chosen, expert_count):
    lanes = lax.broadcasted_iota(jnp.int32, logits.shape, 1)
    routed = lane_softmax(logits, lanes, 0, expert_count)
    mixing = lane_softmax(logits, lanes, expert_count, 2)
    pick = lambda values, lane: jnp.sum(jnp.where(lanes == lane, values, 0.0), axis=-1, keepdims=True)
    return pick(routed, chosen), pick(mixing, expert_count), pick(mixing, expert_count + 1), routed, mixing


def softmax_back(probs, grad):
    return probs * (grad - jnp.sum(probs * grad, axis=-1, keepdims=True))


def line_copy(src, dst, send, recv, group, target):
    return pltpu.make_async_remote_copy(
        src_ref=src, dst_ref=dst, send_sem=send, recv_sem=recv, device_id=(group, target), device_id_type=MESH
    )


def greet_all(cut_count, group_count):
    cut = lax.axis_index("cuts")
    group = lax.axis_index("expert")
    barrier = pltpu.get_barrier_semaphore()
    for hop in range(1, cut_count):
        pl.semaphore_signal(barrier, inc=1, device_id=(group, jnp.bitwise_xor(cut, hop)), device_id_type=MESH)
    for hop in range(1, group_count):
        pl.semaphore_signal(barrier, inc=1, device_id=(jnp.bitwise_xor(group, hop), cut), device_id_type=MESH)
    pl.semaphore_wait(barrier, cut_count + group_count - 2)


class LineGather:
    def __init__(self, buf, far_send, far_recv, pair_send, pair_recv, direct=False):
        self.direct = direct
        self.buf = buf
        self.sems = (far_send, far_recv, pair_send, pair_recv)
        self.cut = lax.axis_index("cuts")
        self.group = lax.axis_index("expert")
        self.level, self.side = self.cut // 2, self.cut % 2
        self.levels = buf.shape[1] // 2

    def place(self, n):
        low, high = self.level, self.levels - 1 - self.level
        near = jnp.minimum(low, high)
        paired = n <= 2 * near
        distance = jnp.where(paired, (n + 1) // 2, n - near)
        below = jnp.where(paired, n % 2 == 1, low > high)
        return jnp.where(below, self.level - distance, self.level + distance), below

    def far_copy(self, m, level, target, send):
        block = self.buf.at[m, 2 * level + self.side]
        return line_copy(block, block, self.sems[0].at[m, send], self.sems[1].at[m, level], self.group, target)

    def pair_copy(self, m, level, side):
        block = self.buf.at[m, 2 * level + side]
        return line_copy(
            block, block, self.sems[2].at[m, level], self.sems[3].at[m, level], self.group, jnp.bitwise_xor(self.cut, 1)
        )

    def straight_copy(self, m, n):
        level, _ = self.place(n)
        return self.far_copy(m, self.level, 2 * level + self.side, level)

    def start(self, m):
        if self.direct:
            for n in range(1, self.levels):
                self.straight_copy(m, n).start()
        else:
            @pl.when(self.level + 1 < self.levels)
            def _():
                self.far_copy(m, self.level, self.cut + 2, self.level).start()

            @pl.when(self.level > 0)
            def _():
                self.far_copy(m, self.level, self.cut - 2, self.levels).start()

        self.pair_copy(m, self.level, self.side).start()

    def receive(self, m, n):
        level, _ = self.place(n)
        self.far_copy(m, level, self.cut, level).wait_recv()
        self.pair_copy(m, level, self.side).start()

    def take_pair(self, m, n):
        level, _ = self.place(n)
        self.pair_copy(m, level, 1 - self.side).wait_recv()

    def take(self, m, n):
        level, below = self.place(n)

        @pl.when(n > 0)
        def _():
            target = jnp.where(below, self.cut + 2, self.cut - 2)
            self.far_copy(m, level, target, level).wait_recv()

            @pl.when(jnp.where(below, self.level + 1 < self.levels, self.level > 0))
            def _():
                self.far_copy(m, level, target, level).start()

            self.pair_copy(m, level, self.side).start()

        self.pair_copy(m, level, 1 - self.side).wait_recv()
        return level

    def finish(self, m):
        if self.direct:
            self.pair_copy(m, self.level, self.side).wait_send()
            for n in range(1, self.levels):
                level, _ = self.place(n)
                self.straight_copy(m, n).wait_send()
                self.pair_copy(m, level, self.side).wait_send()
            return

        @pl.when(self.level + 1 < self.levels)
        def _():
            self.far_copy(m, self.level, self.cut + 2, self.level).wait_send()

        @pl.when(self.level > 0)
        def _():
            self.far_copy(m, self.level, self.cut - 2, self.levels).wait_send()

        for n in range(self.levels):
            level, below = self.place(n)
            if n:
                @pl.when(jnp.where(below, self.level + 1 < self.levels, self.level > 0))
                def _():
                    self.far_copy(m, level, self.cut, level).wait_send()

            self.pair_copy(m, level, self.side).wait_send()


class LineSum:
    def __init__(self, part, pair_buf, far_buf, pair_send, pair_recv, send, recv, own=None, direct=False):
        self.direct = direct
        self.part, self.pair_buf, self.far_buf, self.own = part, pair_buf, far_buf, own
        self.sems = (pair_send, pair_recv, send, recv)
        self.cut = lax.axis_index("cuts")
        self.group = lax.axis_index("expert")
        self.level, self.side = self.cut // 2, self.cut % 2
        self.levels = pair_buf.shape[1]

    def pair_copy(self, m, level):
        return line_copy(
            self.part.at[m, 2 * level + 1 - self.side], self.pair_buf.at[m, level], self.sems[0].at[m, level],
            self.sems[1].at[m, level], self.group, jnp.bitwise_xor(self.cut, 1),
        )

    def far_copy(self, m, level, up):
        target = self.cut + 2 if up else self.cut - 2
        slot = level if up else jnp.where(level == self.level - 1, self.levels, level)
        return line_copy(
            self.pair_buf.at[m, level], self.far_buf.at[m, slot], self.sems[2].at[m, level], self.sems[3].at[m, slot],
            self.group, target,
        )

    def arrived(self, m, slot):
        line_copy(
            self.far_buf.at[m, slot], self.far_buf.at[m, slot], self.sems[2].at[m, 0], self.sems[3].at[m, slot],
            self.group, self.cut,
        ).wait_recv()
        return self.far_buf[m, slot].astype(jnp.float32)

    def start(self, m):
        def one(k, carry):
            self.pair_copy(m, jnp.where(k % 2 == 0, self.levels - 1 - k // 2, k // 2)).start()
            return carry

        lax.fori_loop(0, self.levels, one, 0)

    def pairs(self, m):
        def one(k, carry):
            level = jnp.where(k % 2 == 0, self.levels - 1 - k // 2, k // 2)
            self.pair_copy(m, level).wait_recv()
            mine = self.part[m, 2 * level + self.side] if self.own is None else self.own[m, level]
            total = mine.astype(jnp.float32) + self.pair_buf[m, level].astype(jnp.float32)
            self.pair_buf[m, level] = total.astype(self.pair_buf.dtype)
            self.first(m, level)
            return carry

        lax.fori_loop(0, self.levels, one, 0)

    def straight_copy(self, m, level):
        return line_copy(
            self.pair_buf.at[m, level], self.far_buf.at[m, self.level], self.sems[2].at[m, level],
            self.sems[3].at[m, self.level], self.group, 2 * level + self.side,
        )

    def first(self, m, level):
        if self.direct:
            @pl.when(level != self.level)
            def _():
                self.straight_copy(m, level).start()

            return

        @pl.when((self.level == 0) & (level > 0))
        def _():
            self.far_copy(m, level, True).start()

        @pl.when((self.level == self.levels - 1) & (level < self.levels - 1))
        def _():
            self.far_copy(m, level, False).start()

    def pass_on(self, m, level, up):
        @pl.when((level > self.level) if up else (level < self.level))
        def _():
            total = self.pair_buf[m, level].astype(jnp.float32) + self.arrived(m, level)
            self.pair_buf[m, level] = total.astype(self.pair_buf.dtype)
            self.far_copy(m, level, up).start()

    def hop(self, m, j):
        inner = (self.level > 0) & (self.level < self.levels - 1)
        lower = 2 * self.level < self.levels

        @pl.when(inner & lower)
        def _():
            self.pass_on(m, self.levels - 1 - j, True)
            self.pass_on(m, j, False)

        @pl.when(inner & jnp.logical_not(lower))
        def _():
            self.pass_on(m, j, False)
            self.pass_on(m, self.levels - 1 - j, True)

    def finish(self, m, out_ref):
        if self.direct:
            total = self.pair_buf[m, self.level].astype(jnp.float32)
            for k in range(1, self.levels):
                total = total + self.arrived(m, jnp.bitwise_xor(self.level, k))
            out_ref[m] = total
            for k in range(1, self.levels):
                self.straight_copy(m, jnp.bitwise_xor(self.level, k)).wait_send()
            for level in range(self.levels):
                self.pair_copy(m, level).wait_send()
            return

        out_ref[m] = self.pair_buf[m, self.level].astype(jnp.float32)

        @pl.when(self.level > 0)
        def _():
            out_ref[m] = out_ref[m] + self.arrived(m, self.level)

        @pl.when(self.level < self.levels - 1)
        def _():
            out_ref[m] = out_ref[m] + self.arrived(m, self.levels)

        def one(level, carry):
            if self.part is not None:
                self.pair_copy(m, level).wait_send()

            @pl.when(level > self.level)
            def _():
                self.far_copy(m, level, True).wait_send()

            @pl.when(level < self.level)
            def _():
                self.far_copy(m, level, False).wait_send()

            return carry

        lax.fori_loop(0, self.levels, one, 0)


def row_to_column(values):
    return jnp.transpose(values.astype(jnp.float32))


def one_row(ref):
    values = ref[...].astype(jnp.float32)
    return jnp.concatenate([values[k : k + 1] for k in range(values.shape[0])], axis=1)


def stack_small(router_ref, mixer_ref, stage, small):
    count = router_ref.shape[0]
    stage[...] = jnp.zeros_like(stage)
    stage[0:count] = router_ref[...].astype(jnp.float32)
    stage[count : count + 2] = mixer_ref[...].astype(jnp.float32)
    small[...] = stage[...].astype(small.dtype)


def fill_docs(docs_ref, stage, docs_col):
    stage[...] = jnp.zeros_like(stage)
    micro_count = docs_ref.shape[0]
    stage[0:micro_count] = docs_ref[...].astype(jnp.float32)
    for k in range(stage.shape[1] // 128):
        turned = jnp.transpose(stage[:, k * 128 : (k + 1) * 128]).astype(jnp.int32)
        for m in range(micro_count):
            docs_col[m, k * 128 : (k + 1) * 128, :] = turned[:, m : m + 1]


def front_kernel(
    heads, capacity, slots,
    x_ref, gy_ref, gain_ref, gain_two_ref, w_out_ref, w_query_ref, w_key_ref, w_value_ref, docs_ref, ids_ref, slot_ref, kept_ref, expert_in_ref,
    expert_out_ref,
    h_out_ref, qkv_out_ref, lse_out_ref, att_ref, w_qkv_ref, codes_ref, x_two_ref, h_two_ref, weights_ref,
    weights_out_ref, g_all_ref,
    h_all_ref, qkv_ref, lse_ref, w_out, docs_stage, docs_col_ref, att_part, own_code, far_send, far_recv, pair_send, pair_recv, load_sem, swap_send, swap_recv, swap_own, code_send,
    code_recv, weight_send, weight_recv, pass_send, pass_recv, keep_sem,
    g_far_send, g_far_recv, g_pair_send, g_pair_recv, g_own,
):
    micro_count, cut_count, rows, features = h_all_ref.shape
    group_count = weights_ref.shape[0]
    width = features // cut_count
    cut = lax.axis_index("cuts")
    group = lax.axis_index("expert")
    low = jnp.bfloat16
    loads = []
    for k, ref in enumerate((w_query_ref, w_key_ref, w_value_ref)):
        loads.append(pltpu.make_async_copy(
            ref.at[:, pl.ds(pl.multiple_of(cut * width, width), width)], w_qkv_ref.at[:, k * width : (k + 1) * width],
            load_sem.at[k],
        ))
        loads[-1].start()
    loads.append(pltpu.make_async_copy(w_out_ref, w_out, load_sem.at[3]))
    loads[-1].start()
    g_keep = pltpu.make_async_copy(gy_ref, g_all_ref.at[0, cut], g_own)
    g_keep.start()
    gain, gain_two = one_row(gain_ref), one_row(gain_two_ref)
    greet_all(cut_count, group_count)
    g_line = LineGather(g_all_ref, g_far_send, g_far_recv, g_pair_send, g_pair_recv)

    line = LineGather(h_all_ref, far_send, far_recv, pair_send, pair_recv)

    def norm_step(m, carry):
        normed, _ = norm_parts(x_ref[m].astype(jnp.float32))
        h_all_ref[m, cut] = (normed * gain).astype(low)
        line.start(m)
        return carry

    lax.fori_loop(0, micro_count, norm_step, 0)

    square = group_count == 4

    def weight_copy(kind, hop):
        src, dst = ((expert_in_ref, weights_ref), (expert_out_ref, weights_out_ref))[kind]
        return line_copy(
            src, dst.at[group], weight_send.at[kind, hop - 1], weight_recv.at[kind, hop - 1],
            jnp.bitwise_xor(group, hop), cut,
        )

    def pass_copy(k):
        half = pl.ds(k * (features // 2), features // 2)
        block = weights_ref.at[jnp.bitwise_xor(group, 2 - k), half, :]
        return line_copy(block, block, pass_send.at[k], pass_recv.at[k], jnp.bitwise_xor(group, 1 + k), cut)

    weight_hops = [(0, 1), (0, 2)] if square else [(kind, hop) for kind in range(2) for hop in range(1, group_count)]
    for kind, hop in weight_hops:
        weight_copy(kind, hop).start()

    chosen = jnp.where(kept_ref[...] == 1, ids_ref[...], -1)
    spot = jnp.where(kept_ref[...] == 1, ids_ref[...] * slots + cut % 2 * capacity + slot_ref[...], -1)
    own_code[...] = jnp.zeros_like(own_code)
    for m in range(micro_count):
        own_code[m, 0:1] = chosen[m : m + 1]
        own_code[m, 1:2] = spot[m : m + 1]
    codes_ref[cut] = own_code[...]

    def code_copy(hop):
        return line_copy(
            own_code, codes_ref.at[cut], code_send.at[hop], code_recv.at[hop], group, jnp.bitwise_xor(cut, hop)
        )

    for hop in range(1, cut_count):
        code_copy(hop).start()
    fill_docs(docs_ref, docs_stage, docs_col_ref)
    for load in loads[:3]:
        load.wait()

    def tile_step(n, m):
        level = line.take(m, n)
        h_tile = h_all_ref[m, pl.ds(2 * level, 2)].reshape(2 * rows, features)
        spots = pl.ds(pl.multiple_of(level * 2 * rows, 2 * rows), 2 * rows)
        qkv_ref[m, spots, :] = plain_dot(h_tile, w_qkv_ref[...]).astype(low)

    def early(i, carry):
        tile_step(i // micro_count, i % micro_count)
        return carry

    levels = cut_count // 2
    lax.fori_loop(0, (levels - 1) * micro_count, early, 0)
    g_keep.wait()
    g_line.start(0)
    if square:
        for hop in (1, 2):
            weight_copy(0, hop).wait()
        for k in range(2):
            pass_copy(k).start()

    def swap_copy(m, hop):
        target = jnp.bitwise_xor(cut, hop)
        return line_copy(
            att_part.at[m, pl.ds(pl.multiple_of(target * rows, rows), rows), :],
            att_ref.at[m, :, pl.ds(pl.multiple_of(cut * width, width), width)],
            swap_send.at[m, hop], swap_recv.at[m, hop], group, target,
        )

    def swap_keep(m):
        return pltpu.make_async_copy(
            att_part.at[m, pl.ds(pl.multiple_of(cut * rows, rows), rows), :],
            att_ref.at[m, :, pl.ds(pl.multiple_of(cut * width, width), width)],
            swap_own.at[m],
        )

    def late(m, carry):
        tile_step(levels - 1, m)
        attend_one(heads, m, qkv_ref, docs_ref, docs_col_ref, att_part, lse_ref)
        for hop in range(cut_count - 1, 0, -1):
            swap_copy(m, hop).start()
        swap_keep(m).start()

        @pl.when(m == 0)
        def _():
            g_line.take(0, 0)
            g_line.take(0, 1)

        return carry

    lax.fori_loop(0, micro_count, late, 0)
    for n in range(2, levels):
        g_line.take(0, n)
    keeps = [
        pltpu.make_async_copy(src, dst, keep_sem.at[k])
        for k, (src, dst) in enumerate(((h_all_ref, h_out_ref), (qkv_ref, qkv_out_ref), (lse_ref, lse_out_ref)))
    ]
    for keep in keeps:
        keep.start()

    for hop in range(1, cut_count):
        code_copy(hop).wait()
    for m in range(micro_count):
        line.finish(m)
    loads[3].wait()

    def project_step(m, carry):
        for hop in range(cut_count - 1, 0, -1):
            swap_copy(m, hop).wait()
        swap_keep(m).wait()
        x_two = x_ref[m].astype(jnp.float32) + plain_dot(att_ref[m], w_out[...])
        x_two_ref[m] = x_two
        normed, _ = norm_parts(x_two)
        h_two_ref[m] = (normed * gain_two).astype(low)
        return carry

    lax.fori_loop(0, micro_count, project_step, 0)
    g_line.finish(0)
    for keep in keeps:
        keep.wait()
    if square:
        for k in range(2):
            pass_copy(k).wait()
    else:
        for kind, hop in weight_hops:
            weight_copy(kind, hop).wait()


def front(
    x, gy, gain, gain_two, w_output, w_query, w_key, w_value, docs, ids, slot_ids, kept, expert_in, expert_out, group_count, cut_count, heads, capacity,
    slots, call_id,
):
    micro_count, rows, features = x.shape
    length, levels, width = cut_count * rows, cut_count // 2, features // cut_count
    low, f32 = jnp.bfloat16, jnp.float32
    shape = jax.ShapeDtypeStruct
    dma = pltpu.SemaphoreType.DMA
    vmem, far = pl.BlockSpec(memory_space=pltpu.VMEM), pl.BlockSpec(memory_space=pl.ANY)
    return pl.pallas_call(
        partial(front_kernel, heads, capacity, slots),
        out_shape=(
            shape((micro_count, cut_count, rows, features), low),
            shape((micro_count, length, 3 * width), low),
            shape((micro_count, length, width), f32),
            shape((micro_count, rows, features), low),
            shape((features, 3 * width), low),
            shape((cut_count, micro_count, 8, rows), jnp.int32),
            shape((micro_count, rows, features), f32),
            shape((micro_count, rows, features), low),
            shape((group_count, *expert_in.shape), low),
            shape((16, 128) if group_count == 4 else (group_count, *expert_out.shape), low),
            shape((1, cut_count, rows, features), low),
        ),
        in_specs=[vmem, vmem, vmem, vmem, far, far, far, far, vmem, vmem, vmem, vmem, far, far],
        out_specs=[far] * 3 + [vmem] * 5 + [far] * 3,
        scratch_shapes=[
            pltpu.VMEM((micro_count, cut_count, rows, features), low),
            pltpu.VMEM((micro_count, length, 3 * width), low),
            pltpu.VMEM((micro_count, length, width), f32),
            pltpu.VMEM((features, features), low),
            pltpu.VMEM((8, length), f32),
            pltpu.VMEM((micro_count, length, 1), jnp.int32),
            pltpu.VMEM((micro_count, length, width), low),
            pltpu.VMEM((micro_count, 8, rows), jnp.int32),
            dma((micro_count, levels + 1)), dma((micro_count, levels)), dma((micro_count, levels)), dma((micro_count, levels)),
            dma((4,)), dma((micro_count, cut_count)), dma((micro_count, cut_count)), dma((micro_count,)),
            dma((cut_count,)), dma((cut_count,)), dma((2, group_count - 1)), dma((2, group_count - 1)), dma((2,)), dma((2,)),
            dma((3,)), dma((1, levels + 1)), dma((1, levels)), dma((1, levels)), dma((1, levels)), dma(()),
        ],
        compiler_params=pltpu.CompilerParams(collective_id=call_id, has_side_effects=True, vmem_limit_bytes=62 * 2**20),
    )(x, gy, gain, gain_two, w_output, w_query, w_key, w_value, docs, ids, slot_ids, kept, expert_in, expert_out)


def feed_kernel(
    slots, strided, early, stored,
    x_two_ref, h_own_ref, gy_ref, g_first_ref, router_ref, mixer_ref, codes_ref, dense_in_ref, dense_out_ref,
    weights_in_ref, weights_out_ref, expert_in_ref, expert_out_ref,
    output_ref, dh_ref, sums_ref, d_own_in_ref, d_own_out_ref, d_in_ref, d_out_ref, beside_ref, across_ref,
    got_in_ref, got_out_ref, out_rest_ref,
    h_all, g_buf, sent, g_sent, d_sent, hidden_buf, pre_buf, back_buf, side_buf, own_in, own_out, in_buf, out_buf, inner_buf,
    slope_buf, dots, dots_in, pair_buf, far_buf, o_pair_buf, o_far_buf, out_ref, small_stage, small_ref,
    far_send, far_recv, pair_send, pair_recv, g_far_send, g_far_recv, g_pair_send, g_pair_recv,
    line_send, line_recv, two_send, two_recv, o_line_send, o_line_recv, o_two_send, o_two_recv,
    load_sem, in_sem, out_sem, stage_sem, dot_send, dot_recv, weight_send, weight_recv, early_send, early_recv,
):
    micro_count, cut_count, rows, features = h_all.shape
    group_count = weights_in_ref.shape[0]
    share = own_in.shape[1]
    levels, tile = cut_count // 2, 2 * rows
    expert_count = group_count
    cut = lax.axis_index("cuts")
    group = lax.axis_index("expert")
    low, f32 = jnp.bfloat16, jnp.float32
    loads = []
    g_load = pltpu.make_async_copy(g_first_ref.at[0], g_buf.at[0], load_sem.at[2 + 2 * group_count])
    if strided:
        piece = share // group_count
        for g in range(group_count):
            spot = pl.ds(pl.multiple_of((g * cut_count + cut) * piece, piece), piece)
            here = pl.ds(g * piece, piece)
            loads.append(pltpu.make_async_copy(dense_in_ref.at[:, spot], own_in.at[:, here], load_sem.at[len(loads)]))
            loads.append(pltpu.make_async_copy(dense_out_ref.at[spot, :], own_out.at[here, :], load_sem.at[len(loads)]))
    else:
        loads.append(pltpu.make_async_copy(dense_in_ref, own_in, load_sem.at[len(loads)]))
        loads.append(pltpu.make_async_copy(dense_out_ref, own_out, load_sem.at[len(loads)]))
    for load in loads:
        load.start()
    stack_small(router_ref, mixer_ref, small_stage, small_ref)
    g_load.start()
    for m in range(1, micro_count):
        g_buf[m, cut] = gy_ref[m]
    greet_all(cut_count, group_count)
    line = LineGather(h_all, far_send, far_recv, pair_send, pair_recv)
    g_line = LineGather(g_buf, g_far_send, g_far_recv, g_pair_send, g_pair_recv, direct=True)
    for m in range(micro_count):
        h_all[m, cut] = h_own_ref[m]
        line.start(m)

    square = group_count == 4

    def pass_copy(k):
        half = pl.ds(k * (share // 2), share // 2)
        return line_copy(
            beside_ref.at[1 - k, half, :], across_ref.at[half, :], weight_send.at[k], weight_recv.at[k],
            jnp.bitwise_xor(group, 1 + k), cut,
        )

    def beside_copy(k):
        return line_copy(
            expert_out_ref, beside_ref.at[k], weight_send.at[2 + k], weight_recv.at[2 + k], jnp.bitwise_xor(group, 1 + k),
            cut,
        )

    for k in range(2 if square else 0):
        beside_copy(k).start()
    for load in loads:
        load.wait()
    if not stored:
        d_sent = sent
    lanes = lax.broadcasted_iota(jnp.int32, (tile, 128), 1)

    def columns(m, level):
        both = [row_to_column(codes_ref[2 * level + k, m]) for k in range(2)]
        both = jnp.concatenate(both, axis=0).astype(jnp.int32)
        return both[:, 0:1], both[:, 1:2]

    def places(m, level):
        t = m * levels + level
        return (
            pl.ds(2 * level, 2), pl.ds(pl.multiple_of(t * tile, tile), tile), pl.ds(pl.multiple_of(t * slots, slots), slots)
        )

    def dense_step(i, carry):
        n, m = i // micro_count, i % micro_count
        level = line.take(m, n)
        blocks, here, spots = places(m, level)
        h_two = h_all[m, blocks].reshape(tile, features)
        chosen, spot = columns(m, level)
        gate, mix_dense, mix_expert, _, _ = route(tail_dot(h_two, small_ref[...]), chosen, expert_count)
        side_buf[here, :] = jnp.where(lanes == 0, mix_dense, mix_expert * gate)
        rows_sent = lead_dot(token_table(spot, expert_count * slots), h_two).astype(low)
        for e in range(expert_count):
            sent[e, spots, :] = rows_sent[e * slots : (e + 1) * slots]
        act, slope = gelu_pair(plain_dot(h_two, own_in[...]))
        pre_buf[here, :] = slope.astype(low)
        hidden_buf[here, :] = (mix_dense * act).astype(low)
        out_ref[m, blocks] = plain_dot(act.astype(low), own_out[...]).astype(low).reshape(2, rows, features)
        if square:
            @pl.when(i == levels * micro_count - 3)
            def _():
                for k in range(2):
                    beside_copy(k).wait()
                for k in range(2):
                    pass_copy(k).start()

        return carry

    lax.fori_loop(0, levels * micro_count, dense_step, 0)

    def beside(mask):
        return beside_ref.at[mask - 1]

    def load_at(i, mask, own=False, across=False):
        e = jnp.bitwise_xor(group, mask)
        src_in = expert_in_ref if own else weights_in_ref.at[e]
        src_out = expert_out_ref if own else across_ref if across else beside(mask) if square else weights_out_ref.at[e]
        return (
            pltpu.make_async_copy(src_in, in_buf.at[i % 2], in_sem.at[i % 2]),
            pltpu.make_async_copy(src_out, out_buf.at[i % 2], out_sem.at[i % 2]),
        )

    def load_start(i, mask, own=False, across=False):
        for load in load_at(i, mask, own, across):
            load.start()

    def load_wait(i):
        for load in load_at(i, 0, True):
            load.wait()

    load_start(0, 0, True)
    for m in range(1, micro_count):
        g_line.start(m)

    def forward_step(i, carry):
        @pl.when(i + 1 < expert_count - square)
        def _():
            load_start(i + 1, i + 1)

        if square:
            @pl.when(i == 2)
            def _():
                for k in range(2):
                    pass_copy(k).wait()
                load_start(3, 3, across=True)

        load_wait(i)
        e, at = jnp.bitwise_xor(group, i), i % 2
        act, slope = gelu_pair(plain_dot(sent[e], in_buf[at]))
        inner = act.astype(low)
        if stored:
            inner_buf[e] = inner
            slope_buf[e] = slope.astype(low)
        g_sent[e] = plain_dot(inner, out_buf[at]).astype(low)
        return carry

    lax.fori_loop(0, expert_count, forward_step, 0)

    def mask_at(i):
        return group_count - 1 - i

    load_start(0, mask_at(0), across=square)
    out_total = LineSum(out_ref, o_pair_buf, o_far_buf, o_line_send, o_line_recv, o_two_send, o_two_recv, direct=True)

    def mix_step(m, n, carry):
        if m:
            g_line.take_pair(m, n)

        level, _ = line.place(n)
        blocks, here, spots = places(m, level)
        _, spot = columns(m, level)
        table = token_table(spot, expert_count * slots)
        side = side_buf[here, :]
        mix_dense, mix_gate = side[:, 0:1], side[:, 1:2]
        grad_y = g_buf[m, blocks].reshape(tile, features).astype(f32)
        dense = out_ref[m, blocks].reshape(tile, features).astype(f32)
        part = plain_dot(table, jnp.concatenate([g_sent[e, spots, :] for e in range(expert_count)], axis=0))
        out_ref[m, blocks] = (mix_dense * dense + mix_gate * part).astype(low).reshape(2, rows, features)
        d_dense = jnp.sum(grad_y * dense, axis=-1, keepdims=True)
        d_part = jnp.sum(grad_y * part, axis=-1, keepdims=True)
        d_mix = jnp.where(lanes == 0, d_dense, d_part)
        for k in range(2):
            dots[2 * level + k, m] = jnp.transpose(d_mix[k * rows : (k + 1) * rows])[0:8]
        if m == 0:
            out_total.pair_copy(0, level).start()
        d_pre = tail_dot((mix_dense * grad_y).astype(low), own_out[...]) * pre_buf[here, :].astype(f32)
        d_pre = d_pre.astype(low)
        pre_buf[here, :] = d_pre
        back_buf[m, blocks] = tail_dot(d_pre, own_in[...]).astype(low).reshape(2, rows, features)
        rows_back = lead_dot(table, (mix_gate * grad_y).astype(low)).astype(low)
        for e in range(expert_count):
            g_sent[e, spots, :] = rows_back[e * slots : (e + 1) * slots]
        return carry

    def combine_step(m, k, carry):
        level = jnp.where(k % 2 == 0, levels - 1 - k // 2, k // 2)
        blocks, here, spots = places(m, level)
        if stored:
            spots = pl.ds(pl.multiple_of(level * slots, slots), slots)
        _, spot = columns(m, level)
        table = token_table(spot, expert_count * slots)
        rows_back = jnp.concatenate([d_sent[e, spots, :] for e in range(expert_count)], axis=0)
        back_rows = plain_dot(table, rows_back).reshape(2, rows, features)
        back_buf[m, blocks] = (back_buf[m, blocks].astype(f32) + back_rows).astype(low)
        total.pair_copy(m, level).start()
        return carry

    def input_step(m, i, carry):
        @pl.when(i + 2 < expert_count)
        def _():
            load_start(i + 1, mask_at(i + 1))

        @pl.when(i + 2 == expert_count)
        def _():
            load_start(i + 1, 0, True)

        load_wait(i)
        e, at = jnp.bitwise_xor(group, mask_at(i)), i % 2
        spots = pl.ds(m * levels * slots, levels * slots)
        d_pre = (tail_dot(g_sent[e, spots, :], out_buf[at]) * slope_buf[e, spots, :].astype(f32)).astype(low)
        slope_buf[e, spots, :] = d_pre
        d_sent[e] = tail_dot(d_pre, in_buf[at]).astype(low)
        return carry

    total = LineSum(back_buf, pair_buf, far_buf, line_send, line_recv, two_send, two_recv)
    g_load.wait()
    out_keep = pltpu.make_async_copy(out_ref.at[pl.ds(1, micro_count - 1)], out_rest_ref, out_sem.at[2])
    for m in range(micro_count):
        if m:
            for n in range(1, levels):
                g_line.receive(m, n)
        lax.fori_loop(0, levels, partial(mix_step, m), 0)
        if m == 0:
            out_total.pairs(0)
        if stored:
            lax.fori_loop(0, expert_count, partial(input_step, m), 0)
            if m + 1 < micro_count:
                load_start(0, mask_at(0), across=square)
            lax.fori_loop(0, levels, partial(combine_step, m), 0)
            total.pairs(m)
    out_keep.start()

    def dot_copy(hop):
        target = jnp.bitwise_xor(cut, hop)
        return line_copy(dots.at[target], dots_in.at[hop - 1], dot_send.at[hop - 1], dot_recv.at[hop - 1], group, target)

    for hop in range(1, cut_count):
        dot_copy(hop).start()

    in_stage, out_stage = own_in, own_out

    def keep_in(i):
        return pltpu.make_async_copy(in_stage, d_in_ref.at[jnp.bitwise_xor(group, mask_at(i))], stage_sem.at[0])

    def keep_out(i):
        return pltpu.make_async_copy(out_stage, d_out_ref.at[jnp.bitwise_xor(group, mask_at(i))], stage_sem.at[1])

    def early_copy(kind):
        src, dst = ((d_in_ref, got_in_ref), (d_out_ref, got_out_ref))[kind]
        return line_copy(
            src.at[jnp.bitwise_xor(group, 3)], dst, early_send.at[kind], early_recv.at[kind],
            jnp.bitwise_xor(group, 1 + kind), cut,
        )

    def keep_step(i):
        @pl.when(i > 0)
        def _():
            keep_in(i).wait()
            keep_out(i).wait()

        if early:
            @pl.when(i == 1)
            def _():
                early_copy(0).start()
                early_copy(1).start()

    def weight_step(i, carry):
        e = jnp.bitwise_xor(group, mask_at(i))
        keep_step(i)
        in_stage[...] = lead_dot(sent[e], slope_buf[e]).astype(low)
        keep_in(i).start()
        out_stage[...] = lead_dot(inner_buf[e], g_sent[e]).astype(low)
        keep_out(i).start()
        for j in range(levels - 1):
            @pl.when(i == j + 1)
            def _():
                total.hop(0, j)

        return carry

    def backward_step(i, carry):
        @pl.when(i + 2 < expert_count)
        def _():
            load_start(i + 1, mask_at(i + 1))

        @pl.when(i + 2 == expert_count)
        def _():
            load_start(i + 1, 0, True)

        load_wait(i)
        e, at = jnp.bitwise_xor(group, mask_at(i)), i % 2
        rows_in, rows_back = sent[e], g_sent[e]
        act, slope = gelu_pair(plain_dot(rows_in, in_buf[at]))
        d_pre = (tail_dot(rows_back, out_buf[at]) * slope).astype(low)
        keep_step(i)
        in_stage[...] = lead_dot(rows_in, d_pre).astype(low)
        keep_in(i).start()
        out_stage[...] = lead_dot(act.astype(low), rows_back).astype(low)
        keep_out(i).start()
        d_sent[e] = tail_dot(d_pre, in_buf[at]).astype(low)
        return carry

    if stored:
        lax.fori_loop(0, expert_count, weight_step, 0)
    else:
        lax.fori_loop(0, expert_count, backward_step, 0)
        for m in range(micro_count):
            lax.fori_loop(0, levels, partial(combine_step, m), 0)
            total.pairs(m)
    token_rows = micro_count * cut_count * rows
    h_flat, g_flat = h_all.reshape(token_rows, features), g_buf.reshape(token_rows, features)

    def dense_weights(k):
        part = pl.ds(k * 256, 256)
        in_buf[0, part, :] = lead_dot(h_flat[:, part], pre_buf[...]).astype(low)
        out_buf[0, :, part] = lead_dot(hidden_buf[...], g_flat[:, part]).astype(low)

    slices = features // 256
    for k in range(slices):
        dense_weights(k)
        if k == 0 and not stored:
            for j in range(levels - 1):
                total.hop(0, j)
        if k == slices // 2:
            for m in range(1, micro_count):
                total.hop(m, 0)
    own_keep = (
        pltpu.make_async_copy(in_buf.at[0], d_own_in_ref, in_sem.at[0]),
        pltpu.make_async_copy(out_buf.at[0], d_own_out_ref, out_sem.at[0]),
    )
    for keep in own_keep:
        keep.start()
    for m in range(1, micro_count):
        for j in range(1, levels - 1):
            total.hop(m, j)
    sums = dots[cut]
    for hop in range(1, cut_count):
        dot_copy(hop).wait()
        sums = sums + dots_in[hop - 1]
    sums_ref[...] = sums
    keep_in(0).wait()
    keep_out(0).wait()
    for kind in range(2 if early else 0):
        early_copy(kind).wait()
    for keep in own_keep:
        keep.wait()
    out_keep.wait()
    for m in range(micro_count):
        line.finish(m)
        if m:
            g_line.finish(m)
    out_total.finish(0, dh_ref)
    output_ref[...] = (x_two_ref[0] + dh_ref[0]).astype(low)
    for m in range(micro_count):
        total.finish(m, dh_ref)


def feed(
    x_two, h_own, gy, g_first, router, mixer, codes, dense_in, dense_out, weights_in, weights_out, expert_in,
    expert_out, share, slots, strided, early, call_id,
):
    micro_count, rows, features = x_two.shape
    cut_count = codes.shape[0]
    group_count = weights_in.shape[0]
    levels, total = cut_count // 2, micro_count * cut_count * rows
    low, f32 = jnp.bfloat16, jnp.float32
    shape = jax.ShapeDtypeStruct
    dma = pltpu.SemaphoreType.DMA
    block = lambda *dims: pltpu.VMEM(dims, low)
    vmem, far = pl.BlockSpec(memory_space=pltpu.VMEM), pl.BlockSpec(memory_space=pl.ANY)
    whole = (micro_count, cut_count, rows, features)
    stored = group_count <= 4
    slot_rows = micro_count * levels * slots
    line = (micro_count, levels)
    return pl.pallas_call(
        partial(feed_kernel, slots, strided, early, stored),
        out_shape=(
            shape((rows, features), low),
            shape((micro_count, rows, features), f32),
            shape((micro_count, 8, rows), f32),
            shape((features, share), low),
            shape((share, features), low),
            shape((group_count, features, share), low),
            shape((group_count, share, features), low),
            shape((2, share, features) if group_count == 4 else (16, 128), low),
            shape((share, features) if group_count == 4 else (16, 128), low),
            *(
                (shape((features, share), low), shape((share, features), low))
                if early else (shape((8, 128), low), shape((8, 128), low))
            ),
            shape((micro_count - 1, cut_count, rows, features), low),
        ),
        in_specs=[vmem, vmem, vmem, far, vmem, vmem, vmem, far, far, far, far, far, far],
        out_specs=[vmem] * 3 + [far] * 9,
        scratch_shapes=[
            block(*whole), block(*whole),
            block(group_count, slot_rows, features), block(group_count, slot_rows, features),
            block(group_count, slot_rows // micro_count, features) if stored else block(16, 128),
            block(total, share), block(total, share), block(*whole), pltpu.VMEM((total, 128), f32),
            block(features, share), block(share, features), block(2, features, share), block(2, share, features),
            *([block(group_count, slot_rows, share)] * 2 if stored else [block(16, 128)] * 2),
            pltpu.VMEM((cut_count, micro_count, 8, rows), f32), pltpu.VMEM((cut_count - 1, micro_count, 8, rows), f32),
            block(*line, rows, features), block(micro_count, levels + 1, rows, features),
            block(1, levels, rows, features), block(1, levels + 1, rows, features), block(*whole),
            pltpu.VMEM((128, features), f32), block(128, features),
            *[dma((micro_count, levels + 1)), dma(line), dma(line), dma(line)] * 2,
            *[dma(line), dma(line), dma(line), dma((micro_count, levels + 1))] * 2,
            dma((3 + 2 * group_count,)), dma((2,)), dma((3,)), dma((2,)),
            dma((cut_count - 1,)), dma((cut_count - 1,)), dma((4,)), dma((4,)), dma((4,)), dma((4,)),
        ],
        compiler_params=pltpu.CompilerParams(collective_id=call_id, has_side_effects=True, vmem_limit_bytes=62 * 2**20),
    )(x_two, h_own, gy, g_first, router, mixer, codes, dense_in, dense_out, weights_in, weights_out, expert_in, expert_out)


def attend_back_one(heads, m, qkv_ref, docs_ref, docs_col_ref, lse_ref, back_ref, out_ref, key_acc, value_acc):
    length, width = back_ref.shape[1], back_ref.shape[2]
    rows = min(256, length)
    masks = head_masks(width, heads)
    key_acc[...] = jnp.zeros_like(key_acc)
    value_acc[...] = jnp.zeros_like(value_acc)
    zero = jnp.bfloat16(0)
    for block in range(length // rows):
        start, keys = block * rows, (block + 1) * rows
        allowed = allowed_mask(docs_ref, docs_col_ref, m, start, rows, keys)
        query = qkv_ref[m, pl.ds(start, rows), 0:width] * jnp.bfloat16(score_scale)
        key = qkv_ref[m, 0:keys, width : 2 * width]
        value = qkv_ref[m, 0:keys, 2 * width : 3 * width]
        back = back_ref[m, pl.ds(start, rows), :]
        logs = lse_ref[m, pl.ds(start, rows), :]
        query_grad = jnp.zeros((rows, width), jnp.float32)
        for h, mask in enumerate(masks):
            one_query = jnp.where(mask, query, zero)
            one_back = jnp.where(mask, back, zero)
            scores = jnp.where(allowed, tail_dot(one_query, key), masked_value)
            spot = h * (width // heads)
            probs = jnp.exp(scores - logs[:, spot : spot + 1])
            weighted = probs * tail_dot(one_back, value)
            delta = jnp.sum(weighted, axis=-1, keepdims=True)
            score_grad = (weighted - probs * delta).astype(jnp.bfloat16)
            query_grad = jnp.where(mask, plain_dot(score_grad, key), query_grad)
            key_acc[0:keys, :] += lead_dot(score_grad, one_query)
            value_acc[0:keys, :] += lead_dot(probs.astype(jnp.bfloat16), one_back)
        out_ref[m, pl.ds(start, rows), 0:width] = (query_grad * score_scale).astype(jnp.bfloat16)
    out_ref[m, :, width : 2 * width] = key_acc[...].astype(jnp.bfloat16)
    out_ref[m, :, 2 * width : 3 * width] = value_acc[...].astype(jnp.bfloat16)


def back_kernel(
    heads, expert_count, sums_here,
    dh_ref, dots_ref, codes_ref, h_ref, x_two_ref, gy_ref, att_ref, w_out_ref, docs_ref,
    x_ref, gain_one_ref, gain_two_ref, router_ref, mixer_ref, own_in_ref, own_out_ref,
    qkv_far, lse_far, w_qkv_far, h_all_far, out_part, w_query_ref, w_key_ref, w_value_ref, d_in_ref, d_out_ref,
    got_in_ref, got_out_ref,
    output_ref, tokens_ref, wo_ref, tiny_ref, query_out_ref, key_out_ref, value_out_ref, in_out_ref, out_out_ref, late_in_ref,
    late_out_ref, direct_in_ref, direct_out_ref,
    qkv_ref, lse_ref, w_qkv_ref, h_all_ref, w_rows, docs_stage, docs_col_ref, small_stage, small_ref, out_own, out_pair,
    out_far, g_att, d_att, back_all, d_qkv, key_acc, value_acc, d_small, part, pair_buf, far_buf, d_h_one, in_sum, out_sum,
    wo_part, qkv_part, wo_in, qkv_in, own_in_got, own_out_got, own_in_sum, own_out_sum, own_in_in, own_out_in, wo_mid, wo_pair, wo_far, wo_sum, qkv_mid, in_mid, qkv_end, in_end,
    pair_send, pair_recv, far_send, far_recv, swap_send, swap_recv, swap_own, one_send, one_recv, two_send, two_recv, two_own,
    late_send, late_recv, late_load_sem, load_sem,
    wo_pair_send, wo_pair_recv, wo_far_send, wo_far_recv, own_sem, o_pair_send, o_pair_recv, o_far_send, o_far_recv,
    direct_send, direct_recv, own_send, own_recv,
):
    micro_count, cut_count, rows, features = part.shape
    group_count, split, _ = qkv_part.shape[:3]
    piece_rows = qkv_part.shape[2]
    group_rows = split * piece_rows
    sides, side_rows = wo_part.shape[1:3]
    width = features // cut_count
    cut = lax.axis_index("cuts")
    group = lax.axis_index("expert")
    low, f32 = jnp.bfloat16, jnp.float32
    levels = cut_count // 2
    place = (group * cut_count + cut) * piece_rows
    loads = [
        pltpu.make_async_copy(src, dst, load_sem.at[k])
        for k, (src, dst) in enumerate(
            ((qkv_far, qkv_ref), (lse_far, lse_ref), (w_qkv_far, w_qkv_ref), (h_all_far, h_all_ref))
        )
    ]
    if sums_here:
        own_rows = pl.ds(pl.multiple_of(place, piece_rows), piece_rows)
        for k, ref in enumerate((w_query_ref, w_key_ref, w_value_ref)):
            loads.append(pltpu.make_async_copy(ref.at[own_rows, :], w_rows.at[k], load_sem.at[4 + k]))
    for load in loads:
        load.start()

    rest = micro_count - 1

    def own_load(m, level):
        return pltpu.make_async_copy(out_part.at[m, 2 * level + cut % 2], out_own.at[m, level], own_sem.at[m, level])

    for m in range(rest):
        for level in range(levels):
            own_load(m, level).start()
    stack_small(router_ref, mixer_ref, small_stage, small_ref)
    fill_docs(docs_ref, docs_stage, docs_col_ref)
    greet_all(cut_count, group_count if sums_here else 1)
    out_line = LineSum(out_part, out_pair, out_far, o_pair_send, o_pair_recv, o_far_send, o_far_recv, out_own, direct=True)

    ones = (None, None, (wo_part, wo_in), (qkv_part, qkv_in))

    def one_copy(kind, hop):
        src, dst = ones[kind]
        target = jnp.bitwise_xor(group, hop)
        return line_copy(
            src.at[target, cut % 2] if kind == 2 else src.at[target], dst.at[hop - 1], one_send.at[kind, hop - 1], one_recv.at[kind, hop - 1], target, cut
        )

    def one_start(kind):
        for hop in range(1, group_count):
            one_copy(kind, hop).start()

    def one_finish(kind):
        src, dst = ones[kind]
        total = (src[group, cut % 2] if kind == 2 else src[group]).astype(f32)
        for hop in range(1, group_count):
            one_copy(kind, hop).wait_recv()
            total = total + dst[hop - 1].astype(f32)
        for hop in range(1, group_count):
            one_copy(kind, hop).wait_send()
        return total

    owns = (
        (own_in_ref, own_in_got, own_in_sum, own_in_in, 1), (own_out_ref, own_out_got, own_out_sum, own_out_in, 2)
    )

    def own_first(kind, k):
        own, got, _, _, side = owns[kind]
        return line_copy(
            own.at[jnp.bitwise_xor(group, 3 if k else side)], got.at[k], own_send.at[kind, k], own_recv.at[kind, k],
            jnp.bitwise_xor(group, side), cut,
        )

    def own_second(kind):
        _, _, total, far, side = owns[kind]
        return line_copy(
            total, far, own_send.at[kind, 2], own_recv.at[kind, 2], jnp.bitwise_xor(group, 3 - side), cut
        )

    def own_start(kind):
        own, got, total, _, side = owns[kind]
        own_first(kind, 1).wait()
        total[...] = (own[jnp.bitwise_xor(group, 3 - side)].astype(f32) + got[1].astype(f32)).astype(low)
        own_second(kind).start()

    def own_finish(kind):
        own, got, _, far, _ = owns[kind]
        own_first(kind, 0).wait()
        own_second(kind).wait()
        return own[group].astype(f32) + got[0].astype(f32) + far[...].astype(f32)

    twos = ((in_mid, in_end), None, None, (qkv_mid, qkv_end))

    def two_copy(kind, hop):
        src, dst = twos[kind]
        target = jnp.bitwise_xor(cut, hop)
        return line_copy(src.at[target], dst.at[cut], two_send.at[kind, hop], two_recv.at[kind, hop], group, target)

    def two_keep(kind):
        src, dst = twos[kind]
        return pltpu.make_async_copy(src.at[cut], dst.at[cut], two_own.at[kind])

    def two_start(kind):
        for hop in range(cut_count - 1, 0, -1):
            two_copy(kind, hop).start()
        two_keep(kind).start()

    def two_finish(kind):
        for hop in range(cut_count - 1, 0, -1):
            two_copy(kind, hop).wait()
        two_keep(kind).wait()

    ends = ((d_in_ref, got_in_ref, in_sum, late_in_ref, 2), (d_out_ref, got_out_ref, out_sum, late_out_ref, 1))

    def late_load(kind, k):
        own, got, total, _, side = ends[kind]
        src = got if k else own.at[jnp.bitwise_xor(group, side)]
        return pltpu.make_async_copy(src, total.at[k], late_load_sem.at[kind, k])

    def late_copy(kind):
        _, _, total, late, side = ends[kind]
        return line_copy(
            total.at[0], late, late_send.at[kind], late_recv.at[kind], jnp.bitwise_xor(group, side), cut
        )

    if sums_here:
        for kind in range(2):
            late_load(kind, 0).start()
            late_load(kind, 1).start()
        for k in (1, 0):
            for kind in range(2):
                own_first(kind, k).start()

    def swap_copy(m, hop):
        target = jnp.bitwise_xor(cut, hop)
        return line_copy(
            d_att.at[m, :, pl.ds(pl.multiple_of(target * width, width), width)],
            back_all.at[m, pl.ds(pl.multiple_of(cut * rows, rows), rows), :],
            swap_send.at[m, hop], swap_recv.at[m, hop], group, target,
        )

    def swap_keep(m):
        return pltpu.make_async_copy(
            d_att.at[m, :, pl.ds(pl.multiple_of(cut * width, width), width)],
            back_all.at[m, pl.ds(pl.multiple_of(cut * rows, rows), rows), :],
            swap_own.at[m],
        )

    small = small_ref[...]
    gain_one, gain_two = one_row(gain_one_ref), one_row(gain_two_ref)
    d_small[...] = jnp.zeros_like(d_small)
    lanes = lax.broadcasted_iota(jnp.int32, (rows, 128), 1)

    def norm_two_step(m, carry):
        dots = jnp.transpose(dots_ref[m])
        chosen = row_to_column(codes_ref[cut, m])[:, 0:1].astype(jnp.int32)
        h_two = h_ref[m]
        gate, _, mix_expert, routed, mixing = route(tail_dot(h_two, small), chosen, expert_count)
        d_mixing = jnp.where(lanes == expert_count, dots[:, 0:1], gate * dots[:, 1:2])
        d_gate = jnp.where(lanes == chosen, mix_expert * dots[:, 1:2], 0.0)
        d_logits = (softmax_back(mixing, d_mixing) + softmax_back(routed, d_gate)).astype(low)
        d_h = dh_ref[m] + plain_dot(d_logits, small)
        normed, scale = norm_parts(x_two_ref[m])
        one_lane = (lanes == expert_count + 2).astype(low)
        d_small[...] += lead_dot(h_two, d_logits) + lead_dot((d_h * normed).astype(low), one_lane)
        d_x = gy_ref[m].astype(f32) + norm_back(normed, scale, gain_two, d_h)
        tokens_ref[m] = d_x
        grad = d_x.astype(low)
        g_att[pl.ds(pl.multiple_of(m * rows, rows), rows), :] = grad
        d_att[m] = tail_dot(grad, w_out_ref[...]).astype(low)
        for hop in range(cut_count - 1, 0, -1):
            swap_copy(m, hop).start()
        swap_keep(m).start()
        return carry

    lax.fori_loop(0, micro_count, norm_two_step, 0)
    for m in range(rest):
        out_line.start(m)

    def wo_step(g, carry):
        columns = pl.ds(pl.multiple_of(g * group_rows, group_rows), group_rows)
        grads = lead_dot(att_ref[:, columns], g_att[...]).astype(low)
        smalls = d_small[columns, :].astype(low)
        for side in range(sides):
            for k in range(side_rows):
                part_rows = slice((k * sides + side) * piece_rows, (k * sides + side + 1) * piece_rows)
                wo_part[g, side, k, :, 0:features] = grads[part_rows]
                wo_part[g, side, k, :, features : features + 128] = smalls[part_rows]
        return carry

    lax.fori_loop(0, group_count, wo_step, 0)
    def wo_pair_copy(g):
        return line_copy(
            wo_part.at[g, 1 - cut % 2], wo_pair.at[g], wo_pair_send.at[g], wo_pair_recv.at[g], group,
            jnp.bitwise_xor(cut, 1),
        )

    def wo_pair_step(g, carry):
        wo_pair_copy(g).wait()
        wo_part[g, cut % 2] = (wo_part[g, cut % 2].astype(f32) + wo_pair[g].astype(f32)).astype(low)
        return carry

    def direct_copy(kind):
        src, dst = ((d_in_ref, direct_in_ref), (d_out_ref, direct_out_ref))[kind]
        target = jnp.bitwise_xor(group, 1 + kind)
        return line_copy(src.at[target], dst, direct_send.at[kind], direct_recv.at[kind], target, cut)

    if sums_here:
        for g in range(group_count):
            wo_pair_copy(g).start()
        lax.fori_loop(0, group_count, wo_pair_step, 0)
        one_start(2)
        for kind in range(2):
            own_start(kind)
        for kind in range(2):
            direct_copy(kind).start()
    for load in loads[:3]:
        load.wait()
    line = LineSum(part, pair_buf, far_buf, pair_send, pair_recv, far_send, far_recv)

    def attend_step(m, carry):
        for hop in range(cut_count - 1, 0, -1):
            swap_copy(m, hop).wait()
        swap_keep(m).wait()

        @pl.when(m == 0)
        def _():
            for k in range(rest):
                for level in range(levels):
                    own_load(k, level).wait()
                out_line.pairs(k)

        attend_back_one(heads, m, qkv_ref, docs_ref, docs_col_ref, lse_ref, back_all, d_qkv, key_acc, value_acc)
        for c in range(cut_count):
            part[m, c] = tail_dot(d_qkv[m, c * rows : (c + 1) * rows, :], w_qkv_ref[...]).astype(low)
        line.start(m)
        line.pairs(m)
        return carry

    lax.fori_loop(0, micro_count, attend_step, 0)

    def qkv_step(g, carry):
        columns = pl.ds(pl.multiple_of(g * group_rows, group_rows), group_rows)
        grads = jnp.zeros((group_rows, 3 * width), f32)
        for m in range(micro_count):
            grads = grads + lead_dot(h_all_ref[m, :, columns], d_qkv[m])
        qkv_part[g] = grads.astype(low).reshape(split, piece_rows, 3 * width)
        return carry

    for j in range(levels - 1):
        line.hop(0, j)
    for load in loads[3:]:
        load.wait()
    lax.fori_loop(0, group_count, qkv_step, 0)
    if sums_here:
        one_start(3)
        for kind in range(2):
            total = ends[kind][2]
            late_load(kind, 0).wait()
            late_load(kind, 1).wait()
            total[0] = (total[0].astype(f32) + total[1].astype(f32)).astype(low)
            late_copy(kind).start()
    for m in range(1, micro_count):
        for j in range(levels - 1):
            line.hop(m, j)

    def norm_one_step(m, carry):
        line.finish(m, d_h_one)
        total = d_h_one[m]
        normed, scale = norm_parts(x_ref[m].astype(f32))
        tokens_ref[m] = tokens_ref[m] + norm_back(normed, scale, gain_one, total)
        return carry

    for m in range(rest):
        out_line.finish(m, d_h_one)
        output_ref[m] = (x_two_ref[1 + m] + d_h_one[m]).astype(low)
    if not sums_here:
        lax.fori_loop(0, micro_count, norm_one_step, 0)
        wo_ref[...] = wo_part[...]
        query_out_ref[...] = qkv_part[...]
        return
    in_mid[...] = own_finish(0).astype(low)
    two_start(0)
    wo_line = LineSum(None, wo_mid, wo_far, None, None, wo_far_send, wo_far_recv)
    wo_mid[0] = one_finish(2).astype(low)
    for k in range(levels):
        wo_line.first(0, levels - 1 - k // 2 if k % 2 == 0 else k // 2)
    norm_one_step(0, 0)
    qkv_mid[...] = one_finish(3).astype(low)
    two_start(3)
    out_out_ref[...] = own_finish(1)
    for j in range(levels - 1):
        wo_line.hop(0, j)
    for m in range(1, micro_count):
        norm_one_step(m, 0)
    two_finish(0)
    share_piece = in_end.shape[2] // group_count
    for c in range(cut_count):
        for g in range(group_count):
            spot = (g * cut_count + c) * share_piece
            in_out_ref[:, spot : spot + share_piece] = in_end[c, :, g * share_piece : (g + 1) * share_piece].astype(f32)
    wo_line.finish(0, wo_sum)
    wo_ref[...] = wo_sum[0, :, :features]
    small_sums = wo_sum[0, :, features:]
    two_finish(3)
    norm = jnp.zeros((piece_rows, 1), f32)
    outs = (query_out_ref, key_out_ref, value_out_ref)
    for c in range(cut_count):
        for k in range(3):
            grad = qkv_end[c, :, k * width : (k + 1) * width].astype(f32)
            outs[k][:, c * width : (c + 1) * width] = grad
            weights = w_rows[k, :, c * width : (c + 1) * width].astype(f32)
            norm = norm + jnp.sum(grad * weights, axis=-1, keepdims=True)
    spots = lax.broadcasted_iota(jnp.int32, (piece_rows, features), 1)
    mine = spots == place + lax.broadcasted_iota(jnp.int32, (piece_rows, features), 0)
    norm = norm / jnp.sum(jnp.where(mine, gain_one, 0.0), axis=-1, keepdims=True)
    tiny_lanes = lax.broadcasted_iota(jnp.int32, (piece_rows, 128), 1)
    tiny_ref[...] = jnp.where(tiny_lanes == expert_count + 3, norm, small_sums)
    for kind in range(2):
        late_copy(kind).wait()
        direct_copy(kind).wait()


def back(
    dh, dots, codes, h_two, x_two, gy, attended, w_output, docs, x, gain_one, gain_two, router, mixer, own_in, own_out,
    qkv, lse, w_qkv, h_all, out_rest, w_query, w_key, w_value, d_in, d_out, got_in, got_out, heads, expert_count, sums_here,
    call_id,
):
    micro_count, rows, features = x.shape
    length = qkv.shape[1]
    cut_count = length // rows
    width = features // cut_count
    group_count = own_out.shape[0]
    piece_rows = features // (group_count * cut_count)
    share, piece = own_in.shape[3], own_out.shape[1]
    low, f32 = jnp.bfloat16, jnp.float32
    levels = cut_count // 2
    wide = features + 128
    shape = jax.ShapeDtypeStruct
    parts = (group_count, 2, levels, piece_rows) if sums_here else (features // 256, 1, 1, 256)
    flat = (group_count, cut_count, piece_rows) if sums_here else (features // 256, 1, 256)
    tokens = (micro_count, rows, features)
    none = shape((16, 128), low)
    if sums_here:
        outs = (
            shape((micro_count - 1, rows, features), low),
            shape(tokens, f32), shape((piece_rows, features), f32), shape((piece_rows, 128), f32),
            *[shape((piece_rows, features), f32)] * 3, shape((piece_rows, share * cut_count), f32),
            shape((piece, features), f32), *[shape((features, share), low), shape((share, features), low)] * 2,
        )
    else:
        outs = (
            shape((micro_count - 1, rows, features), low),
            shape(tokens, f32), shape((*parts, wide), low), none, shape((*flat, 3 * width), low),
            *[none] * 8,
        )
    peers = max(group_count - 1, 1) if sums_here else 1
    block = lambda *dims: pltpu.VMEM(dims, low)
    mids = lambda w: block(cut_count, piece_rows, w) if sums_here else block(16, 128)
    ins = lambda w: block(peers, cut_count, piece_rows, w) if sums_here else block(16, 128)
    dma = pltpu.SemaphoreType.DMA
    line = (micro_count, levels)
    vmem, far = pl.BlockSpec(memory_space=pltpu.VMEM), pl.BlockSpec(memory_space=pl.ANY)
    operands = (
        dh, dots, codes, h_two, x_two, gy, attended, w_output, docs, x, gain_one, gain_two, router, mixer, own_in, own_out,
        qkv, lse, w_qkv, h_all, out_rest, w_query, w_key, w_value, d_in, d_out, got_in, got_out,
    )
    rest = (micro_count - 1, levels)
    return pl.pallas_call(
        partial(back_kernel, heads, expert_count, sums_here),
        out_shape=outs,
        in_specs=[vmem] * 16 + [far] * 12,
        out_specs=[vmem] * 9 + [far] * 4,
        scratch_shapes=[
            block(micro_count, length, 3 * width), pltpu.VMEM((micro_count, length, width), f32), block(features, 3 * width),
            block(micro_count, length, features), block(3, piece_rows, features), pltpu.VMEM((8, length), f32),
            pltpu.VMEM((micro_count, length, 1), jnp.int32), pltpu.VMEM((128, features), f32), block(128, features),
            block(*rest, rows, features), block(*rest, rows, features), block(micro_count - 1, levels + 1, rows, features),
            block(micro_count * rows, features),
            block(micro_count, rows, features),
            block(micro_count, length, width),
            block(micro_count, length, 3 * width),
            pltpu.VMEM((length, width), f32),
            pltpu.VMEM((length, width), f32),
            pltpu.VMEM((features, 128), f32),
            block(micro_count, cut_count, rows, features),
            block(*line, rows, features),
            block(micro_count, levels + 1, rows, features),
            pltpu.VMEM(tokens, f32),
            *((block(2, features, share), block(2, share, features)) if sums_here else (block(16, 128), block(16, 128))),
            block(*parts, wide),
            block(*flat, 3 * width),
            block(peers, levels, piece_rows, wide) if sums_here else block(16, 128), ins(3 * width),
            *(
                [block(2, cut_count, piece_rows, share), block(2, piece, features)]
                + [block(cut_count, piece_rows, share), block(piece, features)] * 2
                if sums_here else [block(16, 128)] * 6
            ),
            *(
                (
                    block(1, levels, piece_rows, wide), block(group_count, levels, piece_rows, wide),
                    block(1, levels + 1, piece_rows, wide), pltpu.VMEM((1, piece_rows, wide), f32),
                )
                if sums_here else [block(16, 128)] * 4
            ),
            mids(3 * width), mids(share), mids(3 * width), mids(share),
            dma(line), dma(line), dma(line), dma((micro_count, levels + 1)),
            dma((micro_count, cut_count)), dma((micro_count, cut_count)), dma((micro_count,)),
            dma((4, peers)), dma((4, peers)), dma((4, cut_count)), dma((4, cut_count)), dma((4,)),
            dma((2,)), dma((2,)), dma((2, 2)), dma((7,)),
            dma((group_count,)), dma((group_count,)), dma((1, levels)), dma((1, levels + 1)),
            dma(rest), dma(rest), dma(rest), dma(rest), dma((micro_count - 1, levels + 1)),
            dma((2,)), dma((2,)), dma((2, 3)), dma((2, 3)),
        ],
        compiler_params=pltpu.CompilerParams(
            collective_id=call_id, has_side_effects=True, vmem_limit_bytes=62 * 2**20
        ),
    )(*operands)


def last_kernel(
    expert_count, d_in_ref, got_in_ref, late_in_ref, d_out_ref, got_out_ref, late_out_ref, tiny_ref, *refs,
):
    passed = (len(refs) - 6 - 10 - 1) // 3
    given, refs = refs[: passed + 1], refs[passed + 1 :]
    taken, refs = refs[:passed], refs[passed:]
    held, refs = refs[-passed:], refs[:-passed]
    router_ref, mixer_ref, norm_one_ref, norm_two_ref, sum_in_ref, sum_out_ref = refs[:6]
    in_buf, out_buf, in_sum, out_sum, in_sem, out_sem, in_done, out_done, pass_sem, keep_sem = refs[6:]
    group = lax.axis_index("expert")
    held_parts = (held[0].at[0], held[0].at[pl.ds(1, held[0].shape[0] - 1)], *held[1:])
    passes = [pltpu.make_async_copy(src, dst, pass_sem.at[k]) for k, (src, dst) in enumerate(zip(given, held_parts))]
    keeps = [pltpu.make_async_copy(src, dst, keep_sem.at[k]) for k, (src, dst) in enumerate(zip(held, taken))]
    chunks = in_sem.shape[0]
    work = []
    for ends in (
        ((d_in_ref.at[group], got_in_ref, late_in_ref), in_buf, in_sum, sum_in_ref, in_sem, in_done),
        ((d_out_ref.at[group], got_out_ref, late_out_ref), out_buf, out_sum, sum_out_ref, out_sem, out_done),
    ):
        sources, buf, total, target, sem, done = ends
        step = buf.shape[1] // chunks
        for k in range(chunks):
            part = pl.ds(k * step, step)
            loads = [
                pltpu.make_async_copy(src.at[part, :], buf.at[at, part, :], sem.at[k, at]) for at, src in enumerate(sources)
            ]
            work.append((loads, buf, total, part, pltpu.make_async_copy(total.at[part, :], target.at[part, :], done.at[k])))
    for copy in passes:
        copy.start()
    for loads, *_ in work:
        for load in loads:
            load.start()
    turned = jnp.transpose(tiny_ref[...])
    router_ref[...] = turned[0:expert_count]
    mixer_ref[...] = turned[expert_count : expert_count + 2]
    norm_two_ref[...] = turned[expert_count + 2 : expert_count + 3]
    norm_one_ref[...] = turned[expert_count + 3 : expert_count + 4]
    passes[0].wait()
    for copy, keep in zip(passes[1:], keeps):
        copy.wait()
        keep.start()
    for loads, buf, total, part, keep in work:
        for load in loads:
            load.wait()
        total[part, :] = sum(buf[at, part, :].astype(jnp.float32) for at in range(3))
        keep.start()
    for *_, keep in work:
        keep.wait()
    for keep in keeps:
        keep.wait()


def last(d_in, got_in, late_in, d_out, got_out, late_out, tiny, others, expert_count):
    f32, dma = jnp.float32, pltpu.SemaphoreType.DMA
    shape = jax.ShapeDtypeStruct
    piece_rows = tiny.shape[0]
    micro_count = 1 + others[1].shape[0]
    whole = [shape((micro_count, *others[0].shape), others[0].dtype), *[shape(x.shape, x.dtype) for x in others[2:]]]
    vmem, far = pl.BlockSpec(memory_space=pltpu.VMEM), pl.BlockSpec(memory_space=pl.ANY)
    chunks = 4
    return pl.pallas_call(
        partial(last_kernel, expert_count),
        out_shape=(
            *whole, shape((expert_count, piece_rows), f32), shape((2, piece_rows), f32),
            shape((1, piece_rows), f32), shape((1, piece_rows), f32), shape(late_in.shape, f32), shape(late_out.shape, f32),
        ),
        in_specs=[far] * 6 + [vmem] + [far] * len(others),
        out_specs=[far] * len(whole) + [vmem] * 4 + [far] * 2,
        scratch_shapes=[
            pltpu.VMEM((3, *late_in.shape), late_in.dtype), pltpu.VMEM((3, *late_out.shape), late_out.dtype),
            pltpu.VMEM(late_in.shape, f32), pltpu.VMEM(late_out.shape, f32),
            dma((chunks, 3)), dma((chunks, 3)), dma((chunks,)), dma((chunks,)), dma((len(others),)), dma((len(others),)),
            *[pltpu.VMEM(x.shape, x.dtype) for x in whole],
        ],
        compiler_params=pltpu.CompilerParams(vmem_limit_bytes=62 * 2**20),
    )(d_in, got_in, late_in, d_out, got_out, late_out, tiny, *others)


def local(
    tokens, cotangent, segments, expert_ids, slot_ids, kept_mask, norm1_gain, w_query, w_key, w_value, w_output,
    norm2_gain, dense_in, dense_out, router, mixer, expert_in, expert_out,
):
    micro_count, row_count, features = tokens.shape[1:]
    cut_count = lax.axis_size("cuts")
    group_count = lax.axis_size("expert")
    cut = lax.axis_index("cuts")
    group = lax.axis_index("expert")
    length = cut_count * row_count
    head_width = features // cut_count
    heads = head_width // 64
    expert_count = router.shape[1]
    hidden_count = dense_in.shape[1]
    share = hidden_count // cut_count
    piece = share // group_count
    capacity = max(2, row_count * 5 // (4 * expert_count))
    slots = tile_slots(capacity, row_count, 2 * row_count)
    rows = features // (group_count * cut_count)
    sums_here = rows % 16 == 0 and group_count == 4
    by_rows = lambda v: v.reshape(-1, 128)
    router_t, mixer_t = router.T, mixer.T
    f32, low = jnp.float32, jnp.bfloat16

    strided = piece % 128 == 0
    if strided:
        own_in, own_out = dense_in, dense_out
    else:
        own_in = lax.dynamic_index_in_dim(
            dense_in.reshape(features, group_count, cut_count, piece), cut, 2, keepdims=False
        ).reshape(features, share)
        own_out = lax.dynamic_index_in_dim(
            dense_out.reshape(group_count, cut_count, piece, features), cut, 1, keepdims=False
        ).reshape(share, features)
    h_all, qkv, lse, attended, w_qkv, codes, x_two, h_two, weights_in, weights_out, g_first = front(
        tokens[0], cotangent[0, 0], by_rows(norm1_gain), by_rows(norm2_gain), w_output, w_query, w_key, w_value, segments[0], expert_ids[0], slot_ids[0],
        kept_mask[0], expert_in[0], expert_out[0], group_count, cut_count, heads, capacity, slots, 1,
    )
    first_output, d_h2, dots, d_own_in, d_own_out, d_in, d_out, _, _, got_in, got_out, out_rest = feed(
        x_two, h_two, cotangent[0], g_first, router_t, mixer_t, codes, own_in, own_out, weights_in,
        weights_out, expert_in[0], expert_out[0], share, slots, strided, sums_here, 2,
    )
    rest_output, grad_tokens, grad_output, tiny, grad_query, grad_key, grad_value, grad_dense_in, grad_dense_out, late_in, late_out, *direct = back(
        d_h2, dots, codes, h_two, x_two, cotangent[0], attended.reshape(-1, features), w_output, segments[0], tokens[0],
        by_rows(norm1_gain), by_rows(norm2_gain), router_t, mixer_t, d_own_in.reshape(group_count, cut_count, rows, share),
        d_own_out.reshape(group_count, piece, features), qkv, lse, w_qkv, h_all.reshape(micro_count, length, features),
        out_rest, w_query, w_key, w_value, d_in, d_out, got_in, got_out, heads, expert_count, sums_here, 3,
    )
    sum_groups = lambda part: lax.psum_scatter(
        part.reshape(-1, part.shape[-1]), "expert", scatter_dimension=0, tiled=True
    )
    if sums_here:
        others = (
            first_output, rest_output, grad_tokens, grad_query, grad_key, grad_value, grad_output, grad_dense_in, grad_dense_out
        )
        *others, grad_router, grad_mixer, grad_norm1, grad_norm2, grad_expert_in, grad_expert_out = last(
            d_in, direct[0], late_in, d_out, direct[1], late_out, tiny, others, expert_count
        )
        output, grad_tokens, grad_query, grad_key, grad_value, grad_output, grad_dense_in, grad_dense_out = others
        grad_router, grad_mixer, grad_norm1, grad_norm2 = grad_router.T, grad_mixer.T, grad_norm1[0], grad_norm2[0]
    else:
        swap = lambda part: lax.all_to_all(
            part.reshape(cut_count, rows, -1), "cuts", split_axis=0, concat_axis=0
        ).astype(f32)
        output = jnp.concatenate([first_output[None], rest_output])
        wide = jnp.sum(swap(sum_groups(grad_output)), axis=0)
        grad_output, grad_small = wide[:, :features], wide[:, features:]
        grad_router, grad_mixer = grad_small[:, :expert_count], grad_small[:, expert_count : expert_count + 2]
        grad_norm2 = grad_small[:, expert_count + 2]
        grad_qkv = swap(sum_groups(grad_query)).reshape(cut_count, rows, 3, head_width).transpose(2, 1, 0, 3)
        grad_qkv = grad_qkv.reshape(3, rows, features)
        grad_query, grad_key, grad_value = grad_qkv
        grad_dense_in = swap(sum_groups(d_own_in)).reshape(cut_count, rows, group_count, piece).transpose(1, 2, 0, 3)
        grad_dense_in = grad_dense_in.reshape(rows, hidden_count)
        grad_dense_out = sum_groups(d_own_out).astype(f32)
        grad_expert_in = sum_groups(d_in).astype(f32)
        grad_expert_out = sum_groups(d_out).astype(f32)
        place = (group * cut_count + cut) * rows
        own_rows = lambda w: lax.dynamic_slice_in_dim(w, place, rows, 0).astype(f32)
        grad_norm1 = sum(
            jnp.sum(own_rows(w) * grad_qkv[k], axis=-1) for k, w in enumerate((w_query, w_key, w_value))
        ) / own_rows(norm1_gain)
    return (
        output[None], grad_tokens[None], grad_norm1, grad_query, grad_key, grad_value, grad_output, grad_norm2, grad_dense_in,
        grad_dense_out, grad_router, grad_mixer, grad_expert_in[None], grad_expert_out[None],
    )


def solution(mesh):
    in_specs = (
        P("expert", None, "cuts", None),
        P("expert", None, "cuts", None),
        P("expert", None, None),
        P("expert", None, "cuts"),
        P("expert", None, "cuts"),
        P("expert", None, "cuts"),
        P(),
        P(),
        P(),
        P(),
        P(),
        P(),
        P(),
        P(),
        P(),
        P(),
        P("expert", None, "cuts"),
        P("expert", "cuts", None),
    )
    out_specs = (
        P("expert", None, "cuts", None),
        P("expert", None, "cuts", None),
        P(("expert", "cuts")),
        P(("expert", "cuts"), None),
        P(("expert", "cuts"), None),
        P(("expert", "cuts"), None),
        P(("expert", "cuts"), None),
        P(("expert", "cuts")),
        P(("expert", "cuts"), None),
        P(("expert", "cuts"), None),
        P(("expert", "cuts"), None),
        P(("expert", "cuts"), None),
        P("expert", None, "cuts"),
        P("expert", "cuts", None),
    )
    return jax.shard_map(local, mesh=mesh, in_specs=in_specs, out_specs=out_specs, check_vma=False)
```

```python
from functools import partial

import jax
import jax.numpy as jnp
from jax import lax
from jax.experimental import pallas as pl
from jax.experimental.pallas import tpu as pltpu
from jax.sharding import PartitionSpec as P

MESH = pl.DeviceIdType.MESH
score_scale = 0.125
masked_value = -1e30
norm_eps = 1e-05


def plain_dot(left, right):
    return jnp.dot(left, right, preferred_element_type=jnp.float32)


def lead_dot(left, right):
    return lax.dot_general(
        left, right, (((0,), (0,)), ((), ())), preferred_element_type=jnp.float32
    )


def tail_dot(left, right):
    return lax.dot_general(
        left, right, (((1,), (1,)), ((), ())), preferred_element_type=jnp.float32
    )


def head_masks(width, heads):
    lane = lax.broadcasted_iota(jnp.int32, (1, width), 1)
    size = width // heads
    return [((lane >= h * size) & (lane < (h + 1) * size)) for h in range(heads)]


def allowed_mask(docs_ref, docs_col_ref, m, start, rows, keys):
    query_spots = start + lax.broadcasted_iota(jnp.int32, (rows, keys), 0)
    key_spots = lax.broadcasted_iota(jnp.int32, (rows, keys), 1)
    return (key_spots <= query_spots) & (docs_ref[pl.ds(m, 1), 0:keys] == docs_col_ref[m, pl.ds(start, rows), :])


def attend_one(heads, m, qkv_ref, docs_ref, docs_col_ref, att_ref, lse_ref):
    length, width = att_ref.shape[1], att_ref.shape[2]
    rows = min(256, length)
    masks = head_masks(width, heads)
    for block in range(length // rows):
        start, keys = block * rows, (block + 1) * rows
        allowed = allowed_mask(docs_ref, docs_col_ref, m, start, rows, keys)
        query = qkv_ref[m, pl.ds(start, rows), 0:width] * jnp.bfloat16(score_scale)
        key = qkv_ref[m, 0:keys, width : 2 * width]
        value = qkv_ref[m, 0:keys, 2 * width : 3 * width]
        att = jnp.zeros((rows, width), jnp.float32)
        logs = jnp.zeros((rows, width), jnp.float32)
        for mask in masks:
            scores = tail_dot(jnp.where(mask, query, jnp.bfloat16(0)), key)
            scores = jnp.where(allowed, scores, masked_value)
            top = jnp.max(scores, axis=-1, keepdims=True)
            raised = jnp.exp(scores - top)
            total = jnp.sum(raised, axis=-1, keepdims=True)
            probs = (raised * (1.0 / total)).astype(jnp.bfloat16)
            att = jnp.where(mask, plain_dot(probs, value), att)
            logs = jnp.where(mask, top + jnp.log(total), logs)
        att_ref[m, pl.ds(start, rows), :] = att.astype(jnp.bfloat16)
        lse_ref[m, pl.ds(start, rows), :] = logs


def norm_parts(values):
    center = values - jnp.mean(values, axis=-1, keepdims=True)
    spread = jnp.mean(center * center, axis=-1, keepdims=True)
    scale = lax.rsqrt(spread + norm_eps)
    return center * scale, scale


def norm_back(normed, scale, gain, grad):
    inner = grad * gain
    return scale * (
        inner
        - jnp.mean(inner, axis=-1, keepdims=True)
        - normed * jnp.mean(inner * normed, axis=-1, keepdims=True)
    )


def gelu_pair(values):
    phi = 0.5 * (1.0 + lax.erf(values * (0.5**0.5)))
    bell = jnp.exp(-0.5 * values * values) * ((2.0 * jnp.pi) ** -0.5)
    return values * phi, phi + values * bell


def tile_slots(capacity, row_count, tile):
    return -(-capacity * (tile // row_count) // 16) * 16


def token_table(spot, width):
    return (spot == lax.broadcasted_iota(jnp.int32, (spot.shape[0], width), 1)).astype(jnp.bfloat16)


def lane_softmax(logits, lanes, first, count):
    inside = (lanes >= first) & (lanes < first + count)
    raised = jnp.exp(logits - jnp.max(jnp.where(inside, logits, masked_value), axis=-1, keepdims=True))
    raised = jnp.where(inside, raised, 0.0)
    return raised / jnp.sum(raised, axis=-1, keepdims=True)


def route(logits, chosen, expert_count):
    lanes = lax.broadcasted_iota(jnp.int32, logits.shape, 1)
    routed = lane_softmax(logits, lanes, 0, expert_count)
    mixing = lane_softmax(logits, lanes, expert_count, 2)
    pick = lambda values, lane: jnp.sum(jnp.where(lanes == lane, values, 0.0), axis=-1, keepdims=True)
    return pick(routed, chosen), pick(mixing, expert_count), pick(mixing, expert_count + 1), routed, mixing


def softmax_back(probs, grad):
    return probs * (grad - jnp.sum(probs * grad, axis=-1, keepdims=True))


def line_copy(src, dst, send, recv, group, target):
    return pltpu.make_async_remote_copy(
        src_ref=src, dst_ref=dst, send_sem=send, recv_sem=recv, device_id=(group, target), device_id_type=MESH
    )


def greet_all(cut_count, group_count):
    cut = lax.axis_index("cuts")
    group = lax.axis_index("expert")
    barrier = pltpu.get_barrier_semaphore()
    for hop in range(1, cut_count):
        pl.semaphore_signal(barrier, inc=1, device_id=(group, jnp.bitwise_xor(cut, hop)), device_id_type=MESH)
    for hop in range(1, group_count):
        pl.semaphore_signal(barrier, inc=1, device_id=(jnp.bitwise_xor(group, hop), cut), device_id_type=MESH)
    pl.semaphore_wait(barrier, cut_count + group_count - 2)


class LineGather:
    def __init__(self, buf, far_send, far_recv, pair_send, pair_recv, direct=False):
        self.direct = direct
        self.buf = buf
        self.sems = (far_send, far_recv, pair_send, pair_recv)
        self.cut = lax.axis_index("cuts")
        self.group = lax.axis_index("expert")
        self.level, self.side = self.cut // 2, self.cut % 2
        self.levels = buf.shape[1] // 2

    def place(self, n):
        low, high = self.level, self.levels - 1 - self.level
        near = jnp.minimum(low, high)
        paired = n <= 2 * near
        distance = jnp.where(paired, (n + 1) // 2, n - near)
        below = jnp.where(paired, n % 2 == 1, low > high)
        return jnp.where(below, self.level - distance, self.level + distance), below

    def far_copy(self, m, level, target, send):
        block = self.buf.at[m, 2 * level + self.side]
        return line_copy(block, block, self.sems[0].at[m, send], self.sems[1].at[m, level], self.group, target)

    def pair_copy(self, m, level, side):
        block = self.buf.at[m, 2 * level + side]
        return line_copy(
            block, block, self.sems[2].at[m, level], self.sems[3].at[m, level], self.group, jnp.bitwise_xor(self.cut, 1)
        )

    def straight_copy(self, m, n):
        level, _ = self.place(n)
        return self.far_copy(m, self.level, 2 * level + self.side, level)

    def start(self, m):
        if self.direct:
            for n in range(1, self.levels):
                self.straight_copy(m, n).start()
        else:
            @pl.when(self.level + 1 < self.levels)
            def _():
                self.far_copy(m, self.level, self.cut + 2, self.level).start()

            @pl.when(self.level > 0)
            def _():
                self.far_copy(m, self.level, self.cut - 2, self.levels).start()

        self.pair_copy(m, self.level, self.side).start()

    def receive(self, m, n):
        level, _ = self.place(n)
        self.far_copy(m, level, self.cut, level).wait_recv()
        self.pair_copy(m, level, self.side).start()

    def take_pair(self, m, n):
        level, _ = self.place(n)
        self.pair_copy(m, level, 1 - self.side).wait_recv()

    def take(self, m, n):
        level, below = self.place(n)

        @pl.when(n > 0)
        def _():
            target = jnp.where(below, self.cut + 2, self.cut - 2)
            self.far_copy(m, level, target, level).wait_recv()

            @pl.when(jnp.where(below, self.level + 1 < self.levels, self.level > 0))
            def _():
                self.far_copy(m, level, target, level).start()

            self.pair_copy(m, level, self.side).start()

        self.pair_copy(m, level, 1 - self.side).wait_recv()
        return level

    def finish(self, m):
        if self.direct:
            self.pair_copy(m, self.level, self.side).wait_send()
            for n in range(1, self.levels):
                level, _ = self.place(n)
                self.straight_copy(m, n).wait_send()
                self.pair_copy(m, level, self.side).wait_send()
            return

        @pl.when(self.level + 1 < self.levels)
        def _():
            self.far_copy(m, self.level, self.cut + 2, self.level).wait_send()

        @pl.when(self.level > 0)
        def _():
            self.far_copy(m, self.level, self.cut - 2, self.levels).wait_send()

        for n in range(self.levels):
            level, below = self.place(n)
            if n:
                @pl.when(jnp.where(below, self.level + 1 < self.levels, self.level > 0))
                def _():
                    self.far_copy(m, level, self.cut, level).wait_send()

            self.pair_copy(m, level, self.side).wait_send()


class LineSum:
    def __init__(self, part, pair_buf, far_buf, pair_send, pair_recv, send, recv, own=None, direct=False):
        self.direct = direct
        self.part, self.pair_buf, self.far_buf, self.own = part, pair_buf, far_buf, own
        self.sems = (pair_send, pair_recv, send, recv)
        self.cut = lax.axis_index("cuts")
        self.group = lax.axis_index("expert")
        self.level, self.side = self.cut // 2, self.cut % 2
        self.levels = pair_buf.shape[1]

    def pair_copy(self, m, level):
        return line_copy(
            self.part.at[m, 2 * level + 1 - self.side], self.pair_buf.at[m, level], self.sems[0].at[m, level],
            self.sems[1].at[m, level], self.group, jnp.bitwise_xor(self.cut, 1),
        )

    def far_copy(self, m, level, up):
        target = self.cut + 2 if up else self.cut - 2
        slot = level if up else jnp.where(level == self.level - 1, self.levels, level)
        return line_copy(
            self.pair_buf.at[m, level], self.far_buf.at[m, slot], self.sems[2].at[m, level], self.sems[3].at[m, slot],
            self.group, target,
        )

    def arrived(self, m, slot):
        line_copy(
            self.far_buf.at[m, slot], self.far_buf.at[m, slot], self.sems[2].at[m, 0], self.sems[3].at[m, slot],
            self.group, self.cut,
        ).wait_recv()
        return self.far_buf[m, slot].astype(jnp.float32)

    def start(self, m):
        def one(k, carry):
            self.pair_copy(m, jnp.where(k % 2 == 0, self.levels - 1 - k // 2, k // 2)).start()
            return carry

        lax.fori_loop(0, self.levels, one, 0)

    def pairs(self, m):
        def one(k, carry):
            level = jnp.where(k % 2 == 0, self.levels - 1 - k // 2, k // 2)
            self.pair_copy(m, level).wait_recv()
            mine = self.part[m, 2 * level + self.side] if self.own is None else self.own[m, level]
            total = mine.astype(jnp.float32) + self.pair_buf[m, level].astype(jnp.float32)
            self.pair_buf[m, level] = total.astype(self.pair_buf.dtype)
            self.first(m, level)
            return carry

        lax.fori_loop(0, self.levels, one, 0)

    def straight_copy(self, m, level):
        return line_copy(
            self.pair_buf.at[m, level], self.far_buf.at[m, self.level], self.sems[2].at[m, level],
            self.sems[3].at[m, self.level], self.group, 2 * level + self.side,
        )

    def first(self, m, level):
        if self.direct:
            @pl.when(level != self.level)
            def _():
                self.straight_copy(m, level).start()

            return

        @pl.when((self.level == 0) & (level > 0))
        def _():
            self.far_copy(m, level, True).start()

        @pl.when((self.level == self.levels - 1) & (level < self.levels - 1))
        def _():
            self.far_copy(m, level, False).start()

    def pass_on(self, m, level, up):
        @pl.when((level > self.level) if up else (level < self.level))
        def _():
            total = self.pair_buf[m, level].astype(jnp.float32) + self.arrived(m, level)
            self.pair_buf[m, level] = total.astype(self.pair_buf.dtype)
            self.far_copy(m, level, up).start()

    def hop(self, m, j):
        inner = (self.level > 0) & (self.level < self.levels - 1)
        lower = 2 * self.level < self.levels

        @pl.when(inner & lower)
        def _():
            self.pass_on(m, self.levels - 1 - j, True)
            self.pass_on(m, j, False)

        @pl.when(inner & jnp.logical_not(lower))
        def _():
            self.pass_on(m, j, False)
            self.pass_on(m, self.levels - 1 - j, True)

    def finish(self, m, out_ref):
        if self.direct:
            total = self.pair_buf[m, self.level].astype(jnp.float32)
            for k in range(1, self.levels):
                total = total + self.arrived(m, jnp.bitwise_xor(self.level, k))
            out_ref[m] = total
            for k in range(1, self.levels):
                self.straight_copy(m, jnp.bitwise_xor(self.level, k)).wait_send()
            for level in range(self.levels):
                self.pair_copy(m, level).wait_send()
            return

        out_ref[m] = self.pair_buf[m, self.level].astype(jnp.float32)

        @pl.when(self.level > 0)
        def _():
            out_ref[m] = out_ref[m] + self.arrived(m, self.level)

        @pl.when(self.level < self.levels - 1)
        def _():
            out_ref[m] = out_ref[m] + self.arrived(m, self.levels)

        def one(level, carry):
            if self.part is not None:
                self.pair_copy(m, level).wait_send()

            @pl.when(level > self.level)
            def _():
                self.far_copy(m, level, True).wait_send()

            @pl.when(level < self.level)
            def _():
                self.far_copy(m, level, False).wait_send()

            return carry

        lax.fori_loop(0, self.levels, one, 0)


def row_to_column(values):
    return jnp.transpose(values.astype(jnp.float32))


def one_row(ref):
    values = ref[...].astype(jnp.float32)
    return jnp.concatenate([values[k : k + 1] for k in range(values.shape[0])], axis=1)


def stack_small(router_ref, mixer_ref, stage, small):
    count = router_ref.shape[0]
    stage[...] = jnp.zeros_like(stage)
    stage[0:count] = router_ref[...].astype(jnp.float32)
    stage[count : count + 2] = mixer_ref[...].astype(jnp.float32)
    small[...] = stage[...].astype(small.dtype)


def fill_docs(docs_ref, stage, docs_col):
    stage[...] = jnp.zeros_like(stage)
    micro_count = docs_ref.shape[0]
    stage[0:micro_count] = docs_ref[...].astype(jnp.float32)
    for k in range(stage.shape[1] // 128):
        turned = jnp.transpose(stage[:, k * 128 : (k + 1) * 128]).astype(jnp.int32)
        for m in range(micro_count):
            docs_col[m, k * 128 : (k + 1) * 128, :] = turned[:, m : m + 1]


def front_kernel(
    heads, capacity, slots,
    x_ref, gy_ref, gain_ref, gain_two_ref, w_out_ref, w_query_ref, w_key_ref, w_value_ref, docs_ref, ids_ref, slot_ref, kept_ref, expert_in_ref,
    expert_out_ref,
    h_out_ref, qkv_out_ref, lse_out_ref, att_ref, w_qkv_ref, codes_ref, x_two_ref, h_two_ref, weights_ref,
    weights_out_ref, g_all_ref,
    h_all_ref, qkv_ref, lse_ref, w_out, docs_stage, docs_col_ref, att_part, own_code, far_send, far_recv, pair_send, pair_recv, load_sem, swap_send, swap_recv, swap_own, code_send,
    code_recv, weight_send, weight_recv, pass_send, pass_recv, keep_sem,
    g_far_send, g_far_recv, g_pair_send, g_pair_recv, g_own,
):
    micro_count, cut_count, rows, features = h_all_ref.shape
    group_count = weights_ref.shape[0]
    width = features // cut_count
    cut = lax.axis_index("cuts")
    group = lax.axis_index("expert")
    low = jnp.bfloat16
    loads = []
    for k, ref in enumerate((w_query_ref, w_key_ref, w_value_ref)):
        loads.append(pltpu.make_async_copy(
            ref.at[:, pl.ds(pl.multiple_of(cut * width, width), width)], w_qkv_ref.at[:, k * width : (k + 1) * width],
            load_sem.at[k],
        ))
        loads[-1].start()
    loads.append(pltpu.make_async_copy(w_out_ref, w_out, load_sem.at[3]))
    loads[-1].start()
    g_keep = pltpu.make_async_copy(gy_ref, g_all_ref.at[0, cut], g_own)
    g_keep.start()
    gain, gain_two = one_row(gain_ref), one_row(gain_two_ref)
    greet_all(cut_count, group_count)
    g_line = LineGather(g_all_ref, g_far_send, g_far_recv, g_pair_send, g_pair_recv)

    line = LineGather(h_all_ref, far_send, far_recv, pair_send, pair_recv)

    def norm_step(m, carry):
        normed, _ = norm_parts(x_ref[m].astype(jnp.float32))
        h_all_ref[m, cut] = (normed * gain).astype(low)
        line.start(m)
        return carry

    lax.fori_loop(0, micro_count, norm_step, 0)

    square = group_count == 4

    def weight_copy(kind, hop):
        src, dst = ((expert_in_ref, weights_ref), (expert_out_ref, weights_out_ref))[kind]
        return line_copy(
            src, dst.at[group], weight_send.at[kind, hop - 1], weight_recv.at[kind, hop - 1],
            jnp.bitwise_xor(group, hop), cut,
        )

    def pass_copy(k):
        half = pl.ds(k * (features // 2), features // 2)
        block = weights_ref.at[jnp.bitwise_xor(group, 2 - k), half, :]
        return line_copy(block, block, pass_send.at[k], pass_recv.at[k], jnp.bitwise_xor(group, 1 + k), cut)

    weight_hops = [(0, 1), (0, 2)] if square else [(kind, hop) for kind in range(2) for hop in range(1, group_count)]
    for kind, hop in weight_hops:
        weight_copy(kind, hop).start()

    chosen = jnp.where(kept_ref[...] == 1, ids_ref[...], -1)
    spot = jnp.where(kept_ref[...] == 1, ids_ref[...] * slots + cut % 2 * capacity + slot_ref[...], -1)
    own_code[...] = jnp.zeros_like(own_code)
    for m in range(micro_count):
        own_code[m, 0:1] = chosen[m : m + 1]
        own_code[m, 1:2] = spot[m : m + 1]
    codes_ref[cut] = own_code[...]

    def code_copy(hop):
        return line_copy(
            own_code, codes_ref.at[cut], code_send.at[hop], code_recv.at[hop], group, jnp.bitwise_xor(cut, hop)
        )

    for hop in range(1, cut_count):
        code_copy(hop).start()
    fill_docs(docs_ref, docs_stage, docs_col_ref)
    for load in loads[:3]:
        load.wait()

    def tile_step(n, m):
        level = line.take(m, n)
        h_tile = h_all_ref[m, pl.ds(2 * level, 2)].reshape(2 * rows, features)
        spots = pl.ds(pl.multiple_of(level * 2 * rows, 2 * rows), 2 * rows)
        qkv_ref[m, spots, :] = plain_dot(h_tile, w_qkv_ref[...]).astype(low)

    def early(i, carry):
        tile_step(i // micro_count, i % micro_count)
        return carry

    levels = cut_count // 2
    g_keep.wait()
    g_line.start(0)
    lax.fori_loop(0, (levels - 1) * micro_count, early, 0)
    if square:
        for hop in (1, 2):
            weight_copy(0, hop).wait()
        for k in range(2):
            pass_copy(k).start()

    def swap_copy(m, hop):
        target = jnp.bitwise_xor(cut, hop)
        return line_copy(
            att_part.at[m, pl.ds(pl.multiple_of(target * rows, rows), rows), :],
            att_ref.at[m, :, pl.ds(pl.multiple_of(cut * width, width), width)],
            swap_send.at[m, hop], swap_recv.at[m, hop], group, target,
        )

    def swap_keep(m):
        return pltpu.make_async_copy(
            att_part.at[m, pl.ds(pl.multiple_of(cut * rows, rows), rows), :],
            att_ref.at[m, :, pl.ds(pl.multiple_of(cut * width, width), width)],
            swap_own.at[m],
        )

    def late(m, carry):
        tile_step(levels - 1, m)
        attend_one(heads, m, qkv_ref, docs_ref, docs_col_ref, att_part, lse_ref)
        for hop in range(cut_count - 1, 0, -1):
            swap_copy(m, hop).start()
        swap_keep(m).start()

        @pl.when(m == 0)
        def _():
            g_line.take(0, 0)
            g_line.take(0, 1)

        return carry

    lax.fori_loop(0, micro_count, late, 0)
    for n in range(2, levels):
        g_line.take(0, n)
    keeps = [
        pltpu.make_async_copy(src, dst, keep_sem.at[k])
        for k, (src, dst) in enumerate(((h_all_ref, h_out_ref), (qkv_ref, qkv_out_ref), (lse_ref, lse_out_ref)))
    ]
    for keep in keeps:
        keep.start()

    for hop in range(1, cut_count):
        code_copy(hop).wait()
    for m in range(micro_count):
        line.finish(m)
    loads[3].wait()

    def project_step(m, carry):
        for hop in range(cut_count - 1, 0, -1):
            swap_copy(m, hop).wait()
        swap_keep(m).wait()
        x_two = x_ref[m].astype(jnp.float32) + plain_dot(att_ref[m], w_out[...])
        x_two_ref[m] = x_two
        normed, _ = norm_parts(x_two)
        h_two_ref[m] = (normed * gain_two).astype(low)
        return carry

    lax.fori_loop(0, micro_count, project_step, 0)
    g_line.finish(0)
    for keep in keeps:
        keep.wait()
    if square:
        for k in range(2):
            pass_copy(k).wait()
    else:
        for kind, hop in weight_hops:
            weight_copy(kind, hop).wait()


def front(
    x, gy, gain, gain_two, w_output, w_query, w_key, w_value, docs, ids, slot_ids, kept, expert_in, expert_out, group_count, cut_count, heads, capacity,
    slots, call_id,
):
    micro_count, rows, features = x.shape
    length, levels, width = cut_count * rows, cut_count // 2, features // cut_count
    low, f32 = jnp.bfloat16, jnp.float32
    shape = jax.ShapeDtypeStruct
    dma = pltpu.SemaphoreType.DMA
    vmem, far = pl.BlockSpec(memory_space=pltpu.VMEM), pl.BlockSpec(memory_space=pl.ANY)
    return pl.pallas_call(
        partial(front_kernel, heads, capacity, slots),
        out_shape=(
            shape((micro_count, cut_count, rows, features), low),
            shape((micro_count, length, 3 * width), low),
            shape((micro_count, length, width), f32),
            shape((micro_count, rows, features), low),
            shape((features, 3 * width), low),
            shape((cut_count, micro_count, 8, rows), jnp.int32),
            shape((micro_count, rows, features), f32),
            shape((micro_count, rows, features), low),
            shape((group_count, *expert_in.shape), low),
            shape((16, 128) if group_count == 4 else (group_count, *expert_out.shape), low),
            shape((1, cut_count, rows, features), low),
        ),
        in_specs=[vmem, vmem, vmem, vmem, far, far, far, far, vmem, vmem, vmem, vmem, far, far],
        out_specs=[far] * 3 + [vmem] * 5 + [far] * 3,
        scratch_shapes=[
            pltpu.VMEM((micro_count, cut_count, rows, features), low),
            pltpu.VMEM((micro_count, length, 3 * width), low),
            pltpu.VMEM((micro_count, length, width), f32),
            pltpu.VMEM((features, features), low),
            pltpu.VMEM((8, length), f32),
            pltpu.VMEM((micro_count, length, 1), jnp.int32),
            pltpu.VMEM((micro_count, length, width), low),
            pltpu.VMEM((micro_count, 8, rows), jnp.int32),
            dma((micro_count, levels + 1)), dma((micro_count, levels)), dma((micro_count, levels)), dma((micro_count, levels)),
            dma((4,)), dma((micro_count, cut_count)), dma((micro_count, cut_count)), dma((micro_count,)),
            dma((cut_count,)), dma((cut_count,)), dma((2, group_count - 1)), dma((2, group_count - 1)), dma((2,)), dma((2,)),
            dma((3,)), dma((1, levels + 1)), dma((1, levels)), dma((1, levels)), dma((1, levels)), dma(()),
        ],
        compiler_params=pltpu.CompilerParams(collective_id=call_id, has_side_effects=True, vmem_limit_bytes=62 * 2**20),
    )(x, gy, gain, gain_two, w_output, w_query, w_key, w_value, docs, ids, slot_ids, kept, expert_in, expert_out)


def feed_kernel(
    slots, strided, early, stored,
    x_two_ref, h_own_ref, gy_ref, g_first_ref, router_ref, mixer_ref, codes_ref, dense_in_ref, dense_out_ref,
    weights_in_ref, weights_out_ref, expert_in_ref, expert_out_ref,
    output_ref, dh_ref, sums_ref, d_own_in_ref, d_own_out_ref, d_in_ref, d_out_ref, beside_ref, across_ref,
    got_in_ref, got_out_ref, out_rest_ref,
    h_all, g_buf, sent, g_sent, d_sent, hidden_buf, pre_buf, back_buf, side_buf, own_in, own_out, in_buf, out_buf, inner_buf,
    slope_buf, dots, dots_in, pair_buf, far_buf, o_pair_buf, o_far_buf, out_ref, small_stage, small_ref,
    far_send, far_recv, pair_send, pair_recv, g_far_send, g_far_recv, g_pair_send, g_pair_recv,
    line_send, line_recv, two_send, two_recv, o_line_send, o_line_recv, o_two_send, o_two_recv,
    load_sem, in_sem, out_sem, stage_sem, dot_send, dot_recv, weight_send, weight_recv, early_send, early_recv,
):
    micro_count, cut_count, rows, features = h_all.shape
    group_count = weights_in_ref.shape[0]
    share = own_in.shape[1]
    levels, tile = cut_count // 2, 2 * rows
    expert_count = group_count
    cut = lax.axis_index("cuts")
    group = lax.axis_index("expert")
    low, f32 = jnp.bfloat16, jnp.float32
    loads = []
    g_load = pltpu.make_async_copy(g_first_ref.at[0], g_buf.at[0], load_sem.at[2 + 2 * group_count])
    if strided:
        piece = share // group_count
        for g in range(group_count):
            spot = pl.ds(pl.multiple_of((g * cut_count + cut) * piece, piece), piece)
            here = pl.ds(g * piece, piece)
            loads.append(pltpu.make_async_copy(dense_in_ref.at[:, spot], own_in.at[:, here], load_sem.at[len(loads)]))
            loads.append(pltpu.make_async_copy(dense_out_ref.at[spot, :], own_out.at[here, :], load_sem.at[len(loads)]))
    else:
        loads.append(pltpu.make_async_copy(dense_in_ref, own_in, load_sem.at[len(loads)]))
        loads.append(pltpu.make_async_copy(dense_out_ref, own_out, load_sem.at[len(loads)]))
    for load in loads:
        load.start()
    stack_small(router_ref, mixer_ref, small_stage, small_ref)
    g_load.start()
    for m in range(1, micro_count):
        g_buf[m, cut] = gy_ref[m]
    greet_all(cut_count, group_count)
    line = LineGather(h_all, far_send, far_recv, pair_send, pair_recv)
    g_line = LineGather(g_buf, g_far_send, g_far_recv, g_pair_send, g_pair_recv, direct=True)
    for m in range(micro_count):
        h_all[m, cut] = h_own_ref[m]
        line.start(m)

    square = group_count == 4

    def pass_copy(k):
        half = pl.ds(k * (share // 2), share // 2)
        return line_copy(
            beside_ref.at[1 - k, half, :], across_ref.at[half, :], weight_send.at[k], weight_recv.at[k],
            jnp.bitwise_xor(group, 1 + k), cut,
        )

    def beside_copy(k):
        return line_copy(
            expert_out_ref, beside_ref.at[k], weight_send.at[2 + k], weight_recv.at[2 + k], jnp.bitwise_xor(group, 1 + k),
            cut,
        )

    for k in range(2 if square else 0):
        beside_copy(k).start()
    for load in loads:
        load.wait()
    if not stored:
        d_sent = sent
    lanes = lax.broadcasted_iota(jnp.int32, (tile, 128), 1)

    def columns(m, level):
        both = [row_to_column(codes_ref[2 * level + k, m]) for k in range(2)]
        both = jnp.concatenate(both, axis=0).astype(jnp.int32)
        return both[:, 0:1], both[:, 1:2]

    def places(m, level):
        t = m * levels + level
        return (
            pl.ds(2 * level, 2), pl.ds(pl.multiple_of(t * tile, tile), tile), pl.ds(pl.multiple_of(t * slots, slots), slots)
        )

    def dense_step(i, carry):
        n, m = i // micro_count, i % micro_count
        level = line.take(m, n)
        blocks, here, spots = places(m, level)
        h_two = h_all[m, blocks].reshape(tile, features)
        chosen, spot = columns(m, level)
        gate, mix_dense, mix_expert, _, _ = route(tail_dot(h_two, small_ref[...]), chosen, expert_count)
        side_buf[here, :] = jnp.where(lanes == 0, mix_dense, mix_expert * gate)
        rows_sent = lead_dot(token_table(spot, expert_count * slots), h_two).astype(low)
        for e in range(expert_count):
            sent[e, spots, :] = rows_sent[e * slots : (e + 1) * slots]
        act, slope = gelu_pair(plain_dot(h_two, own_in[...]))
        pre_buf[here, :] = slope.astype(low)
        hidden_buf[here, :] = (mix_dense * act).astype(low)
        out_ref[m, blocks] = plain_dot(act.astype(low), own_out[...]).astype(low).reshape(2, rows, features)
        if square:
            @pl.when(i == levels * micro_count - 3)
            def _():
                for k in range(2):
                    beside_copy(k).wait()
                for k in range(2):
                    pass_copy(k).start()

        return carry

    lax.fori_loop(0, levels * micro_count, dense_step, 0)

    def beside(mask):
        return beside_ref.at[mask - 1]

    def load_at(i, mask, own=False, across=False):
        e = jnp.bitwise_xor(group, mask)
        src_in = expert_in_ref if own else weights_in_ref.at[e]
        src_out = expert_out_ref if own else across_ref if across else beside(mask) if square else weights_out_ref.at[e]
        return (
            pltpu.make_async_copy(src_in, in_buf.at[i % 2], in_sem.at[i % 2]),
            pltpu.make_async_copy(src_out, out_buf.at[i % 2], out_sem.at[i % 2]),
        )

    def load_start(i, mask, own=False, across=False):
        for load in load_at(i, mask, own, across):
            load.start()

    def load_wait(i):
        for load in load_at(i, 0, True):
            load.wait()

    load_start(0, 0, True)
    for m in range(1, micro_count):
        g_line.start(m)

    def forward_step(i, carry):
        @pl.when(i + 1 < expert_count - square)
        def _():
            load_start(i + 1, i + 1)

        if square:
            @pl.when(i == 2)
            def _():
                for k in range(2):
                    pass_copy(k).wait()
                load_start(3, 3, across=True)

        load_wait(i)
        e, at = jnp.bitwise_xor(group, i), i % 2
        act, slope = gelu_pair(plain_dot(sent[e], in_buf[at]))
        inner = act.astype(low)
        if stored:
            inner_buf[e] = inner
            slope_buf[e] = slope.astype(low)
        g_sent[e] = plain_dot(inner, out_buf[at]).astype(low)
        return carry

    lax.fori_loop(0, expert_count, forward_step, 0)

    def mask_at(i):
        return group_count - 1 - i

    load_start(0, mask_at(0), across=square)
    out_total = LineSum(out_ref, o_pair_buf, o_far_buf, o_line_send, o_line_recv, o_two_send, o_two_recv, direct=True)

    def mix_step(m, n, carry):
        if m:
            g_line.take_pair(m, n)

        level, _ = line.place(n)
        blocks, here, spots = places(m, level)
        _, spot = columns(m, level)
        table = token_table(spot, expert_count * slots)
        side = side_buf[here, :]
        mix_dense, mix_gate = side[:, 0:1], side[:, 1:2]
        grad_y = g_buf[m, blocks].reshape(tile, features).astype(f32)
        dense = out_ref[m, blocks].reshape(tile, features).astype(f32)
        part = plain_dot(table, jnp.concatenate([g_sent[e, spots, :] for e in range(expert_count)], axis=0))
        out_ref[m, blocks] = (mix_dense * dense + mix_gate * part).astype(low).reshape(2, rows, features)
        d_dense = jnp.sum(grad_y * dense, axis=-1, keepdims=True)
        d_part = jnp.sum(grad_y * part, axis=-1, keepdims=True)
        d_mix = jnp.where(lanes == 0, d_dense, d_part)
        for k in range(2):
            dots[2 * level + k, m] = jnp.transpose(d_mix[k * rows : (k + 1) * rows])[0:8]
        if m == 0:
            out_total.pair_copy(0, level).start()
        d_pre = tail_dot((mix_dense * grad_y).astype(low), own_out[...]) * pre_buf[here, :].astype(f32)
        d_pre = d_pre.astype(low)
        pre_buf[here, :] = d_pre
        back_buf[m, blocks] = tail_dot(d_pre, own_in[...]).astype(low).reshape(2, rows, features)
        rows_back = lead_dot(table, (mix_gate * grad_y).astype(low)).astype(low)
        for e in range(expert_count):
            g_sent[e, spots, :] = rows_back[e * slots : (e + 1) * slots]
        return carry

    def combine_step(m, k, carry):
        level = jnp.where(k % 2 == 0, levels - 1 - k // 2, k // 2)
        blocks, here, spots = places(m, level)
        if stored:
            spots = pl.ds(pl.multiple_of(level * slots, slots), slots)
        _, spot = columns(m, level)
        table = token_table(spot, expert_count * slots)
        rows_back = jnp.concatenate([d_sent[e, spots, :] for e in range(expert_count)], axis=0)
        back_rows = plain_dot(table, rows_back).reshape(2, rows, features)
        back_buf[m, blocks] = (back_buf[m, blocks].astype(f32) + back_rows).astype(low)
        total.pair_copy(m, level).start()
        return carry

    def input_step(m, i, carry):
        @pl.when(i + 2 < expert_count)
        def _():
            load_start(i + 1, mask_at(i + 1))

        @pl.when(i + 2 == expert_count)
        def _():
            load_start(i + 1, 0, True)

        load_wait(i)
        e, at = jnp.bitwise_xor(group, mask_at(i)), i % 2
        spots = pl.ds(m * levels * slots, levels * slots)
        d_pre = (tail_dot(g_sent[e, spots, :], out_buf[at]) * slope_buf[e, spots, :].astype(f32)).astype(low)
        slope_buf[e, spots, :] = d_pre
        d_sent[e] = tail_dot(d_pre, in_buf[at]).astype(low)
        return carry

    total = LineSum(back_buf, pair_buf, far_buf, line_send, line_recv, two_send, two_recv)
    g_load.wait()
    out_keep = pltpu.make_async_copy(out_ref.at[pl.ds(1, micro_count - 1)], out_rest_ref, out_sem.at[2])
    for m in range(micro_count):
        if m:
            for n in range(1, levels):
                g_line.receive(m, n)
        lax.fori_loop(0, levels, partial(mix_step, m), 0)
        if m == 0:
            out_total.pairs(0)
        if stored:
            lax.fori_loop(0, expert_count, partial(input_step, m), 0)
            if m + 1 < micro_count:
                load_start(0, mask_at(0), across=square)
            lax.fori_loop(0, levels, partial(combine_step, m), 0)
            total.pairs(m)
    out_keep.start()

    def dot_copy(hop):
        target = jnp.bitwise_xor(cut, hop)
        return line_copy(dots.at[target], dots_in.at[hop - 1], dot_send.at[hop - 1], dot_recv.at[hop - 1], group, target)

    for hop in range(1, cut_count):
        dot_copy(hop).start()

    in_stage, out_stage = own_in, own_out

    def keep_in(i):
        return pltpu.make_async_copy(in_stage, d_in_ref.at[jnp.bitwise_xor(group, mask_at(i))], stage_sem.at[0])

    def keep_out(i):
        return pltpu.make_async_copy(out_stage, d_out_ref.at[jnp.bitwise_xor(group, mask_at(i))], stage_sem.at[1])

    def early_copy(kind):
        src, dst = ((d_in_ref, got_in_ref), (d_out_ref, got_out_ref))[kind]
        return line_copy(
            src.at[jnp.bitwise_xor(group, 3)], dst, early_send.at[kind], early_recv.at[kind],
            jnp.bitwise_xor(group, 1 + kind), cut,
        )

    def keep_step(i):
        @pl.when(i > 0)
        def _():
            keep_in(i).wait()
            keep_out(i).wait()

        if early:
            @pl.when(i == 1)
            def _():
                early_copy(0).start()
                early_copy(1).start()

    def weight_step(i, carry):
        e = jnp.bitwise_xor(group, mask_at(i))
        keep_step(i)
        in_stage[...] = lead_dot(sent[e], slope_buf[e]).astype(low)
        keep_in(i).start()
        out_stage[...] = lead_dot(inner_buf[e], g_sent[e]).astype(low)
        keep_out(i).start()
        for j in range(levels - 1):
            @pl.when(i == j + 1)
            def _():
                total.hop(0, j)

        return carry

    def backward_step(i, carry):
        @pl.when(i + 2 < expert_count)
        def _():
            load_start(i + 1, mask_at(i + 1))

        @pl.when(i + 2 == expert_count)
        def _():
            load_start(i + 1, 0, True)

        load_wait(i)
        e, at = jnp.bitwise_xor(group, mask_at(i)), i % 2
        rows_in, rows_back = sent[e], g_sent[e]
        act, slope = gelu_pair(plain_dot(rows_in, in_buf[at]))
        d_pre = (tail_dot(rows_back, out_buf[at]) * slope).astype(low)
        keep_step(i)
        in_stage[...] = lead_dot(rows_in, d_pre).astype(low)
        keep_in(i).start()
        out_stage[...] = lead_dot(act.astype(low), rows_back).astype(low)
        keep_out(i).start()
        d_sent[e] = tail_dot(d_pre, in_buf[at]).astype(low)
        return carry

    if stored:
        lax.fori_loop(0, expert_count, weight_step, 0)
    else:
        lax.fori_loop(0, expert_count, backward_step, 0)
        for m in range(micro_count):
            lax.fori_loop(0, levels, partial(combine_step, m), 0)
            total.pairs(m)
    token_rows = micro_count * cut_count * rows
    h_flat, g_flat = h_all.reshape(token_rows, features), g_buf.reshape(token_rows, features)

    def dense_weights(k):
        part = pl.ds(k * 256, 256)
        in_buf[0, part, :] = lead_dot(h_flat[:, part], pre_buf[...]).astype(low)
        out_buf[0, :, part] = lead_dot(hidden_buf[...], g_flat[:, part]).astype(low)

    slices = features // 256
    for k in range(slices):
        dense_weights(k)
        if k == 0 and not stored:
            for j in range(levels - 1):
                total.hop(0, j)
        if k == slices // 2:
            for m in range(1, micro_count):
                total.hop(m, 0)
    own_keep = (
        pltpu.make_async_copy(in_buf.at[0], d_own_in_ref, in_sem.at[0]),
        pltpu.make_async_copy(out_buf.at[0], d_own_out_ref, out_sem.at[0]),
    )
    for keep in own_keep:
        keep.start()
    for m in range(1, micro_count):
        for j in range(1, levels - 1):
            total.hop(m, j)
    sums = dots[cut]
    for hop in range(1, cut_count):
        dot_copy(hop).wait()
        sums = sums + dots_in[hop - 1]
    sums_ref[...] = sums
    keep_in(0).wait()
    keep_out(0).wait()
    for kind in range(2 if early else 0):
        early_copy(kind).wait()
    for keep in own_keep:
        keep.wait()
    out_keep.wait()
    for m in range(micro_count):
        line.finish(m)
        if m:
            g_line.finish(m)
    out_total.finish(0, dh_ref)
    output_ref[...] = (x_two_ref[0] + dh_ref[0]).astype(low)
    for m in range(micro_count):
        total.finish(m, dh_ref)


def feed(
    x_two, h_own, gy, g_first, router, mixer, codes, dense_in, dense_out, weights_in, weights_out, expert_in,
    expert_out, share, slots, strided, early, call_id,
):
    micro_count, rows, features = x_two.shape
    cut_count = codes.shape[0]
    group_count = weights_in.shape[0]
    levels, total = cut_count // 2, micro_count * cut_count * rows
    low, f32 = jnp.bfloat16, jnp.float32
    shape = jax.ShapeDtypeStruct
    dma = pltpu.SemaphoreType.DMA
    block = lambda *dims: pltpu.VMEM(dims, low)
    vmem, far = pl.BlockSpec(memory_space=pltpu.VMEM), pl.BlockSpec(memory_space=pl.ANY)
    whole = (micro_count, cut_count, rows, features)
    stored = group_count <= 4
    slot_rows = micro_count * levels * slots
    line = (micro_count, levels)
    return pl.pallas_call(
        partial(feed_kernel, slots, strided, early, stored),
        out_shape=(
            shape((rows, features), low),
            shape((micro_count, rows, features), f32),
            shape((micro_count, 8, rows), f32),
            shape((features, share), low),
            shape((share, features), low),
            shape((group_count, features, share), low),
            shape((group_count, share, features), low),
            shape((2, share, features) if group_count == 4 else (16, 128), low),
            shape((share, features) if group_count == 4 else (16, 128), low),
            *(
                (shape((features, share), low), shape((share, features), low))
                if early else (shape((8, 128), low), shape((8, 128), low))
            ),
            shape((micro_count - 1, cut_count, rows, features), low),
        ),
        in_specs=[vmem, vmem, vmem, far, vmem, vmem, vmem, far, far, far, far, far, far],
        out_specs=[vmem] * 3 + [far] * 9,
        scratch_shapes=[
            block(*whole), block(*whole),
            block(group_count, slot_rows, features), block(group_count, slot_rows, features),
            block(group_count, slot_rows // micro_count, features) if stored else block(16, 128),
            block(total, share), block(total, share), block(*whole), pltpu.VMEM((total, 128), f32),
            block(features, share), block(share, features), block(2, features, share), block(2, share, features),
            *([block(group_count, slot_rows, share)] * 2 if stored else [block(16, 128)] * 2),
            pltpu.VMEM((cut_count, micro_count, 8, rows), f32), pltpu.VMEM((cut_count - 1, micro_count, 8, rows), f32),
            block(*line, rows, features), block(micro_count, levels + 1, rows, features),
            block(1, levels, rows, features), block(1, levels + 1, rows, features), block(*whole),
            pltpu.VMEM((128, features), f32), block(128, features),
            *[dma((micro_count, levels + 1)), dma(line), dma(line), dma(line)] * 2,
            *[dma(line), dma(line), dma(line), dma((micro_count, levels + 1))] * 2,
            dma((3 + 2 * group_count,)), dma((2,)), dma((3,)), dma((2,)),
            dma((cut_count - 1,)), dma((cut_count - 1,)), dma((4,)), dma((4,)), dma((4,)), dma((4,)),
        ],
        compiler_params=pltpu.CompilerParams(collective_id=call_id, has_side_effects=True, vmem_limit_bytes=62 * 2**20),
    )(x_two, h_own, gy, g_first, router, mixer, codes, dense_in, dense_out, weights_in, weights_out, expert_in, expert_out)


def attend_back_one(heads, m, qkv_ref, docs_ref, docs_col_ref, lse_ref, back_ref, out_ref, key_acc, value_acc):
    length, width = back_ref.shape[1], back_ref.shape[2]
    rows = min(256, length)
    masks = head_masks(width, heads)
    key_acc[...] = jnp.zeros_like(key_acc)
    value_acc[...] = jnp.zeros_like(value_acc)
    zero = jnp.bfloat16(0)
    for block in range(length // rows):
        start, keys = block * rows, (block + 1) * rows
        allowed = allowed_mask(docs_ref, docs_col_ref, m, start, rows, keys)
        query = qkv_ref[m, pl.ds(start, rows), 0:width] * jnp.bfloat16(score_scale)
        key = qkv_ref[m, 0:keys, width : 2 * width]
        value = qkv_ref[m, 0:keys, 2 * width : 3 * width]
        back = back_ref[m, pl.ds(start, rows), :]
        logs = lse_ref[m, pl.ds(start, rows), :]
        query_grad = jnp.zeros((rows, width), jnp.float32)
        for h, mask in enumerate(masks):
            one_query = jnp.where(mask, query, zero)
            one_back = jnp.where(mask, back, zero)
            scores = jnp.where(allowed, tail_dot(one_query, key), masked_value)
            spot = h * (width // heads)
            probs = jnp.exp(scores - logs[:, spot : spot + 1])
            weighted = probs * tail_dot(one_back, value)
            delta = jnp.sum(weighted, axis=-1, keepdims=True)
            score_grad = (weighted - probs * delta).astype(jnp.bfloat16)
            query_grad = jnp.where(mask, plain_dot(score_grad, key), query_grad)
            key_acc[0:keys, :] += lead_dot(score_grad, one_query)
            value_acc[0:keys, :] += lead_dot(probs.astype(jnp.bfloat16), one_back)
        out_ref[m, pl.ds(start, rows), 0:width] = (query_grad * score_scale).astype(jnp.bfloat16)
    out_ref[m, :, width : 2 * width] = key_acc[...].astype(jnp.bfloat16)
    out_ref[m, :, 2 * width : 3 * width] = value_acc[...].astype(jnp.bfloat16)


def back_kernel(
    heads, expert_count, sums_here,
    dh_ref, dots_ref, codes_ref, h_ref, x_two_ref, gy_ref, att_ref, w_out_ref, docs_ref,
    x_ref, gain_one_ref, gain_two_ref, router_ref, mixer_ref, own_in_ref, own_out_ref,
    qkv_far, lse_far, w_qkv_far, h_all_far, out_part, w_query_ref, w_key_ref, w_value_ref, d_in_ref, d_out_ref,
    got_in_ref, got_out_ref,
    output_ref, tokens_ref, wo_ref, tiny_ref, query_out_ref, key_out_ref, value_out_ref, in_out_ref, out_out_ref, late_in_ref,
    late_out_ref, direct_in_ref, direct_out_ref,
    qkv_ref, lse_ref, w_qkv_ref, h_all_ref, w_rows, docs_stage, docs_col_ref, small_stage, small_ref, out_own, out_pair,
    out_far, g_att, d_att, back_all, d_qkv, key_acc, value_acc, d_small, part, pair_buf, far_buf, d_h_one, in_sum, out_sum,
    wo_part, qkv_part, wo_in, qkv_in, own_in_got, own_out_got, own_in_sum, own_out_sum, own_in_in, own_out_in, wo_mid, wo_pair, wo_far, wo_sum, qkv_mid, in_mid, qkv_end, in_end,
    pair_send, pair_recv, far_send, far_recv, swap_send, swap_recv, swap_own, one_send, one_recv, two_send, two_recv, two_own,
    late_send, late_recv, late_load_sem, load_sem,
    wo_pair_send, wo_pair_recv, wo_far_send, wo_far_recv, own_sem, o_pair_send, o_pair_recv, o_far_send, o_far_recv,
    direct_send, direct_recv, own_send, own_recv,
):
    micro_count, cut_count, rows, features = part.shape
    group_count, split, _ = qkv_part.shape[:3]
    piece_rows = qkv_part.shape[2]
    group_rows = split * piece_rows
    sides, side_rows = wo_part.shape[1:3]
    width = features // cut_count
    cut = lax.axis_index("cuts")
    group = lax.axis_index("expert")
    low, f32 = jnp.bfloat16, jnp.float32
    levels = cut_count // 2
    place = (group * cut_count + cut) * piece_rows
    loads = [
        pltpu.make_async_copy(src, dst, load_sem.at[k])
        for k, (src, dst) in enumerate(
            ((qkv_far, qkv_ref), (lse_far, lse_ref), (w_qkv_far, w_qkv_ref), (h_all_far, h_all_ref))
        )
    ]
    if sums_here:
        own_rows = pl.ds(pl.multiple_of(place, piece_rows), piece_rows)
        for k, ref in enumerate((w_query_ref, w_key_ref, w_value_ref)):
            loads.append(pltpu.make_async_copy(ref.at[own_rows, :], w_rows.at[k], load_sem.at[4 + k]))
    for load in loads:
        load.start()

    rest = micro_count - 1

    def own_load(m, level):
        return pltpu.make_async_copy(out_part.at[m, 2 * level + cut % 2], out_own.at[m, level], own_sem.at[m, level])

    for m in range(rest):
        for level in range(levels):
            own_load(m, level).start()
    stack_small(router_ref, mixer_ref, small_stage, small_ref)
    fill_docs(docs_ref, docs_stage, docs_col_ref)
    greet_all(cut_count, group_count if sums_here else 1)
    out_line = LineSum(out_part, out_pair, out_far, o_pair_send, o_pair_recv, o_far_send, o_far_recv, out_own, direct=True)

    ones = (None, None, (wo_part, wo_in), (qkv_part, qkv_in))

    def one_copy(kind, hop):
        src, dst = ones[kind]
        target = jnp.bitwise_xor(group, hop)
        return line_copy(
            src.at[target, cut % 2] if kind == 2 else src.at[target], dst.at[hop - 1], one_send.at[kind, hop - 1], one_recv.at[kind, hop - 1], target, cut
        )

    def one_start(kind):
        for hop in range(1, group_count):
            one_copy(kind, hop).start()

    def one_finish(kind):
        src, dst = ones[kind]
        total = (src[group, cut % 2] if kind == 2 else src[group]).astype(f32)
        for hop in range(1, group_count):
            one_copy(kind, hop).wait_recv()
            total = total + dst[hop - 1].astype(f32)
        for hop in range(1, group_count):
            one_copy(kind, hop).wait_send()
        return total

    owns = (
        (own_in_ref, own_in_got, own_in_sum, own_in_in, 1), (own_out_ref, own_out_got, own_out_sum, own_out_in, 2)
    )

    def own_first(kind, k):
        own, got, _, _, side = owns[kind]
        return line_copy(
            own.at[jnp.bitwise_xor(group, 3 if k else side)], got.at[k], own_send.at[kind, k], own_recv.at[kind, k],
            jnp.bitwise_xor(group, side), cut,
        )

    def own_second(kind):
        _, _, total, far, side = owns[kind]
        return line_copy(
            total, far, own_send.at[kind, 2], own_recv.at[kind, 2], jnp.bitwise_xor(group, 3 - side), cut
        )

    def own_start(kind):
        own, got, total, _, side = owns[kind]
        own_first(kind, 1).wait()
        total[...] = (own[jnp.bitwise_xor(group, 3 - side)].astype(f32) + got[1].astype(f32)).astype(low)
        own_second(kind).start()

    def own_finish(kind):
        own, got, _, far, _ = owns[kind]
        own_first(kind, 0).wait()
        own_second(kind).wait()
        return own[group].astype(f32) + got[0].astype(f32) + far[...].astype(f32)

    twos = ((in_mid, in_end), None, None, (qkv_mid, qkv_end))

    def two_copy(kind, hop):
        src, dst = twos[kind]
        target = jnp.bitwise_xor(cut, hop)
        return line_copy(src.at[target], dst.at[cut], two_send.at[kind, hop], two_recv.at[kind, hop], group, target)

    def two_keep(kind):
        src, dst = twos[kind]
        return pltpu.make_async_copy(src.at[cut], dst.at[cut], two_own.at[kind])

    def two_start(kind):
        for hop in range(cut_count - 1, 0, -1):
            two_copy(kind, hop).start()
        two_keep(kind).start()

    def two_finish(kind):
        for hop in range(cut_count - 1, 0, -1):
            two_copy(kind, hop).wait()
        two_keep(kind).wait()

    ends = ((d_in_ref, got_in_ref, in_sum, late_in_ref, 2), (d_out_ref, got_out_ref, out_sum, late_out_ref, 1))

    def late_load(kind, k):
        own, got, total, _, side = ends[kind]
        src = got if k else own.at[jnp.bitwise_xor(group, side)]
        return pltpu.make_async_copy(src, total.at[k], late_load_sem.at[kind, k])

    def late_copy(kind):
        _, _, total, late, side = ends[kind]
        return line_copy(
            total.at[0], late, late_send.at[kind], late_recv.at[kind], jnp.bitwise_xor(group, side), cut
        )

    if sums_here:
        for kind in range(2):
            late_load(kind, 0).start()
            late_load(kind, 1).start()
        for k in (1, 0):
            for kind in range(2):
                own_first(kind, k).start()

    def swap_copy(m, hop):
        target = jnp.bitwise_xor(cut, hop)
        return line_copy(
            d_att.at[m, :, pl.ds(pl.multiple_of(target * width, width), width)],
            back_all.at[m, pl.ds(pl.multiple_of(cut * rows, rows), rows), :],
            swap_send.at[m, hop], swap_recv.at[m, hop], group, target,
        )

    def swap_keep(m):
        return pltpu.make_async_copy(
            d_att.at[m, :, pl.ds(pl.multiple_of(cut * width, width), width)],
            back_all.at[m, pl.ds(pl.multiple_of(cut * rows, rows), rows), :],
            swap_own.at[m],
        )

    small = small_ref[...]
    gain_one, gain_two = one_row(gain_one_ref), one_row(gain_two_ref)
    d_small[...] = jnp.zeros_like(d_small)
    lanes = lax.broadcasted_iota(jnp.int32, (rows, 128), 1)

    def norm_two_step(m, carry):
        dots = jnp.transpose(dots_ref[m])
        chosen = row_to_column(codes_ref[cut, m])[:, 0:1].astype(jnp.int32)
        h_two = h_ref[m]
        gate, _, mix_expert, routed, mixing = route(tail_dot(h_two, small), chosen, expert_count)
        d_mixing = jnp.where(lanes == expert_count, dots[:, 0:1], gate * dots[:, 1:2])
        d_gate = jnp.where(lanes == chosen, mix_expert * dots[:, 1:2], 0.0)
        d_logits = (softmax_back(mixing, d_mixing) + softmax_back(routed, d_gate)).astype(low)
        d_h = dh_ref[m] + plain_dot(d_logits, small)
        normed, scale = norm_parts(x_two_ref[m])
        one_lane = (lanes == expert_count + 2).astype(low)
        d_small[...] += lead_dot(h_two, d_logits) + lead_dot((d_h * normed).astype(low), one_lane)
        d_x = gy_ref[m].astype(f32) + norm_back(normed, scale, gain_two, d_h)
        tokens_ref[m] = d_x
        grad = d_x.astype(low)
        g_att[pl.ds(pl.multiple_of(m * rows, rows), rows), :] = grad
        d_att[m] = tail_dot(grad, w_out_ref[...]).astype(low)
        for hop in range(cut_count - 1, 0, -1):
            swap_copy(m, hop).start()
        swap_keep(m).start()
        return carry

    lax.fori_loop(0, micro_count, norm_two_step, 0)
    for m in range(rest):
        out_line.start(m)

    def wo_step(g, carry):
        columns = pl.ds(pl.multiple_of(g * group_rows, group_rows), group_rows)
        grads = lead_dot(att_ref[:, columns], g_att[...]).astype(low)
        smalls = d_small[columns, :].astype(low)
        for side in range(sides):
            for k in range(side_rows):
                part_rows = slice((k * sides + side) * piece_rows, (k * sides + side + 1) * piece_rows)
                wo_part[g, side, k, :, 0:features] = grads[part_rows]
                wo_part[g, side, k, :, features : features + 128] = smalls[part_rows]
        return carry

    lax.fori_loop(0, group_count, wo_step, 0)
    def wo_pair_copy(g):
        return line_copy(
            wo_part.at[g, 1 - cut % 2], wo_pair.at[g], wo_pair_send.at[g], wo_pair_recv.at[g], group,
            jnp.bitwise_xor(cut, 1),
        )

    def wo_pair_step(g, carry):
        wo_pair_copy(g).wait()
        wo_part[g, cut % 2] = (wo_part[g, cut % 2].astype(f32) + wo_pair[g].astype(f32)).astype(low)
        return carry

    def direct_copy(kind):
        src, dst = ((d_in_ref, direct_in_ref), (d_out_ref, direct_out_ref))[kind]
        target = jnp.bitwise_xor(group, 1 + kind)
        return line_copy(src.at[target], dst, direct_send.at[kind], direct_recv.at[kind], target, cut)

    if sums_here:
        for g in range(group_count):
            wo_pair_copy(g).start()
        lax.fori_loop(0, group_count, wo_pair_step, 0)
        one_start(2)
        for kind in range(2):
            own_start(kind)
        for kind in range(2):
            direct_copy(kind).start()
    for load in loads[:3]:
        load.wait()
    line = LineSum(part, pair_buf, far_buf, pair_send, pair_recv, far_send, far_recv)

    def attend_step(m, carry):
        for hop in range(cut_count - 1, 0, -1):
            swap_copy(m, hop).wait()
        swap_keep(m).wait()

        @pl.when(m == 0)
        def _():
            for k in range(rest):
                for level in range(levels):
                    own_load(k, level).wait()
                out_line.pairs(k)

        attend_back_one(heads, m, qkv_ref, docs_ref, docs_col_ref, lse_ref, back_all, d_qkv, key_acc, value_acc)
        for k in range(levels):
            level = levels - 1 - k // 2 if k % 2 == 0 else k // 2
            for c in (2 * level, 2 * level + 1):
                part[m, c] = tail_dot(d_qkv[m, c * rows : (c + 1) * rows, :], w_qkv_ref[...]).astype(low)
            line.pair_copy(m, level).start()
        line.pairs(m)
        return carry

    lax.fori_loop(0, micro_count, attend_step, 0)

    def qkv_step(g, carry):
        columns = pl.ds(pl.multiple_of(g * group_rows, group_rows), group_rows)
        grads = jnp.zeros((group_rows, 3 * width), f32)
        for m in range(micro_count):
            grads = grads + lead_dot(h_all_ref[m, :, columns], d_qkv[m])
        qkv_part[g] = grads.astype(low).reshape(split, piece_rows, 3 * width)
        return carry

    for j in range(levels - 1):
        line.hop(0, j)
    for load in loads[3:]:
        load.wait()
    lax.fori_loop(0, group_count, qkv_step, 0)
    if sums_here:
        one_start(3)
        for kind in range(2):
            total = ends[kind][2]
            late_load(kind, 0).wait()
            late_load(kind, 1).wait()
            total[0] = (total[0].astype(f32) + total[1].astype(f32)).astype(low)
            late_copy(kind).start()
    for m in range(1, micro_count):
        for j in range(levels - 1):
            line.hop(m, j)

    def norm_one_step(m, carry):
        line.finish(m, d_h_one)
        total = d_h_one[m]
        normed, scale = norm_parts(x_ref[m].astype(f32))
        tokens_ref[m] = tokens_ref[m] + norm_back(normed, scale, gain_one, total)
        return carry

    for m in range(rest):
        out_line.finish(m, d_h_one)
        output_ref[m] = (x_two_ref[1 + m] + d_h_one[m]).astype(low)
    if not sums_here:
        lax.fori_loop(0, micro_count, norm_one_step, 0)
        wo_ref[...] = wo_part[...]
        query_out_ref[...] = qkv_part[...]
        return
    in_mid[...] = own_finish(0).astype(low)
    two_start(0)
    wo_line = LineSum(None, wo_mid, wo_far, None, None, wo_far_send, wo_far_recv)
    wo_mid[0] = one_finish(2).astype(low)
    for k in range(levels):
        wo_line.first(0, levels - 1 - k // 2 if k % 2 == 0 else k // 2)
    norm_one_step(0, 0)
    qkv_mid[...] = one_finish(3).astype(low)
    two_start(3)
    out_out_ref[...] = own_finish(1)
    for j in range(levels - 1):
        wo_line.hop(0, j)
    for m in range(1, micro_count):
        norm_one_step(m, 0)
    two_finish(0)
    share_piece = in_end.shape[2] // group_count
    for c in range(cut_count):
        for g in range(group_count):
            spot = (g * cut_count + c) * share_piece
            in_out_ref[:, spot : spot + share_piece] = in_end[c, :, g * share_piece : (g + 1) * share_piece].astype(f32)
    wo_line.finish(0, wo_sum)
    wo_ref[...] = wo_sum[0, :, :features]
    small_sums = wo_sum[0, :, features:]
    two_finish(3)
    norm = jnp.zeros((piece_rows, 1), f32)
    outs = (query_out_ref, key_out_ref, value_out_ref)
    for c in range(cut_count):
        for k in range(3):
            grad = qkv_end[c, :, k * width : (k + 1) * width].astype(f32)
            outs[k][:, c * width : (c + 1) * width] = grad
            weights = w_rows[k, :, c * width : (c + 1) * width].astype(f32)
            norm = norm + jnp.sum(grad * weights, axis=-1, keepdims=True)
    spots = lax.broadcasted_iota(jnp.int32, (piece_rows, features), 1)
    mine = spots == place + lax.broadcasted_iota(jnp.int32, (piece_rows, features), 0)
    norm = norm / jnp.sum(jnp.where(mine, gain_one, 0.0), axis=-1, keepdims=True)
    tiny_lanes = lax.broadcasted_iota(jnp.int32, (piece_rows, 128), 1)
    tiny_ref[...] = jnp.where(tiny_lanes == expert_count + 3, norm, small_sums)
    for kind in range(2):
        late_copy(kind).wait()
        direct_copy(kind).wait()


def back(
    dh, dots, codes, h_two, x_two, gy, attended, w_output, docs, x, gain_one, gain_two, router, mixer, own_in, own_out,
    qkv, lse, w_qkv, h_all, out_rest, w_query, w_key, w_value, d_in, d_out, got_in, got_out, heads, expert_count, sums_here,
    call_id,
):
    micro_count, rows, features = x.shape
    length = qkv.shape[1]
    cut_count = length // rows
    width = features // cut_count
    group_count = own_out.shape[0]
    piece_rows = features // (group_count * cut_count)
    share, piece = own_in.shape[3], own_out.shape[1]
    low, f32 = jnp.bfloat16, jnp.float32
    levels = cut_count // 2
    wide = features + 128
    shape = jax.ShapeDtypeStruct
    parts = (group_count, 2, levels, piece_rows) if sums_here else (features // 256, 1, 1, 256)
    flat = (group_count, cut_count, piece_rows) if sums_here else (features // 256, 1, 256)
    tokens = (micro_count, rows, features)
    none = shape((16, 128), low)
    if sums_here:
        outs = (
            shape((micro_count - 1, rows, features), low),
            shape(tokens, f32), shape((piece_rows, features), f32), shape((piece_rows, 128), f32),
            *[shape((piece_rows, features), f32)] * 3, shape((piece_rows, share * cut_count), f32),
            shape((piece, features), f32), *[shape((features, share), low), shape((share, features), low)] * 2,
        )
    else:
        outs = (
            shape((micro_count - 1, rows, features), low),
            shape(tokens, f32), shape((*parts, wide), low), none, shape((*flat, 3 * width), low),
            *[none] * 8,
        )
    peers = max(group_count - 1, 1) if sums_here else 1
    block = lambda *dims: pltpu.VMEM(dims, low)
    mids = lambda w: block(cut_count, piece_rows, w) if sums_here else block(16, 128)
    ins = lambda w: block(peers, cut_count, piece_rows, w) if sums_here else block(16, 128)
    dma = pltpu.SemaphoreType.DMA
    line = (micro_count, levels)
    vmem, far = pl.BlockSpec(memory_space=pltpu.VMEM), pl.BlockSpec(memory_space=pl.ANY)
    operands = (
        dh, dots, codes, h_two, x_two, gy, attended, w_output, docs, x, gain_one, gain_two, router, mixer, own_in, own_out,
        qkv, lse, w_qkv, h_all, out_rest, w_query, w_key, w_value, d_in, d_out, got_in, got_out,
    )
    rest = (micro_count - 1, levels)
    return pl.pallas_call(
        partial(back_kernel, heads, expert_count, sums_here),
        out_shape=outs,
        in_specs=[vmem] * 16 + [far] * 12,
        out_specs=[vmem] * 9 + [far] * 4,
        scratch_shapes=[
            block(micro_count, length, 3 * width), pltpu.VMEM((micro_count, length, width), f32), block(features, 3 * width),
            block(micro_count, length, features), block(3, piece_rows, features), pltpu.VMEM((8, length), f32),
            pltpu.VMEM((micro_count, length, 1), jnp.int32), pltpu.VMEM((128, features), f32), block(128, features),
            block(*rest, rows, features), block(*rest, rows, features), block(micro_count - 1, levels + 1, rows, features),
            block(micro_count * rows, features),
            block(micro_count, rows, features),
            block(micro_count, length, width),
            block(micro_count, length, 3 * width),
            pltpu.VMEM((length, width), f32),
            pltpu.VMEM((length, width), f32),
            pltpu.VMEM((features, 128), f32),
            block(micro_count, cut_count, rows, features),
            block(*line, rows, features),
            block(micro_count, levels + 1, rows, features),
            pltpu.VMEM(tokens, f32),
            *((block(2, features, share), block(2, share, features)) if sums_here else (block(16, 128), block(16, 128))),
            block(*parts, wide),
            block(*flat, 3 * width),
            block(peers, levels, piece_rows, wide) if sums_here else block(16, 128), ins(3 * width),
            *(
                [block(2, cut_count, piece_rows, share), block(2, piece, features)]
                + [block(cut_count, piece_rows, share), block(piece, features)] * 2
                if sums_here else [block(16, 128)] * 6
            ),
            *(
                (
                    block(1, levels, piece_rows, wide), block(group_count, levels, piece_rows, wide),
                    block(1, levels + 1, piece_rows, wide), pltpu.VMEM((1, piece_rows, wide), f32),
                )
                if sums_here else [block(16, 128)] * 4
            ),
            mids(3 * width), mids(share), mids(3 * width), mids(share),
            dma(line), dma(line), dma(line), dma((micro_count, levels + 1)),
            dma((micro_count, cut_count)), dma((micro_count, cut_count)), dma((micro_count,)),
            dma((4, peers)), dma((4, peers)), dma((4, cut_count)), dma((4, cut_count)), dma((4,)),
            dma((2,)), dma((2,)), dma((2, 2)), dma((7,)),
            dma((group_count,)), dma((group_count,)), dma((1, levels)), dma((1, levels + 1)),
            dma(rest), dma(rest), dma(rest), dma(rest), dma((micro_count - 1, levels + 1)),
            dma((2,)), dma((2,)), dma((2, 3)), dma((2, 3)),
        ],
        compiler_params=pltpu.CompilerParams(
            collective_id=call_id, has_side_effects=True, vmem_limit_bytes=62 * 2**20
        ),
    )(*operands)


def last_kernel(
    expert_count, d_in_ref, got_in_ref, late_in_ref, d_out_ref, got_out_ref, late_out_ref, tiny_ref, *refs,
):
    passed = (len(refs) - 6 - 10 - 1) // 3
    given, refs = refs[: passed + 1], refs[passed + 1 :]
    taken, refs = refs[:passed], refs[passed:]
    held, refs = refs[-passed:], refs[:-passed]
    router_ref, mixer_ref, norm_one_ref, norm_two_ref, sum_in_ref, sum_out_ref = refs[:6]
    in_buf, out_buf, in_sum, out_sum, in_sem, out_sem, in_done, out_done, pass_sem, keep_sem = refs[6:]
    group = lax.axis_index("expert")
    held_parts = (held[0].at[0], held[0].at[pl.ds(1, held[0].shape[0] - 1)], *held[1:])
    passes = [pltpu.make_async_copy(src, dst, pass_sem.at[k]) for k, (src, dst) in enumerate(zip(given, held_parts))]
    keeps = [pltpu.make_async_copy(src, dst, keep_sem.at[k]) for k, (src, dst) in enumerate(zip(held, taken))]
    chunks = in_sem.shape[0]
    work = []
    for ends in (
        ((d_in_ref.at[group], got_in_ref, late_in_ref), in_buf, in_sum, sum_in_ref, in_sem, in_done),
        ((d_out_ref.at[group], got_out_ref, late_out_ref), out_buf, out_sum, sum_out_ref, out_sem, out_done),
    ):
        sources, buf, total, target, sem, done = ends
        step = buf.shape[1] // chunks
        for k in range(chunks):
            part = pl.ds(k * step, step)
            loads = [
                pltpu.make_async_copy(src.at[part, :], buf.at[at, part, :], sem.at[k, at]) for at, src in enumerate(sources)
            ]
            work.append((loads, buf, total, part, pltpu.make_async_copy(total.at[part, :], target.at[part, :], done.at[k])))
    for copy in passes:
        copy.start()
    for loads, *_ in work:
        for load in loads:
            load.start()
    turned = jnp.transpose(tiny_ref[...])
    router_ref[...] = turned[0:expert_count]
    mixer_ref[...] = turned[expert_count : expert_count + 2]
    norm_two_ref[...] = turned[expert_count + 2 : expert_count + 3]
    norm_one_ref[...] = turned[expert_count + 3 : expert_count + 4]
    passes[0].wait()
    for copy, keep in zip(passes[1:], keeps):
        copy.wait()
        keep.start()
    for loads, buf, total, part, keep in work:
        for load in loads:
            load.wait()
        total[part, :] = sum(buf[at, part, :].astype(jnp.float32) for at in range(3))
        keep.start()
    for *_, keep in work:
        keep.wait()
    for keep in keeps:
        keep.wait()


def last(d_in, got_in, late_in, d_out, got_out, late_out, tiny, others, expert_count):
    f32, dma = jnp.float32, pltpu.SemaphoreType.DMA
    shape = jax.ShapeDtypeStruct
    piece_rows = tiny.shape[0]
    micro_count = 1 + others[1].shape[0]
    whole = [shape((micro_count, *others[0].shape), others[0].dtype), *[shape(x.shape, x.dtype) for x in others[2:]]]
    vmem, far = pl.BlockSpec(memory_space=pltpu.VMEM), pl.BlockSpec(memory_space=pl.ANY)
    chunks = 4
    return pl.pallas_call(
        partial(last_kernel, expert_count),
        out_shape=(
            *whole, shape((expert_count, piece_rows), f32), shape((2, piece_rows), f32),
            shape((1, piece_rows), f32), shape((1, piece_rows), f32), shape(late_in.shape, f32), shape(late_out.shape, f32),
        ),
        in_specs=[far] * 6 + [vmem] + [far] * len(others),
        out_specs=[far] * len(whole) + [vmem] * 4 + [far] * 2,
        scratch_shapes=[
            pltpu.VMEM((3, *late_in.shape), late_in.dtype), pltpu.VMEM((3, *late_out.shape), late_out.dtype),
            pltpu.VMEM(late_in.shape, f32), pltpu.VMEM(late_out.shape, f32),
            dma((chunks, 3)), dma((chunks, 3)), dma((chunks,)), dma((chunks,)), dma((len(others),)), dma((len(others),)),
            *[pltpu.VMEM(x.shape, x.dtype) for x in whole],
        ],
        compiler_params=pltpu.CompilerParams(vmem_limit_bytes=62 * 2**20),
    )(d_in, got_in, late_in, d_out, got_out, late_out, tiny, *others)


def local(
    tokens, cotangent, segments, expert_ids, slot_ids, kept_mask, norm1_gain, w_query, w_key, w_value, w_output,
    norm2_gain, dense_in, dense_out, router, mixer, expert_in, expert_out,
):
    micro_count, row_count, features = tokens.shape[1:]
    cut_count = lax.axis_size("cuts")
    group_count = lax.axis_size("expert")
    cut = lax.axis_index("cuts")
    group = lax.axis_index("expert")
    length = cut_count * row_count
    head_width = features // cut_count
    heads = head_width // 64
    expert_count = router.shape[1]
    hidden_count = dense_in.shape[1]
    share = hidden_count // cut_count
    piece = share // group_count
    capacity = max(2, row_count * 5 // (4 * expert_count))
    slots = tile_slots(capacity, row_count, 2 * row_count)
    rows = features // (group_count * cut_count)
    sums_here = rows % 16 == 0 and group_count == 4
    by_rows = lambda v: v.reshape(-1, 128)
    router_t, mixer_t = router.T, mixer.T
    f32, low = jnp.float32, jnp.bfloat16

    strided = piece % 128 == 0
    if strided:
        own_in, own_out = dense_in, dense_out
    else:
        own_in = lax.dynamic_index_in_dim(
            dense_in.reshape(features, group_count, cut_count, piece), cut, 2, keepdims=False
        ).reshape(features, share)
        own_out = lax.dynamic_index_in_dim(
            dense_out.reshape(group_count, cut_count, piece, features), cut, 1, keepdims=False
        ).reshape(share, features)
    h_all, qkv, lse, attended, w_qkv, codes, x_two, h_two, weights_in, weights_out, g_first = front(
        tokens[0], cotangent[0, 0], by_rows(norm1_gain), by_rows(norm2_gain), w_output, w_query, w_key, w_value, segments[0], expert_ids[0], slot_ids[0],
        kept_mask[0], expert_in[0], expert_out[0], group_count, cut_count, heads, capacity, slots, 1,
    )
    first_output, d_h2, dots, d_own_in, d_own_out, d_in, d_out, _, _, got_in, got_out, out_rest = feed(
        x_two, h_two, cotangent[0], g_first, router_t, mixer_t, codes, own_in, own_out, weights_in,
        weights_out, expert_in[0], expert_out[0], share, slots, strided, sums_here, 2,
    )
    rest_output, grad_tokens, grad_output, tiny, grad_query, grad_key, grad_value, grad_dense_in, grad_dense_out, late_in, late_out, *direct = back(
        d_h2, dots, codes, h_two, x_two, cotangent[0], attended.reshape(-1, features), w_output, segments[0], tokens[0],
        by_rows(norm1_gain), by_rows(norm2_gain), router_t, mixer_t, d_own_in.reshape(group_count, cut_count, rows, share),
        d_own_out.reshape(group_count, piece, features), qkv, lse, w_qkv, h_all.reshape(micro_count, length, features),
        out_rest, w_query, w_key, w_value, d_in, d_out, got_in, got_out, heads, expert_count, sums_here, 3,
    )
    sum_groups = lambda part: lax.psum_scatter(
        part.reshape(-1, part.shape[-1]), "expert", scatter_dimension=0, tiled=True
    )
    if sums_here:
        others = (
            first_output, rest_output, grad_tokens, grad_query, grad_key, grad_value, grad_output, grad_dense_in, grad_dense_out
        )
        *others, grad_router, grad_mixer, grad_norm1, grad_norm2, grad_expert_in, grad_expert_out = last(
            d_in, direct[0], late_in, d_out, direct[1], late_out, tiny, others, expert_count
        )
        output, grad_tokens, grad_query, grad_key, grad_value, grad_output, grad_dense_in, grad_dense_out = others
        grad_router, grad_mixer, grad_norm1, grad_norm2 = grad_router.T, grad_mixer.T, grad_norm1[0], grad_norm2[0]
    else:
        swap = lambda part: lax.all_to_all(
            part.reshape(cut_count, rows, -1), "cuts", split_axis=0, concat_axis=0
        ).astype(f32)
        output = jnp.concatenate([first_output[None], rest_output])
        wide = jnp.sum(swap(sum_groups(grad_output)), axis=0)
        grad_output, grad_small = wide[:, :features], wide[:, features:]
        grad_router, grad_mixer = grad_small[:, :expert_count], grad_small[:, expert_count : expert_count + 2]
        grad_norm2 = grad_small[:, expert_count + 2]
        grad_qkv = swap(sum_groups(grad_query)).reshape(cut_count, rows, 3, head_width).transpose(2, 1, 0, 3)
        grad_qkv = grad_qkv.reshape(3, rows, features)
        grad_query, grad_key, grad_value = grad_qkv
        grad_dense_in = swap(sum_groups(d_own_in)).reshape(cut_count, rows, group_count, piece).transpose(1, 2, 0, 3)
        grad_dense_in = grad_dense_in.reshape(rows, hidden_count)
        grad_dense_out = sum_groups(d_own_out).astype(f32)
        grad_expert_in = sum_groups(d_in).astype(f32)
        grad_expert_out = sum_groups(d_out).astype(f32)
        place = (group * cut_count + cut) * rows
        own_rows = lambda w: lax.dynamic_slice_in_dim(w, place, rows, 0).astype(f32)
        grad_norm1 = sum(
            jnp.sum(own_rows(w) * grad_qkv[k], axis=-1) for k, w in enumerate((w_query, w_key, w_value))
        ) / own_rows(norm1_gain)
    return (
        output[None], grad_tokens[None], grad_norm1, grad_query, grad_key, grad_value, grad_output, grad_norm2, grad_dense_in,
        grad_dense_out, grad_router, grad_mixer, grad_expert_in[None], grad_expert_out[None],
    )


def solution(mesh):
    in_specs = (
        P("expert", None, "cuts", None),
        P("expert", None, "cuts", None),
        P("expert", None, None),
        P("expert", None, "cuts"),
        P("expert", None, "cuts"),
        P("expert", None, "cuts"),
        P(),
        P(),
        P(),
        P(),
        P(),
        P(),
        P(),
        P(),
        P(),
        P(),
        P("expert", None, "cuts"),
        P("expert", "cuts", None),
    )
    out_specs = (
        P("expert", None, "cuts", None),
        P("expert", None, "cuts", None),
        P(("expert", "cuts")),
        P(("expert", "cuts"), None),
        P(("expert", "cuts"), None),
        P(("expert", "cuts"), None),
        P(("expert", "cuts"), None),
        P(("expert", "cuts")),
        P(("expert", "cuts"), None),
        P(("expert", "cuts"), None),
        P(("expert", "cuts"), None),
        P(("expert", "cuts"), None),
        P("expert", None, "cuts"),
        P("expert", "cuts", None),
    )
    return jax.shard_map(local, mesh=mesh, in_specs=in_specs, out_specs=out_specs, check_vma=False)
```

```python
from functools import partial

import jax
import jax.numpy as jnp
from jax import lax
from jax.experimental import pallas as pl
from jax.experimental.pallas import tpu as pltpu
from jax.sharding import PartitionSpec as P

MESH = pl.DeviceIdType.MESH
score_scale = 0.125
masked_value = -1e30
norm_eps = 1e-05


def plain_dot(left, right):
    return jnp.dot(left, right, preferred_element_type=jnp.float32)


def lead_dot(left, right):
    return lax.dot_general(
        left, right, (((0,), (0,)), ((), ())), preferred_element_type=jnp.float32
    )


def tail_dot(left, right):
    return lax.dot_general(
        left, right, (((1,), (1,)), ((), ())), preferred_element_type=jnp.float32
    )


def head_masks(width, heads):
    lane = lax.broadcasted_iota(jnp.int32, (1, width), 1)
    size = width // heads
    return [((lane >= h * size) & (lane < (h + 1) * size)) for h in range(heads)]


def allowed_mask(docs_ref, docs_col_ref, m, start, rows, keys):
    query_spots = start + lax.broadcasted_iota(jnp.int32, (rows, keys), 0)
    key_spots = lax.broadcasted_iota(jnp.int32, (rows, keys), 1)
    return (key_spots <= query_spots) & (docs_ref[pl.ds(m, 1), 0:keys] == docs_col_ref[m, pl.ds(start, rows), :])


def attend_one(heads, m, qkv_ref, docs_ref, docs_col_ref, att_ref, lse_ref):
    length, width = att_ref.shape[1], att_ref.shape[2]
    rows = min(256, length)
    masks = head_masks(width, heads)
    for block in range(length // rows):
        start, keys = block * rows, (block + 1) * rows
        allowed = allowed_mask(docs_ref, docs_col_ref, m, start, rows, keys)
        query = qkv_ref[m, pl.ds(start, rows), 0:width] * jnp.bfloat16(score_scale)
        key = qkv_ref[m, 0:keys, width : 2 * width]
        value = qkv_ref[m, 0:keys, 2 * width : 3 * width]
        att = jnp.zeros((rows, width), jnp.float32)
        logs = jnp.zeros((rows, width), jnp.float32)
        for mask in masks:
            scores = tail_dot(jnp.where(mask, query, jnp.bfloat16(0)), key)
            scores = jnp.where(allowed, scores, masked_value)
            top = jnp.max(scores, axis=-1, keepdims=True)
            raised = jnp.exp(scores - top)
            total = jnp.sum(raised, axis=-1, keepdims=True)
            probs = (raised * (1.0 / total)).astype(jnp.bfloat16)
            att = jnp.where(mask, plain_dot(probs, value), att)
            logs = jnp.where(mask, top + jnp.log(total), logs)
        att_ref[m, pl.ds(start, rows), :] = att.astype(jnp.bfloat16)
        lse_ref[m, pl.ds(start, rows), :] = logs


def norm_parts(values):
    center = values - jnp.mean(values, axis=-1, keepdims=True)
    spread = jnp.mean(center * center, axis=-1, keepdims=True)
    scale = lax.rsqrt(spread + norm_eps)
    return center * scale, scale


def norm_back(normed, scale, gain, grad):
    inner = grad * gain
    return scale * (
        inner
        - jnp.mean(inner, axis=-1, keepdims=True)
        - normed * jnp.mean(inner * normed, axis=-1, keepdims=True)
    )


def gelu_pair(values):
    phi = 0.5 * (1.0 + lax.erf(values * (0.5**0.5)))
    bell = jnp.exp(-0.5 * values * values) * ((2.0 * jnp.pi) ** -0.5)
    return values * phi, phi + values * bell


def tile_slots(capacity, row_count, tile):
    return -(-capacity * (tile // row_count) // 16) * 16


def token_table(spot, width):
    return (spot == lax.broadcasted_iota(jnp.int32, (spot.shape[0], width), 1)).astype(jnp.bfloat16)


def lane_softmax(logits, lanes, first, count):
    inside = (lanes >= first) & (lanes < first + count)
    raised = jnp.exp(logits - jnp.max(jnp.where(inside, logits, masked_value), axis=-1, keepdims=True))
    raised = jnp.where(inside, raised, 0.0)
    return raised / jnp.sum(raised, axis=-1, keepdims=True)


def route(logits, chosen, expert_count):
    lanes = lax.broadcasted_iota(jnp.int32, logits.shape, 1)
    routed = lane_softmax(logits, lanes, 0, expert_count)
    mixing = lane_softmax(logits, lanes, expert_count, 2)
    pick = lambda values, lane: jnp.sum(jnp.where(lanes == lane, values, 0.0), axis=-1, keepdims=True)
    return pick(routed, chosen), pick(mixing, expert_count), pick(mixing, expert_count + 1), routed, mixing


def softmax_back(probs, grad):
    return probs * (grad - jnp.sum(probs * grad, axis=-1, keepdims=True))


def line_copy(src, dst, send, recv, group, target):
    return pltpu.make_async_remote_copy(
        src_ref=src, dst_ref=dst, send_sem=send, recv_sem=recv, device_id=(group, target), device_id_type=MESH
    )


def greet_all(cut_count, group_count):
    cut = lax.axis_index("cuts")
    group = lax.axis_index("expert")
    barrier = pltpu.get_barrier_semaphore()
    for hop in range(1, cut_count):
        pl.semaphore_signal(barrier, inc=1, device_id=(group, jnp.bitwise_xor(cut, hop)), device_id_type=MESH)
    for hop in range(1, group_count):
        pl.semaphore_signal(barrier, inc=1, device_id=(jnp.bitwise_xor(group, hop), cut), device_id_type=MESH)
    pl.semaphore_wait(barrier, cut_count + group_count - 2)


class LineGather:
    def __init__(self, buf, far_send, far_recv, pair_send, pair_recv, direct=False):
        self.direct = direct
        self.buf = buf
        self.sems = (far_send, far_recv, pair_send, pair_recv)
        self.cut = lax.axis_index("cuts")
        self.group = lax.axis_index("expert")
        self.level, self.side = self.cut // 2, self.cut % 2
        self.levels = buf.shape[1] // 2

    def place(self, n):
        low, high = self.level, self.levels - 1 - self.level
        near = jnp.minimum(low, high)
        paired = n <= 2 * near
        distance = jnp.where(paired, (n + 1) // 2, n - near)
        below = jnp.where(paired, n % 2 == 1, low > high)
        return jnp.where(below, self.level - distance, self.level + distance), below

    def far_copy(self, m, level, target, send):
        block = self.buf.at[m, 2 * level + self.side]
        return line_copy(block, block, self.sems[0].at[m, send], self.sems[1].at[m, level], self.group, target)

    def pair_copy(self, m, level, side):
        block = self.buf.at[m, 2 * level + side]
        return line_copy(
            block, block, self.sems[2].at[m, level], self.sems[3].at[m, level], self.group, jnp.bitwise_xor(self.cut, 1)
        )

    def straight_copy(self, m, n):
        level, _ = self.place(n)
        return self.far_copy(m, self.level, 2 * level + self.side, level)

    def start(self, m):
        if self.direct:
            for n in range(1, self.levels):
                self.straight_copy(m, n).start()
        else:
            @pl.when(self.level + 1 < self.levels)
            def _():
                self.far_copy(m, self.level, self.cut + 2, self.level).start()

            @pl.when(self.level > 0)
            def _():
                self.far_copy(m, self.level, self.cut - 2, self.levels).start()

        self.pair_copy(m, self.level, self.side).start()

    def receive(self, m, n):
        level, _ = self.place(n)
        self.far_copy(m, level, self.cut, level).wait_recv()
        self.pair_copy(m, level, self.side).start()

    def take_pair(self, m, n):
        level, _ = self.place(n)
        self.pair_copy(m, level, 1 - self.side).wait_recv()

    def take(self, m, n):
        level, below = self.place(n)

        @pl.when(n > 0)
        def _():
            target = jnp.where(below, self.cut + 2, self.cut - 2)
            self.far_copy(m, level, target, level).wait_recv()

            @pl.when(jnp.where(below, self.level + 1 < self.levels, self.level > 0))
            def _():
                self.far_copy(m, level, target, level).start()

            self.pair_copy(m, level, self.side).start()

        self.pair_copy(m, level, 1 - self.side).wait_recv()
        return level

    def finish(self, m):
        if self.direct:
            self.pair_copy(m, self.level, self.side).wait_send()
            for n in range(1, self.levels):
                level, _ = self.place(n)
                self.straight_copy(m, n).wait_send()
                self.pair_copy(m, level, self.side).wait_send()
            return

        @pl.when(self.level + 1 < self.levels)
        def _():
            self.far_copy(m, self.level, self.cut + 2, self.level).wait_send()

        @pl.when(self.level > 0)
        def _():
            self.far_copy(m, self.level, self.cut - 2, self.levels).wait_send()

        for n in range(self.levels):
            level, below = self.place(n)
            if n:
                @pl.when(jnp.where(below, self.level + 1 < self.levels, self.level > 0))
                def _():
                    self.far_copy(m, level, self.cut, level).wait_send()

            self.pair_copy(m, level, self.side).wait_send()


class LineSum:
    def __init__(self, part, pair_buf, far_buf, pair_send, pair_recv, send, recv, own=None, direct=False):
        self.direct = direct
        self.part, self.pair_buf, self.far_buf, self.own = part, pair_buf, far_buf, own
        self.sems = (pair_send, pair_recv, send, recv)
        self.cut = lax.axis_index("cuts")
        self.group = lax.axis_index("expert")
        self.level, self.side = self.cut // 2, self.cut % 2
        self.levels = pair_buf.shape[1]

    def pair_copy(self, m, level):
        return line_copy(
            self.part.at[m, 2 * level + 1 - self.side], self.pair_buf.at[m, level], self.sems[0].at[m, level],
            self.sems[1].at[m, level], self.group, jnp.bitwise_xor(self.cut, 1),
        )

    def far_copy(self, m, level, up):
        target = self.cut + 2 if up else self.cut - 2
        slot = level if up else jnp.where(level == self.level - 1, self.levels, level)
        return line_copy(
            self.pair_buf.at[m, level], self.far_buf.at[m, slot], self.sems[2].at[m, level], self.sems[3].at[m, slot],
            self.group, target,
        )

    def arrived(self, m, slot):
        line_copy(
            self.far_buf.at[m, slot], self.far_buf.at[m, slot], self.sems[2].at[m, 0], self.sems[3].at[m, slot],
            self.group, self.cut,
        ).wait_recv()
        return self.far_buf[m, slot].astype(jnp.float32)

    def start(self, m):
        def one(k, carry):
            self.pair_copy(m, jnp.where(k % 2 == 0, self.levels - 1 - k // 2, k // 2)).start()
            return carry

        lax.fori_loop(0, self.levels, one, 0)

    def pairs(self, m):
        def one(k, carry):
            level = jnp.where(k % 2 == 0, self.levels - 1 - k // 2, k // 2)
            self.pair_copy(m, level).wait_recv()
            mine = self.part[m, 2 * level + self.side] if self.own is None else self.own[m, level]
            total = mine.astype(jnp.float32) + self.pair_buf[m, level].astype(jnp.float32)
            self.pair_buf[m, level] = total.astype(self.pair_buf.dtype)
            self.first(m, level)
            return carry

        lax.fori_loop(0, self.levels, one, 0)

    def straight_copy(self, m, level):
        return line_copy(
            self.pair_buf.at[m, level], self.far_buf.at[m, self.level], self.sems[2].at[m, level],
            self.sems[3].at[m, self.level], self.group, 2 * level + self.side,
        )

    def first(self, m, level):
        if self.direct:
            @pl.when(level != self.level)
            def _():
                self.straight_copy(m, level).start()

            return

        @pl.when((self.level == 0) & (level > 0))
        def _():
            self.far_copy(m, level, True).start()

        @pl.when((self.level == self.levels - 1) & (level < self.levels - 1))
        def _():
            self.far_copy(m, level, False).start()

    def pass_on(self, m, level, up):
        @pl.when((level > self.level) if up else (level < self.level))
        def _():
            total = self.pair_buf[m, level].astype(jnp.float32) + self.arrived(m, level)
            self.pair_buf[m, level] = total.astype(self.pair_buf.dtype)
            self.far_copy(m, level, up).start()

    def hop(self, m, j):
        inner = (self.level > 0) & (self.level < self.levels - 1)
        lower = 2 * self.level < self.levels

        @pl.when(inner & lower)
        def _():
            self.pass_on(m, self.levels - 1 - j, True)
            self.pass_on(m, j, False)

        @pl.when(inner & jnp.logical_not(lower))
        def _():
            self.pass_on(m, j, False)
            self.pass_on(m, self.levels - 1 - j, True)

    def finish(self, m, out_ref):
        if self.direct:
            total = self.pair_buf[m, self.level].astype(jnp.float32)
            for k in range(1, self.levels):
                total = total + self.arrived(m, jnp.bitwise_xor(self.level, k))
            out_ref[m] = total
            for k in range(1, self.levels):
                self.straight_copy(m, jnp.bitwise_xor(self.level, k)).wait_send()
            for level in range(self.levels):
                self.pair_copy(m, level).wait_send()
            return

        out_ref[m] = self.pair_buf[m, self.level].astype(jnp.float32)

        @pl.when(self.level > 0)
        def _():
            out_ref[m] = out_ref[m] + self.arrived(m, self.level)

        @pl.when(self.level < self.levels - 1)
        def _():
            out_ref[m] = out_ref[m] + self.arrived(m, self.levels)

        def one(level, carry):
            if self.part is not None:
                self.pair_copy(m, level).wait_send()

            @pl.when(level > self.level)
            def _():
                self.far_copy(m, level, True).wait_send()

            @pl.when(level < self.level)
            def _():
                self.far_copy(m, level, False).wait_send()

            return carry

        lax.fori_loop(0, self.levels, one, 0)


def row_to_column(values):
    return jnp.transpose(values.astype(jnp.float32))


def one_row(ref):
    values = ref[...].astype(jnp.float32)
    return jnp.concatenate([values[k : k + 1] for k in range(values.shape[0])], axis=1)


def stack_small(router_ref, mixer_ref, stage, small):
    count = router_ref.shape[0]
    stage[...] = jnp.zeros_like(stage)
    stage[0:count] = router_ref[...].astype(jnp.float32)
    stage[count : count + 2] = mixer_ref[...].astype(jnp.float32)
    small[...] = stage[...].astype(small.dtype)


def fill_docs(docs_ref, stage, docs_col):
    stage[...] = jnp.zeros_like(stage)
    micro_count = docs_ref.shape[0]
    stage[0:micro_count] = docs_ref[...].astype(jnp.float32)
    for k in range(stage.shape[1] // 128):
        turned = jnp.transpose(stage[:, k * 128 : (k + 1) * 128]).astype(jnp.int32)
        for m in range(micro_count):
            docs_col[m, k * 128 : (k + 1) * 128, :] = turned[:, m : m + 1]


def front_kernel(
    heads, capacity, slots,
    x_ref, gy_ref, gain_ref, gain_two_ref, w_out_ref, w_query_ref, w_key_ref, w_value_ref, docs_ref, ids_ref, slot_ref, kept_ref, expert_in_ref,
    expert_out_ref,
    h_out_ref, qkv_out_ref, lse_out_ref, att_ref, w_qkv_ref, codes_ref, x_two_ref, h_two_ref, weights_ref,
    weights_out_ref, g_all_ref,
    h_all_ref, qkv_ref, lse_ref, w_out, docs_stage, docs_col_ref, att_part, own_code, far_send, far_recv, pair_send, pair_recv, load_sem, swap_send, swap_recv, swap_own, code_send,
    code_recv, weight_send, weight_recv, pass_send, pass_recv, keep_sem,
    g_far_send, g_far_recv, g_pair_send, g_pair_recv, g_own,
):
    micro_count, cut_count, rows, features = h_all_ref.shape
    group_count = weights_ref.shape[0]
    width = features // cut_count
    cut = lax.axis_index("cuts")
    group = lax.axis_index("expert")
    low = jnp.bfloat16
    loads = []
    for k, ref in enumerate((w_query_ref, w_key_ref, w_value_ref)):
        loads.append(pltpu.make_async_copy(
            ref.at[:, pl.ds(pl.multiple_of(cut * width, width), width)], w_qkv_ref.at[:, k * width : (k + 1) * width],
            load_sem.at[k],
        ))
        loads[-1].start()
    loads.append(pltpu.make_async_copy(w_out_ref, w_out, load_sem.at[3]))
    loads[-1].start()
    g_keep = pltpu.make_async_copy(gy_ref, g_all_ref.at[0, cut], g_own)
    g_keep.start()
    gain, gain_two = one_row(gain_ref), one_row(gain_two_ref)
    greet_all(cut_count, group_count)
    g_line = LineGather(g_all_ref, g_far_send, g_far_recv, g_pair_send, g_pair_recv)

    line = LineGather(h_all_ref, far_send, far_recv, pair_send, pair_recv)

    def norm_step(m, carry):
        normed, _ = norm_parts(x_ref[m].astype(jnp.float32))
        h_all_ref[m, cut] = (normed * gain).astype(low)
        line.start(m)
        return carry

    lax.fori_loop(0, micro_count, norm_step, 0)

    square = group_count == 4

    def weight_copy(kind, hop):
        src, dst = ((expert_in_ref, weights_ref), (expert_out_ref, weights_out_ref))[kind]
        return line_copy(
            src, dst.at[group], weight_send.at[kind, hop - 1], weight_recv.at[kind, hop - 1],
            jnp.bitwise_xor(group, hop), cut,
        )

    def pass_copy(k):
        half = pl.ds(k * (features // 2), features // 2)
        block = weights_ref.at[jnp.bitwise_xor(group, 2 - k), half, :]
        return line_copy(block, block, pass_send.at[k], pass_recv.at[k], jnp.bitwise_xor(group, 1 + k), cut)

    weight_hops = [(0, 1), (0, 2)] if square else [(kind, hop) for kind in range(2) for hop in range(1, group_count)]
    for kind, hop in weight_hops:
        weight_copy(kind, hop).start()

    chosen = jnp.where(kept_ref[...] == 1, ids_ref[...], -1)
    spot = jnp.where(kept_ref[...] == 1, ids_ref[...] * slots + cut % 2 * capacity + slot_ref[...], -1)
    own_code[...] = jnp.zeros_like(own_code)
    for m in range(micro_count):
        own_code[m, 0:1] = chosen[m : m + 1]
        own_code[m, 1:2] = spot[m : m + 1]
    codes_ref[cut] = own_code[...]

    def code_copy(hop):
        return line_copy(
            own_code, codes_ref.at[cut], code_send.at[hop], code_recv.at[hop], group, jnp.bitwise_xor(cut, hop)
        )

    for hop in range(1, cut_count):
        code_copy(hop).start()
    fill_docs(docs_ref, docs_stage, docs_col_ref)
    for load in loads[:3]:
        load.wait()

    def tile_step(n, m):
        level = line.take(m, n)
        h_tile = h_all_ref[m, pl.ds(2 * level, 2)].reshape(2 * rows, features)
        spots = pl.ds(pl.multiple_of(level * 2 * rows, 2 * rows), 2 * rows)
        qkv_ref[m, spots, :] = plain_dot(h_tile, w_qkv_ref[...]).astype(low)

    def early(i, carry):
        tile_step(i // micro_count, i % micro_count)
        return carry

    levels = cut_count // 2
    g_keep.wait()
    g_line.start(0)
    lax.fori_loop(0, (levels - 1) * micro_count, early, 0)
    if square:
        for hop in (1, 2):
            weight_copy(0, hop).wait()
        for k in range(2):
            pass_copy(k).start()

    def swap_copy(m, hop):
        target = jnp.bitwise_xor(cut, hop)
        return line_copy(
            att_part.at[m, pl.ds(pl.multiple_of(target * rows, rows), rows), :],
            att_ref.at[m, :, pl.ds(pl.multiple_of(cut * width, width), width)],
            swap_send.at[m, hop], swap_recv.at[m, hop], group, target,
        )

    def swap_keep(m):
        return pltpu.make_async_copy(
            att_part.at[m, pl.ds(pl.multiple_of(cut * rows, rows), rows), :],
            att_ref.at[m, :, pl.ds(pl.multiple_of(cut * width, width), width)],
            swap_own.at[m],
        )

    def late(m, carry):
        tile_step(levels - 1, m)
        attend_one(heads, m, qkv_ref, docs_ref, docs_col_ref, att_part, lse_ref)
        for hop in range(cut_count - 1, 0, -1):
            swap_copy(m, hop).start()
        swap_keep(m).start()

        @pl.when(m == 0)
        def _():
            g_line.take(0, 0)
            g_line.take(0, 1)

        return carry

    lax.fori_loop(0, micro_count, late, 0)
    for n in range(2, levels):
        g_line.take(0, n)
    keeps = [
        pltpu.make_async_copy(src, dst, keep_sem.at[k])
        for k, (src, dst) in enumerate(((h_all_ref, h_out_ref), (qkv_ref, qkv_out_ref), (lse_ref, lse_out_ref)))
    ]
    for keep in keeps:
        keep.start()

    for hop in range(1, cut_count):
        code_copy(hop).wait()
    for m in range(micro_count):
        line.finish(m)
    loads[3].wait()

    def project_step(m, carry):
        for hop in range(cut_count - 1, 0, -1):
            swap_copy(m, hop).wait()
        swap_keep(m).wait()
        x_two = x_ref[m].astype(jnp.float32) + plain_dot(att_ref[m], w_out[...])
        x_two_ref[m] = x_two
        normed, _ = norm_parts(x_two)
        h_two_ref[m] = (normed * gain_two).astype(low)
        return carry

    lax.fori_loop(0, micro_count, project_step, 0)
    g_line.finish(0)
    for keep in keeps:
        keep.wait()
    if square:
        for k in range(2):
            pass_copy(k).wait()
    else:
        for kind, hop in weight_hops:
            weight_copy(kind, hop).wait()


def front(
    x, gy, gain, gain_two, w_output, w_query, w_key, w_value, docs, ids, slot_ids, kept, expert_in, expert_out, group_count, cut_count, heads, capacity,
    slots, call_id,
):
    micro_count, rows, features = x.shape
    length, levels, width = cut_count * rows, cut_count // 2, features // cut_count
    low, f32 = jnp.bfloat16, jnp.float32
    shape = jax.ShapeDtypeStruct
    dma = pltpu.SemaphoreType.DMA
    vmem, far = pl.BlockSpec(memory_space=pltpu.VMEM), pl.BlockSpec(memory_space=pl.ANY)
    return pl.pallas_call(
        partial(front_kernel, heads, capacity, slots),
        out_shape=(
            shape((micro_count, cut_count, rows, features), low),
            shape((micro_count, length, 3 * width), low),
            shape((micro_count, length, width), f32),
            shape((micro_count, rows, features), low),
            shape((features, 3 * width), low),
            shape((cut_count, micro_count, 8, rows), jnp.int32),
            shape((micro_count, rows, features), f32),
            shape((micro_count, rows, features), low),
            shape((group_count, *expert_in.shape), low),
            shape((16, 128) if group_count == 4 else (group_count, *expert_out.shape), low),
            shape((1, cut_count, rows, features), low),
        ),
        in_specs=[vmem, vmem, vmem, vmem, far, far, far, far, vmem, vmem, vmem, vmem, far, far],
        out_specs=[far] * 3 + [vmem] * 5 + [far] * 3,
        scratch_shapes=[
            pltpu.VMEM((micro_count, cut_count, rows, features), low),
            pltpu.VMEM((micro_count, length, 3 * width), low),
            pltpu.VMEM((micro_count, length, width), f32),
            pltpu.VMEM((features, features), low),
            pltpu.VMEM((8, length), f32),
            pltpu.VMEM((micro_count, length, 1), jnp.int32),
            pltpu.VMEM((micro_count, length, width), low),
            pltpu.VMEM((micro_count, 8, rows), jnp.int32),
            dma((micro_count, levels + 1)), dma((micro_count, levels)), dma((micro_count, levels)), dma((micro_count, levels)),
            dma((4,)), dma((micro_count, cut_count)), dma((micro_count, cut_count)), dma((micro_count,)),
            dma((cut_count,)), dma((cut_count,)), dma((2, group_count - 1)), dma((2, group_count - 1)), dma((2,)), dma((2,)),
            dma((3,)), dma((1, levels + 1)), dma((1, levels)), dma((1, levels)), dma((1, levels)), dma(()),
        ],
        compiler_params=pltpu.CompilerParams(collective_id=call_id, has_side_effects=True, vmem_limit_bytes=62 * 2**20),
    )(x, gy, gain, gain_two, w_output, w_query, w_key, w_value, docs, ids, slot_ids, kept, expert_in, expert_out)


def feed_kernel(
    slots, strided, early, stored,
    x_two_ref, h_own_ref, gy_ref, g_first_ref, router_ref, mixer_ref, codes_ref, dense_in_ref, dense_out_ref,
    weights_in_ref, weights_out_ref, expert_in_ref, expert_out_ref,
    output_ref, dh_ref, sums_ref, d_own_in_ref, d_own_out_ref, d_in_ref, d_out_ref, beside_ref, across_ref,
    got_in_ref, got_out_ref, out_rest_ref,
    h_all, g_buf, sent, g_sent, d_sent, hidden_buf, pre_buf, back_buf, side_buf, own_in, own_out, in_buf, out_buf, inner_buf,
    slope_buf, dots, dots_in, pair_buf, far_buf, o_pair_buf, o_far_buf, out_ref, small_stage, small_ref,
    far_send, far_recv, pair_send, pair_recv, g_far_send, g_far_recv, g_pair_send, g_pair_recv,
    line_send, line_recv, two_send, two_recv, o_line_send, o_line_recv, o_two_send, o_two_recv,
    load_sem, in_sem, out_sem, stage_sem, dot_send, dot_recv, weight_send, weight_recv, early_send, early_recv,
):
    micro_count, cut_count, rows, features = h_all.shape
    group_count = weights_in_ref.shape[0]
    share = own_in.shape[1]
    levels, tile = cut_count // 2, 2 * rows
    expert_count = group_count
    cut = lax.axis_index("cuts")
    group = lax.axis_index("expert")
    low, f32 = jnp.bfloat16, jnp.float32
    loads = []
    g_load = pltpu.make_async_copy(g_first_ref.at[0], g_buf.at[0], load_sem.at[2 + 2 * group_count])
    if strided:
        piece = share // group_count
        for g in range(group_count):
            spot = pl.ds(pl.multiple_of((g * cut_count + cut) * piece, piece), piece)
            here = pl.ds(g * piece, piece)
            loads.append(pltpu.make_async_copy(dense_in_ref.at[:, spot], own_in.at[:, here], load_sem.at[len(loads)]))
            loads.append(pltpu.make_async_copy(dense_out_ref.at[spot, :], own_out.at[here, :], load_sem.at[len(loads)]))
    else:
        loads.append(pltpu.make_async_copy(dense_in_ref, own_in, load_sem.at[len(loads)]))
        loads.append(pltpu.make_async_copy(dense_out_ref, own_out, load_sem.at[len(loads)]))
    for load in loads:
        load.start()
    stack_small(router_ref, mixer_ref, small_stage, small_ref)
    g_load.start()
    for m in range(1, micro_count):
        g_buf[m, cut] = gy_ref[m]
    greet_all(cut_count, group_count)
    line = LineGather(h_all, far_send, far_recv, pair_send, pair_recv)
    g_line = LineGather(g_buf, g_far_send, g_far_recv, g_pair_send, g_pair_recv, direct=True)
    for m in range(micro_count):
        h_all[m, cut] = h_own_ref[m]
        line.start(m)

    square = group_count == 4

    def pass_copy(k):
        half = pl.ds(k * (share // 2), share // 2)
        return line_copy(
            beside_ref.at[1 - k, half, :], across_ref.at[half, :], weight_send.at[k], weight_recv.at[k],
            jnp.bitwise_xor(group, 1 + k), cut,
        )

    def beside_copy(k):
        return line_copy(
            expert_out_ref, beside_ref.at[k], weight_send.at[2 + k], weight_recv.at[2 + k], jnp.bitwise_xor(group, 1 + k),
            cut,
        )

    for k in range(2 if square else 0):
        beside_copy(k).start()
    for load in loads:
        load.wait()
    if not stored:
        d_sent = sent
    lanes = lax.broadcasted_iota(jnp.int32, (tile, 128), 1)

    def columns(m, level):
        both = [row_to_column(codes_ref[2 * level + k, m]) for k in range(2)]
        both = jnp.concatenate(both, axis=0).astype(jnp.int32)
        return both[:, 0:1], both[:, 1:2]

    def places(m, level):
        t = m * levels + level
        return (
            pl.ds(2 * level, 2), pl.ds(pl.multiple_of(t * tile, tile), tile), pl.ds(pl.multiple_of(t * slots, slots), slots)
        )

    def dense_step(i, carry):
        n, m = i // micro_count, i % micro_count
        level = line.take(m, n)
        blocks, here, spots = places(m, level)
        h_two = h_all[m, blocks].reshape(tile, features)
        chosen, spot = columns(m, level)
        gate, mix_dense, mix_expert, _, _ = route(tail_dot(h_two, small_ref[...]), chosen, expert_count)
        side_buf[here, :] = jnp.where(lanes == 0, mix_dense, mix_expert * gate)
        rows_sent = lead_dot(token_table(spot, expert_count * slots), h_two).astype(low)
        for e in range(expert_count):
            sent[e, spots, :] = rows_sent[e * slots : (e + 1) * slots]
        act, slope = gelu_pair(plain_dot(h_two, own_in[...]))
        pre_buf[here, :] = slope.astype(low)
        hidden_buf[here, :] = (mix_dense * act).astype(low)
        out_ref[m, blocks] = plain_dot(act.astype(low), own_out[...]).astype(low).reshape(2, rows, features)
        if square:
            @pl.when(i == levels * micro_count - 3)
            def _():
                for k in range(2):
                    beside_copy(k).wait()
                for k in range(2):
                    pass_copy(k).start()

        return carry

    lax.fori_loop(0, levels * micro_count, dense_step, 0)

    def beside(mask):
        return beside_ref.at[mask - 1]

    def load_at(i, mask, own=False, across=False):
        e = jnp.bitwise_xor(group, mask)
        src_in = expert_in_ref if own else weights_in_ref.at[e]
        src_out = expert_out_ref if own else across_ref if across else beside(mask) if square else weights_out_ref.at[e]
        return (
            pltpu.make_async_copy(src_in, in_buf.at[i % 2], in_sem.at[i % 2]),
            pltpu.make_async_copy(src_out, out_buf.at[i % 2], out_sem.at[i % 2]),
        )

    def load_start(i, mask, own=False, across=False):
        for load in load_at(i, mask, own, across):
            load.start()

    def load_wait(i):
        for load in load_at(i, 0, True):
            load.wait()

    load_start(0, 0, True)
    for m in range(1, micro_count):
        g_line.start(m)

    def forward_step(i, carry):
        @pl.when(i + 1 < expert_count - square)
        def _():
            load_start(i + 1, i + 1)

        if square:
            @pl.when(i == 2)
            def _():
                for k in range(2):
                    pass_copy(k).wait()
                load_start(3, 3, across=True)

        load_wait(i)
        e, at = jnp.bitwise_xor(group, i), i % 2
        act, slope = gelu_pair(plain_dot(sent[e], in_buf[at]))
        inner = act.astype(low)
        if stored:
            inner_buf[e] = inner
            slope_buf[e] = slope.astype(low)
        g_sent[e] = plain_dot(inner, out_buf[at]).astype(low)
        return carry

    lax.fori_loop(0, expert_count, forward_step, 0)

    def mask_at(i):
        return group_count - 1 - i

    load_start(0, mask_at(0), across=square)
    out_total = LineSum(out_ref, o_pair_buf, o_far_buf, o_line_send, o_line_recv, o_two_send, o_two_recv, direct=True)

    def mix_step(m, n, carry):
        if m:
            g_line.take_pair(m, n)

        level, _ = line.place(n)
        blocks, here, spots = places(m, level)
        _, spot = columns(m, level)
        table = token_table(spot, expert_count * slots)
        side = side_buf[here, :]
        mix_dense, mix_gate = side[:, 0:1], side[:, 1:2]
        grad_y = g_buf[m, blocks].reshape(tile, features).astype(f32)
        dense = out_ref[m, blocks].reshape(tile, features).astype(f32)
        part = plain_dot(table, jnp.concatenate([g_sent[e, spots, :] for e in range(expert_count)], axis=0))
        out_ref[m, blocks] = (mix_dense * dense + mix_gate * part).astype(low).reshape(2, rows, features)
        d_dense = jnp.sum(grad_y * dense, axis=-1, keepdims=True)
        d_part = jnp.sum(grad_y * part, axis=-1, keepdims=True)
        d_mix = jnp.where(lanes == 0, d_dense, d_part)
        for k in range(2):
            dots[2 * level + k, m] = jnp.transpose(d_mix[k * rows : (k + 1) * rows])[0:8]
        if m == 0:
            out_total.pair_copy(0, level).start()
        d_pre = tail_dot((mix_dense * grad_y).astype(low), own_out[...]) * pre_buf[here, :].astype(f32)
        d_pre = d_pre.astype(low)
        pre_buf[here, :] = d_pre
        back_buf[m, blocks] = tail_dot(d_pre, own_in[...]).astype(low).reshape(2, rows, features)
        rows_back = lead_dot(table, (mix_gate * grad_y).astype(low)).astype(low)
        for e in range(expert_count):
            g_sent[e, spots, :] = rows_back[e * slots : (e + 1) * slots]
        return carry

    def combine_step(m, k, carry):
        level = jnp.where(k % 2 == 0, levels - 1 - k // 2, k // 2)
        blocks, here, spots = places(m, level)
        if stored:
            spots = pl.ds(pl.multiple_of(level * slots, slots), slots)
        _, spot = columns(m, level)
        table = token_table(spot, expert_count * slots)
        rows_back = jnp.concatenate([d_sent[e, spots, :] for e in range(expert_count)], axis=0)
        back_rows = plain_dot(table, rows_back).reshape(2, rows, features)
        back_buf[m, blocks] = (back_buf[m, blocks].astype(f32) + back_rows).astype(low)
        totals[m].pair_copy(m, level).start()
        return carry

    def input_step(m, i, carry):
        @pl.when(i + 2 < expert_count)
        def _():
            load_start(i + 1, mask_at(i + 1))

        @pl.when(i + 2 == expert_count)
        def _():
            load_start(i + 1, 0, True)

        load_wait(i)
        e, at = jnp.bitwise_xor(group, mask_at(i)), i % 2
        spots = pl.ds(m * levels * slots, levels * slots)
        d_pre = (tail_dot(g_sent[e, spots, :], out_buf[at]) * slope_buf[e, spots, :].astype(f32)).astype(low)
        slope_buf[e, spots, :] = d_pre
        d_sent[e] = tail_dot(d_pre, in_buf[at]).astype(low)
        return carry

    totals = [
        LineSum(back_buf, pair_buf, far_buf, line_send, line_recv, two_send, two_recv, direct=m == 0 and stored)
        for m in range(micro_count)
    ]
    g_load.wait()
    out_keep = pltpu.make_async_copy(out_ref.at[pl.ds(1, micro_count - 1)], out_rest_ref, out_sem.at[2])
    for m in range(micro_count):
        if m:
            for n in range(1, levels):
                g_line.receive(m, n)
        lax.fori_loop(0, levels, partial(mix_step, m), 0)
        if m == 0:
            out_total.pairs(0)
        if stored:
            lax.fori_loop(0, expert_count, partial(input_step, m), 0)
            if m + 1 < micro_count:
                load_start(0, mask_at(0), across=square)
            lax.fori_loop(0, levels, partial(combine_step, m), 0)
            totals[m].pairs(m)
    out_keep.start()

    def dot_copy(hop):
        target = jnp.bitwise_xor(cut, hop)
        return line_copy(dots.at[target], dots_in.at[hop - 1], dot_send.at[hop - 1], dot_recv.at[hop - 1], group, target)

    for hop in range(1, cut_count):
        dot_copy(hop).start()

    in_stage, out_stage = own_in, own_out

    def keep_in(i):
        return pltpu.make_async_copy(in_stage, d_in_ref.at[jnp.bitwise_xor(group, mask_at(i))], stage_sem.at[0])

    def keep_out(i):
        return pltpu.make_async_copy(out_stage, d_out_ref.at[jnp.bitwise_xor(group, mask_at(i))], stage_sem.at[1])

    def early_copy(kind):
        src, dst = ((d_in_ref, got_in_ref), (d_out_ref, got_out_ref))[kind]
        return line_copy(
            src.at[jnp.bitwise_xor(group, 3)], dst, early_send.at[kind], early_recv.at[kind],
            jnp.bitwise_xor(group, 1 + kind), cut,
        )

    def keep_step(i):
        @pl.when(i > 0)
        def _():
            keep_in(i).wait()
            keep_out(i).wait()

        if early:
            @pl.when(i == 1)
            def _():
                early_copy(0).start()
                early_copy(1).start()

    def weight_step(i, carry):
        e = jnp.bitwise_xor(group, mask_at(i))
        keep_step(i)
        in_stage[...] = lead_dot(sent[e], slope_buf[e]).astype(low)
        keep_in(i).start()
        out_stage[...] = lead_dot(inner_buf[e], g_sent[e]).astype(low)
        keep_out(i).start()
        return carry

    def backward_step(i, carry):
        @pl.when(i + 2 < expert_count)
        def _():
            load_start(i + 1, mask_at(i + 1))

        @pl.when(i + 2 == expert_count)
        def _():
            load_start(i + 1, 0, True)

        load_wait(i)
        e, at = jnp.bitwise_xor(group, mask_at(i)), i % 2
        rows_in, rows_back = sent[e], g_sent[e]
        act, slope = gelu_pair(plain_dot(rows_in, in_buf[at]))
        d_pre = (tail_dot(rows_back, out_buf[at]) * slope).astype(low)
        keep_step(i)
        in_stage[...] = lead_dot(rows_in, d_pre).astype(low)
        keep_in(i).start()
        out_stage[...] = lead_dot(act.astype(low), rows_back).astype(low)
        keep_out(i).start()
        d_sent[e] = tail_dot(d_pre, in_buf[at]).astype(low)
        return carry

    if stored:
        lax.fori_loop(0, expert_count, weight_step, 0)
    else:
        lax.fori_loop(0, expert_count, backward_step, 0)
        for m in range(micro_count):
            lax.fori_loop(0, levels, partial(combine_step, m), 0)
            totals[m].pairs(m)
    token_rows = micro_count * cut_count * rows
    h_flat, g_flat = h_all.reshape(token_rows, features), g_buf.reshape(token_rows, features)

    def dense_weights(k):
        part = pl.ds(k * 256, 256)
        in_buf[0, part, :] = lead_dot(h_flat[:, part], pre_buf[...]).astype(low)
        out_buf[0, :, part] = lead_dot(hidden_buf[...], g_flat[:, part]).astype(low)

    slices = features // 256
    for k in range(slices):
        dense_weights(k)
        if k == 0 and not stored:
            for j in range(levels - 1):
                totals[0].hop(0, j)
        if k == slices // 2:
            for m in range(1, micro_count):
                totals[m].hop(m, 0)
    own_keep = (
        pltpu.make_async_copy(in_buf.at[0], d_own_in_ref, in_sem.at[0]),
        pltpu.make_async_copy(out_buf.at[0], d_own_out_ref, out_sem.at[0]),
    )
    for keep in own_keep:
        keep.start()
    for m in range(1, micro_count):
        for j in range(1, levels - 1):
            totals[m].hop(m, j)
    sums = dots[cut]
    for hop in range(1, cut_count):
        dot_copy(hop).wait()
        sums = sums + dots_in[hop - 1]
    sums_ref[...] = sums
    keep_in(0).wait()
    keep_out(0).wait()
    for kind in range(2 if early else 0):
        early_copy(kind).wait()
    for keep in own_keep:
        keep.wait()
    out_keep.wait()
    for m in range(micro_count):
        line.finish(m)
        if m:
            g_line.finish(m)
    out_total.finish(0, dh_ref)
    output_ref[...] = (x_two_ref[0] + dh_ref[0]).astype(low)
    for m in range(micro_count):
        totals[m].finish(m, dh_ref)


def feed(
    x_two, h_own, gy, g_first, router, mixer, codes, dense_in, dense_out, weights_in, weights_out, expert_in,
    expert_out, share, slots, strided, early, call_id,
):
    micro_count, rows, features = x_two.shape
    cut_count = codes.shape[0]
    group_count = weights_in.shape[0]
    levels, total = cut_count // 2, micro_count * cut_count * rows
    low, f32 = jnp.bfloat16, jnp.float32
    shape = jax.ShapeDtypeStruct
    dma = pltpu.SemaphoreType.DMA
    block = lambda *dims: pltpu.VMEM(dims, low)
    vmem, far = pl.BlockSpec(memory_space=pltpu.VMEM), pl.BlockSpec(memory_space=pl.ANY)
    whole = (micro_count, cut_count, rows, features)
    stored = group_count <= 4
    slot_rows = micro_count * levels * slots
    line = (micro_count, levels)
    return pl.pallas_call(
        partial(feed_kernel, slots, strided, early, stored),
        out_shape=(
            shape((rows, features), low),
            shape((micro_count, rows, features), f32),
            shape((micro_count, 8, rows), f32),
            shape((features, share), low),
            shape((share, features), low),
            shape((group_count, features, share), low),
            shape((group_count, share, features), low),
            shape((2, share, features) if group_count == 4 else (16, 128), low),
            shape((share, features) if group_count == 4 else (16, 128), low),
            *(
                (shape((features, share), low), shape((share, features), low))
                if early else (shape((8, 128), low), shape((8, 128), low))
            ),
            shape((micro_count - 1, cut_count, rows, features), low),
        ),
        in_specs=[vmem, vmem, vmem, far, vmem, vmem, vmem, far, far, far, far, far, far],
        out_specs=[vmem] * 3 + [far] * 9,
        scratch_shapes=[
            block(*whole), block(*whole),
            block(group_count, slot_rows, features), block(group_count, slot_rows, features),
            block(group_count, slot_rows // micro_count, features) if stored else block(16, 128),
            block(total, share), block(total, share), block(*whole), pltpu.VMEM((total, 128), f32),
            block(features, share), block(share, features), block(2, features, share), block(2, share, features),
            *([block(group_count, slot_rows, share)] * 2 if stored else [block(16, 128)] * 2),
            pltpu.VMEM((cut_count, micro_count, 8, rows), f32), pltpu.VMEM((cut_count - 1, micro_count, 8, rows), f32),
            block(*line, rows, features), block(micro_count, levels + 1, rows, features),
            block(1, levels, rows, features), block(1, levels + 1, rows, features), block(*whole),
            pltpu.VMEM((128, features), f32), block(128, features),
            *[dma((micro_count, levels + 1)), dma(line), dma(line), dma(line)] * 2,
            *[dma(line), dma(line), dma(line), dma((micro_count, levels + 1))] * 2,
            dma((3 + 2 * group_count,)), dma((2,)), dma((3,)), dma((2,)),
            dma((cut_count - 1,)), dma((cut_count - 1,)), dma((4,)), dma((4,)), dma((4,)), dma((4,)),
        ],
        compiler_params=pltpu.CompilerParams(collective_id=call_id, has_side_effects=True, vmem_limit_bytes=62 * 2**20),
    )(x_two, h_own, gy, g_first, router, mixer, codes, dense_in, dense_out, weights_in, weights_out, expert_in, expert_out)


def attend_back_one(heads, m, qkv_ref, docs_ref, docs_col_ref, lse_ref, back_ref, out_ref, key_acc, value_acc):
    length, width = back_ref.shape[1], back_ref.shape[2]
    rows = min(256, length)
    masks = head_masks(width, heads)
    key_acc[...] = jnp.zeros_like(key_acc)
    value_acc[...] = jnp.zeros_like(value_acc)
    zero = jnp.bfloat16(0)
    for block in range(length // rows):
        start, keys = block * rows, (block + 1) * rows
        allowed = allowed_mask(docs_ref, docs_col_ref, m, start, rows, keys)
        query = qkv_ref[m, pl.ds(start, rows), 0:width] * jnp.bfloat16(score_scale)
        key = qkv_ref[m, 0:keys, width : 2 * width]
        value = qkv_ref[m, 0:keys, 2 * width : 3 * width]
        back = back_ref[m, pl.ds(start, rows), :]
        logs = lse_ref[m, pl.ds(start, rows), :]
        query_grad = jnp.zeros((rows, width), jnp.float32)
        for h, mask in enumerate(masks):
            one_query = jnp.where(mask, query, zero)
            one_back = jnp.where(mask, back, zero)
            scores = jnp.where(allowed, tail_dot(one_query, key), masked_value)
            spot = h * (width // heads)
            probs = jnp.exp(scores - logs[:, spot : spot + 1])
            weighted = probs * tail_dot(one_back, value)
            delta = jnp.sum(weighted, axis=-1, keepdims=True)
            score_grad = (weighted - probs * delta).astype(jnp.bfloat16)
            query_grad = jnp.where(mask, plain_dot(score_grad, key), query_grad)
            key_acc[0:keys, :] += lead_dot(score_grad, one_query)
            value_acc[0:keys, :] += lead_dot(probs.astype(jnp.bfloat16), one_back)
        out_ref[m, pl.ds(start, rows), 0:width] = (query_grad * score_scale).astype(jnp.bfloat16)
    out_ref[m, :, width : 2 * width] = key_acc[...].astype(jnp.bfloat16)
    out_ref[m, :, 2 * width : 3 * width] = value_acc[...].astype(jnp.bfloat16)


def back_kernel(
    heads, expert_count, sums_here,
    dh_ref, dots_ref, codes_ref, h_ref, x_two_ref, gy_ref, att_far, w_out_far, docs_ref,
    x_far, gain_one_ref, gain_two_ref, router_ref, mixer_ref, own_in_far, own_out_far,
    qkv_far, lse_far, w_qkv_far, h_all_far, out_part, w_query_ref, w_key_ref, w_value_ref, d_in_ref, d_out_ref,
    got_in_ref, got_out_ref,
    output_ref, tokens_ref, wo_ref, tiny_ref, query_out_ref, key_out_ref, value_out_ref, in_out_ref, out_out_ref, late_in_ref,
    late_out_ref, direct_in_ref, direct_out_ref,
    att_ref, w_out_ref, x_ref, own_in_ref, own_out_ref, eager_sem, qkv_ref, lse_ref, w_qkv_ref, h_all_ref, w_rows, docs_stage, docs_col_ref, small_stage, small_ref, out_own, out_pair,
    out_far, g_att, d_att, back_all, d_qkv, key_acc, value_acc, d_small, part, pair_buf, far_buf, d_h_one, in_sum, out_sum,
    wo_part, qkv_part, wo_in, qkv_in, own_in_got, own_out_got, own_in_sum, own_out_sum, own_in_in, own_out_in, wo_mid, wo_pair, wo_far, wo_sum, qkv_mid, in_mid, qkv_end, in_end,
    pair_send, pair_recv, far_send, far_recv, swap_send, swap_recv, swap_own, one_send, one_recv, two_send, two_recv, two_own,
    late_send, late_recv, late_load_sem, load_sem,
    wo_pair_send, wo_pair_recv, wo_far_send, wo_far_recv, own_sem, o_pair_send, o_pair_recv, o_far_send, o_far_recv,
    direct_send, direct_recv, own_send, own_recv,
):
    micro_count, cut_count, rows, features = part.shape
    group_count, split, _ = qkv_part.shape[:3]
    piece_rows = qkv_part.shape[2]
    group_rows = split * piece_rows
    sides, side_rows = wo_part.shape[1:3]
    width = features // cut_count
    cut = lax.axis_index("cuts")
    group = lax.axis_index("expert")
    low, f32 = jnp.bfloat16, jnp.float32
    levels = cut_count // 2
    place = (group * cut_count + cut) * piece_rows
    loads = [
        pltpu.make_async_copy(src, dst, load_sem.at[k])
        for k, (src, dst) in enumerate(
            ((qkv_far, qkv_ref), (lse_far, lse_ref), (w_qkv_far, w_qkv_ref), (h_all_far, h_all_ref))
        )
    ]
    if sums_here:
        own_rows = pl.ds(pl.multiple_of(place, piece_rows), piece_rows)
        for k, ref in enumerate((w_query_ref, w_key_ref, w_value_ref)):
            loads.append(pltpu.make_async_copy(ref.at[own_rows, :], w_rows.at[k], load_sem.at[4 + k]))
    eager = [
        pltpu.make_async_copy(src, dst, eager_sem.at[k])
        for k, (src, dst) in enumerate((
            (own_in_far, own_in_ref), (own_out_far, own_out_ref), (w_out_far, w_out_ref), (att_far, att_ref), (x_far, x_ref)
        ))
    ]
    for load in eager + loads:
        load.start()

    rest = micro_count - 1

    def own_load(m, level):
        return pltpu.make_async_copy(out_part.at[m, 2 * level + cut % 2], out_own.at[m, level], own_sem.at[m, level])

    for m in range(rest):
        for level in range(levels):
            own_load(m, level).start()
    stack_small(router_ref, mixer_ref, small_stage, small_ref)
    fill_docs(docs_ref, docs_stage, docs_col_ref)
    greet_all(cut_count, group_count if sums_here else 1)
    for load in eager:
        load.wait()
    out_line = LineSum(out_part, out_pair, out_far, o_pair_send, o_pair_recv, o_far_send, o_far_recv, out_own, direct=True)

    ones = (None, None, (wo_part, wo_in), (qkv_part, qkv_in))

    def one_copy(kind, hop):
        src, dst = ones[kind]
        target = jnp.bitwise_xor(group, hop)
        return line_copy(
            src.at[target, cut % 2] if kind == 2 else src.at[target], dst.at[hop - 1], one_send.at[kind, hop - 1], one_recv.at[kind, hop - 1], target, cut
        )

    def one_start(kind):
        for hop in range(1, group_count):
            one_copy(kind, hop).start()

    def one_finish(kind):
        src, dst = ones[kind]
        total = (src[group, cut % 2] if kind == 2 else src[group]).astype(f32)
        for hop in range(1, group_count):
            one_copy(kind, hop).wait_recv()
            total = total + dst[hop - 1].astype(f32)
        for hop in range(1, group_count):
            one_copy(kind, hop).wait_send()
        return total

    owns = (
        (own_in_ref, own_in_got, own_in_sum, own_in_in, 1), (own_out_ref, own_out_got, own_out_sum, own_out_in, 2)
    )

    def own_first(kind, k):
        own, got, _, _, side = owns[kind]
        return line_copy(
            own.at[jnp.bitwise_xor(group, 3 if k else side)], got.at[k], own_send.at[kind, k], own_recv.at[kind, k],
            jnp.bitwise_xor(group, side), cut,
        )

    def own_second(kind):
        _, _, total, far, side = owns[kind]
        return line_copy(
            total, far, own_send.at[kind, 2], own_recv.at[kind, 2], jnp.bitwise_xor(group, 3 - side), cut
        )

    def own_start(kind):
        own, got, total, _, side = owns[kind]
        own_first(kind, 1).wait()
        total[...] = (own[jnp.bitwise_xor(group, 3 - side)].astype(f32) + got[1].astype(f32)).astype(low)
        own_second(kind).start()

    def own_finish(kind):
        own, got, _, far, _ = owns[kind]
        own_first(kind, 0).wait()
        own_second(kind).wait()
        return own[group].astype(f32) + got[0].astype(f32) + far[...].astype(f32)

    twos = ((in_mid, in_end), None, None, (qkv_mid, qkv_end))

    def two_copy(kind, hop):
        src, dst = twos[kind]
        target = jnp.bitwise_xor(cut, hop)
        return line_copy(src.at[target], dst.at[cut], two_send.at[kind, hop], two_recv.at[kind, hop], group, target)

    def two_keep(kind):
        src, dst = twos[kind]
        return pltpu.make_async_copy(src.at[cut], dst.at[cut], two_own.at[kind])

    def two_start(kind):
        for hop in range(cut_count - 1, 0, -1):
            two_copy(kind, hop).start()
        two_keep(kind).start()

    def two_finish(kind):
        for hop in range(cut_count - 1, 0, -1):
            two_copy(kind, hop).wait()
        two_keep(kind).wait()

    ends = ((d_in_ref, got_in_ref, in_sum, late_in_ref, 2), (d_out_ref, got_out_ref, out_sum, late_out_ref, 1))

    def late_load(kind, k):
        own, got, total, _, side = ends[kind]
        src = got if k else own.at[jnp.bitwise_xor(group, side)]
        return pltpu.make_async_copy(src, total.at[k], late_load_sem.at[kind, k])

    def late_copy(kind):
        _, _, total, late, side = ends[kind]
        return line_copy(
            total.at[0], late, late_send.at[kind], late_recv.at[kind], jnp.bitwise_xor(group, side), cut
        )

    if sums_here:
        for kind in range(2):
            late_load(kind, 0).start()
            late_load(kind, 1).start()
        for k in (1, 0):
            for kind in range(2):
                own_first(kind, k).start()

    def swap_copy(m, hop):
        target = jnp.bitwise_xor(cut, hop)
        return line_copy(
            d_att.at[m, :, pl.ds(pl.multiple_of(target * width, width), width)],
            back_all.at[m, pl.ds(pl.multiple_of(cut * rows, rows), rows), :],
            swap_send.at[m, hop], swap_recv.at[m, hop], group, target,
        )

    def swap_keep(m):
        return pltpu.make_async_copy(
            d_att.at[m, :, pl.ds(pl.multiple_of(cut * width, width), width)],
            back_all.at[m, pl.ds(pl.multiple_of(cut * rows, rows), rows), :],
            swap_own.at[m],
        )

    small = small_ref[...]
    gain_one, gain_two = one_row(gain_one_ref), one_row(gain_two_ref)
    d_small[...] = jnp.zeros_like(d_small)
    lanes = lax.broadcasted_iota(jnp.int32, (rows, 128), 1)

    def norm_two_step(m, carry):
        dots = jnp.transpose(dots_ref[m])
        chosen = row_to_column(codes_ref[cut, m])[:, 0:1].astype(jnp.int32)
        h_two = h_ref[m]
        gate, _, mix_expert, routed, mixing = route(tail_dot(h_two, small), chosen, expert_count)
        d_mixing = jnp.where(lanes == expert_count, dots[:, 0:1], gate * dots[:, 1:2])
        d_gate = jnp.where(lanes == chosen, mix_expert * dots[:, 1:2], 0.0)
        d_logits = (softmax_back(mixing, d_mixing) + softmax_back(routed, d_gate)).astype(low)
        d_h = dh_ref[m] + plain_dot(d_logits, small)
        normed, scale = norm_parts(x_two_ref[m])
        one_lane = (lanes == expert_count + 2).astype(low)
        d_small[...] += lead_dot(h_two, d_logits) + lead_dot((d_h * normed).astype(low), one_lane)
        d_x = gy_ref[m].astype(f32) + norm_back(normed, scale, gain_two, d_h)
        tokens_ref[m] = d_x
        grad = d_x.astype(low)
        g_att[pl.ds(pl.multiple_of(m * rows, rows), rows), :] = grad
        d_att[m] = tail_dot(grad, w_out_ref[...]).astype(low)
        for hop in range(cut_count - 1, 0, -1):
            swap_copy(m, hop).start()
        swap_keep(m).start()
        return carry

    lax.fori_loop(0, micro_count, norm_two_step, 0)
    for m in range(rest):
        out_line.start(m)

    def wo_step(g, carry):
        columns = pl.ds(pl.multiple_of(g * group_rows, group_rows), group_rows)
        grads = lead_dot(att_ref[:, columns], g_att[...]).astype(low)
        smalls = d_small[columns, :].astype(low)
        for side in range(sides):
            for k in range(side_rows):
                part_rows = slice((k * sides + side) * piece_rows, (k * sides + side + 1) * piece_rows)
                wo_part[g, side, k, :, 0:features] = grads[part_rows]
                wo_part[g, side, k, :, features : features + 128] = smalls[part_rows]
        return carry

    lax.fori_loop(0, group_count, wo_step, 0)
    def wo_pair_copy(g):
        return line_copy(
            wo_part.at[g, 1 - cut % 2], wo_pair.at[g], wo_pair_send.at[g], wo_pair_recv.at[g], group,
            jnp.bitwise_xor(cut, 1),
        )

    def wo_pair_step(g, carry):
        wo_pair_copy(g).wait()
        wo_part[g, cut % 2] = (wo_part[g, cut % 2].astype(f32) + wo_pair[g].astype(f32)).astype(low)
        return carry

    def direct_copy(kind):
        src, dst = ((d_in_ref, direct_in_ref), (d_out_ref, direct_out_ref))[kind]
        target = jnp.bitwise_xor(group, 1 + kind)
        return line_copy(src.at[target], dst, direct_send.at[kind], direct_recv.at[kind], target, cut)

    if sums_here:
        for g in range(group_count):
            wo_pair_copy(g).start()
        lax.fori_loop(0, group_count, wo_pair_step, 0)
        one_start(2)
        for kind in range(2):
            own_start(kind)
        for kind in range(2):
            direct_copy(kind).start()
    for load in loads[:3]:
        load.wait()
    line = LineSum(part, pair_buf, far_buf, pair_send, pair_recv, far_send, far_recv)

    def attend_step(m, carry):
        for hop in range(cut_count - 1, 0, -1):
            swap_copy(m, hop).wait()
        swap_keep(m).wait()

        @pl.when(m == 0)
        def _():
            for k in range(rest):
                for level in range(levels):
                    own_load(k, level).wait()
                out_line.pairs(k)

        attend_back_one(heads, m, qkv_ref, docs_ref, docs_col_ref, lse_ref, back_all, d_qkv, key_acc, value_acc)
        for k in range(levels):
            level = levels - 1 - k // 2 if k % 2 == 0 else k // 2
            for c in (2 * level, 2 * level + 1):
                part[m, c] = tail_dot(d_qkv[m, c * rows : (c + 1) * rows, :], w_qkv_ref[...]).astype(low)
            line.pair_copy(m, level).start()
        line.pairs(m)
        return carry

    lax.fori_loop(0, micro_count, attend_step, 0)

    def qkv_step(g, carry):
        columns = pl.ds(pl.multiple_of(g * group_rows, group_rows), group_rows)
        grads = jnp.zeros((group_rows, 3 * width), f32)
        for m in range(micro_count):
            grads = grads + lead_dot(h_all_ref[m, :, columns], d_qkv[m])
        qkv_part[g] = grads.astype(low).reshape(split, piece_rows, 3 * width)
        return carry

    for j in range(levels - 1):
        line.hop(0, j)
    for load in loads[3:]:
        load.wait()
    lax.fori_loop(0, group_count, qkv_step, 0)
    if sums_here:
        one_start(3)
        for kind in range(2):
            total = ends[kind][2]
            late_load(kind, 0).wait()
            late_load(kind, 1).wait()
            total[0] = (total[0].astype(f32) + total[1].astype(f32)).astype(low)
            late_copy(kind).start()
    for m in range(1, micro_count):
        for j in range(levels - 1):
            line.hop(m, j)

    def norm_one_step(m, carry):
        line.finish(m, d_h_one)
        total = d_h_one[m]
        normed, scale = norm_parts(x_ref[m].astype(f32))
        tokens_ref[m] = tokens_ref[m] + norm_back(normed, scale, gain_one, total)
        return carry

    for m in range(rest):
        out_line.finish(m, d_h_one)
        output_ref[m] = (x_two_ref[1 + m] + d_h_one[m]).astype(low)
    if not sums_here:
        lax.fori_loop(0, micro_count, norm_one_step, 0)
        wo_ref[...] = wo_part[...]
        query_out_ref[...] = qkv_part[...]
        return
    in_mid[...] = own_finish(0).astype(low)
    two_start(0)
    wo_line = LineSum(None, wo_mid, wo_far, None, None, wo_far_send, wo_far_recv)
    wo_mid[0] = one_finish(2).astype(low)
    for k in range(levels):
        wo_line.first(0, levels - 1 - k // 2 if k % 2 == 0 else k // 2)
    norm_one_step(0, 0)
    qkv_mid[...] = one_finish(3).astype(low)
    two_start(3)
    out_out_ref[...] = own_finish(1)
    for j in range(levels - 1):
        wo_line.hop(0, j)
    for m in range(1, micro_count):
        norm_one_step(m, 0)
    two_finish(0)
    share_piece = in_end.shape[2] // group_count
    for c in range(cut_count):
        for g in range(group_count):
            spot = (g * cut_count + c) * share_piece
            in_out_ref[:, spot : spot + share_piece] = in_end[c, :, g * share_piece : (g + 1) * share_piece].astype(f32)
    wo_line.finish(0, wo_sum)
    wo_ref[...] = wo_sum[0, :, :features]
    small_sums = wo_sum[0, :, features:]
    two_finish(3)
    norm = jnp.zeros((piece_rows, 1), f32)
    outs = (query_out_ref, key_out_ref, value_out_ref)
    for c in range(cut_count):
        for k in range(3):
            grad = qkv_end[c, :, k * width : (k + 1) * width].astype(f32)
            outs[k][:, c * width : (c + 1) * width] = grad
            weights = w_rows[k, :, c * width : (c + 1) * width].astype(f32)
            norm = norm + jnp.sum(grad * weights, axis=-1, keepdims=True)
    spots = lax.broadcasted_iota(jnp.int32, (piece_rows, features), 1)
    mine = spots == place + lax.broadcasted_iota(jnp.int32, (piece_rows, features), 0)
    norm = norm / jnp.sum(jnp.where(mine, gain_one, 0.0), axis=-1, keepdims=True)
    tiny_lanes = lax.broadcasted_iota(jnp.int32, (piece_rows, 128), 1)
    tiny_ref[...] = jnp.where(tiny_lanes == expert_count + 3, norm, small_sums)
    for kind in range(2):
        late_copy(kind).wait()
        direct_copy(kind).wait()


def back(
    dh, dots, codes, h_two, x_two, gy, attended, w_output, docs, x, gain_one, gain_two, router, mixer, own_in, own_out,
    qkv, lse, w_qkv, h_all, out_rest, w_query, w_key, w_value, d_in, d_out, got_in, got_out, heads, expert_count, sums_here,
    call_id,
):
    micro_count, rows, features = x.shape
    length = qkv.shape[1]
    cut_count = length // rows
    width = features // cut_count
    group_count = own_out.shape[0]
    piece_rows = features // (group_count * cut_count)
    share, piece = own_in.shape[3], own_out.shape[1]
    low, f32 = jnp.bfloat16, jnp.float32
    levels = cut_count // 2
    wide = features + 128
    shape = jax.ShapeDtypeStruct
    parts = (group_count, 2, levels, piece_rows) if sums_here else (features // 256, 1, 1, 256)
    flat = (group_count, cut_count, piece_rows) if sums_here else (features // 256, 1, 256)
    tokens = (micro_count, rows, features)
    none = shape((16, 128), low)
    if sums_here:
        outs = (
            shape((micro_count - 1, rows, features), low),
            shape(tokens, f32), shape((piece_rows, features), f32), shape((piece_rows, 128), f32),
            *[shape((piece_rows, features), f32)] * 3, shape((piece_rows, share * cut_count), f32),
            shape((piece, features), f32), *[shape((features, share), low), shape((share, features), low)] * 2,
        )
    else:
        outs = (
            shape((micro_count - 1, rows, features), low),
            shape(tokens, f32), shape((*parts, wide), low), none, shape((*flat, 3 * width), low),
            *[none] * 8,
        )
    peers = max(group_count - 1, 1) if sums_here else 1
    block = lambda *dims: pltpu.VMEM(dims, low)
    mids = lambda w: block(cut_count, piece_rows, w) if sums_here else block(16, 128)
    ins = lambda w: block(peers, cut_count, piece_rows, w) if sums_here else block(16, 128)
    dma = pltpu.SemaphoreType.DMA
    line = (micro_count, levels)
    vmem, far = pl.BlockSpec(memory_space=pltpu.VMEM), pl.BlockSpec(memory_space=pl.ANY)
    operands = (
        dh, dots, codes, h_two, x_two, gy, attended, w_output, docs, x, gain_one, gain_two, router, mixer, own_in, own_out,
        qkv, lse, w_qkv, h_all, out_rest, w_query, w_key, w_value, d_in, d_out, got_in, got_out,
    )
    rest = (micro_count - 1, levels)
    return pl.pallas_call(
        partial(back_kernel, heads, expert_count, sums_here),
        out_shape=outs,
        in_specs=[far if k in (6, 7, 9, 14, 15) else vmem for k in range(16)] + [far] * 12,
        out_specs=[vmem] * 9 + [far] * 4,
        scratch_shapes=[
            *[block(*given.shape) for given in (attended, w_output, x, own_in, own_out)], dma((5,)),
            block(micro_count, length, 3 * width), pltpu.VMEM((micro_count, length, width), f32), block(features, 3 * width),
            block(micro_count, length, features), block(3, piece_rows, features), pltpu.VMEM((8, length), f32),
            pltpu.VMEM((micro_count, length, 1), jnp.int32), pltpu.VMEM((128, features), f32), block(128, features),
            block(*rest, rows, features), block(*rest, rows, features), block(micro_count - 1, levels + 1, rows, features),
            block(micro_count * rows, features),
            block(micro_count, rows, features),
            block(micro_count, length, width),
            block(micro_count, length, 3 * width),
            pltpu.VMEM((length, width), f32),
            pltpu.VMEM((length, width), f32),
            pltpu.VMEM((features, 128), f32),
            block(micro_count, cut_count, rows, features),
            block(*line, rows, features),
            block(micro_count, levels + 1, rows, features),
            pltpu.VMEM(tokens, f32),
            *((block(2, features, share), block(2, share, features)) if sums_here else (block(16, 128), block(16, 128))),
            block(*parts, wide),
            block(*flat, 3 * width),
            block(peers, levels, piece_rows, wide) if sums_here else block(16, 128), ins(3 * width),
            *(
                [block(2, cut_count, piece_rows, share), block(2, piece, features)]
                + [block(cut_count, piece_rows, share), block(piece, features)] * 2
                if sums_here else [block(16, 128)] * 6
            ),
            *(
                (
                    block(1, levels, piece_rows, wide), block(group_count, levels, piece_rows, wide),
                    block(1, levels + 1, piece_rows, wide), pltpu.VMEM((1, piece_rows, wide), f32),
                )
                if sums_here else [block(16, 128)] * 4
            ),
            mids(3 * width), mids(share), mids(3 * width), mids(share),
            dma(line), dma(line), dma(line), dma((micro_count, levels + 1)),
            dma((micro_count, cut_count)), dma((micro_count, cut_count)), dma((micro_count,)),
            dma((4, peers)), dma((4, peers)), dma((4, cut_count)), dma((4, cut_count)), dma((4,)),
            dma((2,)), dma((2,)), dma((2, 2)), dma((7,)),
            dma((group_count,)), dma((group_count,)), dma((1, levels)), dma((1, levels + 1)),
            dma(rest), dma(rest), dma(rest), dma(rest), dma((micro_count - 1, levels + 1)),
            dma((2,)), dma((2,)), dma((2, 3)), dma((2, 3)),
        ],
        compiler_params=pltpu.CompilerParams(
            collective_id=call_id, has_side_effects=True, vmem_limit_bytes=62 * 2**20
        ),
    )(*operands)


def last_kernel(
    expert_count, d_in_ref, got_in_ref, late_in_ref, d_out_ref, got_out_ref, late_out_ref, tiny_ref, *refs,
):
    passed = (len(refs) - 6 - 10 - 1) // 3
    given, refs = refs[: passed + 1], refs[passed + 1 :]
    taken, refs = refs[:passed], refs[passed:]
    held, refs = refs[-passed:], refs[:-passed]
    router_ref, mixer_ref, norm_one_ref, norm_two_ref, sum_in_ref, sum_out_ref = refs[:6]
    in_buf, out_buf, in_sum, out_sum, in_sem, out_sem, in_done, out_done, pass_sem, keep_sem = refs[6:]
    group = lax.axis_index("expert")
    held_parts = (held[0].at[0], held[0].at[pl.ds(1, held[0].shape[0] - 1)], *held[1:])
    passes = [pltpu.make_async_copy(src, dst, pass_sem.at[k]) for k, (src, dst) in enumerate(zip(given, held_parts))]
    keeps = [pltpu.make_async_copy(src, dst, keep_sem.at[k]) for k, (src, dst) in enumerate(zip(held, taken))]
    chunks = in_sem.shape[0]
    work = []
    for ends in (
        ((d_in_ref.at[group], got_in_ref, late_in_ref), in_buf, in_sum, sum_in_ref, in_sem, in_done),
        ((d_out_ref.at[group], got_out_ref, late_out_ref), out_buf, out_sum, sum_out_ref, out_sem, out_done),
    ):
        sources, buf, total, target, sem, done = ends
        step = buf.shape[1] // chunks
        for k in range(chunks):
            part = pl.ds(k * step, step)
            loads = [
                pltpu.make_async_copy(src.at[part, :], buf.at[at, part, :], sem.at[k, at]) for at, src in enumerate(sources)
            ]
            work.append((loads, buf, total, part, pltpu.make_async_copy(total.at[part, :], target.at[part, :], done.at[k])))
    for copy in passes:
        copy.start()
    for loads, *_ in work:
        for load in loads:
            load.start()
    turned = jnp.transpose(tiny_ref[...])
    router_ref[...] = turned[0:expert_count]
    mixer_ref[...] = turned[expert_count : expert_count + 2]
    norm_two_ref[...] = turned[expert_count + 2 : expert_count + 3]
    norm_one_ref[...] = turned[expert_count + 3 : expert_count + 4]
    passes[0].wait()
    for copy, keep in zip(passes[1:], keeps):
        copy.wait()
        keep.start()
    for loads, buf, total, part, keep in work:
        for load in loads:
            load.wait()
        total[part, :] = sum(buf[at, part, :].astype(jnp.float32) for at in range(3))
        keep.start()
    for *_, keep in work:
        keep.wait()
    for keep in keeps:
        keep.wait()


def last(d_in, got_in, late_in, d_out, got_out, late_out, tiny, others, expert_count):
    f32, dma = jnp.float32, pltpu.SemaphoreType.DMA
    shape = jax.ShapeDtypeStruct
    piece_rows = tiny.shape[0]
    micro_count = 1 + others[1].shape[0]
    whole = [shape((micro_count, *others[0].shape), others[0].dtype), *[shape(x.shape, x.dtype) for x in others[2:]]]
    vmem, far = pl.BlockSpec(memory_space=pltpu.VMEM), pl.BlockSpec(memory_space=pl.ANY)
    chunks = 4
    return pl.pallas_call(
        partial(last_kernel, expert_count),
        out_shape=(
            *whole, shape((expert_count, piece_rows), f32), shape((2, piece_rows), f32),
            shape((1, piece_rows), f32), shape((1, piece_rows), f32), shape(late_in.shape, f32), shape(late_out.shape, f32),
        ),
        in_specs=[far] * 6 + [vmem] + [far] * len(others),
        out_specs=[far] * len(whole) + [vmem] * 4 + [far] * 2,
        scratch_shapes=[
            pltpu.VMEM((3, *late_in.shape), late_in.dtype), pltpu.VMEM((3, *late_out.shape), late_out.dtype),
            pltpu.VMEM(late_in.shape, f32), pltpu.VMEM(late_out.shape, f32),
            dma((chunks, 3)), dma((chunks, 3)), dma((chunks,)), dma((chunks,)), dma((len(others),)), dma((len(others),)),
            *[pltpu.VMEM(x.shape, x.dtype) for x in whole],
        ],
        compiler_params=pltpu.CompilerParams(vmem_limit_bytes=62 * 2**20),
    )(d_in, got_in, late_in, d_out, got_out, late_out, tiny, *others)


def local(
    tokens, cotangent, segments, expert_ids, slot_ids, kept_mask, norm1_gain, w_query, w_key, w_value, w_output,
    norm2_gain, dense_in, dense_out, router, mixer, expert_in, expert_out,
):
    micro_count, row_count, features = tokens.shape[1:]
    cut_count = lax.axis_size("cuts")
    group_count = lax.axis_size("expert")
    cut = lax.axis_index("cuts")
    group = lax.axis_index("expert")
    length = cut_count * row_count
    head_width = features // cut_count
    heads = head_width // 64
    expert_count = router.shape[1]
    hidden_count = dense_in.shape[1]
    share = hidden_count // cut_count
    piece = share // group_count
    capacity = max(2, row_count * 5 // (4 * expert_count))
    slots = tile_slots(capacity, row_count, 2 * row_count)
    rows = features // (group_count * cut_count)
    sums_here = rows % 16 == 0 and group_count == 4
    by_rows = lambda v: v.reshape(-1, 128)
    router_t, mixer_t = router.T, mixer.T
    f32, low = jnp.float32, jnp.bfloat16

    strided = piece % 128 == 0
    if strided:
        own_in, own_out = dense_in, dense_out
    else:
        own_in = lax.dynamic_index_in_dim(
            dense_in.reshape(features, group_count, cut_count, piece), cut, 2, keepdims=False
        ).reshape(features, share)
        own_out = lax.dynamic_index_in_dim(
            dense_out.reshape(group_count, cut_count, piece, features), cut, 1, keepdims=False
        ).reshape(share, features)
    h_all, qkv, lse, attended, w_qkv, codes, x_two, h_two, weights_in, weights_out, g_first = front(
        tokens[0], cotangent[0, 0], by_rows(norm1_gain), by_rows(norm2_gain), w_output, w_query, w_key, w_value, segments[0], expert_ids[0], slot_ids[0],
        kept_mask[0], expert_in[0], expert_out[0], group_count, cut_count, heads, capacity, slots, 1,
    )
    first_output, d_h2, dots, d_own_in, d_own_out, d_in, d_out, _, _, got_in, got_out, out_rest = feed(
        x_two, h_two, cotangent[0], g_first, router_t, mixer_t, codes, own_in, own_out, weights_in,
        weights_out, expert_in[0], expert_out[0], share, slots, strided, sums_here, 2,
    )
    rest_output, grad_tokens, grad_output, tiny, grad_query, grad_key, grad_value, grad_dense_in, grad_dense_out, late_in, late_out, *direct = back(
        d_h2, dots, codes, h_two, x_two, cotangent[0], attended.reshape(-1, features), w_output, segments[0], tokens[0],
        by_rows(norm1_gain), by_rows(norm2_gain), router_t, mixer_t, d_own_in.reshape(group_count, cut_count, rows, share),
        d_own_out.reshape(group_count, piece, features), qkv, lse, w_qkv, h_all.reshape(micro_count, length, features),
        out_rest, w_query, w_key, w_value, d_in, d_out, got_in, got_out, heads, expert_count, sums_here, 3,
    )
    sum_groups = lambda part: lax.psum_scatter(
        part.reshape(-1, part.shape[-1]), "expert", scatter_dimension=0, tiled=True
    )
    if sums_here:
        others = (
            first_output, rest_output, grad_tokens, grad_query, grad_key, grad_value, grad_output, grad_dense_in, grad_dense_out
        )
        *others, grad_router, grad_mixer, grad_norm1, grad_norm2, grad_expert_in, grad_expert_out = last(
            d_in, direct[0], late_in, d_out, direct[1], late_out, tiny, others, expert_count
        )
        output, grad_tokens, grad_query, grad_key, grad_value, grad_output, grad_dense_in, grad_dense_out = others
        grad_router, grad_mixer, grad_norm1, grad_norm2 = grad_router.T, grad_mixer.T, grad_norm1[0], grad_norm2[0]
    else:
        swap = lambda part: lax.all_to_all(
            part.reshape(cut_count, rows, -1), "cuts", split_axis=0, concat_axis=0
        ).astype(f32)
        output = jnp.concatenate([first_output[None], rest_output])
        wide = jnp.sum(swap(sum_groups(grad_output)), axis=0)
        grad_output, grad_small = wide[:, :features], wide[:, features:]
        grad_router, grad_mixer = grad_small[:, :expert_count], grad_small[:, expert_count : expert_count + 2]
        grad_norm2 = grad_small[:, expert_count + 2]
        grad_qkv = swap(sum_groups(grad_query)).reshape(cut_count, rows, 3, head_width).transpose(2, 1, 0, 3)
        grad_qkv = grad_qkv.reshape(3, rows, features)
        grad_query, grad_key, grad_value = grad_qkv
        grad_dense_in = swap(sum_groups(d_own_in)).reshape(cut_count, rows, group_count, piece).transpose(1, 2, 0, 3)
        grad_dense_in = grad_dense_in.reshape(rows, hidden_count)
        grad_dense_out = sum_groups(d_own_out).astype(f32)
        grad_expert_in = sum_groups(d_in).astype(f32)
        grad_expert_out = sum_groups(d_out).astype(f32)
        place = (group * cut_count + cut) * rows
        own_rows = lambda w: lax.dynamic_slice_in_dim(w, place, rows, 0).astype(f32)
        grad_norm1 = sum(
            jnp.sum(own_rows(w) * grad_qkv[k], axis=-1) for k, w in enumerate((w_query, w_key, w_value))
        ) / own_rows(norm1_gain)
    return (
        output[None], grad_tokens[None], grad_norm1, grad_query, grad_key, grad_value, grad_output, grad_norm2, grad_dense_in,
        grad_dense_out, grad_router, grad_mixer, grad_expert_in[None], grad_expert_out[None],
    )


def solution(mesh):
    in_specs = (
        P("expert", None, "cuts", None),
        P("expert", None, "cuts", None),
        P("expert", None, None),
        P("expert", None, "cuts"),
        P("expert", None, "cuts"),
        P("expert", None, "cuts"),
        P(),
        P(),
        P(),
        P(),
        P(),
        P(),
        P(),
        P(),
        P(),
        P(),
        P("expert", None, "cuts"),
        P("expert", "cuts", None),
    )
    out_specs = (
        P("expert", None, "cuts", None),
        P("expert", None, "cuts", None),
        P(("expert", "cuts")),
        P(("expert", "cuts"), None),
        P(("expert", "cuts"), None),
        P(("expert", "cuts"), None),
        P(("expert", "cuts"), None),
        P(("expert", "cuts")),
        P(("expert", "cuts"), None),
        P(("expert", "cuts"), None),
        P(("expert", "cuts"), None),
        P(("expert", "cuts"), None),
        P("expert", None, "cuts"),
        P("expert", "cuts", None),
    )
    return jax.shard_map(local, mesh=mesh, in_specs=in_specs, out_specs=out_specs, check_vma=False)
```
